32 devices in a mesh: tok: 16 (over z, y, core), head: 2 (over x).
Axes of the slice: x: 2, y: 2, z: 4, core: 2. Of those that a mesh axis runs over, the one named last changes fastest.
Arguments:
- query_rows: bfloat16 [4096, 40, 128], P('tok', 'head'), as said below
- key_rows: bfloat16 [4096, 40, 128], P('tok', 'head'), as said below
- value_rows: bfloat16 [4096, 40, 128], P('tok', 'head'), may hold values from -6 to 6
- query_gain: float32 [40, 128], P('head'), may hold values from 1.5 to 4
- key_gain: float32 [40, 128], P('head'), may hold values from 0.25 to 1.75
- rate_in: float32 [40, 4096], P('head', 'tok'), may hold values from 0.05 to 0.5
- rate_out: float32 [40, 4096], P('head', 'tok'), may hold values from 0.0002 to 0.002
- fast_in: bfloat16 [40, 128, 512], P('head'), may hold values from -6 to 6
- fast_out: bfloat16 [40, 256, 128], P('head'), may hold values from -0.375 to 0.375
- half_window: int32 [40], P('head'), may hold values from 128 to 1024, as said below
- boundaries: int32 [3], replicated, may hold values from 2049 to 4095, as said below
Outputs:
- layer_out: bfloat16 [4096, 40, 128], P('tok', 'head')
The draws below stay inside these ranges and needn't reach their ends.
Inputs may be any that keep to these rules, and one draw needn't show every extreme that they name: `half_window`: no head sees more than 1024 tokens on either side; some head has exactly 1024 and some head exactly 128. `boundaries`: non-decreasing; the first is 2049 and the last 4095. `query_rows`: entries within -400 and 400. `key_rows`: entries within -400 and 400.
All inputs are finite; a program needn't handle non-finite values.
Results may differ from the reference program's by a relative error of at most 0.02.
Values may be sent and summed in bfloat16 or wider, within the bound.
No kernel may reach another device: no remote copies, remote signals or barrier semaphores. Data moves between devices by JAX's collectives and lax.ppermute only.
A program may use at most 128 MiB of HBM per device.

```python
import math
import jax
import jax.numpy as jnp
from jax import lax

HEADS = 40
HEAD_DIM = 128
FAST_HID = 256
HALF = 1024
BOUNDS = 3
TOKENS = 4096


def pair_rows(key):
    base_key = jax.random.fold_in(key, 7)
    key_draw, query_draw = jax.random.split(base_key, 2)
    full_shape = (TOKENS, HEADS, HEAD_DIM)
    key_part = jnp.clip(jax.random.normal(key_draw, full_shape, jnp.float32), -6.0, 6.0)
    query_part = jnp.clip(jax.random.normal(query_draw, full_shape, jnp.float32), -6.0, 6.0)
    head_ramp = jnp.sqrt(1.0 + 2.0 * jnp.arange(HEADS, dtype=jnp.float32) / (HEADS - 1))
    key_part = key_part * head_ramp[None, :, None]
    query_part = query_part * head_ramp[None, :, None]
    return (query_part, key_part)


def draw_query_rows(key, part):
    return pair_rows(key)[0].astype(jnp.bfloat16)


def draw_key_rows(key, part):
    return pair_rows(key)[1].astype(jnp.bfloat16)


def draw_half_window(key, part):
    widths = jax.random.randint(jax.random.fold_in(key, 21), (HEADS,), HALF // 8, HALF + 1)
    widest = jax.random.randint(jax.random.fold_in(key, 22), (), 0, HEADS)
    offset = jax.random.randint(jax.random.fold_in(key, 23), (), 1, HEADS)
    narrowest = (widest + offset) % HEADS
    head_ids = jnp.arange(HEADS)
    widths = jnp.where(head_ids == narrowest, HALF // 8, widths)
    return jnp.where(head_ids == widest, HALF, widths).astype(jnp.int32)


def draw_boundaries(key, part):
    starts = jax.random.randint(jax.random.fold_in(key, 31), (BOUNDS,), 2 * HALF + 1, TOKENS)
    starts = jnp.sort(starts)
    slot_ids = jnp.arange(BOUNDS, dtype=jnp.int32)
    starts = jnp.where(slot_ids == 0, 2 * HALF + 1, starts)
    starts = jnp.where(slot_ids == BOUNDS - 1, TOKENS - 1, starts)
    return starts.astype(jnp.int32)


def steps_of(stream_key, dims, cuts, low, top_value):
    gain = 1.0
    for dim, blocks in cuts:
        steps = jax.random.uniform(jax.random.fold_in(jax.random.fold_in(stream_key, 6), dim), (blocks,), jnp.float32, low / len(cuts), top_value / len(cuts))
        gain = gain * jnp.repeat(jnp.exp(steps), dims[dim] // blocks).reshape((-1,) + (1,) * (len(dims) - 1 - dim))
    return gain


def gaussian(rng, dims, deviation, reach, cuts=(), kind=jnp.bfloat16):
    level = steps_of(rng, dims, cuts, -0.22, 0.18) if cuts else 1.0
    values = jax.random.normal(rng, dims, jnp.float32) * deviation * level
    return jnp.minimum(jnp.maximum(values, -reach), reach).astype(kind)


def setup_inputs(seed: int = 0) -> dict:
    key_list = jax.random.split(jax.random.key(seed), 12)
    query_rows = draw_query_rows(jax.random.fold_in(key_list[11], 71), 0)
    key_rows = draw_key_rows(jax.random.fold_in(key_list[11], 71), 0)
    value_rows = gaussian(key_list[2], (TOKENS, HEADS, HEAD_DIM), 1.0, 6.0, ((0, 16), (1, 2)))
    query_gain = jnp.clip(jnp.exp(math.log(4.0) - 0.98082925 * jax.random.uniform(key_list[3], (HEADS, HEAD_DIM), jnp.float32) ** steps_of(key_list[3], (HEADS, HEAD_DIM), ((0, 2),), -0.2, 0.2)), 1.5, 4.0)
    key_gain = jnp.clip(1.0 + 0.15 * jax.random.normal(key_list[4], (HEADS, HEAD_DIM), jnp.float32), 0.25, 1.75)
    rate_in = jnp.clip(jnp.exp(math.log(0.5) - 2.3025851 * jax.random.uniform(key_list[5], (HEADS, TOKENS), jnp.float32) ** steps_of(key_list[5], (HEADS, TOKENS), ((0, 2), (1, 16)), -0.2, 0.2)), 0.05, 0.5)
    rate_out = jnp.clip(jnp.exp(math.log(0.002) - 2.3025852 * jax.random.uniform(key_list[6], (HEADS, TOKENS), jnp.float32) ** steps_of(key_list[6], (HEADS, TOKENS), ((0, 2), (1, 16)), -0.2, 0.2)), 0.0002, 0.002)
    fast_in = gaussian(key_list[7], (HEADS, HEAD_DIM, 2 * FAST_HID), 1.0, 6.0, ((0, 2),))
    fast_out = gaussian(key_list[8], (HEADS, FAST_HID, HEAD_DIM), FAST_HID ** -0.5, 0.375, ((0, 2),))
    half_window = draw_half_window(jax.random.fold_in(key_list[11], 71), 0)
    boundaries = draw_boundaries(jax.random.fold_in(key_list[11], 71), 0)
    return {"query_rows": query_rows, "key_rows": key_rows, "value_rows": value_rows, "query_gain": query_gain, "key_gain": key_gain, "rate_in": rate_in, "rate_out": rate_out, "fast_in": fast_in, "fast_out": fast_out, "half_window": half_window, "boundaries": boundaries}


epsilon = 1e-06

def clip_of(places, boundaries):
    return lax.optimization_barrier(jnp.sum((places[:, None] >= boundaries[None, :]).astype(jnp.int32), axis=1))

def rms_rows(matrix, gain_row):
    as_float = matrix.astype(jnp.float32)
    mean_sq = lax.optimization_barrier(jnp.mean(as_float * as_float, axis=(1, 2), keepdims=True))
    return (as_float * lax.rsqrt(mean_sq + epsilon) * gain_row[None].astype(jnp.float32)).astype(jnp.bfloat16)

def unit_rows(matrix):
    as_float = matrix.astype(jnp.float32)
    return (as_float * lax.rsqrt(lax.optimization_barrier(jnp.sum(as_float * as_float, axis=-1, keepdims=True)) + epsilon)).astype(jnp.bfloat16)

def attend_head(query_head, key_head, value_head, half_reach, boundaries):
    block_rows = math.gcd(TOKENS, 512)
    zero_rows = jnp.zeros((HALF, HEAD_DIM), key_head.dtype)
    key_pad = jnp.concatenate([zero_rows, key_head, zero_rows], axis=0)
    value_pad = jnp.concatenate([zero_rows, value_head, zero_rows], axis=0)
    key_span = block_rows + 2 * HALF
    scaling = 1.0 / math.sqrt(HEAD_DIM)

    def one_block(block_index):
        first_row = (block_index * block_rows).astype(jnp.int32)
        query_block = lax.dynamic_slice_in_dim(query_head, first_row, block_rows, 0)
        key_block = lax.dynamic_slice_in_dim(key_pad, first_row, key_span, 0)
        value_block = lax.dynamic_slice_in_dim(value_pad, first_row, key_span, 0)
        scores = jnp.dot(query_block, key_block.T, preferred_element_type=jnp.float32) * scaling
        query_places = first_row + jnp.arange(block_rows, dtype=jnp.int32)
        key_places = first_row - HALF + jnp.arange(key_span, dtype=jnp.int32)
        inside = (key_places >= 0) & (key_places < TOKENS)
        same_clip = clip_of(query_places, boundaries)[:, None] == clip_of(key_places, boundaries)[None, :]
        allowed = (jnp.abs(query_places[:, None] - key_places[None, :]) <= half_reach) & inside[None, :] & same_clip
        masked = jnp.where(allowed, scores, -jnp.inf)
        row_max = lax.optimization_barrier(jnp.max(masked, axis=1, keepdims=True))
        weights = jnp.exp(masked - row_max)
        denominator = lax.optimization_barrier(jnp.sum(weights, axis=1, keepdims=True))
        return jnp.dot(weights.astype(jnp.bfloat16), value_block, preferred_element_type=jnp.float32) / denominator
    blocks = lax.map(one_block, jnp.arange(TOKENS // block_rows, dtype=jnp.int32))
    return blocks.reshape(TOKENS, HEAD_DIM)

def renormed(initial, gradient):
    base = initial.astype(jnp.float32)
    updated = base - gradient
    base_norm = jnp.sqrt(lax.optimization_barrier(jnp.sum(base * base, axis=0)))
    factor = base_norm / jnp.sqrt(lax.optimization_barrier(jnp.sum(updated * updated, axis=0)) + epsilon)
    return (updated * factor[None, :]).astype(jnp.bfloat16)

def fast_head(query_unit, key_unit, value_head, rate_in_head, rate_out_head, fast_in_head, fast_out_head):
    pre_keys = jnp.dot(key_unit, fast_in_head, preferred_element_type=jnp.float32)
    gate_part = pre_keys[:, :FAST_HID]
    lin_part = pre_keys[:, FAST_HID:]
    sigmoid_gate = jax.nn.sigmoid(gate_part)
    swish_gate = gate_part * sigmoid_gate
    hidden = (swish_gate * lin_part).astype(jnp.bfloat16)
    value_float = value_head.astype(jnp.float32)
    push_out = (-rate_out_head[:, None] * value_float).astype(jnp.bfloat16)
    push_in = (-rate_in_head[:, None] * value_float).astype(jnp.bfloat16)
    grad_out = jnp.dot(hidden.T, push_out, preferred_element_type=jnp.float32)
    hidden_grad = jnp.dot(push_in, fast_out_head.T, preferred_element_type=jnp.float32)
    d_gate = hidden_grad * lin_part * sigmoid_gate * (1.0 + gate_part * (1.0 - sigmoid_gate))
    d_lin = hidden_grad * swish_gate
    d_pre = jnp.concatenate([d_gate, d_lin], axis=1).astype(jnp.bfloat16)
    grad_in = jnp.dot(key_unit.T, d_pre, preferred_element_type=jnp.float32)
    new_in = renormed(fast_in_head, grad_in)
    new_out = renormed(fast_out_head, grad_out)
    pre_query = jnp.dot(query_unit, new_in, preferred_element_type=jnp.float32)
    query_hidden = (jax.nn.silu(pre_query[:, :FAST_HID]) * pre_query[:, FAST_HID:]).astype(jnp.bfloat16)
    return jnp.dot(query_hidden, new_out, preferred_element_type=jnp.float32)

def reference(query_rows, key_rows, value_rows, query_gain, key_gain, rate_in, rate_out, fast_in, fast_out, half_window, boundaries):
    q_normed = rms_rows(query_rows, query_gain)
    k_normed = rms_rows(key_rows, key_gain)
    query_unit = unit_rows(q_normed)
    key_unit = unit_rows(k_normed)

    def per_head(head_items):
        q_head, k_head, v_head, qu_head, ku_head, rin_head, rout_head, fin_head, fout_head, half_reach = head_items
        attended = attend_head(q_head, k_head, v_head, half_reach, boundaries)
        fast_result = fast_head(qu_head, ku_head, v_head, rin_head, rout_head, fin_head, fout_head)
        return (attended + fast_result).astype(jnp.bfloat16)
    heads_first = (jnp.transpose(q_normed, (1, 0, 2)), jnp.transpose(k_normed, (1, 0, 2)), jnp.transpose(value_rows, (1, 0, 2)), jnp.transpose(query_unit, (1, 0, 2)), jnp.transpose(key_unit, (1, 0, 2)), rate_in, rate_out, fast_in, fast_out, half_window)
    result = lax.map(per_head, heads_first)
    return jnp.transpose(result, (1, 0, 2))
```

```python
import functools
import math

import jax
import jax.numpy as jnp
from jax import lax
from jax.experimental import pallas as pl
from jax.experimental.pallas import tpu as pltpu
from jax.sharding import PartitionSpec as P

HALF = 1024


epsilon = 1e-06


def passed_along(x, axis, by):
    peers = lax.axis_size(axis)
    pairs = [(i, i + by) for i in range(peers) if 0 <= i + by < peers]
    return lax.ppermute(x, axis, pairs)


def unit_rows(matrix):
    as_float = matrix.astype(jnp.float32)
    return (
        as_float * lax.rsqrt(jnp.sum(as_float * as_float, axis=-1, keepdims=True) + epsilon)
    ).astype(jnp.bfloat16)


def rescale(updated, base_norm, squares):
    return (updated * (base_norm / jnp.sqrt(squares + epsilon))[:, None, :]).astype(jnp.bfloat16)


def sliding_body(
    query_rows,
    key_rows,
    value_rows,
    query_gain,
    key_gain,
    rate_in,
    rate_out,
    fast_in,
    fast_out,
    half_window,
    boundaries,
):
    tok_rows = query_rows.shape[0]
    local_heads = query_rows.shape[1]
    head_dim = query_rows.shape[2]
    fast_hid = fast_out.shape[1]
    width_all = local_heads * head_dim * lax.axis_size("head")
    tok_count = tok_rows * lax.axis_size("tok")
    own_index = lax.axis_index("tok")
    first_row = own_index * tok_rows
    query_float = query_rows.astype(jnp.float32)
    key_float = key_rows.astype(jnp.float32)
    query_sq, key_sq = lax.psum(
        (
            jnp.sum(query_float * query_float, axis=(1, 2)),
            jnp.sum(key_float * key_float, axis=(1, 2)),
        ),
        "head",
    )
    q_normed = (
        query_float * lax.rsqrt(query_sq / width_all + epsilon)[:, None, None] * query_gain[None]
    ).astype(jnp.bfloat16)
    k_normed = (
        key_float * lax.rsqrt(key_sq / width_all + epsilon)[:, None, None] * key_gain[None]
    ).astype(jnp.bfloat16)

    def clip_of(places):
        return jnp.sum((places[:, None] >= boundaries[None, :]).astype(jnp.int32), axis=1)

    positions = first_row + jnp.arange(tok_rows, dtype=jnp.int32)
    query_clip = clip_of(positions)
    scaling = 1.0 / math.sqrt(head_dim)

    def absorb(state_now, block_keys, block_values, key_first):
        best, denominator, accum = state_now
        key_places = key_first + jnp.arange(tok_rows, dtype=jnp.int32)
        scores = (
            jnp.einsum("qhd,khd->hqk", q_normed, block_keys, preferred_element_type=jnp.float32)
            * scaling
        )
        inside = (key_places >= 0) & (key_places < tok_count)
        pair_ok = (query_clip[:, None] == clip_of(key_places)[None, :]) & inside[None, :]
        distance = jnp.abs(positions[:, None] - key_places[None, :])
        allowed = (distance[None, :, :] <= half_window[:, None, None]) & pair_ok[None, :, :]
        masked = jnp.where(allowed, scores, -jnp.inf)
        new_best = jnp.maximum(best, jnp.max(masked, axis=2))
        weights = jnp.exp(masked - new_best[:, :, None])
        shrink = jnp.exp(best - new_best)
        denominator = denominator * shrink + jnp.sum(weights, axis=2)
        accum = accum * shrink[:, :, None] + jnp.einsum(
            "hqk,khd->hqd",
            weights.astype(jnp.bfloat16),
            block_values,
            preferred_element_type=jnp.float32,
        )
        return (new_best, denominator, accum)

    start_state = (
        jnp.full((local_heads, tok_rows), -jnp.inf, jnp.float32),
        jnp.zeros((local_heads, tok_rows), jnp.float32),
        jnp.zeros((local_heads, tok_rows, head_dim), jnp.float32),
    )
    state_now = absorb(start_state, k_normed, value_rows, first_row)
    reach_blocks = HALF // tok_rows
    for distance_step in range(1, reach_blocks + 1):
        left_keys, left_values = passed_along((k_normed, value_rows), "tok", distance_step)
        state_now = absorb(state_now, left_keys, left_values, first_row - distance_step * tok_rows)
        right_keys, right_values = passed_along((k_normed, value_rows), "tok", -distance_step)
        state_now = absorb(
            state_now, right_keys, right_values, first_row + distance_step * tok_rows
        )
    attended = state_now[2] / state_now[1][:, :, None]
    key_unit = unit_rows(k_normed)
    query_unit = unit_rows(q_normed)
    pre_keys = jnp.einsum("thd,hdf->htf", key_unit, fast_in, preferred_element_type=jnp.float32)
    gate_part = pre_keys[:, :, :fast_hid]
    lin_part = pre_keys[:, :, fast_hid:]
    sigmoid_gate = jax.nn.sigmoid(gate_part)
    swish_gate = gate_part * sigmoid_gate
    hidden = (swish_gate * lin_part).astype(jnp.bfloat16)
    value_float = value_rows.astype(jnp.float32)
    push_out = (-jnp.transpose(rate_out)[:, :, None] * value_float).astype(jnp.bfloat16)
    push_in = (-jnp.transpose(rate_in)[:, :, None] * value_float).astype(jnp.bfloat16)
    grad_out = jnp.einsum("htf,thd->hfd", hidden, push_out, preferred_element_type=jnp.float32)
    hidden_grad = jnp.einsum("thd,hfd->htf", push_in, fast_out, preferred_element_type=jnp.float32)
    d_gate = hidden_grad * lin_part * sigmoid_gate * (1.0 + gate_part * (1.0 - sigmoid_gate))
    d_lin = hidden_grad * swish_gate
    d_pre = jnp.concatenate([d_gate, d_lin], axis=2).astype(jnp.bfloat16)
    grad_in = jnp.einsum("thd,htf->hdf", key_unit, d_pre, preferred_element_type=jnp.float32)
    in_float = fast_in.astype(jnp.float32)
    out_float = fast_out.astype(jnp.float32)
    in_base = jnp.sqrt(jnp.sum(in_float * in_float, axis=1))
    out_base = jnp.sqrt(jnp.sum(out_float * out_float, axis=1))
    summed_in, summed_out = lax.psum((grad_in, grad_out), "tok")
    updated_in = in_float - summed_in
    updated_out = out_float - summed_out
    new_in = rescale(updated_in, in_base, jnp.sum(updated_in * updated_in, axis=1))
    new_out = rescale(updated_out, out_base, jnp.sum(updated_out * updated_out, axis=1))
    pre_query = jnp.einsum("thd,hdf->htf", query_unit, new_in, preferred_element_type=jnp.float32)
    query_gate = pre_query[:, :, :fast_hid]
    query_hidden = (query_gate * jax.nn.sigmoid(query_gate) * pre_query[:, :, fast_hid:]).astype(
        jnp.bfloat16
    )
    fast_result = jnp.einsum(
        "htf,hfd->htd", query_hidden, new_out, preferred_element_type=jnp.float32
    )
    combined = attended + fast_result
    return jnp.transpose(combined, (1, 0, 2)).astype(jnp.bfloat16)


VMEM_BYTES = 56 * 1024 * 1024
HIDDEN_MASK = -1e30
NT = (((1,), (1,)), ((), ()))


def exchanged(x, pairs):
    return lax.ppermute(x, "tok", pairs)


def nt_dot(a, b):
    return lax.dot_general(a, b, NT, preferred_element_type=jnp.float32)


def nn_dot(a, b):
    return jnp.dot(a, b, preferred_element_type=jnp.float32)


def params(**more):
    return pltpu.CompilerParams(vmem_limit_bytes=VMEM_BYTES, **more)


def pack_kernel(peers, rate_rows, place_ref, q_scale_ref, k_scale_ref, *refs):
    inputs, outputs = refs[: 7 * peers], refs[7 * peers : 9 * peers]
    aux_ref = refs[-1]
    rows = q_scale_ref.shape[0]
    q_scale = q_scale_ref[...]
    k_scale = k_scale_ref[...]
    for p in range(peers):
        q_ref, k_ref, v_ref, q_gain_ref, k_gain_ref, rate_in_ref, rate_out_ref = inputs[
            7 * p : 7 * p + 7
        ]
        kv_out, q_out = outputs[2 * p : 2 * p + 2]
        q = (q_ref[0].astype(jnp.float32) * q_scale * q_gain_ref[0]).astype(jnp.bfloat16)
        k = (k_ref[0].astype(jnp.float32) * k_scale * k_gain_ref[0]).astype(jnp.bfloat16)
        v = v_ref[0]
        q_out[0] = q
        kv_out[0, 0:rows, :] = k
        kv_out[0, rows : 2 * rows, :] = v
        aux_ref[...] = jnp.zeros_like(aux_ref)
        at = 0
        for rate_ref in (rate_in_ref, rate_out_ref):
            rate = rate_ref[0]
            high = rate.astype(jnp.bfloat16).astype(jnp.float32)
            aux_ref[at : at + rate_rows, :] = high
            aux_ref[at + rate_rows : at + 2 * rate_rows, :] = rate - high
            at += 2 * rate_rows
        aux_ref[at : at + 1, :] = q[0:8].astype(jnp.float32)[0:1]
        aux_ref[at + 1 : at + 2, :] = k[0:8].astype(jnp.float32)[0:1]
        aux_ref[at + 2 : at + 3, :] = v[0:8].astype(jnp.float32)[0:1]
        kv_out[0, 2 * rows :, :] = aux_ref[...].astype(jnp.bfloat16)


def pack(place, q_scale, k_scale, q, k, v, q_gain, k_gain, rate_in, rate_out, peers, aux_rows):
    heads, rows, dim = q.shape
    share = heads // peers
    rate_rows = rows // 128

    def head_of(p):
        return lambda j, place: ((place[0] ^ p) * share + j, 0, 0)

    whole = pl.BlockSpec((rows, dim), lambda j, place: (0, 0))
    in_specs = [whole, whole]
    operands = [q_scale, k_scale]
    out_specs, out_shape = [], []
    kv_rows = 2 * rows + aux_rows
    for p in range(peers):
        for array in (q, k, v, q_gain, k_gain, rate_in, rate_out):
            in_specs.append(pl.BlockSpec((1,) + array.shape[1:], head_of(p)))
            operands.append(array)
        for out_rows in (kv_rows, rows):
            out_specs.append(pl.BlockSpec((1, out_rows, dim), lambda j, place: (j, 0, 0)))
            out_shape.append(jax.ShapeDtypeStruct((share, out_rows, dim), jnp.bfloat16))
    outs = pl.pallas_call(
        functools.partial(pack_kernel, peers, rate_rows),
        out_shape=out_shape,
        grid_spec=pltpu.PrefetchScalarGridSpec(
            num_scalar_prefetch=1,
            grid=(share,),
            in_specs=in_specs,
            out_specs=out_specs,
            scratch_shapes=[pltpu.VMEM((aux_rows, dim), jnp.float32)],
        ),
        compiler_params=params(),
        name="pack",
    )(place, *operands)
    return outs[0::2], outs[1::2]


def grads_kernel(rows, rate_rows, place_ref, in_t_ref, out_ref, *refs):
    blocks, grad_ref = refs[:-1], refs[-1]
    hid = out_ref.shape[1]
    part = hid // 2
    core = place_ref[1]
    own = pl.multiple_of(core * part, part)
    in_half = jnp.concatenate(
        [in_t_ref[0, pl.ds(own, part), :], in_t_ref[0, pl.ds(hid + own, part), :]], axis=0
    )
    out_half = out_ref[0, pl.ds(own, part), :]
    sum_in = jnp.zeros((2 * part, in_half.shape[1]), jnp.float32)
    sum_out = jnp.zeros((part, in_half.shape[1]), jnp.float32)
    for block in blocks:
        k = block[0, 0:rows, :].astype(jnp.float32)
        v = block[0, rows : 2 * rows, :]
        aux = block[0, 2 * rows :, :].astype(jnp.float32)

        def rate(at):
            both = aux[at : at + rate_rows] + aux[at + rate_rows : at + 2 * rate_rows]
            return jnp.concatenate([both[i : i + 1] for i in range(rate_rows)], axis=1)

        rate_in, rate_out = rate(0), rate(2 * rate_rows)
        unit = (k * lax.rsqrt(jnp.sum(k * k, axis=1, keepdims=True) + epsilon)).astype(
            jnp.bfloat16
        )
        pre = nt_dot(in_half, unit)
        gate, lin = pre[:part], pre[part:]
        sig = jax.nn.sigmoid(gate)
        swish = gate * sig
        pushed = (swish * lin * -rate_out).astype(jnp.bfloat16)
        hidden_grad = nt_dot(out_half, v) * -rate_in
        d_gate = hidden_grad * lin * sig * (1.0 + gate * (1.0 - sig))
        d_lin = hidden_grad * swish
        d_pre = jnp.concatenate([d_gate, d_lin], axis=0).astype(jnp.bfloat16)
        sum_in += nn_dot(d_pre, unit)
        sum_out += nn_dot(pushed, v)
    grad_ref[0, 0 : 2 * part, :] = sum_in.astype(jnp.bfloat16)
    grad_ref[0, 2 * part :, :] = sum_out.astype(jnp.bfloat16)


def gradients(place, in_t, out_base, blocks, rows):
    share, hid, dim = out_base.shape

    def spec(array):
        return pl.BlockSpec((1,) + array.shape[1:], lambda j, place: (j, 0, 0))

    operands = [in_t, out_base, *blocks]
    grad_shape = (share, 3 * hid // 2, dim)
    return pl.pallas_call(
        functools.partial(grads_kernel, rows, rows // 128),
        out_shape=jax.ShapeDtypeStruct(grad_shape, jnp.bfloat16),
        grid_spec=pltpu.PrefetchScalarGridSpec(
            num_scalar_prefetch=1,
            grid=(share,),
            in_specs=[spec(a) for a in operands],
            out_specs=pl.BlockSpec((1,) + grad_shape[1:], lambda j, place: (j, 0, 0)),
        ),
        compiler_params=params(),
        name="gradients",
    )(place, *operands)


def attend_kernel(peers, rows, rate_rows, first_head, place_ref, window_ref, edge_ref, *refs):
    own_blocks, other_blocks = refs[:peers], refs[peers : 2 * peers]
    queries = refs[2 * peers : 3 * peers]
    fwd_ref, out_ref, extra_ref, k_scr, v_scr, q_scr = refs[3 * peers :]
    span = 2 * peers * rows
    pad = fwd_ref.shape[1]
    dim = k_scr.shape[1]
    chip, core, half = place_ref[0], place_ref[1], place_ref[2]
    base = half * span
    limit = span + 1 - half
    step = pl.program_id(0)
    window = window_ref[first_head + step]

    @pl.when(step == 0)
    def _():
        k_scr[...] = jnp.zeros_like(k_scr)
        v_scr[:, 0:dim] = jnp.zeros((v_scr.shape[0], dim), v_scr.dtype)
        v_scr[:, dim:] = jnp.ones((v_scr.shape[0], v_scr.shape[1] - dim), v_scr.dtype)

    for p in range(peers):
        for block, lane in ((own_blocks[p], core), (other_blocks[p], 1 - core)):
            at = pl.multiple_of(((chip ^ p) * 2 + lane) * rows, rows)
            k_scr[pl.ds(at, rows), :] = block[0, 0:rows, :]
            v_scr[pl.ds(at, rows), 0:dim] = block[0, rows : 2 * rows, :]
        q_scr[p, 0:rows, :] = queries[p][0]
    fwd = fwd_ref[0].astype(jnp.float32)
    at = 4 * rate_rows

    def spread(i):
        return jnp.broadcast_to(fwd[at + i : at + i + 1, :], (pad, dim)).astype(jnp.bfloat16)

    for p in range(peers):
        q_scr[p, rows:, :] = spread(0)
    k_scr[span : span + pad, :] = spread(1)
    v_scr[span : span + pad, 0:dim] = spread(2)

    def clip_start(place):
        start = jnp.zeros_like(place)
        for i in range(edge_ref.shape[0]):
            start = jnp.maximum(start, jnp.where(edge_ref[i] <= place, edge_ref[i], 0))
        return start

    def clip_stop(place):
        stop = jnp.full_like(place, base + limit)
        for i in range(edge_ref.shape[0]):
            stop = jnp.minimum(stop, jnp.where(edge_ref[i] > place, edge_ref[i], base + limit))
        return stop

    def lowest(place):
        return jnp.maximum(jnp.maximum(place - window, clip_start(place)), base) - base

    def highest(place):
        return jnp.minimum(place + window, clip_stop(place) - 1) - base

    def one_block(p, carry):
        first = ((chip ^ p) * 2 + core) * rows
        row = lax.broadcasted_iota(jnp.int32, (rows + pad, 1), 0)
        place = base + jnp.where(row < rows, first + row, span)
        low, high = lowest(place), highest(place)
        from_key = lowest(base + first) // 128 * 128
        count = (highest(base + first + rows - 1) - from_key) // 256 + 1
        from_key = pl.multiple_of(from_key, 128)
        q = q_scr[p]

        def variant(chunks):
            width = chunks * 256
            scores = nt_dot(q, k_scr[pl.ds(from_key, width), :])
            key_place = from_key + lax.broadcasted_iota(jnp.int32, (1, width), 1)
            seen = (key_place >= low) & (key_place <= high)
            scores = jnp.where(seen, scores, HIDDEN_MASK)
            top = jnp.max(scores, axis=1, keepdims=True)
            weights = jnp.exp2(scores - top).astype(jnp.bfloat16)
            total = nn_dot(weights, v_scr[pl.ds(from_key, width), :])
            attended = total[:, 0:dim] / total[:, dim:]
            out_ref[0, pl.ds(pl.multiple_of(p * rows, rows), rows), :] = attended[0:rows]

            @pl.when((chip ^ p) == peers - 1)
            def _():
                extra_ref[0] = attended[rows:]

        for chunks in range(1, span // 256 + 2):

            @pl.when(count == chunks)
            def _(chunks=chunks):
                variant(chunks)

        return carry

    lax.fori_loop(0, peers, one_block, 0)


def attend(place, half_window, boundaries, own_kv, other_kv, queries, forwarded, first, heads):
    peers = len(queries)
    _, rows, dim = queries[0].shape
    pad = forwarded.shape[1]
    span = 2 * peers * rows
    scr_rows = span + 256

    def spec(array):
        return pl.BlockSpec((1,) + array.shape[1:], lambda j, *_: (first + j, 0, 0))

    def out_spec(out_rows):
        return pl.BlockSpec((1, out_rows, dim), lambda j, *_: (j, 0, 0))

    operands = [*own_kv, *other_kv, *queries, forwarded]
    return pl.pallas_call(
        functools.partial(attend_kernel, peers, rows, rows // 128, first),
        out_shape=[
            jax.ShapeDtypeStruct((heads, peers * rows, dim), jnp.float32),
            jax.ShapeDtypeStruct((heads, pad, dim), jnp.float32),
        ],
        grid_spec=pltpu.PrefetchScalarGridSpec(
            num_scalar_prefetch=3,
            grid=(heads,),
            in_specs=[spec(a) for a in operands],
            out_specs=[out_spec(peers * rows), out_spec(pad)],
            scratch_shapes=[
                pltpu.VMEM((scr_rows, dim), jnp.bfloat16),
                pltpu.VMEM((scr_rows, 2 * dim), jnp.bfloat16),
                pltpu.VMEM((peers, rows + pad, dim), jnp.bfloat16),
            ],
        ),
        compiler_params=params(),
        name="attend",
    )(place, half_window, boundaries, *operands)


def finish_kernel(peers, rows, unit_epsilon, place_ref, *refs):
    att_ref, in_t_ref, base_out_ref, own_ref, other_ref, patch_ref = refs[:6]
    queries = refs[6 : 6 + peers]
    outs = refs[6 + peers : 6 + 2 * peers]
    grad_in_scr, grad_out_scr = refs[6 + 2 * peers :]
    chip, core, half = place_ref[0], place_ref[1], place_ref[2]
    hid = base_out_ref.shape[1]
    part = hid // 2
    for summed, lane in ((own_ref, core), (other_ref, 1 - core)):
        at = pl.multiple_of(lane * part, part)
        grad_in_scr[pl.ds(at, part), :] = summed[0, 0:part, :].astype(jnp.float32)
        grad_in_scr[pl.ds(hid + at, part), :] = summed[0, part : 2 * part, :].astype(jnp.float32)
        grad_out_scr[pl.ds(at, part), :] = summed[0, 2 * part :, :].astype(jnp.float32)

    def renewed(base, grad, axis):
        base = base.astype(jnp.float32)
        updated = base - grad
        norm = jnp.sqrt(jnp.sum(base * base, axis=axis, keepdims=True))
        squares = jnp.sum(updated * updated, axis=axis, keepdims=True)
        return (updated * (norm / jnp.sqrt(squares + epsilon))).astype(jnp.bfloat16)

    new_in_t = renewed(in_t_ref[0], grad_in_scr[...], 1)
    new_out = renewed(base_out_ref[0], grad_out_scr[...], 0)
    patch = patch_ref[0][0:1, :]
    row = lax.broadcasted_iota(jnp.int32, (rows, 1), 0)
    for p in range(peers):
        q = queries[p][0].astype(jnp.float32)
        unit = (q * lax.rsqrt(jnp.sum(q * q, axis=1, keepdims=True) + unit_epsilon)).astype(
            jnp.bfloat16
        )
        pre = nt_dot(unit, new_in_t)
        gate = pre[:, :hid]
        hidden = (gate * jax.nn.sigmoid(gate) * pre[:, hid:]).astype(jnp.bfloat16)
        attended = att_ref[0, p * rows : (p + 1) * rows, :]
        patched = (half == 1) & (core == 0) & (chip == p)
        attended = jnp.where(patched & (row == 0), patch, attended)
        outs[p][0] = (attended + nn_dot(hidden, new_out)).astype(jnp.bfloat16)


def finish(place, attended, in_t, base_out, own_sum, other_sum, patch, queries, first, unit_epsilon):
    peers = len(queries)
    heads = attended.shape[0]
    _, rows, dim = queries[0].shape
    hid = base_out.shape[1]

    def shifted(array):
        return pl.BlockSpec((1,) + array.shape[1:], lambda j, place: (first + j, 0, 0))

    def plain(shape):
        return pl.BlockSpec((1,) + shape[1:], lambda j, place: (j, 0, 0))

    operands = [attended, in_t, base_out, own_sum, other_sum, patch, *queries]
    in_specs = [plain(attended.shape)] + [shifted(a) for a in (in_t, base_out, own_sum, other_sum)]
    in_specs += [plain(patch.shape)] + [shifted(a) for a in queries]
    out_shape = (heads, rows, dim)
    return pl.pallas_call(
        functools.partial(finish_kernel, peers, rows, unit_epsilon),
        out_shape=[jax.ShapeDtypeStruct(out_shape, jnp.bfloat16)] * peers,
        grid_spec=pltpu.PrefetchScalarGridSpec(
            num_scalar_prefetch=1,
            grid=(heads,),
            in_specs=in_specs,
            out_specs=[plain(out_shape)] * peers,
            scratch_shapes=[
                pltpu.VMEM((2 * hid, dim), jnp.float32),
                pltpu.VMEM((hid, dim), jnp.float32),
            ],
        ),
        compiler_params=params(),
        name="finish",
    )(place, *operands)


def place_kernel(peers, chunks, share, place_ref, *refs):
    pieces, out_ref, sems = refs[:-2], refs[-2], refs[-1]
    copies = []
    for c, (first, heads) in enumerate(chunks):
        for p in range(peers):
            at = (place_ref[0] ^ p) * share + first
            copies.append(
                pltpu.make_async_copy(
                    pieces[c * peers + p], out_ref.at[pl.ds(at, heads)], sems.at[c * peers + p]
                )
            )
    for copy in copies:
        copy.start()
    for copy in copies:
        copy.wait()


def put_in_place(place, pieces, peers, chunks, share):
    _, rows, dim = pieces[0].shape
    anywhere = pl.BlockSpec(memory_space=pl.ANY)
    return pl.pallas_call(
        functools.partial(place_kernel, peers, chunks, share),
        out_shape=jax.ShapeDtypeStruct((peers * share, rows, dim), jnp.bfloat16),
        grid_spec=pltpu.PrefetchScalarGridSpec(
            num_scalar_prefetch=1,
            grid=(1,),
            in_specs=[anywhere] * len(pieces),
            out_specs=anywhere,
            scratch_shapes=[pltpu.SemaphoreType.DMA((len(pieces),))],
        ),
        compiler_params=params(),
        name="put_in_place",
    )(place, *pieces)


def regrouping(tok_peers, rows, heads, dim, hid):
    half_peers = tok_peers // 2
    peers = math.gcd(half_peers, heads)
    fits = tok_peers % 2 == 0 and half_peers * rows == 2 * HALF
    fits = fits and half_peers == 2 * peers and peers & (peers - 1) == 0
    fits = fits and rows % 256 == 0 and dim == 128 and hid % 256 == 0
    return peers if fits else 0


def regrouped_body(
    peers,
    query_rows,
    key_rows,
    value_rows,
    query_gain,
    key_gain,
    rate_in,
    rate_out,
    fast_in,
    fast_out,
    half_window,
    boundaries,
):
    rows, heads, dim = query_rows.shape
    share = heads // peers
    tok_peers = lax.axis_size("tok")
    half_peers = tok_peers // 2
    width_all = heads * dim * lax.axis_size("head")
    rate_rows = rows // 128
    aux_rows = -(-(4 * rate_rows + 3) // 16) * 16
    own_index = lax.axis_index("tok")
    half = own_index // half_peers
    chip = own_index % half_peers // 2
    core = own_index % 2
    place = jnp.stack([chip, core, half]).astype(jnp.int32)

    def across(p):
        return [(t, t // half_peers * half_peers + ((t % half_peers) ^ (2 * p))) for t in range(tok_peers)]

    core_pairs = [(t, t ^ 1) for t in range(tok_peers)]
    half_pairs = [(t, (t + half_peers) % tok_peers) for t in range(tok_peers)]
    forward_pairs = [(t + half_peers, t) for t in range(half_peers)]
    back_pairs = [(t, t - 1 + half_peers) for t in range(half_peers) if t % 2 == 1]

    q = jnp.transpose(query_rows, (1, 0, 2))
    k = jnp.transpose(key_rows, (1, 0, 2))
    v = jnp.transpose(value_rows, (1, 0, 2))
    q_float = q.astype(jnp.float32)
    k_float = k.astype(jnp.float32)
    squares = jnp.stack(
        [jnp.sum(q_float * q_float, axis=(0, 2)), jnp.sum(k_float * k_float, axis=(0, 2))]
    )
    scales = lax.rsqrt(lax.psum(squares, "head") / width_all + epsilon)
    fold = math.log2(math.e) / math.sqrt(dim)
    q_scale = jnp.broadcast_to((scales[0] * fold)[:, None], (rows, dim))
    k_scale = jnp.broadcast_to(scales[1][:, None], (rows, dim))
    sent_kv, sent_q = pack(
        place,
        q_scale,
        k_scale,
        q,
        k,
        v,
        query_gain[:, None, :],
        key_gain[:, None, :],
        rate_in.reshape(heads, rate_rows, 128),
        rate_out.reshape(heads, rate_rows, 128),
        peers,
        aux_rows,
    )
    own_kv = [sent_kv[0]] + [exchanged(sent_kv[p], across(p)) for p in range(1, peers)]
    queries = [sent_q[0]] + [exchanged(sent_q[p], across(p)) for p in range(1, peers)]
    other_kv = [exchanged(x, core_pairs) for x in own_kv]

    first_aux = jnp.zeros((share, aux_rows, dim), jnp.bfloat16)
    for p in range(peers):
        aux = jnp.where(core == 0, own_kv[p][:, 2 * rows :], other_kv[p][:, 2 * rows :])
        first_aux = jnp.where(chip == p, aux, first_aux)
    forwarded = exchanged(first_aux, forward_pairs)

    start = chip * share
    in_t = jnp.transpose(lax.dynamic_slice_in_dim(fast_in, start, share, 0), (0, 2, 1))
    base_out = lax.dynamic_slice_in_dim(fast_out, start, share, 0)
    window = lax.dynamic_slice_in_dim(half_window, start, share, 0)
    grad = gradients(place, in_t, base_out, [*own_kv, *other_kv], rows)
    from_half = exchanged(grad, half_pairs)
    own_sum = (grad.astype(jnp.float32) + from_half.astype(jnp.float32)).astype(jnp.bfloat16)
    other_sum = exchanged(own_sum, core_pairs)

    chunks = [(0, (share + 1) // 2), ((share + 1) // 2, share // 2)]
    pieces = []
    for first, count in chunks:
        attended, extra = attend(
            place, window, boundaries, own_kv, other_kv, queries, forwarded, first, count
        )
        patch = exchanged(extra, back_pairs)
        outs = finish(
            place,
            attended,
            in_t,
            base_out,
            own_sum,
            other_sum,
            patch,
            queries,
            first,
            epsilon * fold * fold,
        )
        pieces += [outs[0]] + [exchanged(outs[p], across(p)) for p in range(1, peers)]
    whole = put_in_place(place, pieces, peers, chunks, share)
    return jnp.transpose(whole, (1, 0, 2))


def body(query_rows, *others):
    rows, heads, dim = query_rows.shape
    hid = others[7].shape[1]
    peers = regrouping(lax.axis_size("tok"), rows, heads, dim, hid)
    if peers:
        return regrouped_body(peers, query_rows, *others)
    return sliding_body(query_rows, *others)


def solution(mesh):
    in_specs = (
        P("tok", "head", None),
        P("tok", "head", None),
        P("tok", "head", None),
        P("head", None),
        P("head", None),
        P("head", "tok"),
        P("head", "tok"),
        P("head", None, None),
        P("head", None, None),
        P("head"),
        P(),
    )
    out_specs = P("tok", "head", None)
    return jax.shard_map(body, mesh=mesh, in_specs=in_specs, out_specs=out_specs, check_vma=False)
```

```python
import functools
import math

import jax
import jax.numpy as jnp
from jax import lax
from jax.experimental import pallas as pl
from jax.experimental.pallas import tpu as pltpu
from jax.sharding import PartitionSpec as P

HALF = 1024


epsilon = 1e-06


def passed_along(x, axis, by):
    peers = lax.axis_size(axis)
    pairs = [(i, i + by) for i in range(peers) if 0 <= i + by < peers]
    return lax.ppermute(x, axis, pairs)


def unit_rows(matrix):
    as_float = matrix.astype(jnp.float32)
    return (
        as_float * lax.rsqrt(jnp.sum(as_float * as_float, axis=-1, keepdims=True) + epsilon)
    ).astype(jnp.bfloat16)


def rescale(updated, base_norm, squares):
    return (updated * (base_norm / jnp.sqrt(squares + epsilon))[:, None, :]).astype(jnp.bfloat16)


def sliding_body(
    query_rows,
    key_rows,
    value_rows,
    query_gain,
    key_gain,
    rate_in,
    rate_out,
    fast_in,
    fast_out,
    half_window,
    boundaries,
):
    tok_rows = query_rows.shape[0]
    local_heads = query_rows.shape[1]
    head_dim = query_rows.shape[2]
    fast_hid = fast_out.shape[1]
    width_all = local_heads * head_dim * lax.axis_size("head")
    tok_count = tok_rows * lax.axis_size("tok")
    own_index = lax.axis_index("tok")
    first_row = own_index * tok_rows
    query_float = query_rows.astype(jnp.float32)
    key_float = key_rows.astype(jnp.float32)
    query_sq, key_sq = lax.psum(
        (
            jnp.sum(query_float * query_float, axis=(1, 2)),
            jnp.sum(key_float * key_float, axis=(1, 2)),
        ),
        "head",
    )
    q_normed = (
        query_float * lax.rsqrt(query_sq / width_all + epsilon)[:, None, None] * query_gain[None]
    ).astype(jnp.bfloat16)
    k_normed = (
        key_float * lax.rsqrt(key_sq / width_all + epsilon)[:, None, None] * key_gain[None]
    ).astype(jnp.bfloat16)

    def clip_of(places):
        return jnp.sum((places[:, None] >= boundaries[None, :]).astype(jnp.int32), axis=1)

    positions = first_row + jnp.arange(tok_rows, dtype=jnp.int32)
    query_clip = clip_of(positions)
    scaling = 1.0 / math.sqrt(head_dim)

    def absorb(state_now, block_keys, block_values, key_first):
        best, denominator, accum = state_now
        key_places = key_first + jnp.arange(tok_rows, dtype=jnp.int32)
        scores = (
            jnp.einsum("qhd,khd->hqk", q_normed, block_keys, preferred_element_type=jnp.float32)
            * scaling
        )
        inside = (key_places >= 0) & (key_places < tok_count)
        pair_ok = (query_clip[:, None] == clip_of(key_places)[None, :]) & inside[None, :]
        distance = jnp.abs(positions[:, None] - key_places[None, :])
        allowed = (distance[None, :, :] <= half_window[:, None, None]) & pair_ok[None, :, :]
        masked = jnp.where(allowed, scores, -jnp.inf)
        new_best = jnp.maximum(best, jnp.max(masked, axis=2))
        weights = jnp.exp(masked - new_best[:, :, None])
        shrink = jnp.exp(best - new_best)
        denominator = denominator * shrink + jnp.sum(weights, axis=2)
        accum = accum * shrink[:, :, None] + jnp.einsum(
            "hqk,khd->hqd",
            weights.astype(jnp.bfloat16),
            block_values,
            preferred_element_type=jnp.float32,
        )
        return (new_best, denominator, accum)

    start_state = (
        jnp.full((local_heads, tok_rows), -jnp.inf, jnp.float32),
        jnp.zeros((local_heads, tok_rows), jnp.float32),
        jnp.zeros((local_heads, tok_rows, head_dim), jnp.float32),
    )
    state_now = absorb(start_state, k_normed, value_rows, first_row)
    reach_blocks = HALF // tok_rows
    for distance_step in range(1, reach_blocks + 1):
        left_keys, left_values = passed_along((k_normed, value_rows), "tok", distance_step)
        state_now = absorb(state_now, left_keys, left_values, first_row - distance_step * tok_rows)
        right_keys, right_values = passed_along((k_normed, value_rows), "tok", -distance_step)
        state_now = absorb(
            state_now, right_keys, right_values, first_row + distance_step * tok_rows
        )
    attended = state_now[2] / state_now[1][:, :, None]
    key_unit = unit_rows(k_normed)
    query_unit = unit_rows(q_normed)
    pre_keys = jnp.einsum("thd,hdf->htf", key_unit, fast_in, preferred_element_type=jnp.float32)
    gate_part = pre_keys[:, :, :fast_hid]
    lin_part = pre_keys[:, :, fast_hid:]
    sigmoid_gate = jax.nn.sigmoid(gate_part)
    swish_gate = gate_part * sigmoid_gate
    hidden = (swish_gate * lin_part).astype(jnp.bfloat16)
    value_float = value_rows.astype(jnp.float32)
    push_out = (-jnp.transpose(rate_out)[:, :, None] * value_float).astype(jnp.bfloat16)
    push_in = (-jnp.transpose(rate_in)[:, :, None] * value_float).astype(jnp.bfloat16)
    grad_out = jnp.einsum("htf,thd->hfd", hidden, push_out, preferred_element_type=jnp.float32)
    hidden_grad = jnp.einsum("thd,hfd->htf", push_in, fast_out, preferred_element_type=jnp.float32)
    d_gate = hidden_grad * lin_part * sigmoid_gate * (1.0 + gate_part * (1.0 - sigmoid_gate))
    d_lin = hidden_grad * swish_gate
    d_pre = jnp.concatenate([d_gate, d_lin], axis=2).astype(jnp.bfloat16)
    grad_in = jnp.einsum("thd,htf->hdf", key_unit, d_pre, preferred_element_type=jnp.float32)
    in_float = fast_in.astype(jnp.float32)
    out_float = fast_out.astype(jnp.float32)
    in_base = jnp.sqrt(jnp.sum(in_float * in_float, axis=1))
    out_base = jnp.sqrt(jnp.sum(out_float * out_float, axis=1))
    summed_in, summed_out = lax.psum((grad_in, grad_out), "tok")
    updated_in = in_float - summed_in
    updated_out = out_float - summed_out
    new_in = rescale(updated_in, in_base, jnp.sum(updated_in * updated_in, axis=1))
    new_out = rescale(updated_out, out_base, jnp.sum(updated_out * updated_out, axis=1))
    pre_query = jnp.einsum("thd,hdf->htf", query_unit, new_in, preferred_element_type=jnp.float32)
    query_gate = pre_query[:, :, :fast_hid]
    query_hidden = (query_gate * jax.nn.sigmoid(query_gate) * pre_query[:, :, fast_hid:]).astype(
        jnp.bfloat16
    )
    fast_result = jnp.einsum(
        "htf,hfd->htd", query_hidden, new_out, preferred_element_type=jnp.float32
    )
    combined = attended + fast_result
    return jnp.transpose(combined, (1, 0, 2)).astype(jnp.bfloat16)


VMEM_BYTES = 56 * 1024 * 1024
HIDDEN_MASK = -1e30
NT = (((1,), (1,)), ((), ()))


def exchanged(x, pairs):
    return lax.ppermute(x, "tok", pairs)


def nt_dot(a, b):
    return lax.dot_general(a, b, NT, preferred_element_type=jnp.float32)


def nn_dot(a, b):
    return jnp.dot(a, b, preferred_element_type=jnp.float32)


def params():
    return pltpu.CompilerParams(vmem_limit_bytes=VMEM_BYTES)


def cost(flops, nbytes):
    return pl.CostEstimate(flops=int(16 * flops), bytes_accessed=int(nbytes), transcendentals=0)


def pack_kernel(peers, place_ref, q_scale_ref, k_scale_ref, *refs):
    q_gain_ref, k_gain_ref, rate_in_ref, rate_out_ref = refs[:4]
    inputs, outputs = refs[4 : 4 + 3 * peers], refs[4 + 3 * peers : 4 + 5 * peers]
    aux_ref = refs[-1]
    rows = q_scale_ref.shape[0]
    rate_rows = rows // 128
    share = q_gain_ref.shape[0] // peers
    q_scale = q_scale_ref[...]
    k_scale = k_scale_ref[...]
    aux_ref[...] = jnp.zeros_like(aux_ref)
    for p in range(peers):
        q_ref, k_ref, v_ref = inputs[3 * p : 3 * p + 3]
        kv_out, q_out = outputs[2 * p : 2 * p + 2]
        head = pl.ds((place_ref[0] ^ p) * share + pl.program_id(0), 1)
        q = (q_ref[0].astype(jnp.float32) * q_scale * q_gain_ref[head, :]).astype(jnp.bfloat16)
        k = (k_ref[0].astype(jnp.float32) * k_scale * k_gain_ref[head, :]).astype(jnp.bfloat16)
        v = v_ref[0]
        q_out[0] = q
        kv_out[0, 0:rows, :] = k
        kv_out[0, rows : 2 * rows, :] = v
        at = 0
        for rate_ref in (rate_in_ref, rate_out_ref):
            rate = rate_ref[head, :]
            high = rate.astype(jnp.bfloat16).astype(jnp.float32)
            for part in (high, rate - high):
                for i in range(rate_rows):
                    aux_ref[at : at + 1, :] = part[:, i * 128 : (i + 1) * 128]
                    at += 1
        for i, array in enumerate((q, k, v)):
            aux_ref[at + i : at + i + 1, :] = array[0:16].astype(jnp.float32)[0:1]
        kv_out[0, 2 * rows :, :] = aux_ref[...].astype(jnp.bfloat16)


def pack(place, q_scale, k_scale, q, k, v, q_gain, k_gain, rate_in, rate_out, peers, aux_rows):
    heads, rows, dim = q.shape
    share = heads // peers

    def head_of(p):
        return lambda j, place: ((place[0] ^ p) * share + j, 0, 0)

    operands = [q_scale, k_scale, q_gain, k_gain, rate_in, rate_out]
    in_specs = [pl.BlockSpec(a.shape, lambda j, place: (0, 0)) for a in operands]
    out_specs, out_shape = [], []
    kv_rows = 2 * rows + aux_rows
    for p in range(peers):
        for array in (q, k, v):
            in_specs.append(pl.BlockSpec((1,) + array.shape[1:], head_of(p)))
            operands.append(array)
        for out_rows in (kv_rows, rows):
            out_specs.append(pl.BlockSpec((1, out_rows, dim), lambda j, place: (j, 0, 0)))
            out_shape.append(jax.ShapeDtypeStruct((share, out_rows, dim), jnp.bfloat16))
    outs = pl.pallas_call(
        functools.partial(pack_kernel, peers),
        out_shape=out_shape,
        grid_spec=pltpu.PrefetchScalarGridSpec(
            num_scalar_prefetch=1,
            grid=(share,),
            in_specs=in_specs,
            out_specs=out_specs,
            scratch_shapes=[pltpu.VMEM((aux_rows, dim), jnp.float32)],
        ),
        compiler_params=params(),
        cost_estimate=cost(0, 12 * heads * rows * dim),
        name="pack",
    )(place, *operands)
    return outs[0::2], outs[1::2]


def grads_kernel(rows, rate_rows, place_ref, in_ref, out_ref, *refs):
    blocks, grad_ref = refs[:-1], refs[-1]
    hid = out_ref.shape[1]
    part = hid // 2
    core = place_ref[1]
    own = pl.multiple_of(core * part, part)
    in_half = jnp.concatenate(
        [
            jnp.transpose(in_ref[0, :, pl.ds(at, part)].astype(jnp.float32))
            for at in (own, pl.multiple_of(hid + own, part))
        ],
        axis=0,
    ).astype(jnp.bfloat16)
    out_half = out_ref[0, pl.ds(own, part), :]
    sum_in = jnp.zeros((2 * part, in_half.shape[1]), jnp.float32)
    sum_out = jnp.zeros((part, in_half.shape[1]), jnp.float32)
    for block in blocks:
        k = block[0, 0:rows, :].astype(jnp.float32)
        v = block[0, rows : 2 * rows, :]
        aux = block[0, 2 * rows :, :].astype(jnp.float32)

        def rate(at):
            both = aux[at : at + rate_rows] + aux[at + rate_rows : at + 2 * rate_rows]
            return jnp.concatenate([both[i : i + 1] for i in range(rate_rows)], axis=1)

        rate_in, rate_out = rate(0), rate(2 * rate_rows)
        unit = (k * lax.rsqrt(jnp.sum(k * k, axis=1, keepdims=True) + epsilon)).astype(
            jnp.bfloat16
        )
        pre = nt_dot(in_half, unit)
        gate, lin = pre[:part], pre[part:]
        sig = jax.nn.sigmoid(gate)
        swish = gate * sig
        pushed = (swish * lin * -rate_out).astype(jnp.bfloat16)
        hidden_grad = nt_dot(out_half, v) * -rate_in
        d_gate = hidden_grad * lin * sig * (1.0 + gate * (1.0 - sig))
        d_lin = hidden_grad * swish
        d_pre = jnp.concatenate([d_gate, d_lin], axis=0).astype(jnp.bfloat16)
        sum_in += nn_dot(d_pre, unit)
        sum_out += nn_dot(pushed, v)
    grad_ref[0, 0 : 2 * part, :] = sum_in.astype(jnp.bfloat16)
    grad_ref[0, 2 * part :, :] = sum_out.astype(jnp.bfloat16)


def gradients(place, fast_in, fast_out, blocks, rows):
    share = blocks[0].shape[0]
    _, hid, dim = fast_out.shape

    def spec(array):
        return pl.BlockSpec((1,) + array.shape[1:], lambda j, place: (j, 0, 0))

    def weights(array):
        return pl.BlockSpec(
            (1,) + array.shape[1:], lambda j, place: (place[0] * share + j, 0, 0)
        )

    operands = [fast_in, fast_out, *blocks]
    grad_shape = (share, 3 * hid // 2, dim)
    return pl.pallas_call(
        functools.partial(grads_kernel, rows, rows // 128),
        out_shape=jax.ShapeDtypeStruct(grad_shape, jnp.bfloat16),
        grid_spec=pltpu.PrefetchScalarGridSpec(
            num_scalar_prefetch=1,
            grid=(share,),
            in_specs=[weights(fast_in), weights(fast_out)] + [spec(a) for a in blocks],
            out_specs=pl.BlockSpec((1,) + grad_shape[1:], lambda j, place: (j, 0, 0)),
        ),
        compiler_params=params(),
        cost_estimate=cost(6 * share * hid * dim * rows * len(blocks), 0),
        name="gradients",
    )(place, *operands)


def attend_kernel(peers, rows, rate_rows, share, first, place_ref, window_ref, edge_ref, *refs):
    own_blocks, other_blocks = refs[:peers], refs[peers : 2 * peers]
    queries = refs[2 * peers : 3 * peers]
    fwd_ref, out_ref, extra_ref, k_scr, vt_scr, q_scr = refs[3 * peers :]
    span = 2 * peers * rows
    dim = k_scr.shape[1]
    pad = fwd_ref.shape[1]
    chip, core, half = place_ref[0], place_ref[1], place_ref[2]
    base = half * span
    limit = span + 1 - half
    step = pl.program_id(0)
    window = window_ref[chip * share + first + step]

    @pl.when(step == 0)
    def _():
        k_scr[span:, :] = jnp.zeros((k_scr.shape[0] - span, dim), k_scr.dtype)
        vt_scr[:, span:] = jnp.zeros((vt_scr.shape[0], vt_scr.shape[1] - span), vt_scr.dtype)
        vt_scr[dim:, :] = jnp.ones((vt_scr.shape[0] - dim, vt_scr.shape[1]), vt_scr.dtype)

    for p in range(peers):
        for block, lane in ((own_blocks[p], core), (other_blocks[p], 1 - core)):
            at = pl.multiple_of(((chip ^ p) * 2 + lane) * rows, rows)
            k_scr[pl.ds(at, rows), :] = block[0, 0:rows, :]
            vt_scr[0:dim, pl.ds(at, rows)] = jnp.transpose(block[0, rows : 2 * rows, :])
        q_scr[p] = queries[p][0]
    fwd = fwd_ref[0].astype(jnp.float32)
    q_lone, k_lone, v_lone = (fwd[4 * rate_rows + i : 4 * rate_rows + i + 1] for i in range(3))
    k_scr[span : span + pad, :] = jnp.broadcast_to(k_lone, (pad, dim)).astype(jnp.bfloat16)
    vt_scr[0:dim, span : span + 128] = jnp.transpose(
        jnp.broadcast_to(v_lone, (128, dim))
    ).astype(jnp.bfloat16)

    def clip_start(place):
        start = jnp.zeros_like(place)
        for i in range(edge_ref.shape[0]):
            start = jnp.maximum(start, jnp.where(edge_ref[i] <= place, edge_ref[i], 0))
        return start

    def clip_stop(place):
        stop = jnp.full_like(place, base + limit)
        for i in range(edge_ref.shape[0]):
            stop = jnp.minimum(stop, jnp.where(edge_ref[i] > place, edge_ref[i], base + limit))
        return stop

    def lowest(place):
        return jnp.maximum(jnp.maximum(place - window, clip_start(place)), base) - base

    def highest(place):
        return jnp.minimum(place + window, clip_stop(place) - 1) - base

    def one_block(p, carry):
        start = ((chip ^ p) * 2 + core) * rows
        place = base + start + lax.broadcasted_iota(jnp.int32, (1, rows), 1)
        low, high = lowest(place), highest(place)
        from_key = lowest(base + start) // 128 * 128
        count = (highest(base + start + rows - 1) - from_key) // 256 + 1
        from_key = pl.multiple_of(from_key, 128)
        low, high = low - from_key, high - from_key
        q = q_scr[p]

        def variant(chunks):
            width = chunks * 256
            scores = nt_dot(k_scr[pl.ds(from_key, width), :], q)
            key = lax.broadcasted_iota(jnp.int32, (width, rows), 0)
            scores = jnp.where((key >= low) & (key <= high), scores, HIDDEN_MASK)
            top = jnp.max(scores, axis=0, keepdims=True)
            weights = jnp.exp2(scores - top).astype(jnp.bfloat16)
            total = nn_dot(vt_scr[:, pl.ds(from_key, width)], weights)
            attended = total[0:dim] * (1.0 / total[dim : dim + 1])
            out_ref[0, pl.ds(pl.multiple_of(p * rows, rows), rows), :] = jnp.transpose(attended)

        for chunks in range(1, span // 256 + 2):

            @pl.when(count == chunks)
            def _(chunks=chunks):
                variant(chunks)

        return carry

    lax.fori_loop(0, peers, one_block, 0)

    extra_ref[0] = jnp.zeros(extra_ref.shape[1:], jnp.float32)

    @pl.when((half == 0) & (core == 1))
    def _():
        near = span - HALF
        width = HALF + 128
        q = jnp.broadcast_to(q_lone, (pad, dim)).astype(jnp.bfloat16)
        scores = nt_dot(q, k_scr[near : near + width, :])
        key = near + lax.broadcasted_iota(jnp.int32, (1, width), 1)
        scores = jnp.where((key >= span - window) & (key <= span), scores, HIDDEN_MASK)
        top = jnp.max(scores, axis=1, keepdims=True)
        weights = jnp.exp2(scores - top).astype(jnp.bfloat16)
        total = nt_dot(weights, vt_scr[:, near : near + width])
        extra_ref[0] = total[:, 0:dim] / total[:, dim : dim + 1]


def attend(place, half_window, boundaries, own_kv, other_kv, queries, forwarded, first, heads):
    peers = len(queries)
    share, rows, dim = queries[0].shape
    pad = forwarded.shape[1]
    span = 2 * peers * rows
    scr_rows = span + 256

    def spec(array):
        return pl.BlockSpec((1,) + array.shape[1:], lambda j, *_: (first + j, 0, 0))

    def out_spec(out_rows):
        return pl.BlockSpec((1, out_rows, dim), lambda j, *_: (j, 0, 0))

    operands = [*own_kv, *other_kv, *queries, forwarded]
    return pl.pallas_call(
        functools.partial(attend_kernel, peers, rows, rows // 128, share, first),
        out_shape=[
            jax.ShapeDtypeStruct((heads, peers * rows, dim), jnp.float32),
            jax.ShapeDtypeStruct((heads, pad, dim), jnp.float32),
        ],
        grid_spec=pltpu.PrefetchScalarGridSpec(
            num_scalar_prefetch=3,
            grid=(heads,),
            in_specs=[spec(a) for a in operands],
            out_specs=[out_spec(peers * rows), out_spec(pad)],
            scratch_shapes=[
                pltpu.VMEM((scr_rows, dim), jnp.bfloat16),
                pltpu.VMEM((dim + 16, scr_rows), jnp.bfloat16),
                pltpu.VMEM((peers, rows, dim), jnp.bfloat16),
            ],
        ),
        compiler_params=params(),
        cost_estimate=cost(4 * heads * peers * rows * HALF * 2 * dim, 0),
        name="attend",
    )(place, half_window, boundaries, *operands)


def finish_kernel(peers, rows, unit_epsilon, place_ref, *refs):
    att_ref, base_in_ref, base_out_ref, own_ref, other_ref, patch_ref = refs[:6]
    queries = refs[6 : 6 + peers]
    outs = refs[6 + peers : 6 + 2 * peers]
    grad_in_scr, grad_out_scr = refs[6 + 2 * peers :]
    chip, core, half = place_ref[0], place_ref[1], place_ref[2]
    hid = base_out_ref.shape[1]
    part = hid // 2
    for summed, lane in ((own_ref, core), (other_ref, 1 - core)):
        at = pl.multiple_of(lane * part, part)
        grad_in_scr[pl.ds(at, part), :] = summed[0, 0:part, :].astype(jnp.float32)
        grad_in_scr[pl.ds(hid + at, part), :] = summed[0, part : 2 * part, :].astype(jnp.float32)
        grad_out_scr[pl.ds(at, part), :] = summed[0, 2 * part :, :].astype(jnp.float32)

    def renewed(base, grad):
        base = base.astype(jnp.float32)
        updated = base - grad
        norm = jnp.sqrt(jnp.sum(base * base, axis=0, keepdims=True))
        squares = jnp.sum(updated * updated, axis=0, keepdims=True)
        return (updated * (norm / jnp.sqrt(squares + epsilon))).astype(jnp.bfloat16)

    new_in = renewed(base_in_ref[0], jnp.transpose(grad_in_scr[...]))
    new_out = renewed(base_out_ref[0], grad_out_scr[...])
    patch = patch_ref[0][0:1, :]
    row = lax.broadcasted_iota(jnp.int32, (rows, 1), 0)
    for p in range(peers):
        q = queries[p][0].astype(jnp.float32)
        unit = (q * lax.rsqrt(jnp.sum(q * q, axis=1, keepdims=True) + unit_epsilon)).astype(
            jnp.bfloat16
        )
        pre = nn_dot(unit, new_in)
        gate = pre[:, :hid]
        hidden = (gate * jax.nn.sigmoid(gate) * pre[:, hid:]).astype(jnp.bfloat16)
        attended = att_ref[0, p * rows : (p + 1) * rows, :]
        patched = (half == 1) & (core == 0) & (chip == p)
        attended = jnp.where(patched & (row == 0), patch, attended)
        outs[p][0] = (attended + nn_dot(hidden, new_out)).astype(jnp.bfloat16)


def finish(
    place, attended, fast_in, fast_out, own_sum, other_sum, patch, queries, first, unit_epsilon
):
    peers = len(queries)
    heads = attended.shape[0]
    share, rows, dim = queries[0].shape
    hid = fast_out.shape[1]

    def weights(array):
        return pl.BlockSpec(
            (1,) + array.shape[1:], lambda j, place: (place[0] * share + first + j, 0, 0)
        )

    def shifted(array):
        return pl.BlockSpec((1,) + array.shape[1:], lambda j, place: (first + j, 0, 0))

    def plain(shape):
        return pl.BlockSpec((1,) + shape[1:], lambda j, place: (j, 0, 0))

    operands = [attended, fast_in, fast_out, own_sum, other_sum, patch, *queries]
    in_specs = [plain(attended.shape), weights(fast_in), weights(fast_out)]
    in_specs += [shifted(own_sum), shifted(other_sum), plain(patch.shape)]
    in_specs += [shifted(a) for a in queries]
    out_shape = (heads, rows, dim)
    return pl.pallas_call(
        functools.partial(finish_kernel, peers, rows, unit_epsilon),
        out_shape=[jax.ShapeDtypeStruct(out_shape, jnp.bfloat16)] * peers,
        grid_spec=pltpu.PrefetchScalarGridSpec(
            num_scalar_prefetch=1,
            grid=(heads,),
            in_specs=in_specs,
            out_specs=[plain(out_shape)] * peers,
            scratch_shapes=[
                pltpu.VMEM((2 * hid, dim), jnp.float32),
                pltpu.VMEM((hid, dim), jnp.float32),
            ],
        ),
        compiler_params=params(),
        cost_estimate=cost(12 * heads * peers * rows * hid * dim, 0),
        name="finish",
    )(place, *operands)


def place_kernel(peers, chunks, share, place_ref, *refs):
    pieces, out_ref, sems = refs[:-2], refs[-2], refs[-1]
    copies = []
    for c, (first, heads) in enumerate(chunks):
        for p in range(peers):
            at = (place_ref[0] ^ p) * share + first
            copies.append(
                pltpu.make_async_copy(
                    pieces[c * peers + p], out_ref.at[pl.ds(at, heads)], sems.at[c * peers + p]
                )
            )
    for copy in copies:
        copy.start()
    for copy in copies:
        copy.wait()


def put_in_place(place, pieces, peers, chunks, share):
    _, rows, dim = pieces[0].shape
    anywhere = pl.BlockSpec(memory_space=pl.ANY)
    return pl.pallas_call(
        functools.partial(place_kernel, peers, chunks, share),
        out_shape=jax.ShapeDtypeStruct((peers * share, rows, dim), jnp.bfloat16),
        grid_spec=pltpu.PrefetchScalarGridSpec(
            num_scalar_prefetch=1,
            grid=(1,),
            in_specs=[pl.BlockSpec(a.shape, lambda j, place: (0, 0, 0)) for a in pieces],
            out_specs=anywhere,
            scratch_shapes=[pltpu.SemaphoreType.DMA((len(pieces),))],
        ),
        compiler_params=params(),
        name="put_in_place",
    )(place, *pieces)


def regrouping(tok_peers, rows, heads, dim, hid):
    half_peers = tok_peers // 2
    peers = math.gcd(half_peers, heads)
    fits = tok_peers % 2 == 0 and half_peers * rows == 2 * HALF
    fits = fits and half_peers == 2 * peers and peers & (peers - 1) == 0
    fits = fits and rows % 256 == 0 and dim == 128 and hid % 256 == 0
    return peers if fits else 0


def regrouped_body(
    peers,
    query_rows,
    key_rows,
    value_rows,
    query_gain,
    key_gain,
    rate_in,
    rate_out,
    fast_in,
    fast_out,
    half_window,
    boundaries,
):
    rows, heads, dim = query_rows.shape
    share = heads // peers
    tok_peers = lax.axis_size("tok")
    half_peers = tok_peers // 2
    width_all = heads * dim * lax.axis_size("head")
    rate_rows = rows // 128
    aux_rows = -(-(4 * rate_rows + 3) // 16) * 16
    own_index = lax.axis_index("tok")
    half = own_index // half_peers
    chip = own_index % half_peers // 2
    core = own_index % 2
    place = jnp.stack([chip, core, half]).astype(jnp.int32)

    def across(p):
        return [(t, t // half_peers * half_peers + ((t % half_peers) ^ (2 * p))) for t in range(tok_peers)]

    core_pairs = [(t, t ^ 1) for t in range(tok_peers)]
    half_pairs = [(t, (t + half_peers) % tok_peers) for t in range(tok_peers)]
    forward_pairs = [(t + half_peers, t) for t in range(half_peers)]
    back_pairs = [(t, t - 1 + half_peers) for t in range(half_peers) if t % 2 == 1]

    q = jnp.transpose(query_rows, (1, 0, 2))
    k = jnp.transpose(key_rows, (1, 0, 2))
    v = jnp.transpose(value_rows, (1, 0, 2))
    q_float = q.astype(jnp.float32)
    k_float = k.astype(jnp.float32)
    squares = jnp.stack(
        [jnp.sum(q_float * q_float, axis=(0, 2)), jnp.sum(k_float * k_float, axis=(0, 2))]
    )
    scales = lax.rsqrt(lax.psum(squares, "head") / width_all + epsilon)
    fold = math.log2(math.e) / math.sqrt(dim)
    q_scale = jnp.broadcast_to((scales[0] * fold)[:, None], (rows, dim))
    k_scale = jnp.broadcast_to(scales[1][:, None], (rows, dim))
    sent_kv, sent_q = pack(
        place,
        q_scale,
        k_scale,
        q,
        k,
        v,
        query_gain,
        key_gain,
        rate_in,
        rate_out,
        peers,
        aux_rows,
    )
    own_kv = [sent_kv[0]] + [exchanged(sent_kv[p], across(p)) for p in range(1, peers)]
    queries = [sent_q[0]] + [exchanged(sent_q[p], across(p)) for p in range(1, peers)]
    other_kv = [exchanged(x, core_pairs) for x in own_kv]

    first_aux = jnp.zeros((share, aux_rows, dim), jnp.bfloat16)
    for p in range(peers):
        aux = jnp.where(core == 0, own_kv[p][:, 2 * rows :], other_kv[p][:, 2 * rows :])
        first_aux = jnp.where(chip == p, aux, first_aux)
    forwarded = exchanged(first_aux, forward_pairs)

    grad = gradients(place, fast_in, fast_out, [*own_kv, *other_kv], rows)
    from_half = exchanged(grad, half_pairs)
    own_sum = (grad.astype(jnp.float32) + from_half.astype(jnp.float32)).astype(jnp.bfloat16)
    other_sum = exchanged(own_sum, core_pairs)

    chunks = [(0, (share + 1) // 2), ((share + 1) // 2, share // 2)]
    pieces = []
    for first, count in chunks:
        attended, extra = attend(
            place, half_window, boundaries, own_kv, other_kv, queries, forwarded, first, count
        )
        patch = exchanged(extra, back_pairs)
        outs = finish(
            place,
            attended,
            fast_in,
            fast_out,
            own_sum,
            other_sum,
            patch,
            queries,
            first,
            epsilon * fold * fold,
        )
        pieces += [outs[0]] + [exchanged(outs[p], across(p)) for p in range(1, peers)]
    whole = put_in_place(place, pieces, peers, chunks, share)
    return jnp.transpose(whole, (1, 0, 2))


def body(query_rows, *others):
    rows, heads, dim = query_rows.shape
    hid = others[7].shape[1]
    peers = regrouping(lax.axis_size("tok"), rows, heads, dim, hid)
    if peers:
        return regrouped_body(peers, query_rows, *others)
    return sliding_body(query_rows, *others)


def solution(mesh):
    in_specs = (
        P("tok", "head", None),
        P("tok", "head", None),
        P("tok", "head", None),
        P("head", None),
        P("head", None),
        P("head", "tok"),
        P("head", "tok"),
        P("head", None, None),
        P("head", None, None),
        P("head"),
        P(),
    )
    out_specs = P("tok", "head", None)
    return jax.shard_map(body, mesh=mesh, in_specs=in_specs, out_specs=out_specs, check_vma=False)
```

```python
import functools
import math

import jax
import jax.numpy as jnp
from jax import lax
from jax.experimental import pallas as pl
from jax.experimental.pallas import tpu as pltpu
from jax.sharding import PartitionSpec as P

HALF = 1024


epsilon = 1e-06


def passed_along(x, axis, by):
    peers = lax.axis_size(axis)
    pairs = [(i, i + by) for i in range(peers) if 0 <= i + by < peers]
    return lax.ppermute(x, axis, pairs)


def unit_rows(matrix):
    as_float = matrix.astype(jnp.float32)
    return (
        as_float * lax.rsqrt(jnp.sum(as_float * as_float, axis=-1, keepdims=True) + epsilon)
    ).astype(jnp.bfloat16)


def rescale(updated, base_norm, squares):
    return (updated * (base_norm / jnp.sqrt(squares + epsilon))[:, None, :]).astype(jnp.bfloat16)


def sliding_body(
    query_rows,
    key_rows,
    value_rows,
    query_gain,
    key_gain,
    rate_in,
    rate_out,
    fast_in,
    fast_out,
    half_window,
    boundaries,
):
    tok_rows = query_rows.shape[0]
    local_heads = query_rows.shape[1]
    head_dim = query_rows.shape[2]
    fast_hid = fast_out.shape[1]
    width_all = local_heads * head_dim * lax.axis_size("head")
    tok_count = tok_rows * lax.axis_size("tok")
    own_index = lax.axis_index("tok")
    first_row = own_index * tok_rows
    query_float = query_rows.astype(jnp.float32)
    key_float = key_rows.astype(jnp.float32)
    query_sq, key_sq = lax.psum(
        (
            jnp.sum(query_float * query_float, axis=(1, 2)),
            jnp.sum(key_float * key_float, axis=(1, 2)),
        ),
        "head",
    )
    q_normed = (
        query_float * lax.rsqrt(query_sq / width_all + epsilon)[:, None, None] * query_gain[None]
    ).astype(jnp.bfloat16)
    k_normed = (
        key_float * lax.rsqrt(key_sq / width_all + epsilon)[:, None, None] * key_gain[None]
    ).astype(jnp.bfloat16)

    def clip_of(places):
        return jnp.sum((places[:, None] >= boundaries[None, :]).astype(jnp.int32), axis=1)

    positions = first_row + jnp.arange(tok_rows, dtype=jnp.int32)
    query_clip = clip_of(positions)
    scaling = 1.0 / math.sqrt(head_dim)

    def absorb(state_now, block_keys, block_values, key_first):
        best, denominator, accum = state_now
        key_places = key_first + jnp.arange(tok_rows, dtype=jnp.int32)
        scores = (
            jnp.einsum("qhd,khd->hqk", q_normed, block_keys, preferred_element_type=jnp.float32)
            * scaling
        )
        inside = (key_places >= 0) & (key_places < tok_count)
        pair_ok = (query_clip[:, None] == clip_of(key_places)[None, :]) & inside[None, :]
        distance = jnp.abs(positions[:, None] - key_places[None, :])
        allowed = (distance[None, :, :] <= half_window[:, None, None]) & pair_ok[None, :, :]
        masked = jnp.where(allowed, scores, -jnp.inf)
        new_best = jnp.maximum(best, jnp.max(masked, axis=2))
        weights = jnp.exp(masked - new_best[:, :, None])
        shrink = jnp.exp(best - new_best)
        denominator = denominator * shrink + jnp.sum(weights, axis=2)
        accum = accum * shrink[:, :, None] + jnp.einsum(
            "hqk,khd->hqd",
            weights.astype(jnp.bfloat16),
            block_values,
            preferred_element_type=jnp.float32,
        )
        return (new_best, denominator, accum)

    start_state = (
        jnp.full((local_heads, tok_rows), -jnp.inf, jnp.float32),
        jnp.zeros((local_heads, tok_rows), jnp.float32),
        jnp.zeros((local_heads, tok_rows, head_dim), jnp.float32),
    )
    state_now = absorb(start_state, k_normed, value_rows, first_row)
    reach_blocks = HALF // tok_rows
    for distance_step in range(1, reach_blocks + 1):
        left_keys, left_values = passed_along((k_normed, value_rows), "tok", distance_step)
        state_now = absorb(state_now, left_keys, left_values, first_row - distance_step * tok_rows)
        right_keys, right_values = passed_along((k_normed, value_rows), "tok", -distance_step)
        state_now = absorb(
            state_now, right_keys, right_values, first_row + distance_step * tok_rows
        )
    attended = state_now[2] / state_now[1][:, :, None]
    key_unit = unit_rows(k_normed)
    query_unit = unit_rows(q_normed)
    pre_keys = jnp.einsum("thd,hdf->htf", key_unit, fast_in, preferred_element_type=jnp.float32)
    gate_part = pre_keys[:, :, :fast_hid]
    lin_part = pre_keys[:, :, fast_hid:]
    sigmoid_gate = jax.nn.sigmoid(gate_part)
    swish_gate = gate_part * sigmoid_gate
    hidden = (swish_gate * lin_part).astype(jnp.bfloat16)
    value_float = value_rows.astype(jnp.float32)
    push_out = (-jnp.transpose(rate_out)[:, :, None] * value_float).astype(jnp.bfloat16)
    push_in = (-jnp.transpose(rate_in)[:, :, None] * value_float).astype(jnp.bfloat16)
    grad_out = jnp.einsum("htf,thd->hfd", hidden, push_out, preferred_element_type=jnp.float32)
    hidden_grad = jnp.einsum("thd,hfd->htf", push_in, fast_out, preferred_element_type=jnp.float32)
    d_gate = hidden_grad * lin_part * sigmoid_gate * (1.0 + gate_part * (1.0 - sigmoid_gate))
    d_lin = hidden_grad * swish_gate
    d_pre = jnp.concatenate([d_gate, d_lin], axis=2).astype(jnp.bfloat16)
    grad_in = jnp.einsum("thd,htf->hdf", key_unit, d_pre, preferred_element_type=jnp.float32)
    in_float = fast_in.astype(jnp.float32)
    out_float = fast_out.astype(jnp.float32)
    in_base = jnp.sqrt(jnp.sum(in_float * in_float, axis=1))
    out_base = jnp.sqrt(jnp.sum(out_float * out_float, axis=1))
    summed_in, summed_out = lax.psum((grad_in, grad_out), "tok")
    updated_in = in_float - summed_in
    updated_out = out_float - summed_out
    new_in = rescale(updated_in, in_base, jnp.sum(updated_in * updated_in, axis=1))
    new_out = rescale(updated_out, out_base, jnp.sum(updated_out * updated_out, axis=1))
    pre_query = jnp.einsum("thd,hdf->htf", query_unit, new_in, preferred_element_type=jnp.float32)
    query_gate = pre_query[:, :, :fast_hid]
    query_hidden = (query_gate * jax.nn.sigmoid(query_gate) * pre_query[:, :, fast_hid:]).astype(
        jnp.bfloat16
    )
    fast_result = jnp.einsum(
        "htf,hfd->htd", query_hidden, new_out, preferred_element_type=jnp.float32
    )
    combined = attended + fast_result
    return jnp.transpose(combined, (1, 0, 2)).astype(jnp.bfloat16)


VMEM_BYTES = 56 * 1024 * 1024
HIDDEN_MASK = -1e30
NT = (((1,), (1,)), ((), ()))


def exchanged(x, pairs):
    return lax.ppermute(x, "tok", pairs)


def nt_dot(a, b):
    return lax.dot_general(a, b, NT, preferred_element_type=jnp.float32)


def nn_dot(a, b):
    return jnp.dot(a, b, preferred_element_type=jnp.float32)


def params():
    return pltpu.CompilerParams(vmem_limit_bytes=VMEM_BYTES)


def cost(flops, nbytes):
    return pl.CostEstimate(flops=int(16 * flops), bytes_accessed=int(nbytes), transcendentals=0)


def untouched(arrays):
    return [pl.BlockSpec(memory_space=pl.ANY)] * len(arrays)


def pack_kernel(peers, width_all, fold, place_ref, *refs):
    squares_ref, more_ref, q_gain_ref, k_gain_ref, rate_in_ref, rate_out_ref = refs[:6]
    inputs, outputs = refs[6 : 6 + 3 * peers], refs[6 + 3 * peers : 6 + 5 * peers]
    aux_ref, q_scale_ref, k_scale_ref = refs[-3:]
    rows, dim = q_scale_ref.shape
    rate_rows = rows // 128
    share = q_gain_ref.shape[0] // peers

    @pl.when(pl.program_id(0) == 0)
    def _():
        scales = lax.rsqrt((squares_ref[...] + more_ref[...]) / width_all + epsilon)
        q_scale_ref[...] = jnp.transpose(jnp.broadcast_to(scales[0:1] * fold, (dim, rows)))
        k_scale_ref[...] = jnp.transpose(jnp.broadcast_to(scales[1:2], (dim, rows)))
        aux_ref[...] = jnp.zeros_like(aux_ref)

    q_scale = q_scale_ref[...]
    k_scale = k_scale_ref[...]
    for p in range(peers):
        q_ref, k_ref, v_ref = inputs[3 * p : 3 * p + 3]
        kv_out, q_out = outputs[2 * p : 2 * p + 2]
        head = pl.ds((place_ref[0] ^ p) * share + pl.program_id(0), 1)
        q = (q_ref[0].astype(jnp.float32) * q_scale * q_gain_ref[head, :]).astype(jnp.bfloat16)
        k = (k_ref[0].astype(jnp.float32) * k_scale * k_gain_ref[head, :]).astype(jnp.bfloat16)
        v = v_ref[0]
        q_out[0] = q
        kv_out[0, 0:rows, :] = k
        for i in range(rate_rows):
            piece = slice(i * 128, (i + 1) * 128)
            kv_out[0, rows + i * 128 : rows + (i + 1) * 128, :] = jnp.transpose(v[piece])
        at = 0
        for rate_ref in (rate_in_ref, rate_out_ref):
            rate = rate_ref[head, :]
            high = rate.astype(jnp.bfloat16).astype(jnp.float32)
            for part in (high, rate - high):
                for i in range(rate_rows):
                    aux_ref[at : at + 1, :] = part[:, i * 128 : (i + 1) * 128]
                    at += 1
        for i, array in enumerate((q, k, v)):
            aux_ref[at + i : at + i + 1, :] = array[0:16].astype(jnp.float32)[0:1]
        kv_out[0, 2 * rows :, :] = aux_ref[...].astype(jnp.bfloat16)


def pack(place, sums, q, k, v, gains, rates, peers, aux_rows, width_all, fold):
    heads, rows, dim = q.shape
    share = heads // peers

    def head_of(p):
        return lambda j, place: ((place[0] ^ p) * share + j, 0, 0)

    operands = [*sums, *gains, *rates]
    in_specs = [pl.BlockSpec(a.shape, lambda j, place: (0, 0)) for a in operands]
    out_specs, out_shape = [], []
    kv_rows = 2 * rows + aux_rows
    for p in range(peers):
        for array in (q, k, v):
            in_specs.append(pl.BlockSpec((1,) + array.shape[1:], head_of(p)))
            operands.append(array)
        for out_rows in (kv_rows, rows):
            out_specs.append(pl.BlockSpec((1, out_rows, dim), lambda j, place: (j, 0, 0)))
            out_shape.append(jax.ShapeDtypeStruct((share, out_rows, dim), jnp.bfloat16))
    outs = pl.pallas_call(
        functools.partial(pack_kernel, peers, width_all, fold),
        out_shape=out_shape,
        grid_spec=pltpu.PrefetchScalarGridSpec(
            num_scalar_prefetch=1,
            grid=(share,),
            in_specs=in_specs,
            out_specs=out_specs,
            scratch_shapes=[
                pltpu.VMEM((aux_rows, dim), jnp.float32),
                pltpu.VMEM((rows, dim), jnp.float32),
                pltpu.VMEM((rows, dim), jnp.float32),
            ],
        ),
        compiler_params=params(),
        cost_estimate=cost(0, 12 * heads * rows * dim),
        name="pack",
    )(place, *operands)
    return outs[0::2], outs[1::2]


def grads_kernel(count, rows, rate_rows, place_ref, in_ref, out_ref, *refs):
    blocks, grad_ref = refs[:count], refs[-1]
    hid = out_ref.shape[1]
    part = hid // 2
    core = place_ref[1]
    own = pl.multiple_of(core * part, part)
    in_half = jnp.concatenate(
        [
            jnp.transpose(in_ref[0, :, pl.ds(at, part)].astype(jnp.float32))
            for at in (own, pl.multiple_of(hid + own, part))
        ],
        axis=0,
    ).astype(jnp.bfloat16)
    out_half = out_ref[0, pl.ds(own, part), :]
    sum_in = jnp.zeros((2 * part, in_half.shape[1]), jnp.float32)
    sum_out = jnp.zeros((part, in_half.shape[1]), jnp.float32)
    for block in blocks:
        k = block[0, 0:rows, :].astype(jnp.float32)
        v_t = jnp.concatenate(
            [block[0, at : at + 128, :] for at in range(rows, 2 * rows, 128)], axis=1
        )
        aux = block[0, 2 * rows :, :].astype(jnp.float32)

        def rate(at):
            both = aux[at : at + rate_rows] + aux[at + rate_rows : at + 2 * rate_rows]
            return jnp.concatenate([both[i : i + 1] for i in range(rate_rows)], axis=1)

        rate_in, rate_out = rate(0), rate(2 * rate_rows)
        unit = (k * lax.rsqrt(jnp.sum(k * k, axis=1, keepdims=True) + epsilon)).astype(
            jnp.bfloat16
        )
        pre = nt_dot(in_half, unit)
        gate, lin = pre[:part], pre[part:]
        sig = jax.nn.sigmoid(gate)
        swish = gate * sig
        pushed = (swish * lin * -rate_out).astype(jnp.bfloat16)
        hidden_grad = nn_dot(out_half, v_t) * -rate_in
        d_gate = hidden_grad * lin * sig * (1.0 + gate * (1.0 - sig))
        d_lin = hidden_grad * swish
        d_pre = jnp.concatenate([d_gate, d_lin], axis=0).astype(jnp.bfloat16)
        sum_in += nn_dot(d_pre, unit)
        sum_out += nt_dot(pushed, v_t)
    grad_ref[0, 0 : 2 * part, :] = sum_in.astype(jnp.bfloat16)
    grad_ref[0, 2 * part :, :] = sum_out.astype(jnp.bfloat16)


def gradients(place, fast_in, fast_out, blocks, rows, first, heads, after):
    share = blocks[0].shape[0]
    _, hid, dim = fast_out.shape

    def spec(array):
        return pl.BlockSpec((1,) + array.shape[1:], lambda j, place: (first + j, 0, 0))

    def weights(array):
        return pl.BlockSpec(
            (1,) + array.shape[1:], lambda j, place: (place[0] * share + first + j, 0, 0)
        )

    operands = [fast_in, fast_out, *blocks, *after]
    grad_shape = (heads, 3 * hid // 2, dim)
    return pl.pallas_call(
        functools.partial(grads_kernel, len(blocks), rows, rows // 128),
        out_shape=jax.ShapeDtypeStruct(grad_shape, jnp.bfloat16),
        grid_spec=pltpu.PrefetchScalarGridSpec(
            num_scalar_prefetch=1,
            grid=(heads,),
            in_specs=[weights(fast_in), weights(fast_out)]
            + [spec(a) for a in blocks]
            + untouched(after),
            out_specs=pl.BlockSpec((1,) + grad_shape[1:], lambda j, place: (j, 0, 0)),
        ),
        compiler_params=params(),
        cost_estimate=cost(6 * heads * hid * dim * rows * len(blocks), 0),
        name="gradients",
    )(place, *operands)


def attend_kernel(peers, rows, rate_rows, share, first, place_ref, window_ref, edge_ref, *refs):
    own_blocks, other_blocks = refs[:peers], refs[peers : 2 * peers]
    queries = refs[2 * peers : 3 * peers]
    fwd_ref = refs[3 * peers]
    out_ref, extra_ref, k_scr, vt_scr, q_scr = refs[-5:]
    span = 2 * peers * rows
    dim = k_scr.shape[1]
    pad = fwd_ref.shape[1]
    chip, core, half = place_ref[0], place_ref[1], place_ref[2]
    base = half * span
    limit = span + 1 - half
    step = pl.program_id(0)
    window = window_ref[chip * share + first + step]

    @pl.when(step == 0)
    def _():
        k_scr[span:, :] = jnp.zeros((k_scr.shape[0] - span, dim), k_scr.dtype)
        vt_scr[:, span:] = jnp.zeros((vt_scr.shape[0], vt_scr.shape[1] - span), vt_scr.dtype)
        vt_scr[dim:, :] = jnp.ones((vt_scr.shape[0] - dim, vt_scr.shape[1]), vt_scr.dtype)

    for p in range(peers):
        for block, lane in ((own_blocks[p], core), (other_blocks[p], 1 - core)):
            at = pl.multiple_of(((chip ^ p) * 2 + lane) * rows, rows)
            k_scr[pl.ds(at, rows), :] = block[0, 0:rows, :]
            for i in range(0, rows, 128):
                piece = block[0, rows + i : rows + i + 128, :]
                vt_scr[0:dim, pl.ds(pl.multiple_of(at + i, 128), 128)] = piece
        q_scr[chip ^ p] = queries[p][0]
    fwd = fwd_ref[0].astype(jnp.float32)
    q_lone, k_lone, v_lone = (fwd[4 * rate_rows + i : 4 * rate_rows + i + 1] for i in range(3))
    k_scr[span : span + pad, :] = jnp.broadcast_to(k_lone, (pad, dim)).astype(jnp.bfloat16)
    vt_scr[0:dim, span : span + 128] = jnp.transpose(
        jnp.broadcast_to(v_lone, (128, dim))
    ).astype(jnp.bfloat16)

    def clip_start(place):
        start = jnp.zeros_like(place)
        for i in range(edge_ref.shape[0]):
            start = jnp.maximum(start, jnp.where(edge_ref[i] <= place, edge_ref[i], 0))
        return start

    def clip_stop(place):
        stop = jnp.full_like(place, base + limit)
        for i in range(edge_ref.shape[0]):
            stop = jnp.minimum(stop, jnp.where(edge_ref[i] > place, edge_ref[i], base + limit))
        return stop

    def lowest(place):
        return jnp.maximum(jnp.maximum(place - window, clip_start(place)), base) - base

    def highest(place):
        return jnp.minimum(place + window, clip_stop(place) - 1) - base

    def one_pair(i, carry):
        pair = []
        for c in (i, peers - 1 - i):
            start = (c * 2 + core) * rows
            place = base + start + lax.broadcasted_iota(jnp.int32, (1, rows), 1)
            from_key = lowest(base + start) // 128 * 128
            count = (highest(base + start + rows - 1) - from_key) // 256 + 1
            pair.append((c, lowest(place), highest(place), from_key, count))
        count = jnp.maximum(pair[0][4], pair[1][4])

        def variant(chunks):
            width = chunks * 256
            key = lax.broadcasted_iota(jnp.int32, (width, rows), 0)
            froms = [
                pl.multiple_of(jnp.minimum(each[3], k_scr.shape[0] - width), 128) for each in pair
            ]
            scores = [
                nt_dot(k_scr[pl.ds(at, width), :], q_scr[each[0]])
                for each, at in zip(pair, froms)
            ]
            scores = [
                jnp.where((key >= each[1] - at) & (key <= each[2] - at), one, HIDDEN_MASK)
                for each, at, one in zip(pair, froms, scores)
            ]
            weights = [
                jnp.exp2(one - jnp.max(one, axis=0, keepdims=True)).astype(jnp.bfloat16)
                for one in scores
            ]
            totals = [
                nn_dot(vt_scr[:, pl.ds(at, width)], one) for at, one in zip(froms, weights)
            ]
            for each, total in zip(pair, totals):
                attended = total[0:dim] * (1.0 / total[dim : dim + 1])
                at = pl.multiple_of((each[0] ^ chip) * rows, rows)
                out_ref[0, pl.ds(at, rows), :] = jnp.transpose(attended)

        for chunks in range(1, span // 256 + 2):

            @pl.when(count == chunks)
            def _(chunks=chunks):
                variant(chunks)

        return carry

    lax.fori_loop(0, peers // 2, one_pair, 0)
    extra_ref[0] = jnp.zeros(extra_ref.shape[1:], jnp.float32)

    @pl.when((half == 0) & (core == 1))
    def _():
        near = span - HALF
        width = HALF + 128
        q = jnp.broadcast_to(q_lone, (pad, dim)).astype(jnp.bfloat16)
        scores = nt_dot(q, k_scr[near : near + width, :])
        key = near + lax.broadcasted_iota(jnp.int32, (1, width), 1)
        scores = jnp.where((key >= span - window) & (key <= span), scores, HIDDEN_MASK)
        top = jnp.max(scores, axis=1, keepdims=True)
        weights = jnp.exp2(scores - top).astype(jnp.bfloat16)
        total = nt_dot(weights, vt_scr[:, near : near + width])
        extra_ref[0] = total[:, 0:dim] / total[:, dim : dim + 1]


def attend(
    place, half_window, boundaries, own_kv, other_kv, queries, forwarded, first, heads, after
):
    peers = len(queries)
    share, rows, dim = queries[0].shape
    pad = forwarded.shape[1]
    span = 2 * peers * rows
    scr_rows = span + 256

    def spec(array):
        return pl.BlockSpec((1,) + array.shape[1:], lambda j, *_: (first + j, 0, 0))

    def out_spec(out_rows):
        return pl.BlockSpec((1, out_rows, dim), lambda j, *_: (j, 0, 0))

    operands = [*own_kv, *other_kv, *queries, forwarded]
    in_specs = [spec(a) for a in operands] + untouched(after)
    operands += after
    return pl.pallas_call(
        functools.partial(attend_kernel, peers, rows, rows // 128, share, first),
        out_shape=[
            jax.ShapeDtypeStruct((heads, peers * rows, dim), jnp.float32),
            jax.ShapeDtypeStruct((heads, pad, dim), jnp.float32),
        ],
        grid_spec=pltpu.PrefetchScalarGridSpec(
            num_scalar_prefetch=3,
            grid=(heads,),
            in_specs=in_specs,
            out_specs=[out_spec(peers * rows), out_spec(pad)],
            scratch_shapes=[
                pltpu.VMEM((scr_rows, dim), jnp.bfloat16),
                pltpu.VMEM((dim + 16, scr_rows), jnp.bfloat16),
                pltpu.VMEM((peers, rows, dim), jnp.bfloat16),
            ],
        ),
        compiler_params=params(),
        cost_estimate=cost(4 * heads * peers * rows * HALF * 2 * dim, 0),
        name="attend",
    )(place, half_window, boundaries, *operands)


def finish_kernel(peers, rows, unit_epsilon, place_ref, *refs):
    att_ref, base_in_ref, base_out_ref, own_ref, other_ref, patch_ref = refs[:6]
    queries = refs[6 : 6 + peers]
    outs = refs[-2 - peers : -2]
    grad_in_scr, grad_out_scr = refs[-2:]
    chip, core, half = place_ref[0], place_ref[1], place_ref[2]
    hid = base_out_ref.shape[1]
    part = hid // 2
    for summed, lane in ((own_ref, core), (other_ref, 1 - core)):
        at = pl.multiple_of(lane * part, part)
        grad_in_scr[pl.ds(at, part), :] = summed[0, 0:part, :].astype(jnp.float32)
        grad_in_scr[pl.ds(hid + at, part), :] = summed[0, part : 2 * part, :].astype(jnp.float32)
        grad_out_scr[pl.ds(at, part), :] = summed[0, 2 * part :, :].astype(jnp.float32)

    def renewed(base, grad):
        base = base.astype(jnp.float32)
        updated = base - grad
        norm = jnp.sqrt(jnp.sum(base * base, axis=0, keepdims=True))
        squares = jnp.sum(updated * updated, axis=0, keepdims=True)
        return (updated * (norm / jnp.sqrt(squares + epsilon))).astype(jnp.bfloat16)

    new_in = renewed(base_in_ref[0], jnp.transpose(grad_in_scr[...]))
    new_out = renewed(base_out_ref[0], grad_out_scr[...])
    patch = patch_ref[0][0:1, :]
    row = lax.broadcasted_iota(jnp.int32, (rows, 1), 0)
    for p in range(peers):
        q = queries[p][0].astype(jnp.float32)
        unit = (q * lax.rsqrt(jnp.sum(q * q, axis=1, keepdims=True) + unit_epsilon)).astype(
            jnp.bfloat16
        )
        pre = nn_dot(unit, new_in)
        gate = pre[:, :hid]
        hidden = (gate * jax.nn.sigmoid(gate) * pre[:, hid:]).astype(jnp.bfloat16)
        attended = att_ref[0, p * rows : (p + 1) * rows, :]
        patched = (half == 1) & (core == 0) & (chip == p)
        attended = jnp.where(patched & (row == 0), patch, attended)
        outs[p][0] = (attended + nn_dot(hidden, new_out)).astype(jnp.bfloat16)


def finish(
    place, attended, fast_in, fast_out, sums, patch, queries, first, unit_epsilon, after
):
    peers = len(queries)
    heads = attended.shape[0]
    share, rows, dim = queries[0].shape
    hid = fast_out.shape[1]

    def weights(array):
        return pl.BlockSpec(
            (1,) + array.shape[1:], lambda j, place: (place[0] * share + first + j, 0, 0)
        )

    def shifted(array):
        return pl.BlockSpec((1,) + array.shape[1:], lambda j, place: (first + j, 0, 0))

    def plain(shape):
        return pl.BlockSpec((1,) + shape[1:], lambda j, place: (j, 0, 0))

    own_sum, other_sum = sums
    operands = [attended, fast_in, fast_out, own_sum, other_sum, patch, *queries, *after]
    in_specs = [plain(attended.shape), weights(fast_in), weights(fast_out)]
    in_specs += [plain(own_sum.shape), plain(other_sum.shape), plain(patch.shape)]
    in_specs += [shifted(a) for a in queries] + untouched(after)
    out_shape = (heads, rows, dim)
    return pl.pallas_call(
        functools.partial(finish_kernel, peers, rows, unit_epsilon),
        out_shape=[jax.ShapeDtypeStruct(out_shape, jnp.bfloat16)] * peers,
        grid_spec=pltpu.PrefetchScalarGridSpec(
            num_scalar_prefetch=1,
            grid=(heads,),
            in_specs=in_specs,
            out_specs=[plain(out_shape)] * peers,
            scratch_shapes=[
                pltpu.VMEM((2 * hid, dim), jnp.float32),
                pltpu.VMEM((hid, dim), jnp.float32),
            ],
        ),
        compiler_params=params(),
        cost_estimate=cost(12 * heads * peers * rows * hid * dim, 0),
        name="finish",
    )(place, *operands)


def place_kernel(peers, chunks, share, place_ref, *refs):
    pieces, out_ref, sems = refs[:-2], refs[-2], refs[-1]
    copies = []
    for c, (first, heads) in enumerate(chunks):
        for p in range(peers):
            at = (place_ref[0] ^ p) * share + first
            copies.append(
                pltpu.make_async_copy(
                    pieces[c * peers + p], out_ref.at[pl.ds(at, heads)], sems.at[c * peers + p]
                )
            )
    for copy in copies:
        copy.start()
    for copy in copies:
        copy.wait()


def put_in_place(place, pieces, peers, chunks, share):
    _, rows, dim = pieces[0].shape
    anywhere = pl.BlockSpec(memory_space=pl.ANY)
    return pl.pallas_call(
        functools.partial(place_kernel, peers, chunks, share),
        out_shape=jax.ShapeDtypeStruct((peers * share, rows, dim), jnp.bfloat16),
        grid_spec=pltpu.PrefetchScalarGridSpec(
            num_scalar_prefetch=1,
            grid=(1,),
            in_specs=[pl.BlockSpec(a.shape, lambda j, place: (0, 0, 0)) for a in pieces],
            out_specs=anywhere,
            scratch_shapes=[pltpu.SemaphoreType.DMA((len(pieces),))],
        ),
        compiler_params=params(),
        name="put_in_place",
    )(place, *pieces)


def regrouping(tok_peers, rows, heads, dim, hid):
    half_peers = tok_peers // 2
    peers = math.gcd(half_peers, heads)
    fits = tok_peers % 2 == 0 and half_peers * rows == 2 * HALF
    fits = fits and half_peers == 2 * peers and peers & (peers - 1) == 0
    fits = fits and rows % 256 == 0 and dim == 128 and hid % 256 == 0
    return peers if fits else 0


def regrouped_body(
    peers,
    query_rows,
    key_rows,
    value_rows,
    query_gain,
    key_gain,
    rate_in,
    rate_out,
    fast_in,
    fast_out,
    half_window,
    boundaries,
):
    rows, heads, dim = query_rows.shape
    share = heads // peers
    tok_peers = lax.axis_size("tok")
    half_peers = tok_peers // 2
    width_all = heads * dim * lax.axis_size("head")
    rate_rows = rows // 128
    aux_rows = -(-(4 * rate_rows + 3) // 16) * 16
    own_index = lax.axis_index("tok")
    half = own_index // half_peers
    chip = own_index % half_peers // 2
    core = own_index % 2
    place = jnp.stack([chip, core, half]).astype(jnp.int32)

    def across(p):
        return [(t, t // half_peers * half_peers + ((t % half_peers) ^ (2 * p))) for t in range(tok_peers)]

    core_pairs = [(t, t ^ 1) for t in range(tok_peers)]
    half_pairs = [(t, (t + half_peers) % tok_peers) for t in range(tok_peers)]
    forward_pairs = [(t + half_peers, t) for t in range(half_peers)]
    back_pairs = [(t, t - 1 + half_peers) for t in range(half_peers) if t % 2 == 1]

    q = jnp.transpose(query_rows, (1, 0, 2))
    k = jnp.transpose(key_rows, (1, 0, 2))
    v = jnp.transpose(value_rows, (1, 0, 2))
    q_float = q.astype(jnp.float32)
    k_float = k.astype(jnp.float32)
    squares = jnp.stack(
        [jnp.sum(q_float * q_float, axis=(0, 2)), jnp.sum(k_float * k_float, axis=(0, 2))]
    )
    if lax.axis_size("head") == 2:
        sums = (squares, lax.ppermute(squares, "head", [(0, 1), (1, 0)]))
    else:
        sums = (lax.psum(squares, "head"), jnp.zeros_like(squares))
    fold = math.log2(math.e) / math.sqrt(dim)
    sent_kv, sent_q = pack(
        place,
        sums,
        q,
        k,
        v,
        (query_gain, key_gain),
        (rate_in, rate_out),
        peers,
        aux_rows,
        width_all,
        fold,
    )
    own_kv = [sent_kv[0]] + [exchanged(sent_kv[p], across(p)) for p in range(1, peers)]
    queries = [sent_q[0]] + [exchanged(sent_q[p], across(p)) for p in range(1, peers)]
    other_kv = [exchanged(x, core_pairs) for x in own_kv]

    first_aux = jnp.zeros((share, aux_rows, dim), jnp.bfloat16)
    for p in range(peers):
        aux = jnp.where(core == 0, own_kv[p][:, 2 * rows :], other_kv[p][:, 2 * rows :])
        first_aux = jnp.where(chip == p, aux, first_aux)
    forwarded = exchanged(first_aux, forward_pairs)

    chunks = [(0, (share + 1) // 2), ((share + 1) // 2, share // 2)]
    grads = []
    after = []
    for first, count in chunks:
        grad = gradients(
            place, fast_in, fast_out, [*own_kv, *other_kv], rows, first, count, after
        )
        after = [grad]
        grads.append((grad, exchanged(grad, half_pairs)))
    sums = []
    answers = []
    for i, (first, count) in enumerate(chunks):
        attended, extra = attend(
            place, half_window, boundaries, own_kv, other_kv, queries, forwarded, first, count, after
        )
        answers.append((attended, exchanged(extra, back_pairs)))
        grad, from_half = grads[i]
        from_half, _ = lax.optimization_barrier((from_half, attended))
        own_sum = (grad.astype(jnp.float32) + from_half.astype(jnp.float32)).astype(jnp.bfloat16)
        sums.append((own_sum, exchanged(own_sum, core_pairs)))
        after = [attended, own_sum]
    pieces = []
    for (first, count), each, (attended, patch) in zip(chunks, sums, answers):
        outs = finish(
            place,
            attended,
            fast_in,
            fast_out,
            each,
            patch,
            queries,
            first,
            epsilon * fold * fold,
            after,
        )
        after = [outs[0]]
        pieces += [outs[0]] + [exchanged(outs[p], across(p)) for p in range(1, peers)]
    whole = put_in_place(place, pieces, peers, chunks, share)
    return jnp.transpose(whole, (1, 0, 2))


def body(query_rows, *others):
    rows, heads, dim = query_rows.shape
    hid = others[7].shape[1]
    peers = regrouping(lax.axis_size("tok"), rows, heads, dim, hid)
    if peers:
        return regrouped_body(peers, query_rows, *others)
    return sliding_body(query_rows, *others)


def solution(mesh):
    in_specs = (
        P("tok", "head", None),
        P("tok", "head", None),
        P("tok", "head", None),
        P("head", None),
        P("head", None),
        P("head", "tok"),
        P("head", "tok"),
        P("head", None, None),
        P("head", None, None),
        P("head"),
        P(),
    )
    out_specs = P("tok", "head", None)
    return jax.shard_map(body, mesh=mesh, in_specs=in_specs, out_specs=out_specs, check_vma=False)
```

```python
import functools
import math

import jax
import jax.numpy as jnp
from jax import lax
from jax.experimental import pallas as pl
from jax.experimental.pallas import tpu as pltpu
from jax.sharding import PartitionSpec as P

HALF = 1024


epsilon = 1e-06


def passed_along(x, axis, by):
    peers = lax.axis_size(axis)
    pairs = [(i, i + by) for i in range(peers) if 0 <= i + by < peers]
    return lax.ppermute(x, axis, pairs)


def unit_rows(matrix):
    as_float = matrix.astype(jnp.float32)
    return (
        as_float * lax.rsqrt(jnp.sum(as_float * as_float, axis=-1, keepdims=True) + epsilon)
    ).astype(jnp.bfloat16)


def rescale(updated, base_norm, squares):
    return (updated * (base_norm / jnp.sqrt(squares + epsilon))[:, None, :]).astype(jnp.bfloat16)


def sliding_body(
    query_rows,
    key_rows,
    value_rows,
    query_gain,
    key_gain,
    rate_in,
    rate_out,
    fast_in,
    fast_out,
    half_window,
    boundaries,
):
    tok_rows = query_rows.shape[0]
    local_heads = query_rows.shape[1]
    head_dim = query_rows.shape[2]
    fast_hid = fast_out.shape[1]
    width_all = local_heads * head_dim * lax.axis_size("head")
    tok_count = tok_rows * lax.axis_size("tok")
    own_index = lax.axis_index("tok")
    first_row = own_index * tok_rows
    query_float = query_rows.astype(jnp.float32)
    key_float = key_rows.astype(jnp.float32)
    query_sq, key_sq = lax.psum(
        (
            jnp.sum(query_float * query_float, axis=(1, 2)),
            jnp.sum(key_float * key_float, axis=(1, 2)),
        ),
        "head",
    )
    q_normed = (
        query_float * lax.rsqrt(query_sq / width_all + epsilon)[:, None, None] * query_gain[None]
    ).astype(jnp.bfloat16)
    k_normed = (
        key_float * lax.rsqrt(key_sq / width_all + epsilon)[:, None, None] * key_gain[None]
    ).astype(jnp.bfloat16)

    def clip_of(places):
        return jnp.sum((places[:, None] >= boundaries[None, :]).astype(jnp.int32), axis=1)

    positions = first_row + jnp.arange(tok_rows, dtype=jnp.int32)
    query_clip = clip_of(positions)
    scaling = 1.0 / math.sqrt(head_dim)

    def absorb(state_now, block_keys, block_values, key_first):
        best, denominator, accum = state_now
        key_places = key_first + jnp.arange(tok_rows, dtype=jnp.int32)
        scores = (
            jnp.einsum("qhd,khd->hqk", q_normed, block_keys, preferred_element_type=jnp.float32)
            * scaling
        )
        inside = (key_places >= 0) & (key_places < tok_count)
        pair_ok = (query_clip[:, None] == clip_of(key_places)[None, :]) & inside[None, :]
        distance = jnp.abs(positions[:, None] - key_places[None, :])
        allowed = (distance[None, :, :] <= half_window[:, None, None]) & pair_ok[None, :, :]
        masked = jnp.where(allowed, scores, -jnp.inf)
        new_best = jnp.maximum(best, jnp.max(masked, axis=2))
        weights = jnp.exp(masked - new_best[:, :, None])
        shrink = jnp.exp(best - new_best)
        denominator = denominator * shrink + jnp.sum(weights, axis=2)
        accum = accum * shrink[:, :, None] + jnp.einsum(
            "hqk,khd->hqd",
            weights.astype(jnp.bfloat16),
            block_values,
            preferred_element_type=jnp.float32,
        )
        return (new_best, denominator, accum)

    start_state = (
        jnp.full((local_heads, tok_rows), -jnp.inf, jnp.float32),
        jnp.zeros((local_heads, tok_rows), jnp.float32),
        jnp.zeros((local_heads, tok_rows, head_dim), jnp.float32),
    )
    state_now = absorb(start_state, k_normed, value_rows, first_row)
    reach_blocks = HALF // tok_rows
    for distance_step in range(1, reach_blocks + 1):
        left_keys, left_values = passed_along((k_normed, value_rows), "tok", distance_step)
        state_now = absorb(state_now, left_keys, left_values, first_row - distance_step * tok_rows)
        right_keys, right_values = passed_along((k_normed, value_rows), "tok", -distance_step)
        state_now = absorb(
            state_now, right_keys, right_values, first_row + distance_step * tok_rows
        )
    attended = state_now[2] / state_now[1][:, :, None]
    key_unit = unit_rows(k_normed)
    query_unit = unit_rows(q_normed)
    pre_keys = jnp.einsum("thd,hdf->htf", key_unit, fast_in, preferred_element_type=jnp.float32)
    gate_part = pre_keys[:, :, :fast_hid]
    lin_part = pre_keys[:, :, fast_hid:]
    sigmoid_gate = jax.nn.sigmoid(gate_part)
    swish_gate = gate_part * sigmoid_gate
    hidden = (swish_gate * lin_part).astype(jnp.bfloat16)
    value_float = value_rows.astype(jnp.float32)
    push_out = (-jnp.transpose(rate_out)[:, :, None] * value_float).astype(jnp.bfloat16)
    push_in = (-jnp.transpose(rate_in)[:, :, None] * value_float).astype(jnp.bfloat16)
    grad_out = jnp.einsum("htf,thd->hfd", hidden, push_out, preferred_element_type=jnp.float32)
    hidden_grad = jnp.einsum("thd,hfd->htf", push_in, fast_out, preferred_element_type=jnp.float32)
    d_gate = hidden_grad * lin_part * sigmoid_gate * (1.0 + gate_part * (1.0 - sigmoid_gate))
    d_lin = hidden_grad * swish_gate
    d_pre = jnp.concatenate([d_gate, d_lin], axis=2).astype(jnp.bfloat16)
    grad_in = jnp.einsum("thd,htf->hdf", key_unit, d_pre, preferred_element_type=jnp.float32)
    in_float = fast_in.astype(jnp.float32)
    out_float = fast_out.astype(jnp.float32)
    in_base = jnp.sqrt(jnp.sum(in_float * in_float, axis=1))
    out_base = jnp.sqrt(jnp.sum(out_float * out_float, axis=1))
    summed_in, summed_out = lax.psum((grad_in, grad_out), "tok")
    updated_in = in_float - summed_in
    updated_out = out_float - summed_out
    new_in = rescale(updated_in, in_base, jnp.sum(updated_in * updated_in, axis=1))
    new_out = rescale(updated_out, out_base, jnp.sum(updated_out * updated_out, axis=1))
    pre_query = jnp.einsum("thd,hdf->htf", query_unit, new_in, preferred_element_type=jnp.float32)
    query_gate = pre_query[:, :, :fast_hid]
    query_hidden = (query_gate * jax.nn.sigmoid(query_gate) * pre_query[:, :, fast_hid:]).astype(
        jnp.bfloat16
    )
    fast_result = jnp.einsum(
        "htf,hfd->htd", query_hidden, new_out, preferred_element_type=jnp.float32
    )
    combined = attended + fast_result
    return jnp.transpose(combined, (1, 0, 2)).astype(jnp.bfloat16)


VMEM_BYTES = 32 * 1024 * 1024
HIDDEN_MASK = -1e30
NT = (((1,), (1,)), ((), ()))


def exchanged(x, pairs):
    return lax.ppermute(x, "tok", pairs)


def nt_dot(a, b):
    return lax.dot_general(a, b, NT, preferred_element_type=jnp.float32)


def nn_dot(a, b):
    return jnp.dot(a, b, preferred_element_type=jnp.float32)


def params():
    return pltpu.CompilerParams(vmem_limit_bytes=VMEM_BYTES)


def cost(flops, nbytes):
    return pl.CostEstimate(flops=int(16 * flops), bytes_accessed=int(nbytes), transcendentals=0)


def untouched(arrays):
    return [pl.BlockSpec(memory_space=pl.ANY)] * len(arrays)


def pack_kernel(first, width_all, fold, *refs):
    squares_ref, more_ref, q_gain_ref, k_gain_ref, rate_in_ref, rate_out_ref = refs[:6]
    q_ref, k_ref, v_ref, out_ref = refs[6:10]
    aux_ref, q_scale_ref, k_scale_ref = refs[-3:]
    rows, dim = q_scale_ref.shape
    rate_rows = rows // 128
    peers = q_ref.shape[0]
    share = q_gain_ref.shape[0] // peers

    @pl.when(pl.program_id(0) == 0)
    def _():
        scales = lax.rsqrt((squares_ref[...] + more_ref[...]) / width_all + epsilon)
        q_scale_ref[...] = jnp.transpose(jnp.broadcast_to(scales[0:1] * fold, (dim, rows)))
        k_scale_ref[...] = jnp.transpose(jnp.broadcast_to(scales[1:2], (dim, rows)))
        aux_ref[...] = jnp.zeros_like(aux_ref)

    q_scale = q_scale_ref[...]
    k_scale = k_scale_ref[...]
    for c in range(peers):
        head = pl.ds(c * share + first + pl.program_id(0), 1)
        q = (q_ref[c, 0].astype(jnp.float32) * q_scale * q_gain_ref[head, :]).astype(jnp.bfloat16)
        k = (k_ref[c, 0].astype(jnp.float32) * k_scale * k_gain_ref[head, :]).astype(jnp.bfloat16)
        v = v_ref[c, 0]
        out_ref[c, 0, 0:rows, :] = q
        out_ref[c, 0, rows : 2 * rows, :] = k
        for i in range(0, rows, 128):
            out_ref[c, 0, 2 * rows + i : 2 * rows + i + 128, :] = jnp.transpose(v[i : i + 128])
        at = 0
        for rate_ref in (rate_in_ref, rate_out_ref):
            rate = rate_ref[head, :]
            high = rate.astype(jnp.bfloat16).astype(jnp.float32)
            for part in (high, rate - high):
                for i in range(rate_rows):
                    aux_ref[at : at + 1, :] = part[:, i * 128 : (i + 1) * 128]
                    at += 1
        for i, array in enumerate((q, k, v)):
            aux_ref[at + i : at + i + 1, :] = array[0:16].astype(jnp.float32)[0:1]
        out_ref[c, 0, 3 * rows :, :] = aux_ref[...].astype(jnp.bfloat16)


def pack(sums, q, k, v, gains, rates, peers, aux_rows, first, count, width_all, fold):
    heads, rows, dim = q.shape
    packet = 3 * rows + aux_rows
    dealt = [x.reshape(peers, heads // peers, rows, dim) for x in (q, k, v)]
    whole = [*sums, *gains, *rates]
    return pl.pallas_call(
        functools.partial(pack_kernel, first, width_all, fold),
        out_shape=jax.ShapeDtypeStruct((peers, count, packet, dim), jnp.bfloat16),
        grid=(count,),
        in_specs=[pl.BlockSpec(a.shape, lambda j: (0, 0)) for a in whole]
        + [pl.BlockSpec((peers, 1, rows, dim), lambda j: (0, first + j, 0, 0))] * 3,
        out_specs=pl.BlockSpec((peers, 1, packet, dim), lambda j: (0, j, 0, 0)),
        scratch_shapes=[
            pltpu.VMEM((aux_rows, dim), jnp.float32),
            pltpu.VMEM((rows, dim), jnp.float32),
            pltpu.VMEM((rows, dim), jnp.float32),
        ],
        compiler_params=params(),
        cost_estimate=cost(0, 12 * peers * count * rows * dim),
        name="pack",
    )(*whole, *dealt)


def grads_kernel(rows, rate_rows, place_ref, in_ref, out_ref, own_ref, other_ref, *refs):
    grad_ref = refs[-1]
    hid = out_ref.shape[1]
    part = hid // 2
    core = place_ref[1]
    own = pl.multiple_of(core * part, part)
    in_half = jnp.concatenate(
        [
            jnp.transpose(in_ref[0, :, pl.ds(at, part)].astype(jnp.float32))
            for at in (own, pl.multiple_of(hid + own, part))
        ],
        axis=0,
    ).astype(jnp.bfloat16)
    out_half = out_ref[0, pl.ds(own, part), :]
    sum_in = jnp.zeros((2 * part, in_half.shape[1]), jnp.float32)
    sum_out = jnp.zeros((part, in_half.shape[1]), jnp.float32)
    for block in [ref.at[c, 0] for ref in (own_ref, other_ref) for c in range(own_ref.shape[0])]:
        k = block[rows : 2 * rows, :].astype(jnp.float32)
        v_t = jnp.concatenate(
            [block[at : at + 128, :] for at in range(2 * rows, 3 * rows, 128)], axis=1
        )
        aux = block[3 * rows :, :].astype(jnp.float32)

        def rate(at):
            both = aux[at : at + rate_rows] + aux[at + rate_rows : at + 2 * rate_rows]
            return jnp.concatenate([both[i : i + 1] for i in range(rate_rows)], axis=1)

        rate_in, rate_out = rate(0), rate(2 * rate_rows)
        unit = (k * lax.rsqrt(jnp.sum(k * k, axis=1, keepdims=True) + epsilon)).astype(
            jnp.bfloat16
        )
        pre = nt_dot(in_half, unit)
        gate, lin = pre[:part], pre[part:]
        sig = jax.nn.sigmoid(gate)
        swish = gate * sig
        pushed = (swish * lin * -rate_out).astype(jnp.bfloat16)
        hidden_grad = nn_dot(out_half, v_t) * -rate_in
        d_gate = hidden_grad * lin * sig * (1.0 + gate * (1.0 - sig))
        d_lin = hidden_grad * swish
        d_pre = jnp.concatenate([d_gate, d_lin], axis=0).astype(jnp.bfloat16)
        sum_in += nn_dot(d_pre, unit)
        sum_out += nt_dot(pushed, v_t)
    grad_ref[0, 0 : 2 * part, :] = sum_in.astype(jnp.bfloat16)
    grad_ref[0, 2 * part :, :] = sum_out.astype(jnp.bfloat16)


def chip_weights(array, share, first):
    return pl.BlockSpec(
        (1,) + array.shape[1:], lambda j, place, *_: (place[0] * share + first + j, 0, 0)
    )


def by_head(shape):
    return pl.BlockSpec((shape[0], 1) + shape[2:], lambda j, *_: (0, j, 0, 0))


def gradients(place, fast_in, fast_out, own, other, share, rows, first, after):
    _, hid, dim = fast_out.shape
    peers, heads = own.shape[:2]
    grad_shape = (heads, 3 * hid // 2, dim)
    return pl.pallas_call(
        functools.partial(grads_kernel, rows, rows // 128),
        out_shape=jax.ShapeDtypeStruct(grad_shape, jnp.bfloat16),
        grid_spec=pltpu.PrefetchScalarGridSpec(
            num_scalar_prefetch=1,
            grid=(heads,),
            in_specs=[chip_weights(a, share, first) for a in (fast_in, fast_out)]
            + [by_head(own.shape)] * 2
            + untouched(after),
            out_specs=pl.BlockSpec((1,) + grad_shape[1:], lambda j, place: (j, 0, 0)),
        ),
        compiler_params=params(),
        cost_estimate=cost(6 * heads * hid * dim * rows * 2 * peers, 0),
        name="gradients",
    )(place, fast_in, fast_out, own, other, *after)


def attend_kernel(rows, rate_rows, share, first, place_ref, window_ref, edge_ref, *refs):
    own_ref, other_ref, fwd_ref = refs[:3]
    out_ref, extra_ref, k_scr, vt_scr = refs[-4:]
    peers = own_ref.shape[0]
    span = 2 * peers * rows
    dim = k_scr.shape[1]
    pad = fwd_ref.shape[1]
    chip, core, half = place_ref[0], place_ref[1], place_ref[2]
    base = half * span
    limit = span + 1 - half
    step = pl.program_id(0)
    window = window_ref[chip * share + first + step]

    @pl.when(step == 0)
    def _():
        k_scr[span:, :] = jnp.zeros((k_scr.shape[0] - span, dim), k_scr.dtype)
        vt_scr[:, span:] = jnp.zeros((vt_scr.shape[0], vt_scr.shape[1] - span), vt_scr.dtype)
        vt_scr[dim:, :] = jnp.ones((vt_scr.shape[0] - dim, vt_scr.shape[1]), vt_scr.dtype)

    for c in range(peers):
        for ref, lane in ((own_ref, core), (other_ref, 1 - core)):
            at = pl.multiple_of((c * 2 + lane) * rows, rows)
            k_scr[pl.ds(at, rows), :] = ref[c, 0, rows : 2 * rows, :]
            for i in range(0, rows, 128):
                piece = ref[c, 0, 2 * rows + i : 2 * rows + i + 128, :]
                vt_scr[0:dim, pl.ds(pl.multiple_of(at + i, 128), 128)] = piece
    fwd = fwd_ref[0].astype(jnp.float32)
    q_lone, k_lone, v_lone = (fwd[4 * rate_rows + i : 4 * rate_rows + i + 1] for i in range(3))
    k_scr[span : span + pad, :] = jnp.broadcast_to(k_lone, (pad, dim)).astype(jnp.bfloat16)
    vt_scr[0:dim, span : span + 128] = jnp.transpose(
        jnp.broadcast_to(v_lone, (128, dim))
    ).astype(jnp.bfloat16)

    def clip_start(place):
        start = jnp.zeros_like(place)
        for i in range(edge_ref.shape[0]):
            start = jnp.maximum(start, jnp.where(edge_ref[i] <= place, edge_ref[i], 0))
        return start

    def clip_stop(place):
        stop = jnp.full_like(place, base + limit)
        for i in range(edge_ref.shape[0]):
            stop = jnp.minimum(stop, jnp.where(edge_ref[i] > place, edge_ref[i], base + limit))
        return stop

    def lowest(place):
        return jnp.maximum(jnp.maximum(place - window, clip_start(place)), base) - base

    def highest(place):
        return jnp.minimum(place + window, clip_stop(place) - 1) - base

    def one_pair(i, carry):
        pair = []
        for c in (i, peers - 1 - i):
            start = (c * 2 + core) * rows
            place = base + start + lax.broadcasted_iota(jnp.int32, (1, rows), 1)
            from_key = lowest(base + start) // 128 * 128
            count = (highest(base + start + rows - 1) - from_key) // 256 + 1
            pair.append((c, lowest(place), highest(place), from_key, count))
        count = jnp.maximum(pair[0][4], pair[1][4])

        def variant(chunks):
            width = chunks * 256
            key = lax.broadcasted_iota(jnp.int32, (width, rows), 0)
            froms = [
                pl.multiple_of(jnp.minimum(each[3], k_scr.shape[0] - width), 128) for each in pair
            ]
            scores = [
                nt_dot(k_scr[pl.ds(at, width), :], own_ref[each[0], 0, 0:rows, :])
                for each, at in zip(pair, froms)
            ]
            scores = [
                jnp.where((key >= each[1] - at) & (key <= each[2] - at), one, HIDDEN_MASK)
                for each, at, one in zip(pair, froms, scores)
            ]
            weights = [
                jnp.exp2(one - jnp.max(one, axis=0, keepdims=True)).astype(jnp.bfloat16)
                for one in scores
            ]
            totals = [
                nn_dot(vt_scr[:, pl.ds(at, width)], one) for at, one in zip(froms, weights)
            ]
            for each, total in zip(pair, totals):
                attended = total[0:dim] * (1.0 / total[dim : dim + 1])
                out_ref[each[0], 0] = jnp.transpose(attended)

        for chunks in range(1, span // 256 + 2):

            @pl.when(count == chunks)
            def _(chunks=chunks):
                variant(chunks)

        return carry

    lax.fori_loop(0, peers // 2, one_pair, 0)
    extra_ref[0] = jnp.zeros(extra_ref.shape[1:], jnp.float32)

    @pl.when((half == 0) & (core == 1))
    def _():
        near = span - HALF
        width = HALF + 128
        q = jnp.broadcast_to(q_lone, (pad, dim)).astype(jnp.bfloat16)
        scores = nt_dot(q, k_scr[near : near + width, :])
        key = near + lax.broadcasted_iota(jnp.int32, (1, width), 1)
        scores = jnp.where((key >= span - window) & (key <= span), scores, HIDDEN_MASK)
        top = jnp.max(scores, axis=1, keepdims=True)
        weights = jnp.exp2(scores - top).astype(jnp.bfloat16)
        total = nt_dot(weights, vt_scr[:, near : near + width])
        extra_ref[0] = total[:, 0:dim] / total[:, dim : dim + 1]


def attend(place, half_window, boundaries, own, other, forwarded, share, rows, first, after):
    peers, heads, _, dim = own.shape
    pad = forwarded.shape[1]
    span = 2 * peers * rows
    scr_rows = span + 256
    out_shapes = [(peers, heads, rows, dim), (heads, pad, dim)]
    one_head = pl.BlockSpec((1, pad, dim), lambda j, *_: (j, 0, 0))
    return pl.pallas_call(
        functools.partial(attend_kernel, rows, rows // 128, share, first),
        out_shape=[jax.ShapeDtypeStruct(shape, jnp.float32) for shape in out_shapes],
        grid_spec=pltpu.PrefetchScalarGridSpec(
            num_scalar_prefetch=3,
            grid=(heads,),
            in_specs=[by_head(own.shape)] * 2 + [one_head] + untouched(after),
            out_specs=[by_head(out_shapes[0]), one_head],
            scratch_shapes=[
                pltpu.VMEM((scr_rows, dim), jnp.bfloat16),
                pltpu.VMEM((dim + 16, scr_rows), jnp.bfloat16),
            ],
        ),
        compiler_params=params(),
        cost_estimate=cost(4 * heads * peers * rows * HALF * 2 * dim, 0),
        name="attend",
    )(place, half_window, boundaries, own, other, forwarded, *after)


def finish_kernel(unit_epsilon, place_ref, *refs):
    att_ref, base_in_ref, base_out_ref, own_ref, other_ref, patch_ref, q_ref = refs[:7]
    out_ref, grad_in_scr, grad_out_scr = refs[-3:]
    core, half = place_ref[1], place_ref[2]
    peers, _, rows, _ = q_ref.shape
    hid = base_out_ref.shape[1]
    part = hid // 2
    for summed, lane in ((own_ref, core), (other_ref, 1 - core)):
        at = pl.multiple_of(lane * part, part)
        grad_in_scr[pl.ds(at, part), :] = summed[0, 0:part, :].astype(jnp.float32)
        grad_in_scr[pl.ds(hid + at, part), :] = summed[0, part : 2 * part, :].astype(jnp.float32)
        grad_out_scr[pl.ds(at, part), :] = summed[0, 2 * part :, :].astype(jnp.float32)

    def renewed(base, grad):
        base = base.astype(jnp.float32)
        updated = base - grad
        norm = jnp.sqrt(jnp.sum(base * base, axis=0, keepdims=True))
        squares = jnp.sum(updated * updated, axis=0, keepdims=True)
        return (updated * (norm / jnp.sqrt(squares + epsilon))).astype(jnp.bfloat16)

    new_in = renewed(base_in_ref[0], jnp.transpose(grad_in_scr[...]))
    new_out = renewed(base_out_ref[0], grad_out_scr[...])
    patch = patch_ref[0][0:1, :]
    row = lax.broadcasted_iota(jnp.int32, (rows, 1), 0)
    for c in range(peers):
        q = q_ref[c, 0].astype(jnp.float32)
        unit = (q * lax.rsqrt(jnp.sum(q * q, axis=1, keepdims=True) + unit_epsilon)).astype(
            jnp.bfloat16
        )
        pre = nn_dot(unit, new_in)
        gate = pre[:, :hid]
        hidden = (gate * jax.nn.sigmoid(gate) * pre[:, hid:]).astype(jnp.bfloat16)
        attended = att_ref[c, 0]
        if c == 0:
            attended = jnp.where((half == 1) & (core == 0) & (row == 0), patch, attended)
        out_ref[c, 0] = (attended + nn_dot(hidden, new_out)).astype(jnp.bfloat16)


def finish(
    place, attended, fast_in, fast_out, sums, patch, own, share, first, unit_epsilon, after
):
    peers, heads, rows, dim = attended.shape
    hid = fast_out.shape[1]

    def plain(array):
        return pl.BlockSpec((1,) + array.shape[1:], lambda j, place: (j, 0, 0))

    in_specs = [by_head(attended.shape)]
    in_specs += [chip_weights(a, share, first) for a in (fast_in, fast_out)]
    in_specs += [plain(a) for a in (*sums, patch)]
    in_specs += [by_head(attended.shape)] + untouched(after)
    return pl.pallas_call(
        functools.partial(finish_kernel, unit_epsilon),
        out_shape=jax.ShapeDtypeStruct(attended.shape, jnp.bfloat16),
        grid_spec=pltpu.PrefetchScalarGridSpec(
            num_scalar_prefetch=1,
            grid=(heads,),
            in_specs=in_specs,
            out_specs=by_head(attended.shape),
            scratch_shapes=[
                pltpu.VMEM((2 * hid, dim), jnp.float32),
                pltpu.VMEM((hid, dim), jnp.float32),
            ],
        ),
        compiler_params=params(),
        cost_estimate=cost(12 * heads * peers * rows * hid * dim, 0),
        name="finish",
    )(place, attended, fast_in, fast_out, *sums, patch, own, *after)


def place_kernel(chunks, share, *refs):
    pieces, out_ref, sems = refs[:-2], refs[-2], refs[-1]
    peers = pieces[0].shape[0]
    copies = []
    for piece, (first, heads) in zip(pieces, chunks):
        for c in range(peers):
            copies.append(
                pltpu.make_async_copy(
                    piece.at[c],
                    out_ref.at[pl.ds(c * share + first, heads)],
                    sems.at[len(copies)],
                )
            )
    for copy in copies:
        copy.start()
    for copy in copies:
        copy.wait()


def put_in_place(pieces, chunks, share):
    peers, _, rows, dim = pieces[0].shape
    return pl.pallas_call(
        functools.partial(place_kernel, chunks, share),
        out_shape=jax.ShapeDtypeStruct((peers * share, rows, dim), jnp.bfloat16),
        in_specs=[pl.BlockSpec(memory_space=pltpu.VMEM)] * len(pieces),
        out_specs=pl.BlockSpec(memory_space=pl.ANY),
        scratch_shapes=[pltpu.SemaphoreType.DMA((peers * len(pieces),))],
        compiler_params=params(),
        name="put_in_place",
    )(*pieces)


def regrouping(tok_peers, rows, heads, dim, hid):
    half_peers = tok_peers // 2
    peers = math.gcd(half_peers, heads)
    fits = tok_peers % 2 == 0 and half_peers * rows == 2 * HALF
    fits = fits and half_peers == 2 * peers and peers & (peers - 1) == 0
    fits = fits and rows % 256 == 0 and dim == 128 and hid % 256 == 0
    return peers if fits else 0


def regrouped_body(
    peers,
    query_rows,
    key_rows,
    value_rows,
    query_gain,
    key_gain,
    rate_in,
    rate_out,
    fast_in,
    fast_out,
    half_window,
    boundaries,
):
    rows, heads, dim = query_rows.shape
    share = heads // peers
    tok_peers = lax.axis_size("tok")
    half_peers = tok_peers // 2
    width_all = heads * dim * lax.axis_size("head")
    rate_rows = rows // 128
    aux_rows = -(-(4 * rate_rows + 3) // 16) * 16
    own_index = lax.axis_index("tok")
    half = own_index // half_peers
    chip = own_index % half_peers // 2
    core = own_index % 2
    place = jnp.stack([chip, core, half]).astype(jnp.int32)

    teams = [
        [side * half_peers + c * 2 + lane for c in range(peers)]
        for side in range(2)
        for lane in range(2)
    ]

    def dealt(x):
        return lax.all_to_all(x, "tok", 0, 0, axis_index_groups=teams)

    core_pairs = [(t, t ^ 1) for t in range(tok_peers)]
    half_pairs = [(t, (t + half_peers) % tok_peers) for t in range(tok_peers)]
    forward_pairs = [(t + half_peers, t) for t in range(half_peers)]
    back_pairs = [(t, t - 1 + half_peers) for t in range(half_peers) if t % 2 == 1]

    q = jnp.transpose(query_rows, (1, 0, 2))
    k = jnp.transpose(key_rows, (1, 0, 2))
    v = jnp.transpose(value_rows, (1, 0, 2))
    q_float = q.astype(jnp.float32)
    k_float = k.astype(jnp.float32)
    squares = jnp.stack(
        [jnp.sum(q_float * q_float, axis=(0, 2)), jnp.sum(k_float * k_float, axis=(0, 2))]
    )
    if lax.axis_size("head") == 2:
        sums = (squares, lax.ppermute(squares, "head", [(0, 1), (1, 0)]))
    else:
        sums = (lax.psum(squares, "head"), jnp.zeros_like(squares))
    fold = math.log2(math.e) / math.sqrt(dim)
    chunks = [(0, (share + 1) // 2), ((share + 1) // 2, share // 2)]
    packets = []
    for first, count in chunks:
        sent = pack(
            sums,
            q,
            k,
            v,
            (query_gain, key_gain),
            (rate_in, rate_out),
            peers,
            aux_rows,
            first,
            count,
            width_all,
            fold,
        )
        own = dealt(sent)
        other = exchanged(own, core_pairs)
        aux = jnp.where(core == 0, own[0, :, 3 * rows :], other[0, :, 3 * rows :])
        packets.append((own, other, exchanged(aux, forward_pairs)))
    after = []
    grads = []
    answers = []
    sums = []
    for (first, count), (own, other, forwarded) in zip(chunks, packets):
        grad = gradients(place, fast_in, fast_out, own, other, share, rows, first, after)
        from_half = exchanged(grad, half_pairs)
        attended, extra = attend(
            place, half_window, boundaries, own, other, forwarded, share, rows, first, [grad]
        )
        after = [attended]
        answers.append((attended, exchanged(extra, back_pairs)))
        from_half, _ = lax.optimization_barrier((from_half, attended))
        own_sum = (grad.astype(jnp.float32) + from_half.astype(jnp.float32)).astype(jnp.bfloat16)
        sums.append((own_sum, exchanged(own_sum, core_pairs)))
    after = []
    pieces = []
    for (first, count), each, (attended, patch), (own, *_) in zip(chunks, sums, answers, packets):
        outs = finish(
            place,
            attended,
            fast_in,
            fast_out,
            each,
            patch,
            own,
            share,
            first,
            epsilon * fold * fold,
            after,
        )
        after = [outs]
        pieces.append(dealt(outs))
    return jnp.transpose(put_in_place(pieces, chunks, share), (1, 0, 2))


def body(query_rows, *others):
    rows, heads, dim = query_rows.shape
    hid = others[7].shape[1]
    peers = regrouping(lax.axis_size("tok"), rows, heads, dim, hid)
    if peers:
        return regrouped_body(peers, query_rows, *others)
    return sliding_body(query_rows, *others)


def solution(mesh):
    in_specs = (
        P("tok", "head", None),
        P("tok", "head", None),
        P("tok", "head", None),
        P("head", None),
        P("head", None),
        P("head", "tok"),
        P("head", "tok"),
        P("head", None, None),
        P("head", None, None),
        P("head"),
        P(),
    )
    out_specs = P("tok", "head", None)
    return jax.shard_map(body, mesh=mesh, in_specs=in_specs, out_specs=out_specs, check_vma=False)
```

```python
import functools
import math

import jax
import jax.numpy as jnp
from jax import lax
from jax.experimental import pallas as pl
from jax.experimental.pallas import tpu as pltpu
from jax.sharding import PartitionSpec as P

HALF = 1024


epsilon = 1e-06


def passed_along(x, axis, by):
    peers = lax.axis_size(axis)
    pairs = [(i, i + by) for i in range(peers) if 0 <= i + by < peers]
    return lax.ppermute(x, axis, pairs)


def unit_rows(matrix):
    as_float = matrix.astype(jnp.float32)
    return (
        as_float * lax.rsqrt(jnp.sum(as_float * as_float, axis=-1, keepdims=True) + epsilon)
    ).astype(jnp.bfloat16)


def rescale(updated, base_norm, squares):
    return (updated * (base_norm / jnp.sqrt(squares + epsilon))[:, None, :]).astype(jnp.bfloat16)


def sliding_body(
    query_rows,
    key_rows,
    value_rows,
    query_gain,
    key_gain,
    rate_in,
    rate_out,
    fast_in,
    fast_out,
    half_window,
    boundaries,
):
    tok_rows = query_rows.shape[0]
    local_heads = query_rows.shape[1]
    head_dim = query_rows.shape[2]
    fast_hid = fast_out.shape[1]
    width_all = local_heads * head_dim * lax.axis_size("head")
    tok_count = tok_rows * lax.axis_size("tok")
    own_index = lax.axis_index("tok")
    first_row = own_index * tok_rows
    query_float = query_rows.astype(jnp.float32)
    key_float = key_rows.astype(jnp.float32)
    query_sq, key_sq = lax.psum(
        (
            jnp.sum(query_float * query_float, axis=(1, 2)),
            jnp.sum(key_float * key_float, axis=(1, 2)),
        ),
        "head",
    )
    q_normed = (
        query_float * lax.rsqrt(query_sq / width_all + epsilon)[:, None, None] * query_gain[None]
    ).astype(jnp.bfloat16)
    k_normed = (
        key_float * lax.rsqrt(key_sq / width_all + epsilon)[:, None, None] * key_gain[None]
    ).astype(jnp.bfloat16)

    def clip_of(places):
        return jnp.sum((places[:, None] >= boundaries[None, :]).astype(jnp.int32), axis=1)

    positions = first_row + jnp.arange(tok_rows, dtype=jnp.int32)
    query_clip = clip_of(positions)
    scaling = 1.0 / math.sqrt(head_dim)

    def absorb(state_now, block_keys, block_values, key_first):
        best, denominator, accum = state_now
        key_places = key_first + jnp.arange(tok_rows, dtype=jnp.int32)
        scores = (
            jnp.einsum("qhd,khd->hqk", q_normed, block_keys, preferred_element_type=jnp.float32)
            * scaling
        )
        inside = (key_places >= 0) & (key_places < tok_count)
        pair_ok = (query_clip[:, None] == clip_of(key_places)[None, :]) & inside[None, :]
        distance = jnp.abs(positions[:, None] - key_places[None, :])
        allowed = (distance[None, :, :] <= half_window[:, None, None]) & pair_ok[None, :, :]
        masked = jnp.where(allowed, scores, -jnp.inf)
        new_best = jnp.maximum(best, jnp.max(masked, axis=2))
        weights = jnp.exp(masked - new_best[:, :, None])
        shrink = jnp.exp(best - new_best)
        denominator = denominator * shrink + jnp.sum(weights, axis=2)
        accum = accum * shrink[:, :, None] + jnp.einsum(
            "hqk,khd->hqd",
            weights.astype(jnp.bfloat16),
            block_values,
            preferred_element_type=jnp.float32,
        )
        return (new_best, denominator, accum)

    start_state = (
        jnp.full((local_heads, tok_rows), -jnp.inf, jnp.float32),
        jnp.zeros((local_heads, tok_rows), jnp.float32),
        jnp.zeros((local_heads, tok_rows, head_dim), jnp.float32),
    )
    state_now = absorb(start_state, k_normed, value_rows, first_row)
    reach_blocks = HALF // tok_rows
    for distance_step in range(1, reach_blocks + 1):
        left_keys, left_values = passed_along((k_normed, value_rows), "tok", distance_step)
        state_now = absorb(state_now, left_keys, left_values, first_row - distance_step * tok_rows)
        right_keys, right_values = passed_along((k_normed, value_rows), "tok", -distance_step)
        state_now = absorb(
            state_now, right_keys, right_values, first_row + distance_step * tok_rows
        )
    attended = state_now[2] / state_now[1][:, :, None]
    key_unit = unit_rows(k_normed)
    query_unit = unit_rows(q_normed)
    pre_keys = jnp.einsum("thd,hdf->htf", key_unit, fast_in, preferred_element_type=jnp.float32)
    gate_part = pre_keys[:, :, :fast_hid]
    lin_part = pre_keys[:, :, fast_hid:]
    sigmoid_gate = jax.nn.sigmoid(gate_part)
    swish_gate = gate_part * sigmoid_gate
    hidden = (swish_gate * lin_part).astype(jnp.bfloat16)
    value_float = value_rows.astype(jnp.float32)
    push_out = (-jnp.transpose(rate_out)[:, :, None] * value_float).astype(jnp.bfloat16)
    push_in = (-jnp.transpose(rate_in)[:, :, None] * value_float).astype(jnp.bfloat16)
    grad_out = jnp.einsum("htf,thd->hfd", hidden, push_out, preferred_element_type=jnp.float32)
    hidden_grad = jnp.einsum("thd,hfd->htf", push_in, fast_out, preferred_element_type=jnp.float32)
    d_gate = hidden_grad * lin_part * sigmoid_gate * (1.0 + gate_part * (1.0 - sigmoid_gate))
    d_lin = hidden_grad * swish_gate
    d_pre = jnp.concatenate([d_gate, d_lin], axis=2).astype(jnp.bfloat16)
    grad_in = jnp.einsum("thd,htf->hdf", key_unit, d_pre, preferred_element_type=jnp.float32)
    in_float = fast_in.astype(jnp.float32)
    out_float = fast_out.astype(jnp.float32)
    in_base = jnp.sqrt(jnp.sum(in_float * in_float, axis=1))
    out_base = jnp.sqrt(jnp.sum(out_float * out_float, axis=1))
    summed_in, summed_out = lax.psum((grad_in, grad_out), "tok")
    updated_in = in_float - summed_in
    updated_out = out_float - summed_out
    new_in = rescale(updated_in, in_base, jnp.sum(updated_in * updated_in, axis=1))
    new_out = rescale(updated_out, out_base, jnp.sum(updated_out * updated_out, axis=1))
    pre_query = jnp.einsum("thd,hdf->htf", query_unit, new_in, preferred_element_type=jnp.float32)
    query_gate = pre_query[:, :, :fast_hid]
    query_hidden = (query_gate * jax.nn.sigmoid(query_gate) * pre_query[:, :, fast_hid:]).astype(
        jnp.bfloat16
    )
    fast_result = jnp.einsum(
        "htf,hfd->htd", query_hidden, new_out, preferred_element_type=jnp.float32
    )
    combined = attended + fast_result
    return jnp.transpose(combined, (1, 0, 2)).astype(jnp.bfloat16)


VMEM_BYTES = 32 * 1024 * 1024
HIDDEN_MASK = -1e30
NT = (((1,), (1,)), ((), ()))


def exchanged(x, pairs):
    return lax.ppermute(x, "tok", pairs)


def nt_dot(a, b):
    return lax.dot_general(a, b, NT, preferred_element_type=jnp.float32)


def nn_dot(a, b):
    return jnp.dot(a, b, preferred_element_type=jnp.float32)


def params():
    return pltpu.CompilerParams(vmem_limit_bytes=VMEM_BYTES)


def cost(flops, nbytes):
    return pl.CostEstimate(flops=int(16 * flops), bytes_accessed=int(nbytes), transcendentals=0)


def untouched(arrays):
    return [pl.BlockSpec(memory_space=pl.ANY)] * len(arrays)


def pack_values_kernel(peers, place_ref, rate_in_ref, rate_out_ref, v_ref, *refs):
    outs, aux_ref = refs[:peers], refs[-1]
    rows = v_ref.shape[2]
    share = rate_in_ref.shape[0] // peers
    aux_ref[...] = jnp.zeros_like(aux_ref)
    for p in range(peers):
        c = place_ref[0] ^ p
        head = pl.ds(c * share + pl.program_id(0), 1)
        for i in range(0, rows, 128):
            outs[p][0, i : i + 128, :] = jnp.transpose(v_ref[c, 0, i : i + 128, :])
        at = 0
        for rate_ref in (rate_in_ref, rate_out_ref):
            rate = rate_ref[head, :]
            high = rate.astype(jnp.bfloat16).astype(jnp.float32)
            for part in (high, rate - high):
                for i in range(0, rows, 128):
                    aux_ref[at : at + 1, :] = part[:, i : i + 128]
                    at += 1
        outs[p][0, rows:, :] = aux_ref[...].astype(jnp.bfloat16)


def pack_values(place, v, rates, peers, aux_rows):
    heads, rows, dim = v.shape
    share = heads // peers
    out_shape = (share, rows + aux_rows, dim)
    return pl.pallas_call(
        functools.partial(pack_values_kernel, peers),
        out_shape=[jax.ShapeDtypeStruct(out_shape, jnp.bfloat16)] * peers,
        grid_spec=pltpu.PrefetchScalarGridSpec(
            num_scalar_prefetch=1,
            grid=(share,),
            in_specs=[pl.BlockSpec(a.shape, lambda j, place: (0, 0)) for a in rates]
            + [pl.BlockSpec((peers, 1, rows, dim), lambda j, place: (0, j, 0, 0))],
            out_specs=[pl.BlockSpec((1,) + out_shape[1:], lambda j, place: (j, 0, 0))] * peers,
            scratch_shapes=[pltpu.VMEM((aux_rows, dim), jnp.float32)],
        ),
        compiler_params=params(),
        cost_estimate=cost(0, 4 * heads * rows * dim),
        name="pack_values",
    )(place, *rates, v.reshape(peers, share, rows, dim))


def pack_kernel(peers, first, width_all, fold, place_ref, *refs):
    squares_ref, more_ref, q_gain_ref, k_gain_ref, q_ref, k_ref, v_ref = refs[:7]
    outs = refs[7 : 7 + peers]
    aux_ref, q_scale_ref, k_scale_ref = refs[-3:]
    rows, dim = q_scale_ref.shape
    share = q_gain_ref.shape[0] // peers

    @pl.when(pl.program_id(0) == 0)
    def _():
        scales = lax.rsqrt((squares_ref[...] + more_ref[...]) / width_all + epsilon)
        q_scale_ref[...] = jnp.transpose(jnp.broadcast_to(scales[0:1] * fold, (dim, rows)))
        k_scale_ref[...] = jnp.transpose(jnp.broadcast_to(scales[1:2], (dim, rows)))
        aux_ref[...] = jnp.zeros_like(aux_ref)

    q_scale = q_scale_ref[...]
    k_scale = k_scale_ref[...]
    for p in range(peers):
        c = place_ref[0] ^ p
        head = pl.ds(c * share + first + pl.program_id(0), 1)
        q = (q_ref[c, 0].astype(jnp.float32) * q_scale * q_gain_ref[head, :]).astype(jnp.bfloat16)
        k = (k_ref[c, 0].astype(jnp.float32) * k_scale * k_gain_ref[head, :]).astype(jnp.bfloat16)
        outs[p][0, 0:rows, :] = q
        outs[p][0, rows : 2 * rows, :] = k
        for i, array in enumerate((q, k, v_ref[c, 0])):
            aux_ref[i : i + 1, :] = array[0:16].astype(jnp.float32)[0:1]
        outs[p][0, 2 * rows :, :] = aux_ref[...].astype(jnp.bfloat16)


def pack(place, sums, q, k, v, gains, peers, aux_rows, first, count, width_all, fold):
    heads, rows, dim = q.shape
    out_shape = (count, 2 * rows + aux_rows, dim)
    whole = [*sums, *gains]

    def spec(block_rows):
        return pl.BlockSpec((peers, 1, block_rows, dim), lambda j, place: (0, first + j, 0, 0))

    return pl.pallas_call(
        functools.partial(pack_kernel, peers, first, width_all, fold),
        out_shape=[jax.ShapeDtypeStruct(out_shape, jnp.bfloat16)] * peers,
        grid_spec=pltpu.PrefetchScalarGridSpec(
            num_scalar_prefetch=1,
            grid=(count,),
            in_specs=[pl.BlockSpec(a.shape, lambda j, place: (0, 0)) for a in whole]
            + [spec(rows), spec(rows), spec(16)],
            out_specs=[pl.BlockSpec((1,) + out_shape[1:], lambda j, place: (j, 0, 0))] * peers,
            scratch_shapes=[
                pltpu.VMEM((aux_rows, dim), jnp.float32),
                pltpu.VMEM((rows, dim), jnp.float32),
                pltpu.VMEM((rows, dim), jnp.float32),
            ],
        ),
        compiler_params=params(),
        cost_estimate=cost(0, 8 * peers * count * rows * dim),
        name="pack",
    )(place, *whole, *[x.reshape(peers, heads // peers, rows, dim) for x in (q, k, v)])


def key_value_blocks(peers, rows, refs):
    own_v, other_v = refs[:peers], refs[peers]
    own_qk, other_k = refs[peers + 1 : 2 * peers + 1], refs[2 * peers + 1]
    for p in range(peers):
        yield p, True, own_qk[p].at[0, rows : 2 * rows], own_v[p].at[0]
        yield p, False, other_k.at[p, 0, 0:rows], other_v.at[p, 0]


def key_value_operands(values, keys, first):
    own_v, other_v = values
    own_qk, other_k = keys

    def single(array, at):
        return pl.BlockSpec((1,) + array.shape[1:], lambda j, *_: (at + j, 0, 0))

    def stacked(array, at):
        shape = (array.shape[0], 1) + array.shape[2:]
        return pl.BlockSpec(shape, lambda j, *_: (0, at + j, 0, 0))

    specs = [single(a, first) for a in own_v] + [stacked(other_v, first)]
    specs += [single(a, 0) for a in own_qk] + [stacked(other_k, 0)]
    return [*own_v, other_v, *own_qk, other_k], specs


def grads_kernel(peers, rows, rate_rows, place_ref, in_ref, out_ref, *refs):
    grad_ref = refs[-1]
    hid = out_ref.shape[1]
    part = hid // 2
    core = place_ref[1]
    own = pl.multiple_of(core * part, part)
    in_half = jnp.concatenate(
        [
            jnp.transpose(in_ref[0, :, pl.ds(at, part)].astype(jnp.float32))
            for at in (own, pl.multiple_of(hid + own, part))
        ],
        axis=0,
    ).astype(jnp.bfloat16)
    out_half = out_ref[0, pl.ds(own, part), :]
    sum_in = jnp.zeros((2 * part, in_half.shape[1]), jnp.float32)
    sum_out = jnp.zeros((part, in_half.shape[1]), jnp.float32)
    for _, _, keys, values in key_value_blocks(peers, rows, refs):
        k = keys[...].astype(jnp.float32)
        v_t = jnp.concatenate([values[at : at + 128, :] for at in range(0, rows, 128)], axis=1)
        aux = values[rows:, :].astype(jnp.float32)

        def rate(at):
            both = aux[at : at + rate_rows] + aux[at + rate_rows : at + 2 * rate_rows]
            return jnp.concatenate([both[i : i + 1] for i in range(rate_rows)], axis=1)

        rate_in, rate_out = rate(0), rate(2 * rate_rows)
        unit = (k * lax.rsqrt(jnp.sum(k * k, axis=1, keepdims=True) + epsilon)).astype(
            jnp.bfloat16
        )
        pre = nt_dot(in_half, unit)
        gate, lin = pre[:part], pre[part:]
        sig = jax.nn.sigmoid(gate)
        swish = gate * sig
        pushed = (swish * lin * -rate_out).astype(jnp.bfloat16)
        hidden_grad = nn_dot(out_half, v_t) * -rate_in
        d_gate = hidden_grad * lin * sig * (1.0 + gate * (1.0 - sig))
        d_lin = hidden_grad * swish
        d_pre = jnp.concatenate([d_gate, d_lin], axis=0).astype(jnp.bfloat16)
        sum_in += nn_dot(d_pre, unit)
        sum_out += nt_dot(pushed, v_t)
    grad_ref[0, 0 : 2 * part, :] = sum_in.astype(jnp.bfloat16)
    grad_ref[0, 2 * part :, :] = sum_out.astype(jnp.bfloat16)


def chip_weights(array, share, first):
    return pl.BlockSpec(
        (1,) + array.shape[1:], lambda j, place, *_: (place[0] * share + first + j, 0, 0)
    )


def by_head(shape):
    return pl.BlockSpec((shape[0], 1) + shape[2:], lambda j, *_: (0, j, 0, 0))


def gradients(place, fast_in, fast_out, values, keys, share, rows, first, after):
    _, hid, dim = fast_out.shape
    peers = len(keys[0])
    heads = keys[0][0].shape[0]
    grad_shape = (heads, 3 * hid // 2, dim)
    blocks, block_specs = key_value_operands(values, keys, first)
    return pl.pallas_call(
        functools.partial(grads_kernel, peers, rows, rows // 128),
        out_shape=jax.ShapeDtypeStruct(grad_shape, jnp.bfloat16),
        grid_spec=pltpu.PrefetchScalarGridSpec(
            num_scalar_prefetch=1,
            grid=(heads,),
            in_specs=[chip_weights(a, share, first) for a in (fast_in, fast_out)]
            + block_specs
            + untouched(after),
            out_specs=pl.BlockSpec((1,) + grad_shape[1:], lambda j, place: (j, 0, 0)),
        ),
        compiler_params=params(),
        cost_estimate=cost(0, 0),
        name="gradients",
    )(place, fast_in, fast_out, *blocks, *after)


def attend_kernel(peers, rows, share, first, place_ref, window_ref, edge_ref, *refs):
    own_qk = refs[peers + 1 : 2 * peers + 1]
    fwd_ref = refs[2 * peers + 2]
    out_ref, extra_ref, k_scr, vt_scr, q_scr = refs[-5:]
    span = 2 * peers * rows
    dim = k_scr.shape[1]
    pad = fwd_ref.shape[1]
    chip, core, half = place_ref[0], place_ref[1], place_ref[2]
    base = half * span
    limit = span + 1 - half
    step = pl.program_id(0)
    window = window_ref[chip * share + first + step]

    @pl.when(step == 0)
    def _():
        k_scr[span:, :] = jnp.zeros((k_scr.shape[0] - span, dim), k_scr.dtype)
        vt_scr[:, span:] = jnp.zeros((vt_scr.shape[0], vt_scr.shape[1] - span), vt_scr.dtype)
        vt_scr[dim:, :] = jnp.ones((vt_scr.shape[0] - dim, vt_scr.shape[1]), vt_scr.dtype)

    for p, own, keys, values in key_value_blocks(peers, rows, refs):
        at = pl.multiple_of(((chip ^ p) * 2 + (core if own else 1 - core)) * rows, rows)
        k_scr[pl.ds(at, rows), :] = keys[...]
        for i in range(0, rows, 128):
            vt_scr[0:dim, pl.ds(pl.multiple_of(at + i, 128), 128)] = values[i : i + 128, :]
    for p in range(peers):
        q_scr[chip ^ p] = own_qk[p][0, 0:rows, :]
    fwd = fwd_ref[0].astype(jnp.float32)
    q_lone, k_lone, v_lone = (fwd[i : i + 1] for i in range(3))
    k_scr[span : span + pad, :] = jnp.broadcast_to(k_lone, (pad, dim)).astype(jnp.bfloat16)
    vt_scr[0:dim, span : span + 128] = jnp.transpose(
        jnp.broadcast_to(v_lone, (128, dim))
    ).astype(jnp.bfloat16)

    def clip_start(place):
        start = jnp.zeros_like(place)
        for i in range(edge_ref.shape[0]):
            start = jnp.maximum(start, jnp.where(edge_ref[i] <= place, edge_ref[i], 0))
        return start

    def clip_stop(place):
        stop = jnp.full_like(place, base + limit)
        for i in range(edge_ref.shape[0]):
            stop = jnp.minimum(stop, jnp.where(edge_ref[i] > place, edge_ref[i], base + limit))
        return stop

    def lowest(place):
        return jnp.maximum(jnp.maximum(place - window, clip_start(place)), base) - base

    def highest(place):
        return jnp.minimum(place + window, clip_stop(place) - 1) - base

    def one_pair(i, carry):
        pair = []
        for c in (i, peers - 1 - i):
            start = (c * 2 + core) * rows
            place = base + start + lax.broadcasted_iota(jnp.int32, (1, rows), 1)
            from_key = lowest(base + start) // 128 * 128
            count = (highest(base + start + rows - 1) - from_key) // 256 + 1
            pair.append((c, lowest(place), highest(place), from_key, count))
        count = jnp.maximum(pair[0][4], pair[1][4])

        def variant(chunks):
            width = chunks * 256
            key = lax.broadcasted_iota(jnp.int32, (width, rows), 0)
            froms = [
                pl.multiple_of(jnp.minimum(each[3], k_scr.shape[0] - width), 128) for each in pair
            ]
            scores = [
                nt_dot(k_scr[pl.ds(at, width), :], q_scr[each[0]])
                for each, at in zip(pair, froms)
            ]
            scores = [
                jnp.where((key >= each[1] - at) & (key <= each[2] - at), one, HIDDEN_MASK)
                for each, at, one in zip(pair, froms, scores)
            ]
            weights = [
                jnp.exp2(one - jnp.max(one, axis=0, keepdims=True)).astype(jnp.bfloat16)
                for one in scores
            ]
            totals = [
                nn_dot(vt_scr[:, pl.ds(at, width)], one) for at, one in zip(froms, weights)
            ]
            for each, total in zip(pair, totals):
                attended = total[0:dim] * (1.0 / total[dim : dim + 1])
                out_ref[each[0], 0] = jnp.transpose(attended)

        for chunks in range(1, span // 256 + 2):

            @pl.when(count == chunks)
            def _(chunks=chunks):
                variant(chunks)

        return carry

    lax.fori_loop(0, peers // 2, one_pair, 0)
    extra_ref[0] = jnp.zeros(extra_ref.shape[1:], jnp.float32)

    @pl.when((half == 0) & (core == 1))
    def _():
        near = span - HALF
        width = HALF + 128
        q = jnp.broadcast_to(q_lone, (pad, dim)).astype(jnp.bfloat16)
        scores = nt_dot(q, k_scr[near : near + width, :])
        key = near + lax.broadcasted_iota(jnp.int32, (1, width), 1)
        scores = jnp.where((key >= span - window) & (key <= span), scores, HIDDEN_MASK)
        top = jnp.max(scores, axis=1, keepdims=True)
        weights = jnp.exp2(scores - top).astype(jnp.bfloat16)
        total = nt_dot(weights, vt_scr[:, near : near + width])
        extra_ref[0] = total[:, 0:dim] / total[:, dim : dim + 1]


def attend(place, half_window, boundaries, values, keys, forwarded, share, rows, first, after):
    peers = len(keys[0])
    heads, pad, dim = forwarded.shape
    scr_rows = 2 * peers * rows + 256
    out_shapes = [(peers, heads, rows, dim), (heads, pad, dim)]
    one_head = pl.BlockSpec((1, pad, dim), lambda j, *_: (j, 0, 0))
    blocks, block_specs = key_value_operands(values, keys, first)
    return pl.pallas_call(
        functools.partial(attend_kernel, peers, rows, share, first),
        out_shape=[jax.ShapeDtypeStruct(shape, jnp.float32) for shape in out_shapes],
        grid_spec=pltpu.PrefetchScalarGridSpec(
            num_scalar_prefetch=3,
            grid=(heads,),
            in_specs=block_specs + [one_head] + untouched(after),
            out_specs=[by_head(out_shapes[0]), one_head],
            scratch_shapes=[
                pltpu.VMEM((scr_rows, dim), jnp.bfloat16),
                pltpu.VMEM((dim + 16, scr_rows), jnp.bfloat16),
                pltpu.VMEM((peers, rows, dim), jnp.bfloat16),
            ],
        ),
        compiler_params=params(),
        cost_estimate=cost(4 * heads * peers * rows * HALF * 2 * dim, 0),
        name="attend",
    )(place, half_window, boundaries, *blocks, forwarded, *after)


def finish_kernel(peers, unit_epsilon, place_ref, *refs):
    att_ref, base_in_ref, base_out_ref, own_ref, other_ref, patch_ref = refs[:6]
    queries = refs[6 : 6 + peers]
    outs = refs[-2 - peers : -2]
    grad_in_scr, grad_out_scr = refs[-2:]
    chip, core, half = place_ref[0], place_ref[1], place_ref[2]
    rows = att_ref.shape[2]
    hid = base_out_ref.shape[1]
    part = hid // 2
    for summed, lane in ((own_ref, core), (other_ref, 1 - core)):
        at = pl.multiple_of(lane * part, part)
        grad_in_scr[pl.ds(at, part), :] = summed[0, 0:part, :].astype(jnp.float32)
        grad_in_scr[pl.ds(hid + at, part), :] = summed[0, part : 2 * part, :].astype(jnp.float32)
        grad_out_scr[pl.ds(at, part), :] = summed[0, 2 * part :, :].astype(jnp.float32)

    def renewed(base, grad):
        base = base.astype(jnp.float32)
        updated = base - grad
        norm = jnp.sqrt(jnp.sum(base * base, axis=0, keepdims=True))
        squares = jnp.sum(updated * updated, axis=0, keepdims=True)
        return (updated * (norm / jnp.sqrt(squares + epsilon))).astype(jnp.bfloat16)

    new_in = renewed(base_in_ref[0], jnp.transpose(grad_in_scr[...]))
    new_out = renewed(base_out_ref[0], grad_out_scr[...])
    patch = patch_ref[0][0:1, :]
    row = lax.broadcasted_iota(jnp.int32, (rows, 1), 0)
    for p in range(peers):
        q = queries[p][0].astype(jnp.float32)
        unit = (q * lax.rsqrt(jnp.sum(q * q, axis=1, keepdims=True) + unit_epsilon)).astype(
            jnp.bfloat16
        )
        pre = nn_dot(unit, new_in)
        gate = pre[:, :hid]
        hidden = (gate * jax.nn.sigmoid(gate) * pre[:, hid:]).astype(jnp.bfloat16)
        patched = (half == 1) & (core == 0) & (chip == p)
        attended = jnp.where(patched & (row == 0), patch, att_ref[chip ^ p, 0])
        outs[p][0] = (attended + nn_dot(hidden, new_out)).astype(jnp.bfloat16)


def finish(place, attended, fast_in, fast_out, sums, patch, own_qk, share, first, unit_epsilon, after):
    peers, heads, rows, dim = attended.shape
    hid = fast_out.shape[1]

    def plain(shape):
        return pl.BlockSpec((1,) + shape[1:], lambda j, place: (j, 0, 0))

    out_shape = (heads, rows, dim)
    in_specs = [by_head(attended.shape)]
    in_specs += [chip_weights(a, share, first) for a in (fast_in, fast_out)]
    in_specs += [plain(a.shape) for a in (*sums, patch)]
    in_specs += [plain(out_shape)] * peers + untouched(after)
    return pl.pallas_call(
        functools.partial(finish_kernel, peers, unit_epsilon),
        out_shape=[jax.ShapeDtypeStruct(out_shape, jnp.bfloat16)] * peers,
        grid_spec=pltpu.PrefetchScalarGridSpec(
            num_scalar_prefetch=1,
            grid=(heads,),
            in_specs=in_specs,
            out_specs=[plain(out_shape)] * peers,
            scratch_shapes=[
                pltpu.VMEM((2 * hid, dim), jnp.float32),
                pltpu.VMEM((hid, dim), jnp.float32),
            ],
        ),
        compiler_params=params(),
        cost_estimate=cost(12 * heads * peers * rows * hid * dim, 0),
        name="finish",
    )(place, attended, fast_in, fast_out, *sums, patch, *own_qk, *after)


def place_kernel(peers, chunks, share, place_ref, *refs):
    pieces, out_ref, sems = refs[:-2], refs[-2], refs[-1]
    copies = []
    for first, heads in chunks:
        for p in range(peers):
            at = (place_ref[0] ^ p) * share + first
            i = len(copies)
            copies.append(
                pltpu.make_async_copy(pieces[i], out_ref.at[pl.ds(at, heads)], sems.at[i])
            )
    for copy in copies:
        copy.start()
    for copy in copies:
        copy.wait()


def put_in_place(place, pieces, peers, chunks, share):
    _, rows, dim = pieces[0].shape
    return pl.pallas_call(
        functools.partial(place_kernel, peers, chunks, share),
        out_shape=jax.ShapeDtypeStruct((peers * share, rows, dim), jnp.bfloat16),
        in_specs=[pl.BlockSpec(memory_space=pltpu.SMEM)]
        + [pl.BlockSpec(memory_space=pltpu.VMEM)] * len(pieces),
        out_specs=pl.BlockSpec(memory_space=pl.ANY),
        scratch_shapes=[pltpu.SemaphoreType.DMA((len(pieces),))],
        compiler_params=params(),
        name="put_in_place",
    )(place, *pieces)


def regrouping(tok_peers, rows, heads, dim, hid):
    half_peers = tok_peers // 2
    peers = math.gcd(half_peers, heads)
    fits = tok_peers % 2 == 0 and half_peers * rows == 2 * HALF
    fits = fits and half_peers == 2 * peers and peers & (peers - 1) == 0
    fits = fits and rows % 256 == 0 and dim == 128 and hid % 256 == 0
    return peers if fits else 0


def regrouped_body(
    peers,
    query_rows,
    key_rows,
    value_rows,
    query_gain,
    key_gain,
    rate_in,
    rate_out,
    fast_in,
    fast_out,
    half_window,
    boundaries,
):
    rows, heads, dim = query_rows.shape
    share = heads // peers
    tok_peers = lax.axis_size("tok")
    half_peers = tok_peers // 2
    width_all = heads * dim * lax.axis_size("head")
    rate_rows = rows // 128
    aux_rows = -(-4 * rate_rows // 16) * 16
    own_index = lax.axis_index("tok")
    half = own_index // half_peers
    chip = own_index % half_peers // 2
    core = own_index % 2
    place = jnp.stack([chip, core, half]).astype(jnp.int32)

    def dealt(sent):
        pairs = [
            [(t, t // half_peers * half_peers + ((t % half_peers) ^ (2 * p))) for t in range(tok_peers)]
            for p in range(peers)
        ]
        return [sent[0]] + [exchanged(sent[p], pairs[p]) for p in range(1, peers)]

    core_pairs = [(t, t ^ 1) for t in range(tok_peers)]
    half_pairs = [(t, (t + half_peers) % tok_peers) for t in range(tok_peers)]
    forward_pairs = [(t + half_peers, t) for t in range(half_peers)]
    back_pairs = [(t, t - 1 + half_peers) for t in range(half_peers) if t % 2 == 1]

    q = jnp.transpose(query_rows, (1, 0, 2))
    k = jnp.transpose(key_rows, (1, 0, 2))
    v = jnp.transpose(value_rows, (1, 0, 2))
    sent_v = pack_values(place, v, (rate_in, rate_out), peers, aux_rows)
    *sent_v, q, k = lax.optimization_barrier((*sent_v, q, k))
    q_float = q.astype(jnp.float32)
    k_float = k.astype(jnp.float32)
    squares = jnp.stack(
        [jnp.sum(q_float * q_float, axis=(0, 2)), jnp.sum(k_float * k_float, axis=(0, 2))]
    )
    if lax.axis_size("head") == 2:
        sums = (squares, lax.ppermute(squares, "head", [(0, 1), (1, 0)]))
    else:
        sums = (lax.psum(squares, "head"), jnp.zeros_like(squares))
    fold = math.log2(math.e) / math.sqrt(dim)
    chunks = [(0, (share + 1) // 2), ((share + 1) // 2, share // 2)]
    own_v = dealt(sent_v)
    values = (own_v, exchanged(jnp.stack(own_v), core_pairs))
    sent = [
        pack(
            place,
            sums,
            q,
            k,
            v,
            (query_gain, key_gain),
            peers,
            aux_rows,
            first,
            count,
            width_all,
            fold,
        )
        for first, count in chunks
    ]
    received = []
    for each in sent:
        if received:
            each = [lax.optimization_barrier(pair)[0] for pair in zip(each, received[-1])]
        received.append(dealt(each))
    answers = []
    grads = []
    after = []
    for (first, count), own_qk in zip(chunks, received):
        if answers:
            *own_qk, _ = lax.optimization_barrier((*own_qk, grads[-1][0]))
        own_k = jnp.stack([x[:, rows:] for x in own_qk])
        other_k = exchanged(own_k, core_pairs)
        keys = (own_qk, other_k)
        aux = jnp.zeros((count, aux_rows, dim), jnp.bfloat16)
        for p in range(peers):
            here = jnp.where(core == 0, own_k[p, :, rows:], other_k[p, :, rows:])
            aux = jnp.where(chip == p, here, aux)
        forwarded = exchanged(aux, forward_pairs)
        grad = gradients(place, fast_in, fast_out, values, keys, share, rows, first, after)
        from_half = exchanged(grad, half_pairs)
        attended, extra = attend(
            place, half_window, boundaries, values, keys, forwarded, share, rows, first, [grad]
        )
        after = [attended]
        answers.append((attended, exchanged(extra, back_pairs), own_qk))
        grads.append((grad, from_half))

    def summed(grad, from_half, then):
        from_half, _ = lax.optimization_barrier((from_half, then))
        own_sum = (grad.astype(jnp.float32) + from_half.astype(jnp.float32)).astype(jnp.bfloat16)
        return own_sum, exchanged(own_sum, core_pairs)

    thens = [grad for grad, _ in grads[1:]] + [answers[-1][0]]
    sums = [summed(*each, then) for each, then in zip(grads, thens)]
    after = []
    pieces = []
    for (first, count), each, (attended, patch, own_qk) in zip(chunks, sums, answers):
        outs = finish(
            place,
            attended,
            fast_in,
            fast_out,
            each,
            patch,
            own_qk,
            share,
            first,
            epsilon * fold * fold,
            after,
        )
        after = [outs[0]]
        pieces += dealt(outs)
    whole = put_in_place(place, pieces, peers, chunks, share)
    return jnp.transpose(whole, (1, 0, 2))


def body(query_rows, *others):
    rows, heads, dim = query_rows.shape
    hid = others[7].shape[1]
    peers = regrouping(lax.axis_size("tok"), rows, heads, dim, hid)
    if peers:
        return regrouped_body(peers, query_rows, *others)
    return sliding_body(query_rows, *others)


def solution(mesh):
    in_specs = (
        P("tok", "head", None),
        P("tok", "head", None),
        P("tok", "head", None),
        P("head", None),
        P("head", None),
        P("head", "tok"),
        P("head", "tok"),
        P("head", None, None),
        P("head", None, None),
        P("head"),
        P(),
    )
    out_specs = P("tok", "head", None)
    return jax.shard_map(body, mesh=mesh, in_specs=in_specs, out_specs=out_specs, check_vma=False)
```

```python
import functools
import math

import jax
import jax.numpy as jnp
from jax import lax
from jax.experimental import pallas as pl
from jax.experimental.pallas import tpu as pltpu
from jax.sharding import PartitionSpec as P

HALF = 1024


epsilon = 1e-06


def passed_along(x, axis, by):
    peers = lax.axis_size(axis)
    pairs = [(i, i + by) for i in range(peers) if 0 <= i + by < peers]
    return lax.ppermute(x, axis, pairs)


def unit_rows(matrix):
    as_float = matrix.astype(jnp.float32)
    return (
        as_float * lax.rsqrt(jnp.sum(as_float * as_float, axis=-1, keepdims=True) + epsilon)
    ).astype(jnp.bfloat16)


def rescale(updated, base_norm, squares):
    return (updated * (base_norm / jnp.sqrt(squares + epsilon))[:, None, :]).astype(jnp.bfloat16)


def sliding_body(
    query_rows,
    key_rows,
    value_rows,
    query_gain,
    key_gain,
    rate_in,
    rate_out,
    fast_in,
    fast_out,
    half_window,
    boundaries,
):
    tok_rows = query_rows.shape[0]
    local_heads = query_rows.shape[1]
    head_dim = query_rows.shape[2]
    fast_hid = fast_out.shape[1]
    width_all = local_heads * head_dim * lax.axis_size("head")
    tok_count = tok_rows * lax.axis_size("tok")
    own_index = lax.axis_index("tok")
    first_row = own_index * tok_rows
    query_float = query_rows.astype(jnp.float32)
    key_float = key_rows.astype(jnp.float32)
    query_sq, key_sq = lax.psum(
        (
            jnp.sum(query_float * query_float, axis=(1, 2)),
            jnp.sum(key_float * key_float, axis=(1, 2)),
        ),
        "head",
    )
    q_normed = (
        query_float * lax.rsqrt(query_sq / width_all + epsilon)[:, None, None] * query_gain[None]
    ).astype(jnp.bfloat16)
    k_normed = (
        key_float * lax.rsqrt(key_sq / width_all + epsilon)[:, None, None] * key_gain[None]
    ).astype(jnp.bfloat16)

    def clip_of(places):
        return jnp.sum((places[:, None] >= boundaries[None, :]).astype(jnp.int32), axis=1)

    positions = first_row + jnp.arange(tok_rows, dtype=jnp.int32)
    query_clip = clip_of(positions)
    scaling = 1.0 / math.sqrt(head_dim)

    def absorb(state_now, block_keys, block_values, key_first):
        best, denominator, accum = state_now
        key_places = key_first + jnp.arange(tok_rows, dtype=jnp.int32)
        scores = (
            jnp.einsum("qhd,khd->hqk", q_normed, block_keys, preferred_element_type=jnp.float32)
            * scaling
        )
        inside = (key_places >= 0) & (key_places < tok_count)
        pair_ok = (query_clip[:, None] == clip_of(key_places)[None, :]) & inside[None, :]
        distance = jnp.abs(positions[:, None] - key_places[None, :])
        allowed = (distance[None, :, :] <= half_window[:, None, None]) & pair_ok[None, :, :]
        masked = jnp.where(allowed, scores, -jnp.inf)
        new_best = jnp.maximum(best, jnp.max(masked, axis=2))
        weights = jnp.exp(masked - new_best[:, :, None])
        shrink = jnp.exp(best - new_best)
        denominator = denominator * shrink + jnp.sum(weights, axis=2)
        accum = accum * shrink[:, :, None] + jnp.einsum(
            "hqk,khd->hqd",
            weights.astype(jnp.bfloat16),
            block_values,
            preferred_element_type=jnp.float32,
        )
        return (new_best, denominator, accum)

    start_state = (
        jnp.full((local_heads, tok_rows), -jnp.inf, jnp.float32),
        jnp.zeros((local_heads, tok_rows), jnp.float32),
        jnp.zeros((local_heads, tok_rows, head_dim), jnp.float32),
    )
    state_now = absorb(start_state, k_normed, value_rows, first_row)
    reach_blocks = HALF // tok_rows
    for distance_step in range(1, reach_blocks + 1):
        left_keys, left_values = passed_along((k_normed, value_rows), "tok", distance_step)
        state_now = absorb(state_now, left_keys, left_values, first_row - distance_step * tok_rows)
        right_keys, right_values = passed_along((k_normed, value_rows), "tok", -distance_step)
        state_now = absorb(
            state_now, right_keys, right_values, first_row + distance_step * tok_rows
        )
    attended = state_now[2] / state_now[1][:, :, None]
    key_unit = unit_rows(k_normed)
    query_unit = unit_rows(q_normed)
    pre_keys = jnp.einsum("thd,hdf->htf", key_unit, fast_in, preferred_element_type=jnp.float32)
    gate_part = pre_keys[:, :, :fast_hid]
    lin_part = pre_keys[:, :, fast_hid:]
    sigmoid_gate = jax.nn.sigmoid(gate_part)
    swish_gate = gate_part * sigmoid_gate
    hidden = (swish_gate * lin_part).astype(jnp.bfloat16)
    value_float = value_rows.astype(jnp.float32)
    push_out = (-jnp.transpose(rate_out)[:, :, None] * value_float).astype(jnp.bfloat16)
    push_in = (-jnp.transpose(rate_in)[:, :, None] * value_float).astype(jnp.bfloat16)
    grad_out = jnp.einsum("htf,thd->hfd", hidden, push_out, preferred_element_type=jnp.float32)
    hidden_grad = jnp.einsum("thd,hfd->htf", push_in, fast_out, preferred_element_type=jnp.float32)
    d_gate = hidden_grad * lin_part * sigmoid_gate * (1.0 + gate_part * (1.0 - sigmoid_gate))
    d_lin = hidden_grad * swish_gate
    d_pre = jnp.concatenate([d_gate, d_lin], axis=2).astype(jnp.bfloat16)
    grad_in = jnp.einsum("thd,htf->hdf", key_unit, d_pre, preferred_element_type=jnp.float32)
    in_float = fast_in.astype(jnp.float32)
    out_float = fast_out.astype(jnp.float32)
    in_base = jnp.sqrt(jnp.sum(in_float * in_float, axis=1))
    out_base = jnp.sqrt(jnp.sum(out_float * out_float, axis=1))
    summed_in, summed_out = lax.psum((grad_in, grad_out), "tok")
    updated_in = in_float - summed_in
    updated_out = out_float - summed_out
    new_in = rescale(updated_in, in_base, jnp.sum(updated_in * updated_in, axis=1))
    new_out = rescale(updated_out, out_base, jnp.sum(updated_out * updated_out, axis=1))
    pre_query = jnp.einsum("thd,hdf->htf", query_unit, new_in, preferred_element_type=jnp.float32)
    query_gate = pre_query[:, :, :fast_hid]
    query_hidden = (query_gate * jax.nn.sigmoid(query_gate) * pre_query[:, :, fast_hid:]).astype(
        jnp.bfloat16
    )
    fast_result = jnp.einsum(
        "htf,hfd->htd", query_hidden, new_out, preferred_element_type=jnp.float32
    )
    combined = attended + fast_result
    return jnp.transpose(combined, (1, 0, 2)).astype(jnp.bfloat16)


VMEM_BYTES = 16 * 1024 * 1024
HIDDEN_MASK = -1e30
NT = (((1,), (1,)), ((), ()))


def exchanged(x, pairs):
    return lax.ppermute(x, "tok", pairs)


def nt_dot(a, b):
    return lax.dot_general(a, b, NT, preferred_element_type=jnp.float32)


def nn_dot(a, b):
    return jnp.dot(a, b, preferred_element_type=jnp.float32)


def params():
    return pltpu.CompilerParams(vmem_limit_bytes=VMEM_BYTES)


def cost(flops, nbytes):
    return pl.CostEstimate(flops=int(16 * flops), bytes_accessed=int(nbytes), transcendentals=0)


def untouched(arrays):
    return [pl.BlockSpec(memory_space=pl.ANY)] * len(arrays)


def pack_values_kernel(peers, place_ref, rate_in_ref, rate_out_ref, v_ref, *refs):
    outs, aux_ref = refs[:peers], refs[-1]
    rows = v_ref.shape[2]
    share = rate_in_ref.shape[0] // peers
    aux_ref[...] = jnp.zeros_like(aux_ref)
    for p in range(peers):
        c = place_ref[0] ^ p
        head = pl.ds(c * share + pl.program_id(0), 1)
        for i in range(0, rows, 128):
            outs[p][0, i : i + 128, :] = jnp.transpose(v_ref[c, 0, i : i + 128, :])
        at = 0
        for rate_ref in (rate_in_ref, rate_out_ref):
            rate = rate_ref[head, :]
            high = rate.astype(jnp.bfloat16).astype(jnp.float32)
            for part in (high, rate - high):
                for i in range(0, rows, 128):
                    aux_ref[at : at + 1, :] = part[:, i : i + 128]
                    at += 1
        outs[p][0, rows:, :] = aux_ref[...].astype(jnp.bfloat16)


def pack_values(place, v, rates, peers, aux_rows):
    heads, rows, dim = v.shape
    share = heads // peers
    out_shape = (share, rows + aux_rows, dim)
    return pl.pallas_call(
        functools.partial(pack_values_kernel, peers),
        out_shape=[jax.ShapeDtypeStruct(out_shape, jnp.bfloat16)] * peers,
        grid_spec=pltpu.PrefetchScalarGridSpec(
            num_scalar_prefetch=1,
            grid=(share,),
            in_specs=[pl.BlockSpec(a.shape, lambda j, place: (0, 0)) for a in rates]
            + [pl.BlockSpec((peers, 1, rows, dim), lambda j, place: (0, j, 0, 0))],
            out_specs=[pl.BlockSpec((1,) + out_shape[1:], lambda j, place: (j, 0, 0))] * peers,
            scratch_shapes=[pltpu.VMEM((aux_rows, dim), jnp.float32)],
        ),
        compiler_params=params(),
        cost_estimate=cost(0, 4 * heads * rows * dim),
        name="pack_values",
    )(place, *rates, v.reshape(peers, share, rows, dim))


def pack_kernel(peers, first, width_all, fold, with_lone, place_ref, *refs):
    squares_ref, more_ref, q_gain_ref, k_gain_ref, q_ref, k_ref = refs[:6]
    outs = refs[-3 - peers : -3]
    lone = refs[6 : -3 - peers]
    aux_ref, q_scale_ref, k_scale_ref = refs[-3:]
    rows, dim = q_scale_ref.shape
    share = q_gain_ref.shape[0] // peers
    count = pl.num_programs(0)
    step = pl.program_id(0)

    @pl.when(step == 0)
    def _():
        scales = lax.rsqrt((squares_ref[...] + more_ref[...]) / width_all + epsilon)
        q_scale_ref[...] = jnp.transpose(jnp.broadcast_to(scales[0:1] * fold, (dim, rows)))
        k_scale_ref[...] = jnp.transpose(jnp.broadcast_to(scales[1:2], (dim, rows)))
        aux_ref[...] = jnp.zeros_like(aux_ref)

    def normed(ref, c, scale_ref, gain_ref, head, some):
        gain = gain_ref[pl.ds(c * share + head, 1), :]
        scaled = ref[c, 0, 0:some].astype(jnp.float32) * scale_ref[0:some] * gain
        return scaled.astype(jnp.bfloat16)

    for p in range(peers):
        c = place_ref[0] ^ p
        outs[p][0, 0:rows, :] = normed(q_ref, c, q_scale_ref, q_gain_ref, first + step, rows)
        outs[p][0, rows : 2 * rows, :] = normed(
            k_ref, c, k_scale_ref, k_gain_ref, first + step, rows
        )
        if with_lone:
            for i in range(len(lone) // 3):
                head = jnp.minimum(step + i * count, share - 1)
                q0 = normed(lone[3 * i], c, q_scale_ref, q_gain_ref, head, 16)
                k0 = normed(lone[3 * i + 1], c, k_scale_ref, k_gain_ref, head, 16)
                for at, array in enumerate((q0, k0, lone[3 * i + 2][c, 0])):
                    at += 3 * i
                    aux_ref[at : at + 1, :] = array.astype(jnp.float32)[0:1]
            outs[p][0, 2 * rows :, :] = aux_ref[...].astype(jnp.bfloat16)


def pack(place, sums, q, k, v, gains, peers, aux_rows, first, count, width_all, fold):
    heads, rows, dim = q.shape
    share = heads // peers
    out_shape = (count, 2 * rows + (0 if first else aux_rows), dim)
    whole = [*sums, *gains]
    q, k, v = [x.reshape(peers, share, rows, dim) for x in (q, k, v)]
    operands = [*whole, q, k]
    here = pl.BlockSpec((peers, 1, rows, dim), lambda j, place: (0, first + j, 0, 0))
    in_specs = [pl.BlockSpec(a.shape, lambda j, place: (0, 0)) for a in whole] + [here, here]
    if not first:
        for i in range(-(-share // count)):
            operands += [q, k, v]
            in_specs += [
                pl.BlockSpec(
                    (peers, 1, 16, dim),
                    lambda j, place, i=i: (0, jnp.minimum(j + i * count, share - 1), 0, 0),
                )
            ] * 3
    return pl.pallas_call(
        functools.partial(pack_kernel, peers, first, width_all, fold, not first),
        out_shape=[jax.ShapeDtypeStruct(out_shape, jnp.bfloat16)] * peers,
        grid_spec=pltpu.PrefetchScalarGridSpec(
            num_scalar_prefetch=1,
            grid=(count,),
            in_specs=in_specs,
            out_specs=[pl.BlockSpec((1,) + out_shape[1:], lambda j, place: (j, 0, 0))] * peers,
            scratch_shapes=[
                pltpu.VMEM((aux_rows, dim), jnp.float32),
                pltpu.VMEM((rows, dim), jnp.float32),
                pltpu.VMEM((rows, dim), jnp.float32),
            ],
        ),
        compiler_params=params(),
        cost_estimate=cost(0, 8 * peers * count * rows * dim),
        name="pack",
    )(place, *operands)


def stack_kernel(from_row, *refs):
    for p, ref in enumerate(refs[:-1]):
        refs[-1][p] = ref[:, from_row:, :]


def stacked(arrays, from_row):
    heads, rows, dim = arrays[0].shape
    return pl.pallas_call(
        functools.partial(stack_kernel, from_row),
        out_shape=jax.ShapeDtypeStruct((len(arrays), heads, rows - from_row, dim), jnp.bfloat16),
        in_specs=[pl.BlockSpec(memory_space=pltpu.VMEM)] * len(arrays),
        out_specs=pl.BlockSpec(memory_space=pltpu.VMEM),
        compiler_params=params(),
        name="stack",
    )(*arrays)


def key_value_blocks(peers, rows, refs):
    own_v, other_v = refs[:peers], refs[peers]
    own_qk, other_k = refs[peers + 1 : 2 * peers + 1], refs[2 * peers + 1]
    for p in range(peers):
        yield p, True, own_qk[p].at[0, rows : 2 * rows], own_v[p].at[0]
        yield p, False, other_k.at[p, 0, 0:rows], other_v.at[p, 0]


def key_value_operands(values, keys, first):
    own_v, other_v = values
    own_qk, other_k = keys

    def single(array, at):
        return pl.BlockSpec((1,) + array.shape[1:], lambda j, *_: (at + j, 0, 0))

    def stacked(array, at):
        shape = (array.shape[0], 1) + array.shape[2:]
        return pl.BlockSpec(shape, lambda j, *_: (0, at + j, 0, 0))

    specs = [single(a, first) for a in own_v] + [stacked(other_v, first)]
    specs += [single(a, 0) for a in own_qk] + [stacked(other_k, 0)]
    return [*own_v, other_v, *own_qk, other_k], specs


def grads_kernel(peers, rows, rate_rows, place_ref, in_ref, out_ref, *refs):
    grad_ref = refs[-1]
    hid = out_ref.shape[1]
    part = hid // 2
    core = place_ref[1]
    own = pl.multiple_of(core * part, part)
    in_half = jnp.concatenate(
        [
            jnp.transpose(in_ref[0, :, pl.ds(at, part)].astype(jnp.float32))
            for at in (own, pl.multiple_of(hid + own, part))
        ],
        axis=0,
    ).astype(jnp.bfloat16)
    out_half = out_ref[0, pl.ds(own, part), :]
    sum_in = jnp.zeros((2 * part, in_half.shape[1]), jnp.float32)
    sum_out = jnp.zeros((part, in_half.shape[1]), jnp.float32)
    for _, _, keys, values in key_value_blocks(peers, rows, refs):
        k = keys[...].astype(jnp.float32)
        v_t = jnp.concatenate([values[at : at + 128, :] for at in range(0, rows, 128)], axis=1)
        aux = values[rows:, :].astype(jnp.float32)

        def rate(at):
            both = aux[at : at + rate_rows] + aux[at + rate_rows : at + 2 * rate_rows]
            return jnp.concatenate([both[i : i + 1] for i in range(rate_rows)], axis=1)

        rate_in, rate_out = rate(0), rate(2 * rate_rows)
        unit = (k * lax.rsqrt(jnp.sum(k * k, axis=1, keepdims=True) + epsilon)).astype(
            jnp.bfloat16
        )
        pre = nt_dot(in_half, unit)
        gate, lin = pre[:part], pre[part:]
        sig = jax.nn.sigmoid(gate)
        swish = gate * sig
        pushed = (swish * lin * -rate_out).astype(jnp.bfloat16)
        hidden_grad = nn_dot(out_half, v_t) * -rate_in
        d_gate = hidden_grad * lin * sig * (1.0 + gate * (1.0 - sig))
        d_lin = hidden_grad * swish
        d_pre = jnp.concatenate([d_gate, d_lin], axis=0).astype(jnp.bfloat16)
        sum_in += nn_dot(d_pre, unit)
        sum_out += nt_dot(pushed, v_t)
    grad_ref[0, 0 : 2 * part, :] = sum_in.astype(jnp.bfloat16)
    grad_ref[0, 2 * part :, :] = sum_out.astype(jnp.bfloat16)


def chip_weights(array, share, first):
    return pl.BlockSpec(
        (1,) + array.shape[1:], lambda j, place, *_: (place[0] * share + first + j, 0, 0)
    )


def by_head(shape):
    return pl.BlockSpec((shape[0], 1) + shape[2:], lambda j, *_: (0, j, 0, 0))


def gradients(place, fast_in, fast_out, values, keys, share, rows, first, after):
    _, hid, dim = fast_out.shape
    peers = len(keys[0])
    heads = keys[0][0].shape[0]
    grad_shape = (heads, 3 * hid // 2, dim)
    blocks, block_specs = key_value_operands(values, keys, first)
    return pl.pallas_call(
        functools.partial(grads_kernel, peers, rows, rows // 128),
        out_shape=jax.ShapeDtypeStruct(grad_shape, jnp.bfloat16),
        grid_spec=pltpu.PrefetchScalarGridSpec(
            num_scalar_prefetch=1,
            grid=(heads,),
            in_specs=[chip_weights(a, share, first) for a in (fast_in, fast_out)]
            + block_specs
            + untouched(after),
            out_specs=pl.BlockSpec((1,) + grad_shape[1:], lambda j, place: (j, 0, 0)),
        ),
        compiler_params=params(),
        cost_estimate=cost(0, 0),
        name="gradients",
    )(place, fast_in, fast_out, *blocks, *after)


def attend_kernel(peers, rows, share, first, fwd_heads, place_ref, window_ref, edge_ref, *refs):
    own_qk = refs[peers + 1 : 2 * peers + 1]
    fwd_ref = refs[2 * peers + 2]
    out_ref, extra_ref, k_scr, vt_scr, q_scr = refs[-5:]
    span = 2 * peers * rows
    dim = k_scr.shape[1]
    pad = fwd_ref.shape[1]
    chip, core, half = place_ref[0], place_ref[1], place_ref[2]
    base = half * span
    limit = span + 1 - half
    step = pl.program_id(0)
    window = window_ref[chip * share + first + step]

    @pl.when(step == 0)
    def _():
        k_scr[span:, :] = jnp.zeros((k_scr.shape[0] - span, dim), k_scr.dtype)
        vt_scr[:, span:] = jnp.zeros((vt_scr.shape[0], vt_scr.shape[1] - span), vt_scr.dtype)
        vt_scr[dim:, :] = jnp.ones((vt_scr.shape[0] - dim, vt_scr.shape[1]), vt_scr.dtype)

    for p, own, keys, values in key_value_blocks(peers, rows, refs):
        at = pl.multiple_of(((chip ^ p) * 2 + (core if own else 1 - core)) * rows, rows)
        k_scr[pl.ds(at, rows), :] = keys[...]
        for i in range(0, rows, 128):
            vt_scr[0:dim, pl.ds(pl.multiple_of(at + i, 128), 128)] = values[i : i + 128, :]
    for p in range(peers):
        q_scr[chip ^ p] = own_qk[p][0, 0:rows, :]
    fwd = fwd_ref[0].astype(jnp.float32)
    turn = (first + step) // fwd_heads
    q_lone, k_lone, v_lone = (
        sum(
            jnp.where(turn == t, fwd[3 * t + i : 3 * t + i + 1], 0.0)
            for t in range(-(-share // fwd_heads))
        )
        for i in range(3)
    )
    k_scr[span : span + pad, :] = jnp.broadcast_to(k_lone, (pad, dim)).astype(jnp.bfloat16)
    vt_scr[0:dim, span : span + 128] = jnp.transpose(
        jnp.broadcast_to(v_lone, (128, dim))
    ).astype(jnp.bfloat16)

    def clip_start(place):
        start = jnp.zeros_like(place)
        for i in range(edge_ref.shape[0]):
            start = jnp.maximum(start, jnp.where(edge_ref[i] <= place, edge_ref[i], 0))
        return start

    def clip_stop(place):
        stop = jnp.full_like(place, base + limit)
        for i in range(edge_ref.shape[0]):
            stop = jnp.minimum(stop, jnp.where(edge_ref[i] > place, edge_ref[i], base + limit))
        return stop

    def lowest(place):
        return jnp.maximum(jnp.maximum(place - window, clip_start(place)), base) - base

    def highest(place):
        return jnp.minimum(place + window, clip_stop(place) - 1) - base

    def one_pair(i, carry):
        pair = []
        for c in (i, peers - 1 - i):
            start = (c * 2 + core) * rows
            place = base + start + lax.broadcasted_iota(jnp.int32, (1, rows), 1)
            from_key = lowest(base + start) // 128 * 128
            count = (highest(base + start + rows - 1) - from_key) // 256 + 1
            pair.append((c, lowest(place), highest(place), from_key, count))
        count = jnp.maximum(pair[0][4], pair[1][4])

        def variant(chunks):
            width = chunks * 256
            key = lax.broadcasted_iota(jnp.int32, (width, rows), 0)
            froms = [
                pl.multiple_of(jnp.minimum(each[3], k_scr.shape[0] - width), 128) for each in pair
            ]
            scores = [
                nt_dot(k_scr[pl.ds(at, width), :], q_scr[each[0]])
                for each, at in zip(pair, froms)
            ]
            scores = [
                jnp.where((key >= each[1] - at) & (key <= each[2] - at), one, HIDDEN_MASK)
                for each, at, one in zip(pair, froms, scores)
            ]
            weights = [
                jnp.exp2(one - jnp.max(one, axis=0, keepdims=True)).astype(jnp.bfloat16)
                for one in scores
            ]
            totals = [
                nn_dot(vt_scr[:, pl.ds(at, width)], one) for at, one in zip(froms, weights)
            ]
            for each, total in zip(pair, totals):
                attended = total[0:dim] * (1.0 / total[dim : dim + 1])
                out_ref[each[0], 0] = jnp.transpose(attended)

        for chunks in range(1, span // 256 + 2):

            @pl.when(count == chunks)
            def _(chunks=chunks):
                variant(chunks)

        return carry

    lax.fori_loop(0, peers // 2, one_pair, 0)
    extra_ref[0] = jnp.zeros(extra_ref.shape[1:], jnp.float32)

    @pl.when((half == 0) & (core == 1))
    def _():
        near = span - HALF
        width = HALF + 128
        q = jnp.broadcast_to(q_lone, (pad, dim)).astype(jnp.bfloat16)
        scores = nt_dot(q, k_scr[near : near + width, :])
        key = near + lax.broadcasted_iota(jnp.int32, (1, width), 1)
        scores = jnp.where((key >= span - window) & (key <= span), scores, HIDDEN_MASK)
        top = jnp.max(scores, axis=1, keepdims=True)
        weights = jnp.exp2(scores - top).astype(jnp.bfloat16)
        total = nt_dot(weights, vt_scr[:, near : near + width])
        extra_ref[0] = total[:, 0:dim] / total[:, dim : dim + 1]


def attend(place, half_window, boundaries, values, keys, forwarded, share, rows, first, after):
    peers = len(keys[0])
    heads = keys[0][0].shape[0]
    fwd_heads, pad, dim = forwarded.shape
    scr_rows = 2 * peers * rows + 256
    out_shapes = [(peers, heads, rows, dim), (heads, pad, dim)]
    one_head = pl.BlockSpec((1, pad, dim), lambda j, *_: (j, 0, 0))
    lone = pl.BlockSpec((1, pad, dim), lambda j, *_: (lax.rem(first + j, fwd_heads), 0, 0))
    blocks, block_specs = key_value_operands(values, keys, first)
    return pl.pallas_call(
        functools.partial(attend_kernel, peers, rows, share, first, fwd_heads),
        out_shape=[jax.ShapeDtypeStruct(shape, jnp.float32) for shape in out_shapes],
        grid_spec=pltpu.PrefetchScalarGridSpec(
            num_scalar_prefetch=3,
            grid=(heads,),
            in_specs=block_specs + [lone] + untouched(after),
            out_specs=[by_head(out_shapes[0]), one_head],
            scratch_shapes=[
                pltpu.VMEM((scr_rows, dim), jnp.bfloat16),
                pltpu.VMEM((dim + 16, scr_rows), jnp.bfloat16),
                pltpu.VMEM((peers, rows, dim), jnp.bfloat16),
            ],
        ),
        compiler_params=params(),
        cost_estimate=cost(4 * heads * peers * rows * HALF * 2 * dim, 0),
        name="attend",
    )(place, half_window, boundaries, *blocks, forwarded, *after)


def finish_kernel(peers, unit_epsilon, place_ref, *refs):
    att_ref, base_in_ref, base_out_ref, own_ref, other_ref, patch_ref = refs[:6]
    queries = refs[6 : 6 + peers]
    outs = refs[-2 - peers : -2]
    grad_in_scr, grad_out_scr = refs[-2:]
    chip, core, half = place_ref[0], place_ref[1], place_ref[2]
    rows = att_ref.shape[2]
    hid = base_out_ref.shape[1]
    part = hid // 2
    for summed, lane in ((own_ref, core), (other_ref, 1 - core)):
        at = pl.multiple_of(lane * part, part)
        grad_in_scr[pl.ds(at, part), :] = summed[0, 0:part, :].astype(jnp.float32)
        grad_in_scr[pl.ds(hid + at, part), :] = summed[0, part : 2 * part, :].astype(jnp.float32)
        grad_out_scr[pl.ds(at, part), :] = summed[0, 2 * part :, :].astype(jnp.float32)

    def renewed(base, grad):
        base = base.astype(jnp.float32)
        updated = base - grad
        norm = jnp.sqrt(jnp.sum(base * base, axis=0, keepdims=True))
        squares = jnp.sum(updated * updated, axis=0, keepdims=True)
        return (updated * (norm / jnp.sqrt(squares + epsilon))).astype(jnp.bfloat16)

    new_in = renewed(base_in_ref[0], jnp.transpose(grad_in_scr[...]))
    new_out = renewed(base_out_ref[0], grad_out_scr[...])
    patch = patch_ref[0][0:1, :]
    row = lax.broadcasted_iota(jnp.int32, (rows, 1), 0)
    for p in range(peers):
        q = queries[p][0].astype(jnp.float32)
        unit = (q * lax.rsqrt(jnp.sum(q * q, axis=1, keepdims=True) + unit_epsilon)).astype(
            jnp.bfloat16
        )
        pre = nn_dot(unit, new_in)
        gate = pre[:, :hid]
        hidden = (gate * jax.nn.sigmoid(gate) * pre[:, hid:]).astype(jnp.bfloat16)
        patched = (half == 1) & (core == 0) & (chip == p)
        attended = jnp.where(patched & (row == 0), patch, att_ref[chip ^ p, 0])
        outs[p][0] = (attended + nn_dot(hidden, new_out)).astype(jnp.bfloat16)


def finish(place, attended, fast_in, fast_out, sums, patch, own_qk, share, first, unit_epsilon, after):
    peers, heads, rows, dim = attended.shape
    hid = fast_out.shape[1]

    def plain(shape):
        return pl.BlockSpec((1,) + shape[1:], lambda j, place: (j, 0, 0))

    out_shape = (heads, rows, dim)
    in_specs = [by_head(attended.shape)]
    in_specs += [chip_weights(a, share, first) for a in (fast_in, fast_out)]
    in_specs += [plain(a.shape) for a in (*sums, patch)]
    in_specs += [plain(out_shape)] * peers + untouched(after)
    return pl.pallas_call(
        functools.partial(finish_kernel, peers, unit_epsilon),
        out_shape=[jax.ShapeDtypeStruct(out_shape, jnp.bfloat16)] * peers,
        grid_spec=pltpu.PrefetchScalarGridSpec(
            num_scalar_prefetch=1,
            grid=(heads,),
            in_specs=in_specs,
            out_specs=[plain(out_shape)] * peers,
            scratch_shapes=[
                pltpu.VMEM((2 * hid, dim), jnp.float32),
                pltpu.VMEM((hid, dim), jnp.float32),
            ],
        ),
        compiler_params=params(),
        cost_estimate=cost(12 * heads * peers * rows * hid * dim, 0),
        name="finish",
    )(place, attended, fast_in, fast_out, *sums, patch, *own_qk, *after)


def place_kernel(peers, chunks, share, place_ref, *refs):
    pieces, out_ref, sems = refs[:-2], refs[-2], refs[-1]
    copies = []
    for first, heads in chunks:
        for p in range(peers):
            at = (place_ref[0] ^ p) * share + first
            i = len(copies)
            copies.append(
                pltpu.make_async_copy(pieces[i], out_ref.at[pl.ds(at, heads)], sems.at[i])
            )
    for copy in copies:
        copy.start()
    for copy in copies:
        copy.wait()


def put_in_place(place, pieces, peers, chunks, share):
    _, rows, dim = pieces[0].shape
    return pl.pallas_call(
        functools.partial(place_kernel, peers, chunks, share),
        out_shape=jax.ShapeDtypeStruct((peers * share, rows, dim), jnp.bfloat16),
        in_specs=[pl.BlockSpec(memory_space=pltpu.SMEM)]
        + [pl.BlockSpec(memory_space=pltpu.VMEM)] * len(pieces),
        out_specs=pl.BlockSpec(memory_space=pl.ANY),
        scratch_shapes=[pltpu.SemaphoreType.DMA((len(pieces),))],
        compiler_params=params(),
        name="put_in_place",
    )(place, *pieces)


def regrouping(tok_peers, rows, heads, dim, hid):
    half_peers = tok_peers // 2
    peers = math.gcd(half_peers, heads)
    fits = tok_peers % 2 == 0 and half_peers * rows == 2 * HALF
    fits = fits and half_peers == 2 * peers and peers & (peers - 1) == 0
    fits = fits and rows % 256 == 0 and dim == 128 and hid % 256 == 0
    return peers if fits else 0


def regrouped_body(
    peers,
    query_rows,
    key_rows,
    value_rows,
    query_gain,
    key_gain,
    rate_in,
    rate_out,
    fast_in,
    fast_out,
    half_window,
    boundaries,
):
    rows, heads, dim = query_rows.shape
    share = heads // peers
    tok_peers = lax.axis_size("tok")
    half_peers = tok_peers // 2
    width_all = heads * dim * lax.axis_size("head")
    chunks = [(0, (share + 1) // 2), ((share + 1) // 2, share // 2)]
    aux_rows = -(-max(4 * (rows // 128), 3 * -(-share // chunks[0][1])) // 16) * 16
    own_index = lax.axis_index("tok")
    half = own_index // half_peers
    chip = own_index % half_peers // 2
    core = own_index % 2
    place = jnp.stack([chip, core, half]).astype(jnp.int32)

    def dealt(sent):
        pairs = [
            [(t, t // half_peers * half_peers + ((t % half_peers) ^ (2 * p))) for t in range(tok_peers)]
            for p in range(peers)
        ]
        return [sent[0]] + [exchanged(sent[p], pairs[p]) for p in range(1, peers)]

    core_pairs = [(t, t ^ 1) for t in range(tok_peers)]
    half_pairs = [(t, (t + half_peers) % tok_peers) for t in range(tok_peers)]
    forward_pairs = [(t + half_peers, t) for t in range(half_peers)]
    back_pairs = [(t, t - 1 + half_peers) for t in range(half_peers) if t % 2 == 1]

    q = jnp.transpose(query_rows, (1, 0, 2))
    k = jnp.transpose(key_rows, (1, 0, 2))
    v = jnp.transpose(value_rows, (1, 0, 2))
    sent_v = pack_values(place, v, (rate_in, rate_out), peers, aux_rows)
    *sent_v, q, k = lax.optimization_barrier((*sent_v, q, k))
    q_float = q.astype(jnp.float32)
    k_float = k.astype(jnp.float32)
    squares = jnp.stack(
        [jnp.sum(q_float * q_float, axis=(0, 2)), jnp.sum(k_float * k_float, axis=(0, 2))]
    )
    if lax.axis_size("head") == 2:
        sums = (squares, lax.ppermute(squares, "head", [(0, 1), (1, 0)]))
    else:
        sums = (lax.psum(squares, "head"), jnp.zeros_like(squares))
    fold = math.log2(math.e) / math.sqrt(dim)
    own_v = dealt(sent_v)
    sent = [
        pack(
            place,
            sums,
            q,
            k,
            v,
            (query_gain, key_gain),
            peers,
            aux_rows,
            first,
            count,
            width_all,
            fold,
        )
        for first, count in chunks
    ]
    own_v = lax.optimization_barrier((*own_v, *sent[-1]))[:peers]
    values = (own_v, exchanged(stacked(own_v, 0), core_pairs))
    received = []
    for each in sent:
        if received:
            each = [lax.optimization_barrier(pair)[0] for pair in zip(each, received[-1])]
        received.append(dealt(each))
    forwarded = None
    pieces = []
    after = []
    for (first, count), own_qk in zip(chunks, received):
        if after:
            *own_qk, _ = lax.optimization_barrier((*own_qk, grad))
        own_k = stacked(own_qk, rows)
        other_k = exchanged(own_k, core_pairs)
        keys = (own_qk, other_k)
        if forwarded is None:
            aux = jnp.zeros((count, aux_rows, dim), jnp.bfloat16)
            for p in range(peers):
                here = jnp.where(core == 0, own_k[p, :, rows:], other_k[p, :, rows:])
                aux = jnp.where(chip == p, here, aux)
            forwarded = exchanged(aux, forward_pairs)
        grad = gradients(
            place, fast_in, fast_out, values, keys, share, rows, first, [attended] if after else []
        )
        from_half = exchanged(grad, half_pairs)
        attended, extra = attend(
            place,
            half_window,
            boundaries,
            values,
            keys,
            forwarded,
            share,
            rows,
            first,
            [grad] + after,
        )
        patch = exchanged(extra, back_pairs)
        from_half, _ = lax.optimization_barrier((from_half, attended))
        own_sum = (grad.astype(jnp.float32) + from_half.astype(jnp.float32)).astype(jnp.bfloat16)
        outs = finish(
            place,
            attended,
            fast_in,
            fast_out,
            (own_sum, exchanged(own_sum, core_pairs)),
            patch,
            own_qk,
            share,
            first,
            epsilon * fold * fold,
            pieces,
        )
        after = [outs[0]]
        pieces = pieces + dealt(outs)
    whole = put_in_place(place, pieces, peers, chunks, share)
    return jnp.transpose(whole, (1, 0, 2))


def body(query_rows, *others):
    rows, heads, dim = query_rows.shape
    hid = others[7].shape[1]
    peers = regrouping(lax.axis_size("tok"), rows, heads, dim, hid)
    if peers:
        return regrouped_body(peers, query_rows, *others)
    return sliding_body(query_rows, *others)


def solution(mesh):
    in_specs = (
        P("tok", "head", None),
        P("tok", "head", None),
        P("tok", "head", None),
        P("head", None),
        P("head", None),
        P("head", "tok"),
        P("head", "tok"),
        P("head", None, None),
        P("head", None, None),
        P("head"),
        P(),
    )
    out_specs = P("tok", "head", None)
    return jax.shard_map(body, mesh=mesh, in_specs=in_specs, out_specs=out_specs, check_vma=False)
```

```python
import functools
import math

import jax
import jax.numpy as jnp
from jax import lax
from jax.experimental import pallas as pl
from jax.experimental.pallas import tpu as pltpu
from jax.sharding import PartitionSpec as P

HALF = 1024


epsilon = 1e-06


def passed_along(x, axis, by):
    peers = lax.axis_size(axis)
    pairs = [(i, i + by) for i in range(peers) if 0 <= i + by < peers]
    return lax.ppermute(x, axis, pairs)


def unit_rows(matrix):
    as_float = matrix.astype(jnp.float32)
    return (
        as_float * lax.rsqrt(jnp.sum(as_float * as_float, axis=-1, keepdims=True) + epsilon)
    ).astype(jnp.bfloat16)


def rescale(updated, base_norm, squares):
    return (updated * (base_norm / jnp.sqrt(squares + epsilon))[:, None, :]).astype(jnp.bfloat16)


def sliding_body(
    query_rows,
    key_rows,
    value_rows,
    query_gain,
    key_gain,
    rate_in,
    rate_out,
    fast_in,
    fast_out,
    half_window,
    boundaries,
):
    tok_rows = query_rows.shape[0]
    local_heads = query_rows.shape[1]
    head_dim = query_rows.shape[2]
    fast_hid = fast_out.shape[1]
    width_all = local_heads * head_dim * lax.axis_size("head")
    tok_count = tok_rows * lax.axis_size("tok")
    own_index = lax.axis_index("tok")
    first_row = own_index * tok_rows
    query_float = query_rows.astype(jnp.float32)
    key_float = key_rows.astype(jnp.float32)
    query_sq, key_sq = lax.psum(
        (
            jnp.sum(query_float * query_float, axis=(1, 2)),
            jnp.sum(key_float * key_float, axis=(1, 2)),
        ),
        "head",
    )
    q_normed = (
        query_float * lax.rsqrt(query_sq / width_all + epsilon)[:, None, None] * query_gain[None]
    ).astype(jnp.bfloat16)
    k_normed = (
        key_float * lax.rsqrt(key_sq / width_all + epsilon)[:, None, None] * key_gain[None]
    ).astype(jnp.bfloat16)

    def clip_of(places):
        return jnp.sum((places[:, None] >= boundaries[None, :]).astype(jnp.int32), axis=1)

    positions = first_row + jnp.arange(tok_rows, dtype=jnp.int32)
    query_clip = clip_of(positions)
    scaling = 1.0 / math.sqrt(head_dim)

    def absorb(state_now, block_keys, block_values, key_first):
        best, denominator, accum = state_now
        key_places = key_first + jnp.arange(tok_rows, dtype=jnp.int32)
        scores = (
            jnp.einsum("qhd,khd->hqk", q_normed, block_keys, preferred_element_type=jnp.float32)
            * scaling
        )
        inside = (key_places >= 0) & (key_places < tok_count)
        pair_ok = (query_clip[:, None] == clip_of(key_places)[None, :]) & inside[None, :]
        distance = jnp.abs(positions[:, None] - key_places[None, :])
        allowed = (distance[None, :, :] <= half_window[:, None, None]) & pair_ok[None, :, :]
        masked = jnp.where(allowed, scores, -jnp.inf)
        new_best = jnp.maximum(best, jnp.max(masked, axis=2))
        weights = jnp.exp(masked - new_best[:, :, None])
        shrink = jnp.exp(best - new_best)
        denominator = denominator * shrink + jnp.sum(weights, axis=2)
        accum = accum * shrink[:, :, None] + jnp.einsum(
            "hqk,khd->hqd",
            weights.astype(jnp.bfloat16),
            block_values,
            preferred_element_type=jnp.float32,
        )
        return (new_best, denominator, accum)

    start_state = (
        jnp.full((local_heads, tok_rows), -jnp.inf, jnp.float32),
        jnp.zeros((local_heads, tok_rows), jnp.float32),
        jnp.zeros((local_heads, tok_rows, head_dim), jnp.float32),
    )
    state_now = absorb(start_state, k_normed, value_rows, first_row)
    reach_blocks = HALF // tok_rows
    for distance_step in range(1, reach_blocks + 1):
        left_keys, left_values = passed_along((k_normed, value_rows), "tok", distance_step)
        state_now = absorb(state_now, left_keys, left_values, first_row - distance_step * tok_rows)
        right_keys, right_values = passed_along((k_normed, value_rows), "tok", -distance_step)
        state_now = absorb(
            state_now, right_keys, right_values, first_row + distance_step * tok_rows
        )
    attended = state_now[2] / state_now[1][:, :, None]
    key_unit = unit_rows(k_normed)
    query_unit = unit_rows(q_normed)
    pre_keys = jnp.einsum("thd,hdf->htf", key_unit, fast_in, preferred_element_type=jnp.float32)
    gate_part = pre_keys[:, :, :fast_hid]
    lin_part = pre_keys[:, :, fast_hid:]
    sigmoid_gate = jax.nn.sigmoid(gate_part)
    swish_gate = gate_part * sigmoid_gate
    hidden = (swish_gate * lin_part).astype(jnp.bfloat16)
    value_float = value_rows.astype(jnp.float32)
    push_out = (-jnp.transpose(rate_out)[:, :, None] * value_float).astype(jnp.bfloat16)
    push_in = (-jnp.transpose(rate_in)[:, :, None] * value_float).astype(jnp.bfloat16)
    grad_out = jnp.einsum("htf,thd->hfd", hidden, push_out, preferred_element_type=jnp.float32)
    hidden_grad = jnp.einsum("thd,hfd->htf", push_in, fast_out, preferred_element_type=jnp.float32)
    d_gate = hidden_grad * lin_part * sigmoid_gate * (1.0 + gate_part * (1.0 - sigmoid_gate))
    d_lin = hidden_grad * swish_gate
    d_pre = jnp.concatenate([d_gate, d_lin], axis=2).astype(jnp.bfloat16)
    grad_in = jnp.einsum("thd,htf->hdf", key_unit, d_pre, preferred_element_type=jnp.float32)
    in_float = fast_in.astype(jnp.float32)
    out_float = fast_out.astype(jnp.float32)
    in_base = jnp.sqrt(jnp.sum(in_float * in_float, axis=1))
    out_base = jnp.sqrt(jnp.sum(out_float * out_float, axis=1))
    summed_in, summed_out = lax.psum((grad_in, grad_out), "tok")
    updated_in = in_float - summed_in
    updated_out = out_float - summed_out
    new_in = rescale(updated_in, in_base, jnp.sum(updated_in * updated_in, axis=1))
    new_out = rescale(updated_out, out_base, jnp.sum(updated_out * updated_out, axis=1))
    pre_query = jnp.einsum("thd,hdf->htf", query_unit, new_in, preferred_element_type=jnp.float32)
    query_gate = pre_query[:, :, :fast_hid]
    query_hidden = (query_gate * jax.nn.sigmoid(query_gate) * pre_query[:, :, fast_hid:]).astype(
        jnp.bfloat16
    )
    fast_result = jnp.einsum(
        "htf,hfd->htd", query_hidden, new_out, preferred_element_type=jnp.float32
    )
    combined = attended + fast_result
    return jnp.transpose(combined, (1, 0, 2)).astype(jnp.bfloat16)


VMEM_BYTES = 16 * 1024 * 1024
HIDDEN_MASK = -1e30
NT = (((1,), (1,)), ((), ()))


def exchanged(x, pairs):
    return lax.ppermute(x, "tok", pairs)


def nt_dot(a, b):
    return lax.dot_general(a, b, NT, preferred_element_type=jnp.float32)


def nn_dot(a, b):
    return jnp.dot(a, b, preferred_element_type=jnp.float32)


def params():
    return pltpu.CompilerParams(vmem_limit_bytes=VMEM_BYTES)


def cost(flops, nbytes):
    return pl.CostEstimate(flops=int(16 * flops), bytes_accessed=int(nbytes), transcendentals=0)


def untouched(arrays):
    return [pl.BlockSpec(memory_space=pl.ANY)] * len(arrays)


def pack_kernel(peers, first, width_all, fold, with_lone, place_ref, *refs):
    squares_ref, more_ref, q_gain_ref, k_gain_ref, rate_in_ref, rate_out_ref = refs[:6]
    q_ref, k_ref, v_ref = refs[6:9]
    outs = refs[-3 - peers : -3]
    lone = refs[9 : -3 - peers]
    aux_ref, q_scale_ref, k_scale_ref = refs[-3:]
    rows, dim = q_scale_ref.shape
    share = q_gain_ref.shape[0] // peers
    count = pl.num_programs(0)
    step = pl.program_id(0)

    @pl.when(step == 0)
    def _():
        scales = lax.rsqrt((squares_ref[...] + more_ref[...]) / width_all + epsilon)
        q_scale_ref[...] = jnp.transpose(jnp.broadcast_to(scales[0:1] * fold, (dim, rows)))
        k_scale_ref[...] = jnp.transpose(jnp.broadcast_to(scales[1:2], (dim, rows)))
        aux_ref[...] = jnp.zeros_like(aux_ref)

    def normed(ref, c, scale_ref, gain_ref, head, some):
        gain = gain_ref[pl.ds(c * share + head, 1), :]
        scaled = ref[c, 0, 0:some].astype(jnp.float32) * scale_ref[0:some] * gain
        return scaled.astype(jnp.bfloat16)

    for p in range(peers):
        c = place_ref[0] ^ p
        outs[p][0, 0:rows, :] = normed(q_ref, c, q_scale_ref, q_gain_ref, first + step, rows)
        outs[p][0, rows : 2 * rows, :] = normed(
            k_ref, c, k_scale_ref, k_gain_ref, first + step, rows
        )
        at = 2 * rows
        for i in range(0, rows, 128):
            outs[p][0, at + i : at + i + 128, :] = jnp.transpose(v_ref[c, 0, i : i + 128, :])
        at = 0
        for rate_ref in (rate_in_ref, rate_out_ref):
            rate = rate_ref[pl.ds(c * share + first + step, 1), :]
            high = rate.astype(jnp.bfloat16).astype(jnp.float32)
            for part in (high, rate - high):
                for i in range(0, rows, 128):
                    aux_ref[at : at + 1, :] = part[:, i : i + 128]
                    at += 1
        if with_lone:
            for i in range(len(lone) // 3):
                head = jnp.minimum(step + i * count, share - 1)
                q0 = normed(lone[3 * i], c, q_scale_ref, q_gain_ref, head, 16)
                k0 = normed(lone[3 * i + 1], c, k_scale_ref, k_gain_ref, head, 16)
                for at, array in enumerate((q0, k0, lone[3 * i + 2][c, 0])):
                    at += aux_ref.shape[0] // 2 + 3 * i
                    aux_ref[at : at + 1, :] = array.astype(jnp.float32)[0:1]
        outs[p][0, 3 * rows :, :] = aux_ref[0 : outs[p].shape[1] - 3 * rows, :].astype(
            jnp.bfloat16
        )


def pack(place, sums, q, k, v, gains, rates, peers, aux_rows, first, count, width_all, fold):
    heads, rows, dim = q.shape
    share = heads // peers
    out_shape = (count, 3 * rows + aux_rows // (2 if first else 1), dim)
    whole = [*sums, *gains, *rates]
    q, k, v = [x.reshape(peers, share, rows, dim) for x in (q, k, v)]
    operands = [*whole, q, k, v]
    here = pl.BlockSpec((peers, 1, rows, dim), lambda j, place: (0, first + j, 0, 0))
    in_specs = [pl.BlockSpec(a.shape, lambda j, place: (0, 0)) for a in whole] + [here] * 3
    if not first:
        for i in range(-(-share // count)):
            operands += [q, k, v]
            in_specs += [
                pl.BlockSpec(
                    (peers, 1, 16, dim),
                    lambda j, place, i=i: (0, jnp.minimum(j + i * count, share - 1), 0, 0),
                )
            ] * 3
    return pl.pallas_call(
        functools.partial(pack_kernel, peers, first, width_all, fold, not first),
        out_shape=[jax.ShapeDtypeStruct(out_shape, jnp.bfloat16)] * peers,
        grid_spec=pltpu.PrefetchScalarGridSpec(
            num_scalar_prefetch=1,
            grid=(count,),
            in_specs=in_specs,
            out_specs=[pl.BlockSpec((1,) + out_shape[1:], lambda j, place: (j, 0, 0))] * peers,
            scratch_shapes=[
                pltpu.VMEM((aux_rows, dim), jnp.float32),
                pltpu.VMEM((rows, dim), jnp.float32),
                pltpu.VMEM((rows, dim), jnp.float32),
            ],
        ),
        compiler_params=params(),
        cost_estimate=cost(0, 8 * peers * count * rows * dim),
        name="pack",
    )(place, *operands)


def stack_kernel(from_row, *refs):
    for p, ref in enumerate(refs[:-1]):
        refs[-1][p] = ref[:, from_row:, :]


def stacked(arrays, from_row):
    heads, rows, dim = arrays[0].shape
    return pl.pallas_call(
        functools.partial(stack_kernel, from_row),
        out_shape=jax.ShapeDtypeStruct((len(arrays), heads, rows - from_row, dim), jnp.bfloat16),
        in_specs=[pl.BlockSpec(memory_space=pltpu.VMEM)] * len(arrays),
        out_specs=pl.BlockSpec(memory_space=pltpu.VMEM),
        compiler_params=params(),
        cost_estimate=cost(0, 0),
        name="stack",
    )(*arrays)


def lone_kernel(place_ref, own_ref, other_ref, out_ref):
    mine = jnp.full(out_ref.shape, place_ref[1]) == 0
    own, other = own_ref[0].astype(jnp.float32), other_ref[0].astype(jnp.float32)
    out_ref[...] = jnp.where(mine, own, other).astype(jnp.bfloat16)


def lone_rows(place, own_k, other_k, rows):
    peers, count, all_rows, dim = own_k.shape
    extra = (all_rows - 2 * rows) // 2
    block = pl.BlockSpec(
        (1, count, extra, dim), lambda i, place: (place[0], 0, all_rows // extra - 1, 0)
    )
    return pl.pallas_call(
        lone_kernel,
        out_shape=jax.ShapeDtypeStruct((count, extra, dim), jnp.bfloat16),
        grid_spec=pltpu.PrefetchScalarGridSpec(
            num_scalar_prefetch=1,
            grid=(1,),
            in_specs=[block, block],
            out_specs=pl.BlockSpec((count, extra, dim), lambda i, place: (0, 0, 0)),
        ),
        compiler_params=params(),
        cost_estimate=cost(0, 0),
        name="lone_rows",
    )(place, own_k, other_k)


def key_value_blocks(peers, rows, refs):
    for p in range(peers):
        yield p, True, refs[p].at[0, rows : 2 * rows], refs[p].at[0, 2 * rows :]
        yield p, False, refs[peers].at[p, 0, 0:rows], refs[peers].at[p, 0, rows:]


def key_value_operands(packets):
    own, other = packets

    def single(array):
        return pl.BlockSpec((1,) + array.shape[1:], lambda j, *_: (j, 0, 0))

    return [*own, other], [single(a) for a in own] + [by_head(other.shape)]


def grads_kernel(peers, rows, rate_rows, place_ref, in_ref, out_ref, *refs):
    grad_ref = refs[-1]
    hid = out_ref.shape[1]
    part = hid // 2
    core = place_ref[1]
    own = pl.multiple_of(core * part, part)
    in_half = jnp.concatenate(
        [
            jnp.transpose(in_ref[0, :, pl.ds(at, part)].astype(jnp.float32))
            for at in (own, pl.multiple_of(hid + own, part))
        ],
        axis=0,
    ).astype(jnp.bfloat16)
    out_half = out_ref[0, pl.ds(own, part), :]
    sum_in = jnp.zeros((2 * part, in_half.shape[1]), jnp.float32)
    sum_out = jnp.zeros((part, in_half.shape[1]), jnp.float32)
    for _, _, keys, values in key_value_blocks(peers, rows, refs):
        k = keys[...].astype(jnp.float32)
        v_t = jnp.concatenate([values[at : at + 128, :] for at in range(0, rows, 128)], axis=1)
        aux = values[rows : rows + 16, :].astype(jnp.float32)

        def rate(at):
            both = aux[at : at + rate_rows] + aux[at + rate_rows : at + 2 * rate_rows]
            return jnp.concatenate([both[i : i + 1] for i in range(rate_rows)], axis=1)

        rate_in, rate_out = rate(0), rate(2 * rate_rows)
        unit = (k * lax.rsqrt(jnp.sum(k * k, axis=1, keepdims=True) + epsilon)).astype(
            jnp.bfloat16
        )
        pre = nt_dot(in_half, unit)
        gate, lin = pre[:part], pre[part:]
        sig = jax.nn.sigmoid(gate)
        swish = gate * sig
        pushed = (swish * lin * -rate_out).astype(jnp.bfloat16)
        hidden_grad = nn_dot(out_half, v_t) * -rate_in
        d_gate = hidden_grad * lin * sig * (1.0 + gate * (1.0 - sig))
        d_lin = hidden_grad * swish
        d_pre = jnp.concatenate([d_gate, d_lin], axis=0).astype(jnp.bfloat16)
        sum_in += nn_dot(d_pre, unit)
        sum_out += nt_dot(pushed, v_t)
    grad_ref[0, 0 : 2 * part, :] = sum_in.astype(jnp.bfloat16)
    grad_ref[0, 2 * part :, :] = sum_out.astype(jnp.bfloat16)


def chip_weights(array, share, first):
    return pl.BlockSpec(
        (1,) + array.shape[1:], lambda j, place, *_: (place[0] * share + first + j, 0, 0)
    )


def by_head(shape):
    return pl.BlockSpec((shape[0], 1) + shape[2:], lambda j, *_: (0, j, 0, 0))


def gradients(place, fast_in, fast_out, packets, share, rows, first, after):
    _, hid, dim = fast_out.shape
    peers = len(packets[0])
    heads = packets[0][0].shape[0]
    grad_shape = (heads, 3 * hid // 2, dim)
    blocks, block_specs = key_value_operands(packets)
    return pl.pallas_call(
        functools.partial(grads_kernel, peers, rows, rows // 128),
        out_shape=jax.ShapeDtypeStruct(grad_shape, jnp.bfloat16),
        grid_spec=pltpu.PrefetchScalarGridSpec(
            num_scalar_prefetch=1,
            grid=(heads,),
            in_specs=[chip_weights(a, share, first) for a in (fast_in, fast_out)]
            + block_specs
            + untouched(after),
            out_specs=pl.BlockSpec((1,) + grad_shape[1:], lambda j, place: (j, 0, 0)),
        ),
        compiler_params=params(),
        cost_estimate=cost(0, 0),
        name="gradients",
    )(place, fast_in, fast_out, *blocks, *after)


def attend_kernel(peers, rows, share, first, fwd_heads, place_ref, window_ref, edge_ref, *refs):
    fwd_ref = refs[peers + 1]
    out_ref, extra_ref, k_scr, vt_scr, q_scr = refs[-5:]
    span = 2 * peers * rows
    dim = k_scr.shape[1]
    pad = fwd_ref.shape[1]
    chip, core, half = place_ref[0], place_ref[1], place_ref[2]
    base = half * span
    limit = span + 1 - half
    step = pl.program_id(0)
    window = window_ref[chip * share + first + step]

    @pl.when(step == 0)
    def _():
        k_scr[span:, :] = jnp.zeros((k_scr.shape[0] - span, dim), k_scr.dtype)
        vt_scr[:, span:] = jnp.zeros((vt_scr.shape[0], vt_scr.shape[1] - span), vt_scr.dtype)
        vt_scr[dim:, :] = jnp.ones((vt_scr.shape[0] - dim, vt_scr.shape[1]), vt_scr.dtype)

    for p, own, keys, values in key_value_blocks(peers, rows, refs):
        at = pl.multiple_of(((chip ^ p) * 2 + (core if own else 1 - core)) * rows, rows)
        k_scr[pl.ds(at, rows), :] = keys[...]
        for i in range(0, rows, 128):
            vt_scr[0:dim, pl.ds(pl.multiple_of(at + i, 128), 128)] = values[i : i + 128, :]
    for p in range(peers):
        q_scr[chip ^ p] = refs[p][0, 0:rows, :]
    fwd = fwd_ref[0].astype(jnp.float32)
    turn = (first + step) // fwd_heads
    q_lone, k_lone, v_lone = (
        sum(
            jnp.where(turn == t, fwd[3 * t + i : 3 * t + i + 1], 0.0)
            for t in range(-(-share // fwd_heads))
        )
        for i in range(3)
    )
    k_scr[span : span + pad, :] = jnp.broadcast_to(k_lone, (pad, dim)).astype(jnp.bfloat16)
    vt_scr[0:dim, span : span + 128] = jnp.transpose(
        jnp.broadcast_to(v_lone, (128, dim))
    ).astype(jnp.bfloat16)

    def clip_start(place):
        start = jnp.zeros_like(place)
        for i in range(edge_ref.shape[0]):
            start = jnp.maximum(start, jnp.where(edge_ref[i] <= place, edge_ref[i], 0))
        return start

    def clip_stop(place):
        stop = jnp.full_like(place, base + limit)
        for i in range(edge_ref.shape[0]):
            stop = jnp.minimum(stop, jnp.where(edge_ref[i] > place, edge_ref[i], base + limit))
        return stop

    def lowest(place):
        return jnp.maximum(jnp.maximum(place - window, clip_start(place)), base) - base

    def highest(place):
        return jnp.minimum(place + window, clip_stop(place) - 1) - base

    def one_pair(i, carry):
        pair = []
        for c in (i, peers - 1 - i):
            start = (c * 2 + core) * rows
            place = base + start + lax.broadcasted_iota(jnp.int32, (1, rows), 1)
            from_key = lowest(base + start) // 128 * 128
            count = (highest(base + start + rows - 1) - from_key) // 256 + 1
            pair.append((c, lowest(place), highest(place), from_key, count))
        count = jnp.maximum(pair[0][4], pair[1][4])

        def variant(chunks):
            width = chunks * 256
            key = lax.broadcasted_iota(jnp.int32, (width, rows), 0)
            froms = [
                pl.multiple_of(jnp.minimum(each[3], k_scr.shape[0] - width), 128) for each in pair
            ]
            scores = [
                nt_dot(k_scr[pl.ds(at, width), :], q_scr[each[0]])
                for each, at in zip(pair, froms)
            ]
            scores = [
                jnp.where((key >= each[1] - at) & (key <= each[2] - at), one, HIDDEN_MASK)
                for each, at, one in zip(pair, froms, scores)
            ]
            weights = [
                jnp.exp2(one - jnp.max(one, axis=0, keepdims=True)).astype(jnp.bfloat16)
                for one in scores
            ]
            totals = [
                nn_dot(vt_scr[:, pl.ds(at, width)], one) for at, one in zip(froms, weights)
            ]
            for each, total in zip(pair, totals):
                attended = total[0:dim] * (1.0 / total[dim : dim + 1])
                out_ref[each[0], 0] = jnp.transpose(attended)

        for chunks in range(1, span // 256 + 2):

            @pl.when(count == chunks)
            def _(chunks=chunks):
                variant(chunks)

        return carry

    lax.fori_loop(0, peers // 2, one_pair, 0)
    extra_ref[0] = jnp.zeros(extra_ref.shape[1:], jnp.float32)

    @pl.when((half == 0) & (core == 1))
    def _():
        near = span - HALF
        width = HALF + 128
        q = jnp.broadcast_to(q_lone, (pad, dim)).astype(jnp.bfloat16)
        scores = nt_dot(q, k_scr[near : near + width, :])
        key = near + lax.broadcasted_iota(jnp.int32, (1, width), 1)
        scores = jnp.where((key >= span - window) & (key <= span), scores, HIDDEN_MASK)
        top = jnp.max(scores, axis=1, keepdims=True)
        weights = jnp.exp2(scores - top).astype(jnp.bfloat16)
        total = nt_dot(weights, vt_scr[:, near : near + width])
        extra_ref[0] = total[:, 0:dim] / total[:, dim : dim + 1]


def attend(place, half_window, boundaries, packets, forwarded, share, rows, first, after):
    peers = len(packets[0])
    heads = packets[0][0].shape[0]
    fwd_heads, pad, dim = forwarded.shape
    scr_rows = 2 * peers * rows + 256
    out_shapes = [(peers, heads, rows, dim), (heads, pad, dim)]
    one_head = pl.BlockSpec((1, pad, dim), lambda j, *_: (j, 0, 0))
    lone = pl.BlockSpec((1, pad, dim), lambda j, *_: (lax.rem(first + j, fwd_heads), 0, 0))
    blocks, block_specs = key_value_operands(packets)
    return pl.pallas_call(
        functools.partial(attend_kernel, peers, rows, share, first, fwd_heads),
        out_shape=[jax.ShapeDtypeStruct(shape, jnp.float32) for shape in out_shapes],
        grid_spec=pltpu.PrefetchScalarGridSpec(
            num_scalar_prefetch=3,
            grid=(heads,),
            in_specs=block_specs + [lone] + untouched(after),
            out_specs=[by_head(out_shapes[0]), one_head],
            scratch_shapes=[
                pltpu.VMEM((scr_rows, dim), jnp.bfloat16),
                pltpu.VMEM((dim + 16, scr_rows), jnp.bfloat16),
                pltpu.VMEM((peers, rows, dim), jnp.bfloat16),
            ],
        ),
        compiler_params=params(),
        cost_estimate=cost(4 * heads * peers * rows * HALF * 2 * dim, 0),
        name="attend",
    )(place, half_window, boundaries, *blocks, forwarded, *after)


def finish_kernel(peers, unit_epsilon, place_ref, *refs):
    att_ref, base_in_ref, base_out_ref, own_ref, other_ref, patch_ref = refs[:6]
    queries = refs[6 : 6 + peers]
    outs = refs[-2 - peers : -2]
    grad_in_scr, grad_out_scr = refs[-2:]
    chip, core, half = place_ref[0], place_ref[1], place_ref[2]
    rows = att_ref.shape[2]
    hid = base_out_ref.shape[1]
    part = hid // 2
    for summed, lane in ((own_ref, core), (other_ref, 1 - core)):
        at = pl.multiple_of(lane * part, part)
        grad_in_scr[pl.ds(at, part), :] = summed[0, 0:part, :].astype(jnp.float32)
        grad_in_scr[pl.ds(hid + at, part), :] = summed[0, part : 2 * part, :].astype(jnp.float32)
        grad_out_scr[pl.ds(at, part), :] = summed[0, 2 * part :, :].astype(jnp.float32)

    def renewed(base, grad):
        base = base.astype(jnp.float32)
        updated = base - grad
        norm = jnp.sqrt(jnp.sum(base * base, axis=0, keepdims=True))
        squares = jnp.sum(updated * updated, axis=0, keepdims=True)
        return (updated * (norm / jnp.sqrt(squares + epsilon))).astype(jnp.bfloat16)

    new_in = renewed(base_in_ref[0], jnp.transpose(grad_in_scr[...]))
    new_out = renewed(base_out_ref[0], grad_out_scr[...])
    patch = patch_ref[0][0:1, :]
    row = lax.broadcasted_iota(jnp.int32, (rows, 1), 0)
    for p in range(peers):
        q = queries[p][0].astype(jnp.float32)
        unit = (q * lax.rsqrt(jnp.sum(q * q, axis=1, keepdims=True) + unit_epsilon)).astype(
            jnp.bfloat16
        )
        pre = nn_dot(unit, new_in)
        gate = pre[:, :hid]
        hidden = (gate * jax.nn.sigmoid(gate) * pre[:, hid:]).astype(jnp.bfloat16)
        patched = (half == 1) & (core == 0) & (chip == p)
        attended = jnp.where(patched & (row == 0), patch, att_ref[chip ^ p, 0])
        outs[p][0] = (attended + nn_dot(hidden, new_out)).astype(jnp.bfloat16)


def finish(place, attended, fast_in, fast_out, sums, patch, own, share, first, unit_epsilon, after):
    peers, heads, rows, dim = attended.shape
    hid = fast_out.shape[1]

    def plain(shape):
        return pl.BlockSpec((1,) + shape[1:], lambda j, place: (j, 0, 0))

    out_shape = (heads, rows, dim)
    in_specs = [by_head(attended.shape)]
    in_specs += [chip_weights(a, share, first) for a in (fast_in, fast_out)]
    in_specs += [plain(a.shape) for a in (*sums, patch)]
    in_specs += [plain(out_shape)] * peers + untouched(after)
    return pl.pallas_call(
        functools.partial(finish_kernel, peers, unit_epsilon),
        out_shape=[jax.ShapeDtypeStruct(out_shape, jnp.bfloat16)] * peers,
        grid_spec=pltpu.PrefetchScalarGridSpec(
            num_scalar_prefetch=1,
            grid=(heads,),
            in_specs=in_specs,
            out_specs=[plain(out_shape)] * peers,
            scratch_shapes=[
                pltpu.VMEM((2 * hid, dim), jnp.float32),
                pltpu.VMEM((hid, dim), jnp.float32),
            ],
        ),
        compiler_params=params(),
        cost_estimate=cost(12 * heads * peers * rows * hid * dim, 0),
        name="finish",
    )(place, attended, fast_in, fast_out, *sums, patch, *own, *after)


def place_kernel(peers, chunks, share, place_ref, *refs):
    pieces, out_ref, sems = refs[:-2], refs[-2], refs[-1]
    copies = []
    for first, heads in chunks:
        for p in range(peers):
            at = (place_ref[0] ^ p) * share + first
            i = len(copies)
            copies.append(
                pltpu.make_async_copy(pieces[i], out_ref.at[pl.ds(at, heads)], sems.at[i])
            )
    for copy in copies:
        copy.start()
    for copy in copies:
        copy.wait()


def put_in_place(place, pieces, peers, chunks, share):
    _, rows, dim = pieces[0].shape
    return pl.pallas_call(
        functools.partial(place_kernel, peers, chunks, share),
        out_shape=jax.ShapeDtypeStruct((peers * share, rows, dim), jnp.bfloat16),
        in_specs=[pl.BlockSpec(memory_space=pltpu.SMEM)]
        + [pl.BlockSpec(memory_space=pltpu.VMEM)] * len(pieces),
        out_specs=pl.BlockSpec(memory_space=pl.ANY),
        scratch_shapes=[pltpu.SemaphoreType.DMA((len(pieces),))],
        compiler_params=params(),
        name="put_in_place",
    )(place, *pieces)


def regrouping(tok_peers, rows, heads, dim, hid):
    half_peers = tok_peers // 2
    peers = math.gcd(half_peers, heads)
    fits = tok_peers % 2 == 0 and half_peers * rows == 2 * HALF
    fits = fits and half_peers == 2 * peers and peers & (peers - 1) == 0
    fits = fits and rows % 256 == 0 and dim == 128 and hid % 256 == 0
    return peers if fits else 0


def regrouped_body(
    peers,
    query_rows,
    key_rows,
    value_rows,
    query_gain,
    key_gain,
    rate_in,
    rate_out,
    fast_in,
    fast_out,
    half_window,
    boundaries,
):
    rows, heads, dim = query_rows.shape
    share = heads // peers
    tok_peers = lax.axis_size("tok")
    half_peers = tok_peers // 2
    width_all = heads * dim * lax.axis_size("head")
    chunks = [(0, (share + 1) // 2), ((share + 1) // 2, share // 2)]
    aux_rows = 2 * -(-max(4 * (rows // 128), 3 * -(-share // chunks[0][1])) // 16) * 16
    own_index = lax.axis_index("tok")
    half = own_index // half_peers
    chip = own_index % half_peers // 2
    core = own_index % 2
    place = jnp.stack([chip, core, half]).astype(jnp.int32)

    def dealt(sent):
        pairs = [
            [(t, t // half_peers * half_peers + ((t % half_peers) ^ (2 * p))) for t in range(tok_peers)]
            for p in range(peers)
        ]
        return [sent[0]] + [exchanged(sent[p], pairs[p]) for p in range(1, peers)]

    core_pairs = [(t, t ^ 1) for t in range(tok_peers)]
    half_pairs = [(t, (t + half_peers) % tok_peers) for t in range(tok_peers)]
    forward_pairs = [(t + half_peers, t) for t in range(half_peers)]
    back_pairs = [(t, t - 1 + half_peers) for t in range(half_peers) if t % 2 == 1]

    q = jnp.transpose(query_rows, (1, 0, 2))
    k = jnp.transpose(key_rows, (1, 0, 2))
    v = jnp.transpose(value_rows, (1, 0, 2))
    q_float = q.astype(jnp.float32)
    k_float = k.astype(jnp.float32)
    squares = jnp.stack(
        [jnp.sum(q_float * q_float, axis=(0, 2)), jnp.sum(k_float * k_float, axis=(0, 2))]
    )
    if lax.axis_size("head") == 2:
        sums = (squares, lax.ppermute(squares, "head", [(0, 1), (1, 0)]))
    else:
        sums = (lax.psum(squares, "head"), jnp.zeros_like(squares))
    fold = math.log2(math.e) / math.sqrt(dim)
    sent = [
        pack(
            place,
            sums,
            q,
            k,
            v,
            (query_gain, key_gain),
            (rate_in, rate_out),
            peers,
            aux_rows,
            first,
            count,
            width_all,
            fold,
        )
        for first, count in chunks
    ]
    received = []
    for each in sent:
        if received:
            each = [lax.optimization_barrier(pair)[0] for pair in zip(each, received[-1])]
        received.append(dealt(each))
    def finished(ready, after):
        attended, sums, patch, own, first = ready
        return finish(
            place,
            attended,
            fast_in,
            fast_out,
            sums,
            patch,
            own,
            share,
            first,
            epsilon * fold * fold,
            after,
        )

    forwarded = ready = None
    pieces = []
    for (first, count), own in zip(chunks, received):
        if ready:
            *own, _ = lax.optimization_barrier((*own, grad))
        else:
            own = lax.optimization_barrier((*own, *sent[-1]))[:peers]
        stack = stacked(own, rows)
        packets = (own, exchanged(stack, core_pairs))
        if forwarded is None:
            forwarded = exchanged(lone_rows(place, stack, packets[1], rows), forward_pairs)
        before = [ready[0]] if ready else []
        grad = gradients(place, fast_in, fast_out, packets, share, rows, first, before)
        from_half = exchanged(grad, half_pairs)
        before = [grad]
        if ready:
            outs = finished(ready, [grad])
            before.append(outs[0])
            pieces = pieces + dealt(outs)
        attended, extra = attend(
            place,
            half_window,
            boundaries,
            packets,
            forwarded,
            share,
            rows,
            first,
            before,
        )
        patch = exchanged(extra, back_pairs)
        from_half, _ = lax.optimization_barrier((from_half, attended))
        own_sum = (grad.astype(jnp.float32) + from_half.astype(jnp.float32)).astype(jnp.bfloat16)
        ready = (attended, (own_sum, exchanged(own_sum, core_pairs)), patch, own, first)
    pieces = pieces + dealt(finished(ready, pieces))
    whole = put_in_place(place, pieces, peers, chunks, share)
    return jnp.transpose(whole, (1, 0, 2))


def body(query_rows, *others):
    rows, heads, dim = query_rows.shape
    hid = others[7].shape[1]
    peers = regrouping(lax.axis_size("tok"), rows, heads, dim, hid)
    if peers:
        return regrouped_body(peers, query_rows, *others)
    return sliding_body(query_rows, *others)


def solution(mesh):
    in_specs = (
        P("tok", "head", None),
        P("tok", "head", None),
        P("tok", "head", None),
        P("head", None),
        P("head", None),
        P("head", "tok"),
        P("head", "tok"),
        P("head", None, None),
        P("head", None, None),
        P("head"),
        P(),
    )
    out_specs = P("tok", "head", None)
    return jax.shard_map(body, mesh=mesh, in_specs=in_specs, out_specs=out_specs, check_vma=False)
```

```python
import functools
import math

import jax
import jax.numpy as jnp
from jax import lax
from jax.experimental import pallas as pl
from jax.experimental.pallas import tpu as pltpu
from jax.sharding import PartitionSpec as P

HALF = 1024


epsilon = 1e-06


def passed_along(x, axis, by):
    peers = lax.axis_size(axis)
    pairs = [(i, i + by) for i in range(peers) if 0 <= i + by < peers]
    return lax.ppermute(x, axis, pairs)


def unit_rows(matrix):
    as_float = matrix.astype(jnp.float32)
    return (
        as_float * lax.rsqrt(jnp.sum(as_float * as_float, axis=-1, keepdims=True) + epsilon)
    ).astype(jnp.bfloat16)


def rescale(updated, base_norm, squares):
    return (updated * (base_norm / jnp.sqrt(squares + epsilon))[:, None, :]).astype(jnp.bfloat16)


def sliding_body(
    query_rows,
    key_rows,
    value_rows,
    query_gain,
    key_gain,
    rate_in,
    rate_out,
    fast_in,
    fast_out,
    half_window,
    boundaries,
):
    tok_rows = query_rows.shape[0]
    local_heads = query_rows.shape[1]
    head_dim = query_rows.shape[2]
    fast_hid = fast_out.shape[1]
    width_all = local_heads * head_dim * lax.axis_size("head")
    tok_count = tok_rows * lax.axis_size("tok")
    own_index = lax.axis_index("tok")
    first_row = own_index * tok_rows
    query_float = query_rows.astype(jnp.float32)
    key_float = key_rows.astype(jnp.float32)
    query_sq, key_sq = lax.psum(
        (
            jnp.sum(query_float * query_float, axis=(1, 2)),
            jnp.sum(key_float * key_float, axis=(1, 2)),
        ),
        "head",
    )
    q_normed = (
        query_float * lax.rsqrt(query_sq / width_all + epsilon)[:, None, None] * query_gain[None]
    ).astype(jnp.bfloat16)
    k_normed = (
        key_float * lax.rsqrt(key_sq / width_all + epsilon)[:, None, None] * key_gain[None]
    ).astype(jnp.bfloat16)

    def clip_of(places):
        return jnp.sum((places[:, None] >= boundaries[None, :]).astype(jnp.int32), axis=1)

    positions = first_row + jnp.arange(tok_rows, dtype=jnp.int32)
    query_clip = clip_of(positions)
    scaling = 1.0 / math.sqrt(head_dim)

    def absorb(state_now, block_keys, block_values, key_first):
        best, denominator, accum = state_now
        key_places = key_first + jnp.arange(tok_rows, dtype=jnp.int32)
        scores = (
            jnp.einsum("qhd,khd->hqk", q_normed, block_keys, preferred_element_type=jnp.float32)
            * scaling
        )
        inside = (key_places >= 0) & (key_places < tok_count)
        pair_ok = (query_clip[:, None] == clip_of(key_places)[None, :]) & inside[None, :]
        distance = jnp.abs(positions[:, None] - key_places[None, :])
        allowed = (distance[None, :, :] <= half_window[:, None, None]) & pair_ok[None, :, :]
        masked = jnp.where(allowed, scores, -jnp.inf)
        new_best = jnp.maximum(best, jnp.max(masked, axis=2))
        weights = jnp.exp(masked - new_best[:, :, None])
        shrink = jnp.exp(best - new_best)
        denominator = denominator * shrink + jnp.sum(weights, axis=2)
        accum = accum * shrink[:, :, None] + jnp.einsum(
            "hqk,khd->hqd",
            weights.astype(jnp.bfloat16),
            block_values,
            preferred_element_type=jnp.float32,
        )
        return (new_best, denominator, accum)

    start_state = (
        jnp.full((local_heads, tok_rows), -jnp.inf, jnp.float32),
        jnp.zeros((local_heads, tok_rows), jnp.float32),
        jnp.zeros((local_heads, tok_rows, head_dim), jnp.float32),
    )
    state_now = absorb(start_state, k_normed, value_rows, first_row)
    reach_blocks = HALF // tok_rows
    for distance_step in range(1, reach_blocks + 1):
        left_keys, left_values = passed_along((k_normed, value_rows), "tok", distance_step)
        state_now = absorb(state_now, left_keys, left_values, first_row - distance_step * tok_rows)
        right_keys, right_values = passed_along((k_normed, value_rows), "tok", -distance_step)
        state_now = absorb(
            state_now, right_keys, right_values, first_row + distance_step * tok_rows
        )
    attended = state_now[2] / state_now[1][:, :, None]
    key_unit = unit_rows(k_normed)
    query_unit = unit_rows(q_normed)
    pre_keys = jnp.einsum("thd,hdf->htf", key_unit, fast_in, preferred_element_type=jnp.float32)
    gate_part = pre_keys[:, :, :fast_hid]
    lin_part = pre_keys[:, :, fast_hid:]
    sigmoid_gate = jax.nn.sigmoid(gate_part)
    swish_gate = gate_part * sigmoid_gate
    hidden = (swish_gate * lin_part).astype(jnp.bfloat16)
    value_float = value_rows.astype(jnp.float32)
    push_out = (-jnp.transpose(rate_out)[:, :, None] * value_float).astype(jnp.bfloat16)
    push_in = (-jnp.transpose(rate_in)[:, :, None] * value_float).astype(jnp.bfloat16)
    grad_out = jnp.einsum("htf,thd->hfd", hidden, push_out, preferred_element_type=jnp.float32)
    hidden_grad = jnp.einsum("thd,hfd->htf", push_in, fast_out, preferred_element_type=jnp.float32)
    d_gate = hidden_grad * lin_part * sigmoid_gate * (1.0 + gate_part * (1.0 - sigmoid_gate))
    d_lin = hidden_grad * swish_gate
    d_pre = jnp.concatenate([d_gate, d_lin], axis=2).astype(jnp.bfloat16)
    grad_in = jnp.einsum("thd,htf->hdf", key_unit, d_pre, preferred_element_type=jnp.float32)
    in_float = fast_in.astype(jnp.float32)
    out_float = fast_out.astype(jnp.float32)
    in_base = jnp.sqrt(jnp.sum(in_float * in_float, axis=1))
    out_base = jnp.sqrt(jnp.sum(out_float * out_float, axis=1))
    summed_in, summed_out = lax.psum((grad_in, grad_out), "tok")
    updated_in = in_float - summed_in
    updated_out = out_float - summed_out
    new_in = rescale(updated_in, in_base, jnp.sum(updated_in * updated_in, axis=1))
    new_out = rescale(updated_out, out_base, jnp.sum(updated_out * updated_out, axis=1))
    pre_query = jnp.einsum("thd,hdf->htf", query_unit, new_in, preferred_element_type=jnp.float32)
    query_gate = pre_query[:, :, :fast_hid]
    query_hidden = (query_gate * jax.nn.sigmoid(query_gate) * pre_query[:, :, fast_hid:]).astype(
        jnp.bfloat16
    )
    fast_result = jnp.einsum(
        "htf,hfd->htd", query_hidden, new_out, preferred_element_type=jnp.float32
    )
    combined = attended + fast_result
    return jnp.transpose(combined, (1, 0, 2)).astype(jnp.bfloat16)


VMEM_BYTES = 16 * 1024 * 1024
HIDDEN_MASK = -1e30
NT = (((1,), (1,)), ((), ()))


def exchanged(x, pairs):
    return lax.ppermute(x, "tok", pairs)


def nt_dot(a, b):
    return lax.dot_general(a, b, NT, preferred_element_type=jnp.float32)


def nn_dot(a, b):
    return jnp.dot(a, b, preferred_element_type=jnp.float32)


def params():
    return pltpu.CompilerParams(vmem_limit_bytes=VMEM_BYTES)


def cost(flops, nbytes):
    return pl.CostEstimate(flops=int(16 * flops), bytes_accessed=int(nbytes), transcendentals=0)


def untouched(arrays):
    return [pl.BlockSpec(memory_space=pl.ANY)] * len(arrays)


def pack_kernel(peers, first, width_all, fold, with_lone, place_ref, *refs):
    squares_ref, more_ref, q_gain_ref, k_gain_ref, rate_in_ref, rate_out_ref = refs[:6]
    q_ref, k_ref, v_ref = refs[6:9]
    outs = refs[-3 - peers : -3]
    lone = refs[9 : -3 - peers]
    aux_ref, q_scale_ref, k_scale_ref = refs[-3:]
    rows, dim = q_scale_ref.shape
    share = q_gain_ref.shape[0] // peers
    count = pl.num_programs(0)
    step = pl.program_id(0)

    @pl.when(step == 0)
    def _():
        scales = lax.rsqrt((squares_ref[...] + more_ref[...]) / width_all + epsilon)
        q_scale_ref[...] = jnp.transpose(jnp.broadcast_to(scales[0:1] * fold, (dim, rows)))
        k_scale_ref[...] = jnp.transpose(jnp.broadcast_to(scales[1:2], (dim, rows)))
        aux_ref[...] = jnp.zeros_like(aux_ref)

    def normed(ref, c, scale_ref, gain_ref, head, some):
        gain = gain_ref[pl.ds(c * share + head, 1), :]
        scaled = ref[c, 0, 0:some].astype(jnp.float32) * scale_ref[0:some] * gain
        return scaled.astype(jnp.bfloat16)

    for p in range(peers):
        c = place_ref[0] ^ p
        outs[p][0, 0:rows, :] = normed(q_ref, c, q_scale_ref, q_gain_ref, first + step, rows)
        outs[p][0, rows : 2 * rows, :] = normed(
            k_ref, c, k_scale_ref, k_gain_ref, first + step, rows
        )
        at = 2 * rows
        for i in range(0, rows, 128):
            outs[p][0, at + i : at + i + 128, :] = jnp.transpose(v_ref[c, 0, i : i + 128, :])
        at = 0
        for rate_ref in (rate_in_ref, rate_out_ref):
            rate = rate_ref[pl.ds(c * share + first + step, 1), :]
            high = rate.astype(jnp.bfloat16).astype(jnp.float32)
            for part in (high, rate - high):
                for i in range(0, rows, 128):
                    aux_ref[at : at + 1, :] = part[:, i : i + 128]
                    at += 1
        if with_lone:
            for i in range(len(lone) // 3):
                head = jnp.minimum(step + i * count, share - 1)
                q0 = normed(lone[3 * i], c, q_scale_ref, q_gain_ref, head, 16)
                k0 = normed(lone[3 * i + 1], c, k_scale_ref, k_gain_ref, head, 16)
                for at, array in enumerate((q0, k0, lone[3 * i + 2][c, 0])):
                    at += aux_ref.shape[0] // 2 + 3 * i
                    aux_ref[at : at + 1, :] = array.astype(jnp.float32)[0:1]
        outs[p][0, 3 * rows :, :] = aux_ref[0 : outs[p].shape[1] - 3 * rows, :].astype(
            jnp.bfloat16
        )


def pack(place, sums, q, k, v, gains, rates, peers, aux_rows, first, count, width_all, fold):
    heads, rows, dim = q.shape
    share = heads // peers
    out_shape = (count, 3 * rows + aux_rows // (2 if first else 1), dim)
    whole = [*sums, *gains, *rates]
    q, k, v = [x.reshape(peers, share, rows, dim) for x in (q, k, v)]
    operands = [*whole, q, k, v]
    here = pl.BlockSpec((peers, 1, rows, dim), lambda j, place: (0, first + j, 0, 0))
    in_specs = [pl.BlockSpec(a.shape, lambda j, place: (0, 0)) for a in whole] + [here] * 3
    if not first:
        for i in range(-(-share // count)):
            operands += [q, k, v]
            in_specs += [
                pl.BlockSpec(
                    (peers, 1, 16, dim),
                    lambda j, place, i=i: (0, jnp.minimum(j + i * count, share - 1), 0, 0),
                )
            ] * 3
    return pl.pallas_call(
        functools.partial(pack_kernel, peers, first, width_all, fold, not first),
        out_shape=[jax.ShapeDtypeStruct(out_shape, jnp.bfloat16)] * peers,
        grid_spec=pltpu.PrefetchScalarGridSpec(
            num_scalar_prefetch=1,
            grid=(count,),
            in_specs=in_specs,
            out_specs=[pl.BlockSpec((1,) + out_shape[1:], lambda j, place: (j, 0, 0))] * peers,
            scratch_shapes=[
                pltpu.VMEM((aux_rows, dim), jnp.float32),
                pltpu.VMEM((rows, dim), jnp.float32),
                pltpu.VMEM((rows, dim), jnp.float32),
            ],
        ),
        compiler_params=params(),
        cost_estimate=cost(0, 8 * peers * count * rows * dim),
        name="pack",
    )(place, *operands)


def stack_kernel(from_row, *refs):
    for p, ref in enumerate(refs[:-1]):
        refs[-1][p] = ref[:, from_row:, :]


def stacked(arrays, from_row):
    heads, rows, dim = arrays[0].shape
    return pl.pallas_call(
        functools.partial(stack_kernel, from_row),
        out_shape=jax.ShapeDtypeStruct((len(arrays), heads, rows - from_row, dim), jnp.bfloat16),
        in_specs=[pl.BlockSpec(memory_space=pltpu.VMEM)] * len(arrays),
        out_specs=pl.BlockSpec(memory_space=pltpu.VMEM),
        compiler_params=params(),
        cost_estimate=cost(0, 0),
        name="stack",
    )(*arrays)


def lone_kernel(place_ref, own_ref, other_ref, out_ref):
    mine = jnp.full(out_ref.shape, place_ref[1]) == 0
    own, other = own_ref[0].astype(jnp.float32), other_ref[0].astype(jnp.float32)
    out_ref[...] = jnp.where(mine, own, other).astype(jnp.bfloat16)


def lone_rows(place, own_k, other_k, rows):
    peers, count, all_rows, dim = own_k.shape
    extra = (all_rows - 2 * rows) // 2
    block = pl.BlockSpec(
        (1, count, extra, dim), lambda i, place: (place[0], 0, all_rows // extra - 1, 0)
    )
    return pl.pallas_call(
        lone_kernel,
        out_shape=jax.ShapeDtypeStruct((count, extra, dim), jnp.bfloat16),
        grid_spec=pltpu.PrefetchScalarGridSpec(
            num_scalar_prefetch=1,
            grid=(1,),
            in_specs=[block, block],
            out_specs=pl.BlockSpec((count, extra, dim), lambda i, place: (0, 0, 0)),
        ),
        compiler_params=params(),
        cost_estimate=cost(0, 0),
        name="lone_rows",
    )(place, own_k, other_k)


def key_value_blocks(peers, rows, refs):
    for p in range(peers):
        yield p, True, refs[p].at[0, rows : 2 * rows], refs[p].at[0, 2 * rows :]
        yield p, False, refs[peers].at[p, 0, 0:rows], refs[peers].at[p, 0, rows:]


def key_value_operands(packets):
    own, other = packets

    def single(array):
        return pl.BlockSpec((1,) + array.shape[1:], lambda j, *_: (j, 0, 0))

    return [*own, other], [single(a) for a in own] + [by_head(other.shape)]


def grads_kernel(peers, rows, rate_rows, place_ref, in_ref, out_ref, *refs):
    grad_ref = refs[-1]
    hid = out_ref.shape[1]
    part = hid // 2
    core = place_ref[1]
    own = pl.multiple_of(core * part, part)
    in_half = jnp.concatenate(
        [
            jnp.transpose(in_ref[0, :, pl.ds(at, part)].astype(jnp.float32))
            for at in (own, pl.multiple_of(hid + own, part))
        ],
        axis=0,
    ).astype(jnp.bfloat16)
    out_half = out_ref[0, pl.ds(own, part), :]
    sum_in = jnp.zeros((2 * part, in_half.shape[1]), jnp.float32)
    sum_out = jnp.zeros((part, in_half.shape[1]), jnp.float32)
    for _, _, keys, values in key_value_blocks(peers, rows, refs):
        k = keys[...].astype(jnp.float32)
        v_t = jnp.concatenate([values[at : at + 128, :] for at in range(0, rows, 128)], axis=1)
        aux = values[rows : rows + 16, :].astype(jnp.float32)

        def rate(at):
            both = aux[at : at + rate_rows] + aux[at + rate_rows : at + 2 * rate_rows]
            return jnp.concatenate([both[i : i + 1] for i in range(rate_rows)], axis=1)

        rate_in, rate_out = rate(0), rate(2 * rate_rows)
        unit = (k * lax.rsqrt(jnp.sum(k * k, axis=1, keepdims=True) + epsilon)).astype(
            jnp.bfloat16
        )
        pre = nt_dot(in_half, unit)
        gate, lin = pre[:part], pre[part:]
        sig = jax.nn.sigmoid(gate)
        swish = gate * sig
        pushed = (swish * lin * -rate_out).astype(jnp.bfloat16)
        hidden_grad = nn_dot(out_half, v_t) * -rate_in
        d_gate = hidden_grad * lin * sig * (1.0 + gate * (1.0 - sig))
        d_lin = hidden_grad * swish
        d_pre = jnp.concatenate([d_gate, d_lin], axis=0).astype(jnp.bfloat16)
        sum_in += nn_dot(d_pre, unit)
        sum_out += nt_dot(pushed, v_t)
    grad_ref[0, 0 : 2 * part, :] = sum_in.astype(jnp.bfloat16)
    grad_ref[0, 2 * part :, :] = sum_out.astype(jnp.bfloat16)


def chip_weights(array, share, first):
    return pl.BlockSpec(
        (1,) + array.shape[1:], lambda j, place, *_: (place[0] * share + first + j, 0, 0)
    )


def by_head(shape):
    return pl.BlockSpec((shape[0], 1) + shape[2:], lambda j, *_: (0, j, 0, 0))


def gradients(place, fast_in, fast_out, packets, share, rows, first, after):
    _, hid, dim = fast_out.shape
    peers = len(packets[0])
    heads = packets[0][0].shape[0]
    grad_shape = (heads, 3 * hid // 2, dim)
    blocks, block_specs = key_value_operands(packets)
    return pl.pallas_call(
        functools.partial(grads_kernel, peers, rows, rows // 128),
        out_shape=jax.ShapeDtypeStruct(grad_shape, jnp.bfloat16),
        grid_spec=pltpu.PrefetchScalarGridSpec(
            num_scalar_prefetch=1,
            grid=(heads,),
            in_specs=[chip_weights(a, share, first) for a in (fast_in, fast_out)]
            + block_specs
            + untouched(after),
            out_specs=pl.BlockSpec((1,) + grad_shape[1:], lambda j, place: (j, 0, 0)),
        ),
        compiler_params=params(),
        cost_estimate=cost(0, 0),
        name="gradients",
    )(place, fast_in, fast_out, *blocks, *after)


def attend_kernel(peers, rows, share, first, fwd_heads, place_ref, window_ref, edge_ref, *refs):
    fwd_ref = refs[peers + 1]
    out_ref, extra_ref, k_scr, vt_scr, q_scr = refs[-5:]
    span = 2 * peers * rows
    dim = k_scr.shape[1]
    pad = fwd_ref.shape[1]
    chip, core, half = place_ref[0], place_ref[1], place_ref[2]
    base = half * span
    limit = span + 1 - half
    step = pl.program_id(0)
    window = window_ref[chip * share + first + step]

    @pl.when(step == 0)
    def _():
        k_scr[span:, :] = jnp.zeros((k_scr.shape[0] - span, dim), k_scr.dtype)
        vt_scr[:, span:] = jnp.zeros((vt_scr.shape[0], vt_scr.shape[1] - span), vt_scr.dtype)
        vt_scr[dim:, :] = jnp.ones((vt_scr.shape[0] - dim, vt_scr.shape[1]), vt_scr.dtype)

    for p, own, keys, values in key_value_blocks(peers, rows, refs):
        at = pl.multiple_of(((chip ^ p) * 2 + (core if own else 1 - core)) * rows, rows)
        k_scr[pl.ds(at, rows), :] = keys[...]
        for i in range(0, rows, 128):
            vt_scr[0:dim, pl.ds(pl.multiple_of(at + i, 128), 128)] = values[i : i + 128, :]
    for p in range(peers):
        q_scr[chip ^ p] = refs[p][0, 0:rows, :]
    fwd = fwd_ref[0].astype(jnp.float32)
    turn = (first + step) // fwd_heads
    q_lone, k_lone, v_lone = (
        sum(
            jnp.where(turn == t, fwd[3 * t + i : 3 * t + i + 1], 0.0)
            for t in range(-(-share // fwd_heads))
        )
        for i in range(3)
    )
    k_scr[span : span + pad, :] = jnp.broadcast_to(k_lone, (pad, dim)).astype(jnp.bfloat16)
    vt_scr[0:dim, span : span + 128] = jnp.transpose(
        jnp.broadcast_to(v_lone, (128, dim))
    ).astype(jnp.bfloat16)

    def clip_start(place):
        start = jnp.zeros_like(place)
        for i in range(edge_ref.shape[0]):
            start = jnp.maximum(start, jnp.where(edge_ref[i] <= place, edge_ref[i], 0))
        return start

    def clip_stop(place):
        stop = jnp.full_like(place, base + limit)
        for i in range(edge_ref.shape[0]):
            stop = jnp.minimum(stop, jnp.where(edge_ref[i] > place, edge_ref[i], base + limit))
        return stop

    def lowest(place):
        return jnp.maximum(jnp.maximum(place - window, clip_start(place)), base) - base

    def highest(place):
        return jnp.minimum(place + window, clip_stop(place) - 1) - base

    def one_pair(i, carry):
        pair = []
        for c in (i, peers - 1 - i):
            start = (c * 2 + core) * rows
            place = base + start + lax.broadcasted_iota(jnp.int32, (1, rows), 1)
            from_key = lowest(base + start) // 128 * 128
            count = (highest(base + start + rows - 1) - from_key) // 256 + 1
            pair.append((c, lowest(place), highest(place), from_key, count))
        count = jnp.maximum(pair[0][4], pair[1][4])

        def variant(chunks):
            froms = [
                pl.multiple_of(jnp.minimum(each[3], k_scr.shape[0] - chunks * 256), 128)
                for each in pair
            ]
            key = lax.broadcasted_iota(jnp.int32, (256, rows), 0)
            scores = [[], []]
            tops = [None, None]
            for i in range(chunks):
                for n, (each, at) in enumerate(zip(pair, froms)):
                    from_key = pl.multiple_of(at + i * 256, 128)
                    piece = nt_dot(k_scr[pl.ds(from_key, 256), :], q_scr[each[0]])
                    seen = (key >= each[1] - from_key) & (key <= each[2] - from_key)
                    piece = jnp.where(seen, piece, HIDDEN_MASK)
                    top = jnp.max(piece.reshape(32, 8, rows), axis=0)
                    tops[n] = top if i == 0 else jnp.maximum(tops[n], top)
                    scores[n].append(piece)
            tops = [jnp.max(top, axis=0, keepdims=True) for top in tops]
            totals = [0.0, 0.0]
            for i in range(chunks):
                for n, at in enumerate(froms):
                    weights = jnp.exp2(scores[n][i] - tops[n]).astype(jnp.bfloat16)
                    from_key = pl.multiple_of(at + i * 256, 128)
                    totals[n] += nn_dot(vt_scr[:, pl.ds(from_key, 256)], weights)
            for each, total in zip(pair, totals):
                attended = total[0:dim] * (1.0 / total[dim : dim + 1])
                out_ref[each[0], 0] = jnp.transpose(attended)

        for chunks in range(1, span // 256 + 2):

            @pl.when(count == chunks)
            def _(chunks=chunks):
                variant(chunks)

        return carry

    lax.fori_loop(0, peers // 2, one_pair, 0)
    extra_ref[0] = jnp.zeros(extra_ref.shape[1:], jnp.float32)

    @pl.when((half == 0) & (core == 1))
    def _():
        near = span - HALF
        width = HALF + 128
        q = jnp.broadcast_to(q_lone, (pad, dim)).astype(jnp.bfloat16)
        scores = nt_dot(q, k_scr[near : near + width, :])
        key = near + lax.broadcasted_iota(jnp.int32, (1, width), 1)
        scores = jnp.where((key >= span - window) & (key <= span), scores, HIDDEN_MASK)
        top = jnp.max(scores, axis=1, keepdims=True)
        weights = jnp.exp2(scores - top).astype(jnp.bfloat16)
        total = nt_dot(weights, vt_scr[:, near : near + width])
        extra_ref[0] = total[:, 0:dim] / total[:, dim : dim + 1]


def attend(place, half_window, boundaries, packets, forwarded, share, rows, first, after):
    peers = len(packets[0])
    heads = packets[0][0].shape[0]
    fwd_heads, pad, dim = forwarded.shape
    scr_rows = 2 * peers * rows + 256
    out_shapes = [(peers, heads, rows, dim), (heads, pad, dim)]
    one_head = pl.BlockSpec((1, pad, dim), lambda j, *_: (j, 0, 0))
    lone = pl.BlockSpec((1, pad, dim), lambda j, *_: (lax.rem(first + j, fwd_heads), 0, 0))
    blocks, block_specs = key_value_operands(packets)
    return pl.pallas_call(
        functools.partial(attend_kernel, peers, rows, share, first, fwd_heads),
        out_shape=[jax.ShapeDtypeStruct(shape, jnp.float32) for shape in out_shapes],
        grid_spec=pltpu.PrefetchScalarGridSpec(
            num_scalar_prefetch=3,
            grid=(heads,),
            in_specs=block_specs + [lone] + untouched(after),
            out_specs=[by_head(out_shapes[0]), one_head],
            scratch_shapes=[
                pltpu.VMEM((scr_rows, dim), jnp.bfloat16),
                pltpu.VMEM((dim + 16, scr_rows), jnp.bfloat16),
                pltpu.VMEM((peers, rows, dim), jnp.bfloat16),
            ],
        ),
        compiler_params=params(),
        cost_estimate=cost(4 * heads * peers * rows * HALF * 2 * dim, 0),
        name="attend",
    )(place, half_window, boundaries, *blocks, forwarded, *after)


def finish_kernel(peers, unit_epsilon, place_ref, *refs):
    att_ref, base_in_ref, base_out_ref, own_ref, other_ref, patch_ref = refs[:6]
    queries = refs[6 : 6 + peers]
    outs = refs[-2 - peers : -2]
    grad_in_scr, grad_out_scr = refs[-2:]
    chip, core, half = place_ref[0], place_ref[1], place_ref[2]
    rows = att_ref.shape[2]
    hid = base_out_ref.shape[1]
    part = hid // 2
    for summed, lane in ((own_ref, core), (other_ref, 1 - core)):
        at = pl.multiple_of(lane * part, part)
        grad_in_scr[pl.ds(at, part), :] = summed[0, 0:part, :].astype(jnp.float32)
        grad_in_scr[pl.ds(hid + at, part), :] = summed[0, part : 2 * part, :].astype(jnp.float32)
        grad_out_scr[pl.ds(at, part), :] = summed[0, 2 * part :, :].astype(jnp.float32)

    def renewed(base, grad):
        base = base.astype(jnp.float32)
        updated = base - grad
        norm = jnp.sqrt(jnp.sum(base * base, axis=0, keepdims=True))
        squares = jnp.sum(updated * updated, axis=0, keepdims=True)
        return (updated * (norm / jnp.sqrt(squares + epsilon))).astype(jnp.bfloat16)

    new_in = renewed(base_in_ref[0], jnp.transpose(grad_in_scr[...]))
    new_out = renewed(base_out_ref[0], grad_out_scr[...])
    patch = patch_ref[0][0:1, :]
    row = lax.broadcasted_iota(jnp.int32, (rows, 1), 0)
    for p in range(peers):
        q = queries[p][0].astype(jnp.float32)
        unit = (q * lax.rsqrt(jnp.sum(q * q, axis=1, keepdims=True) + unit_epsilon)).astype(
            jnp.bfloat16
        )
        pre = nn_dot(unit, new_in)
        gate = pre[:, :hid]
        hidden = (gate * jax.nn.sigmoid(gate) * pre[:, hid:]).astype(jnp.bfloat16)
        patched = (half == 1) & (core == 0) & (chip == p)
        attended = jnp.where(patched & (row == 0), patch, att_ref[chip ^ p, 0])
        outs[p][0] = (attended + nn_dot(hidden, new_out)).astype(jnp.bfloat16)


def finish(place, attended, fast_in, fast_out, sums, patch, own, share, first, unit_epsilon, after):
    peers, heads, rows, dim = attended.shape
    hid = fast_out.shape[1]

    def plain(shape):
        return pl.BlockSpec((1,) + shape[1:], lambda j, place: (j, 0, 0))

    out_shape = (heads, rows, dim)
    in_specs = [by_head(attended.shape)]
    in_specs += [chip_weights(a, share, first) for a in (fast_in, fast_out)]
    in_specs += [plain(a.shape) for a in (*sums, patch)]
    in_specs += [plain(out_shape)] * peers + untouched(after)
    return pl.pallas_call(
        functools.partial(finish_kernel, peers, unit_epsilon),
        out_shape=[jax.ShapeDtypeStruct(out_shape, jnp.bfloat16)] * peers,
        grid_spec=pltpu.PrefetchScalarGridSpec(
            num_scalar_prefetch=1,
            grid=(heads,),
            in_specs=in_specs,
            out_specs=[plain(out_shape)] * peers,
            scratch_shapes=[
                pltpu.VMEM((2 * hid, dim), jnp.float32),
                pltpu.VMEM((hid, dim), jnp.float32),
            ],
        ),
        compiler_params=params(),
        cost_estimate=cost(12 * heads * peers * rows * hid * dim, 0),
        name="finish",
    )(place, attended, fast_in, fast_out, *sums, patch, *own, *after)


def place_kernel(peers, chunks, share, place_ref, *refs):
    pieces, out_ref, sems = refs[:-2], refs[-2], refs[-1]
    copies = []
    for first, heads in chunks:
        for p in range(peers):
            at = (place_ref[0] ^ p) * share + first
            i = len(copies)
            copies.append(
                pltpu.make_async_copy(pieces[i], out_ref.at[pl.ds(at, heads)], sems.at[i])
            )
    for copy in copies:
        copy.start()
    for copy in copies:
        copy.wait()


def put_in_place(place, pieces, peers, chunks, share):
    _, rows, dim = pieces[0].shape
    return pl.pallas_call(
        functools.partial(place_kernel, peers, chunks, share),
        out_shape=jax.ShapeDtypeStruct((peers * share, rows, dim), jnp.bfloat16),
        in_specs=[pl.BlockSpec(memory_space=pltpu.SMEM)]
        + [pl.BlockSpec(memory_space=pltpu.VMEM)] * len(pieces),
        out_specs=pl.BlockSpec(memory_space=pl.ANY),
        scratch_shapes=[pltpu.SemaphoreType.DMA((len(pieces),))],
        compiler_params=params(),
        name="put_in_place",
    )(place, *pieces)


def regrouping(tok_peers, rows, heads, dim, hid):
    half_peers = tok_peers // 2
    peers = math.gcd(half_peers, heads)
    fits = tok_peers % 2 == 0 and half_peers * rows == 2 * HALF
    fits = fits and half_peers == 2 * peers and peers & (peers - 1) == 0
    fits = fits and rows % 256 == 0 and dim == 128 and hid % 256 == 0
    return peers if fits else 0


def regrouped_body(
    peers,
    query_rows,
    key_rows,
    value_rows,
    query_gain,
    key_gain,
    rate_in,
    rate_out,
    fast_in,
    fast_out,
    half_window,
    boundaries,
):
    rows, heads, dim = query_rows.shape
    share = heads // peers
    tok_peers = lax.axis_size("tok")
    half_peers = tok_peers // 2
    width_all = heads * dim * lax.axis_size("head")
    chunks = [(0, (share + 1) // 2), ((share + 1) // 2, share // 2)]
    aux_rows = 2 * -(-max(4 * (rows // 128), 3 * -(-share // chunks[0][1])) // 16) * 16
    own_index = lax.axis_index("tok")
    half = own_index // half_peers
    chip = own_index % half_peers // 2
    core = own_index % 2
    place = jnp.stack([chip, core, half]).astype(jnp.int32)

    def dealt(sent):
        pairs = [
            [(t, t // half_peers * half_peers + ((t % half_peers) ^ (2 * p))) for t in range(tok_peers)]
            for p in range(peers)
        ]
        return [sent[0]] + [exchanged(sent[p], pairs[p]) for p in range(1, peers)]

    core_pairs = [(t, t ^ 1) for t in range(tok_peers)]
    half_pairs = [(t, (t + half_peers) % tok_peers) for t in range(tok_peers)]
    forward_pairs = [(t + half_peers, t) for t in range(half_peers)]
    back_pairs = [(t, t - 1 + half_peers) for t in range(half_peers) if t % 2 == 1]

    q = jnp.transpose(query_rows, (1, 0, 2))
    k = jnp.transpose(key_rows, (1, 0, 2))
    v = jnp.transpose(value_rows, (1, 0, 2))
    q_float = q.astype(jnp.float32)
    k_float = k.astype(jnp.float32)
    squares = jnp.stack(
        [jnp.sum(q_float * q_float, axis=(0, 2)), jnp.sum(k_float * k_float, axis=(0, 2))]
    )
    if lax.axis_size("head") == 2:
        sums = (squares, lax.ppermute(squares, "head", [(0, 1), (1, 0)]))
    else:
        sums = (lax.psum(squares, "head"), jnp.zeros_like(squares))
    fold = math.log2(math.e) / math.sqrt(dim)
    sent = [
        pack(
            place,
            sums,
            q,
            k,
            v,
            (query_gain, key_gain),
            (rate_in, rate_out),
            peers,
            aux_rows,
            first,
            count,
            width_all,
            fold,
        )
        for first, count in chunks
    ]
    received = []
    for each in sent:
        if received:
            each = [lax.optimization_barrier(pair)[0] for pair in zip(each, received[-1])]
        received.append(dealt(each))
    def finished(ready, after):
        attended, sums, patch, own, first = ready
        return finish(
            place,
            attended,
            fast_in,
            fast_out,
            sums,
            patch,
            own,
            share,
            first,
            epsilon * fold * fold,
            after,
        )

    forwarded = ready = None
    pieces = []
    for (first, count), own in zip(chunks, received):
        if ready:
            *own, _ = lax.optimization_barrier((*own, ready[1][0]))
        else:
            own = lax.optimization_barrier((*own, *sent[-1]))[:peers]
        stack = stacked(own, rows)
        packets = (own, exchanged(stack, core_pairs))
        if forwarded is None:
            forwarded = exchanged(lone_rows(place, stack, packets[1], rows), forward_pairs)
        before = [ready[0]] if ready else []
        grad = gradients(place, fast_in, fast_out, packets, share, rows, first, before)
        from_half = exchanged(grad, half_pairs)
        before = [grad]
        if ready:
            outs = finished(ready, [grad])
            before.append(outs[0])
            pieces = pieces + dealt(outs)
        attended, extra = attend(
            place,
            half_window,
            boundaries,
            packets,
            forwarded,
            share,
            rows,
            first,
            before,
        )
        patch = exchanged(extra, back_pairs)
        from_half, _ = lax.optimization_barrier((from_half, attended))
        own_sum = (grad.astype(jnp.float32) + from_half.astype(jnp.float32)).astype(jnp.bfloat16)
        ready = (attended, (own_sum, exchanged(own_sum, core_pairs)), patch, own, first)
    pieces = pieces + dealt(finished(ready, pieces))
    whole = put_in_place(place, pieces, peers, chunks, share)
    return jnp.transpose(whole, (1, 0, 2))


def body(query_rows, *others):
    rows, heads, dim = query_rows.shape
    hid = others[7].shape[1]
    peers = regrouping(lax.axis_size("tok"), rows, heads, dim, hid)
    if peers:
        return regrouped_body(peers, query_rows, *others)
    return sliding_body(query_rows, *others)


def solution(mesh):
    in_specs = (
        P("tok", "head", None),
        P("tok", "head", None),
        P("tok", "head", None),
        P("head", None),
        P("head", None),
        P("head", "tok"),
        P("head", "tok"),
        P("head", None, None),
        P("head", None, None),
        P("head"),
        P(),
    )
    out_specs = P("tok", "head", None)
    return jax.shard_map(body, mesh=mesh, in_specs=in_specs, out_specs=out_specs, check_vma=False)
```

```python
import functools
import math

import jax
import jax.numpy as jnp
from jax import lax
from jax.experimental import pallas as pl
from jax.experimental.pallas import tpu as pltpu
from jax.sharding import PartitionSpec as P

HALF = 1024


epsilon = 1e-06


def passed_along(x, axis, by):
    peers = lax.axis_size(axis)
    pairs = [(i, i + by) for i in range(peers) if 0 <= i + by < peers]
    return lax.ppermute(x, axis, pairs)


def unit_rows(matrix):
    as_float = matrix.astype(jnp.float32)
    return (
        as_float * lax.rsqrt(jnp.sum(as_float * as_float, axis=-1, keepdims=True) + epsilon)
    ).astype(jnp.bfloat16)


def rescale(updated, base_norm, squares):
    return (updated * (base_norm / jnp.sqrt(squares + epsilon))[:, None, :]).astype(jnp.bfloat16)


def sliding_body(
    query_rows,
    key_rows,
    value_rows,
    query_gain,
    key_gain,
    rate_in,
    rate_out,
    fast_in,
    fast_out,
    half_window,
    boundaries,
):
    tok_rows = query_rows.shape[0]
    local_heads = query_rows.shape[1]
    head_dim = query_rows.shape[2]
    fast_hid = fast_out.shape[1]
    width_all = local_heads * head_dim * lax.axis_size("head")
    tok_count = tok_rows * lax.axis_size("tok")
    own_index = lax.axis_index("tok")
    first_row = own_index * tok_rows
    query_float = query_rows.astype(jnp.float32)
    key_float = key_rows.astype(jnp.float32)
    query_sq, key_sq = lax.psum(
        (
            jnp.sum(query_float * query_float, axis=(1, 2)),
            jnp.sum(key_float * key_float, axis=(1, 2)),
        ),
        "head",
    )
    q_normed = (
        query_float * lax.rsqrt(query_sq / width_all + epsilon)[:, None, None] * query_gain[None]
    ).astype(jnp.bfloat16)
    k_normed = (
        key_float * lax.rsqrt(key_sq / width_all + epsilon)[:, None, None] * key_gain[None]
    ).astype(jnp.bfloat16)

    def clip_of(places):
        return jnp.sum((places[:, None] >= boundaries[None, :]).astype(jnp.int32), axis=1)

    positions = first_row + jnp.arange(tok_rows, dtype=jnp.int32)
    query_clip = clip_of(positions)
    scaling = 1.0 / math.sqrt(head_dim)

    def absorb(state_now, block_keys, block_values, key_first):
        best, denominator, accum = state_now
        key_places = key_first + jnp.arange(tok_rows, dtype=jnp.int32)
        scores = (
            jnp.einsum("qhd,khd->hqk", q_normed, block_keys, preferred_element_type=jnp.float32)
            * scaling
        )
        inside = (key_places >= 0) & (key_places < tok_count)
        pair_ok = (query_clip[:, None] == clip_of(key_places)[None, :]) & inside[None, :]
        distance = jnp.abs(positions[:, None] - key_places[None, :])
        allowed = (distance[None, :, :] <= half_window[:, None, None]) & pair_ok[None, :, :]
        masked = jnp.where(allowed, scores, -jnp.inf)
        new_best = jnp.maximum(best, jnp.max(masked, axis=2))
        weights = jnp.exp(masked - new_best[:, :, None])
        shrink = jnp.exp(best - new_best)
        denominator = denominator * shrink + jnp.sum(weights, axis=2)
        accum = accum * shrink[:, :, None] + jnp.einsum(
            "hqk,khd->hqd",
            weights.astype(jnp.bfloat16),
            block_values,
            preferred_element_type=jnp.float32,
        )
        return (new_best, denominator, accum)

    start_state = (
        jnp.full((local_heads, tok_rows), -jnp.inf, jnp.float32),
        jnp.zeros((local_heads, tok_rows), jnp.float32),
        jnp.zeros((local_heads, tok_rows, head_dim), jnp.float32),
    )
    state_now = absorb(start_state, k_normed, value_rows, first_row)
    reach_blocks = HALF // tok_rows
    for distance_step in range(1, reach_blocks + 1):
        left_keys, left_values = passed_along((k_normed, value_rows), "tok", distance_step)
        state_now = absorb(state_now, left_keys, left_values, first_row - distance_step * tok_rows)
        right_keys, right_values = passed_along((k_normed, value_rows), "tok", -distance_step)
        state_now = absorb(
            state_now, right_keys, right_values, first_row + distance_step * tok_rows
        )
    attended = state_now[2] / state_now[1][:, :, None]
    key_unit = unit_rows(k_normed)
    query_unit = unit_rows(q_normed)
    pre_keys = jnp.einsum("thd,hdf->htf", key_unit, fast_in, preferred_element_type=jnp.float32)
    gate_part = pre_keys[:, :, :fast_hid]
    lin_part = pre_keys[:, :, fast_hid:]
    sigmoid_gate = jax.nn.sigmoid(gate_part)
    swish_gate = gate_part * sigmoid_gate
    hidden = (swish_gate * lin_part).astype(jnp.bfloat16)
    value_float = value_rows.astype(jnp.float32)
    push_out = (-jnp.transpose(rate_out)[:, :, None] * value_float).astype(jnp.bfloat16)
    push_in = (-jnp.transpose(rate_in)[:, :, None] * value_float).astype(jnp.bfloat16)
    grad_out = jnp.einsum("htf,thd->hfd", hidden, push_out, preferred_element_type=jnp.float32)
    hidden_grad = jnp.einsum("thd,hfd->htf", push_in, fast_out, preferred_element_type=jnp.float32)
    d_gate = hidden_grad * lin_part * sigmoid_gate * (1.0 + gate_part * (1.0 - sigmoid_gate))
    d_lin = hidden_grad * swish_gate
    d_pre = jnp.concatenate([d_gate, d_lin], axis=2).astype(jnp.bfloat16)
    grad_in = jnp.einsum("thd,htf->hdf", key_unit, d_pre, preferred_element_type=jnp.float32)
    in_float = fast_in.astype(jnp.float32)
    out_float = fast_out.astype(jnp.float32)
    in_base = jnp.sqrt(jnp.sum(in_float * in_float, axis=1))
    out_base = jnp.sqrt(jnp.sum(out_float * out_float, axis=1))
    summed_in, summed_out = lax.psum((grad_in, grad_out), "tok")
    updated_in = in_float - summed_in
    updated_out = out_float - summed_out
    new_in = rescale(updated_in, in_base, jnp.sum(updated_in * updated_in, axis=1))
    new_out = rescale(updated_out, out_base, jnp.sum(updated_out * updated_out, axis=1))
    pre_query = jnp.einsum("thd,hdf->htf", query_unit, new_in, preferred_element_type=jnp.float32)
    query_gate = pre_query[:, :, :fast_hid]
    query_hidden = (query_gate * jax.nn.sigmoid(query_gate) * pre_query[:, :, fast_hid:]).astype(
        jnp.bfloat16
    )
    fast_result = jnp.einsum(
        "htf,hfd->htd", query_hidden, new_out, preferred_element_type=jnp.float32
    )
    combined = attended + fast_result
    return jnp.transpose(combined, (1, 0, 2)).astype(jnp.bfloat16)


VMEM_BYTES = 16 * 1024 * 1024
HIDDEN_MASK = -1e30
NT = (((1,), (1,)), ((), ()))


def exchanged(x, pairs):
    return lax.ppermute(x, "tok", pairs)


def nt_dot(a, b):
    return lax.dot_general(a, b, NT, preferred_element_type=jnp.float32)


def nn_dot(a, b):
    return jnp.dot(a, b, preferred_element_type=jnp.float32)


def in_vmem(kernel, name, scalars, arrays, after, out_shape, flops=0, scratch=()):
    specs = [pl.BlockSpec(memory_space=pltpu.SMEM)] * len(scalars)
    specs += [pl.BlockSpec(memory_space=pltpu.VMEM)] * len(arrays)
    specs += [pl.BlockSpec(memory_space=pl.ANY)] * len(after)
    return pl.pallas_call(
        kernel,
        out_shape=out_shape,
        in_specs=specs,
        out_specs=jax.tree.map(lambda _: pl.BlockSpec(memory_space=pltpu.VMEM), out_shape),
        scratch_shapes=scratch,
        compiler_params=pltpu.CompilerParams(vmem_limit_bytes=VMEM_BYTES),
        cost_estimate=pl.CostEstimate(flops=16 * flops, bytes_accessed=0, transcendentals=0),
        name=name,
    )(*scalars, *arrays, *after)


def pack_kernel(peers, first, count, width_all, fold, with_lone, place_ref, *refs):
    squares_ref, more_ref, q_gain_ref, k_gain_ref, rate_in_ref, rate_out_ref = refs[:6]
    q_ref, k_ref, v_ref = refs[6:9]
    outs = refs[-3 - peers : -3]
    aux_ref, q_scale_ref, k_scale_ref = refs[-3:]
    rows, dim = q_scale_ref.shape
    share = q_gain_ref.shape[0] // peers
    scales = lax.rsqrt((squares_ref[...] + more_ref[...]) / width_all + epsilon)
    q_scale_ref[...] = jnp.transpose(jnp.broadcast_to(scales[0:1] * fold, (dim, rows)))
    k_scale_ref[...] = jnp.transpose(jnp.broadcast_to(scales[1:2], (dim, rows)))
    aux_ref[...] = jnp.zeros_like(aux_ref)

    def normed(ref, c, scale_ref, gain_ref, head, some):
        gain = gain_ref[pl.ds(c * share + head, 1), :]
        scaled = ref[c, head, 0:some].astype(jnp.float32) * scale_ref[0:some] * gain
        return scaled.astype(jnp.bfloat16)

    def one_head(step, carry):
        for p in range(peers):
            c = place_ref[0] ^ p
            head = first + step
            outs[p][step, 0:rows, :] = normed(q_ref, c, q_scale_ref, q_gain_ref, head, rows)
            outs[p][step, rows : 2 * rows, :] = normed(
                k_ref, c, k_scale_ref, k_gain_ref, head, rows
            )
            for i in range(0, rows, 128):
                outs[p][step, 2 * rows + i : 2 * rows + i + 128, :] = jnp.transpose(
                    v_ref[c, head, i : i + 128, :]
                )
            at = 0
            for rate_ref in (rate_in_ref, rate_out_ref):
                rate = rate_ref[pl.ds(c * share + head, 1), :]
                high = rate.astype(jnp.bfloat16).astype(jnp.float32)
                for part in (high, rate - high):
                    for i in range(0, rows, 128):
                        aux_ref[at : at + 1, :] = part[:, i : i + 128]
                        at += 1
            if with_lone:
                for i in range(-(-share // count)):
                    head = jnp.minimum(step + i * count, share - 1)
                    q0 = normed(q_ref, c, q_scale_ref, q_gain_ref, head, 16)
                    k0 = normed(k_ref, c, k_scale_ref, k_gain_ref, head, 16)
                    for at, array in enumerate((q0, k0, v_ref[c, head, 0:16])):
                        at += aux_ref.shape[0] // 2 + 3 * i
                        aux_ref[at : at + 1, :] = array.astype(jnp.float32)[0:1]
            some = outs[p].shape[1] - 3 * rows
            outs[p][step, 3 * rows :, :] = aux_ref[0:some, :].astype(jnp.bfloat16)
        return carry

    lax.fori_loop(0, count, one_head, 0)


def pack(place, sums, q, k, v, gains, rates, peers, aux_rows, first, count, width_all, fold):
    heads, rows, dim = q.shape
    out_shape = (count, 3 * rows + aux_rows // (2 if first else 1), dim)
    q, k, v = [x.reshape(peers, heads // peers, rows, dim) for x in (q, k, v)]
    return in_vmem(
        functools.partial(pack_kernel, peers, first, count, width_all, fold, not first),
        "pack",
        [place],
        [*sums, *gains, *rates, q, k, v],
        [],
        [jax.ShapeDtypeStruct(out_shape, jnp.bfloat16)] * peers,
        scratch=[
            pltpu.VMEM((aux_rows, dim), jnp.float32),
            pltpu.VMEM((rows, dim), jnp.float32),
            pltpu.VMEM((rows, dim), jnp.float32),
        ],
    )


def stack_kernel(from_row, *refs):
    for p, ref in enumerate(refs[:-1]):
        refs[-1][p] = ref[:, from_row:, :]


def stacked(arrays, from_row):
    heads, rows, dim = arrays[0].shape
    return in_vmem(
        functools.partial(stack_kernel, from_row),
        "stack",
        [],
        arrays,
        [],
        jax.ShapeDtypeStruct((len(arrays), heads, rows - from_row, dim), jnp.bfloat16),
    )


def lone_kernel(place_ref, own_ref, other_ref, out_ref):
    extra = out_ref.shape[1]
    at = own_ref.shape[2] - extra
    mine = jnp.full(out_ref.shape, place_ref[1]) == 0
    own = own_ref[place_ref[0], :, at:, :].astype(jnp.float32)
    other = other_ref[place_ref[0], :, at:, :].astype(jnp.float32)
    out_ref[...] = jnp.where(mine, own, other).astype(jnp.bfloat16)


def lone_rows(place, own, other, rows):
    _, count, all_rows, dim = own.shape
    out_shape = (count, (all_rows - 2 * rows) // 2, dim)
    return in_vmem(
        lone_kernel,
        "lone_rows",
        [place],
        [own, other],
        [],
        jax.ShapeDtypeStruct(out_shape, jnp.bfloat16),
    )


def key_value_blocks(peers, rows, step, refs):
    for p in range(peers):
        yield p, True, refs[p].at[step, rows : 2 * rows], refs[p].at[step, 2 * rows :]
        yield p, False, refs[peers].at[p, step, 0:rows], refs[peers].at[p, step, rows:]


def grads_kernel(peers, rows, rate_rows, share, first, place_ref, in_ref, out_ref, *refs):
    grad_ref = refs[-1]
    hid = out_ref.shape[1]
    part = hid // 2
    own = pl.multiple_of(place_ref[1] * part, part)

    def one_head(step, carry):
        head = place_ref[0] * share + first + step
        in_half = jnp.concatenate(
            [
                jnp.transpose(in_ref[head, :, pl.ds(at, part)].astype(jnp.float32))
                for at in (own, pl.multiple_of(hid + own, part))
            ],
            axis=0,
        ).astype(jnp.bfloat16)
        out_half = out_ref[head, pl.ds(own, part), :]
        sum_in = jnp.zeros((2 * part, in_half.shape[1]), jnp.float32)
        sum_out = jnp.zeros((part, in_half.shape[1]), jnp.float32)
        for _, _, keys, values in key_value_blocks(peers, rows, step, refs):
            k = keys[...].astype(jnp.float32)
            v_t = jnp.concatenate([values[at : at + 128, :] for at in range(0, rows, 128)], axis=1)
            aux = values[rows : rows + 16, :].astype(jnp.float32)

            def rate(at):
                both = aux[at : at + rate_rows] + aux[at + rate_rows : at + 2 * rate_rows]
                return jnp.concatenate([both[i : i + 1] for i in range(rate_rows)], axis=1)

            rate_in, rate_out = rate(0), rate(2 * rate_rows)
            unit = (k * lax.rsqrt(jnp.sum(k * k, axis=1, keepdims=True) + epsilon)).astype(
                jnp.bfloat16
            )
            pre = nt_dot(in_half, unit)
            gate, lin = pre[:part], pre[part:]
            sig = jax.nn.sigmoid(gate)
            swish = gate * sig
            pushed = (swish * lin * -rate_out).astype(jnp.bfloat16)
            hidden_grad = nn_dot(out_half, v_t) * -rate_in
            d_gate = hidden_grad * lin * sig * (1.0 + gate * (1.0 - sig))
            d_lin = hidden_grad * swish
            d_pre = jnp.concatenate([d_gate, d_lin], axis=0).astype(jnp.bfloat16)
            sum_in += nn_dot(d_pre, unit)
            sum_out += nt_dot(pushed, v_t)
        grad_ref[step, 0 : 2 * part, :] = sum_in.astype(jnp.bfloat16)
        grad_ref[step, 2 * part :, :] = sum_out.astype(jnp.bfloat16)
        return carry

    lax.fori_loop(0, grad_ref.shape[0], one_head, 0)


def gradients(place, fast_in, fast_out, packets, share, rows, first, after):
    _, hid, dim = fast_out.shape
    own, other = packets
    peers, heads = other.shape[:2]
    return in_vmem(
        functools.partial(grads_kernel, peers, rows, rows // 128, share, first),
        "gradients",
        [place],
        [fast_in, fast_out, *own, other],
        after,
        jax.ShapeDtypeStruct((heads, 3 * hid // 2, dim), jnp.bfloat16),
    )


def attend_kernel(peers, rows, share, first, fwd_heads, place_ref, window_ref, edge_ref, *refs):
    fwd_ref = refs[peers + 1]
    out_ref, extra_ref, k_scr, vt_scr, q_scr = refs[-5:]
    span = 2 * peers * rows
    dim = k_scr.shape[1]
    pad = fwd_ref.shape[1]
    chip, core, half = place_ref[0], place_ref[1], place_ref[2]
    base = half * span
    limit = span + 1 - half
    k_scr[span:, :] = jnp.zeros((k_scr.shape[0] - span, dim), k_scr.dtype)
    vt_scr[:, span:] = jnp.zeros((vt_scr.shape[0], vt_scr.shape[1] - span), vt_scr.dtype)
    vt_scr[dim:, :] = jnp.ones((vt_scr.shape[0] - dim, vt_scr.shape[1]), vt_scr.dtype)

    def one_head(step, carry):
        window = window_ref[chip * share + first + step]
        for p, own, keys, values in key_value_blocks(peers, rows, step, refs):
            at = pl.multiple_of(((chip ^ p) * 2 + (core if own else 1 - core)) * rows, rows)
            k_scr[pl.ds(at, rows), :] = keys[...]
            for i in range(0, rows, 128):
                vt_scr[0:dim, pl.ds(pl.multiple_of(at + i, 128), 128)] = values[i : i + 128, :]
        for p in range(peers):
            q_scr[chip ^ p] = refs[p][step, 0:rows, :]
        fwd = fwd_ref[lax.rem(first + step, fwd_heads)].astype(jnp.float32)
        turn = (first + step) // fwd_heads
        q_lone, k_lone, v_lone = (
            sum(
                jnp.where(turn == t, fwd[3 * t + i : 3 * t + i + 1], 0.0)
                for t in range(-(-share // fwd_heads))
            )
            for i in range(3)
        )
        k_scr[span : span + pad, :] = jnp.broadcast_to(k_lone, (pad, dim)).astype(jnp.bfloat16)
        vt_scr[0:dim, span : span + 128] = jnp.transpose(
            jnp.broadcast_to(v_lone, (128, dim))
        ).astype(jnp.bfloat16)

        def clip_start(place):
            start = jnp.zeros_like(place)
            for i in range(edge_ref.shape[0]):
                start = jnp.maximum(start, jnp.where(edge_ref[i] <= place, edge_ref[i], 0))
            return start

        def clip_stop(place):
            stop = jnp.full_like(place, base + limit)
            for i in range(edge_ref.shape[0]):
                stop = jnp.minimum(stop, jnp.where(edge_ref[i] > place, edge_ref[i], base + limit))
            return stop

        def lowest(place):
            return jnp.maximum(jnp.maximum(place - window, clip_start(place)), base) - base

        def highest(place):
            return jnp.minimum(place + window, clip_stop(place) - 1) - base

        def one_pair(i, carry):
            pair = []
            for c in (i, peers - 1 - i):
                start = (c * 2 + core) * rows
                place = base + start + lax.broadcasted_iota(jnp.int32, (1, rows), 1)
                from_key = lowest(base + start) // 128 * 128
                count = (highest(base + start + rows - 1) - from_key) // 256 + 1
                pair.append((c, lowest(place), highest(place), from_key, count))
            count = jnp.maximum(pair[0][4], pair[1][4])

            def variant(chunks):
                froms = [
                    pl.multiple_of(jnp.minimum(each[3], k_scr.shape[0] - chunks * 256), 128)
                    for each in pair
                ]
                key = lax.broadcasted_iota(jnp.int32, (256, rows), 0)
                scores = [[], []]
                tops = [None, None]
                for i in range(chunks):
                    for n, (each, at) in enumerate(zip(pair, froms)):
                        from_key = pl.multiple_of(at + i * 256, 128)
                        piece = nt_dot(k_scr[pl.ds(from_key, 256), :], q_scr[each[0]])
                        seen = (key >= each[1] - from_key) & (key <= each[2] - from_key)
                        piece = jnp.where(seen, piece, HIDDEN_MASK)
                        top = jnp.max(piece.reshape(32, 8, rows), axis=0)
                        tops[n] = top if i == 0 else jnp.maximum(tops[n], top)
                        scores[n].append(piece)
                tops = [jnp.max(top, axis=0, keepdims=True) for top in tops]
                totals = [0.0, 0.0]
                for i in range(chunks):
                    for n, at in enumerate(froms):
                        weights = jnp.exp2(scores[n][i] - tops[n]).astype(jnp.bfloat16)
                        from_key = pl.multiple_of(at + i * 256, 128)
                        totals[n] += nn_dot(vt_scr[:, pl.ds(from_key, 256)], weights)
                for each, total in zip(pair, totals):
                    attended = total[0:dim] * (1.0 / total[dim : dim + 1])
                    out_ref[each[0], step] = jnp.transpose(attended)

            for chunks in range(1, span // 256 + 2):

                @pl.when(count == chunks)
                def _(chunks=chunks):
                    variant(chunks)

            return carry

        lax.fori_loop(0, peers // 2, one_pair, 0)
        extra_ref[step] = jnp.zeros(extra_ref.shape[1:], jnp.float32)

        @pl.when((half == 0) & (core == 1))
        def _():
            near = span - HALF
            width = HALF + 128
            q = jnp.broadcast_to(q_lone, (pad, dim)).astype(jnp.bfloat16)
            scores = nt_dot(q, k_scr[near : near + width, :])
            key = near + lax.broadcasted_iota(jnp.int32, (1, width), 1)
            scores = jnp.where((key >= span - window) & (key <= span), scores, HIDDEN_MASK)
            top = jnp.max(scores, axis=1, keepdims=True)
            weights = jnp.exp2(scores - top).astype(jnp.bfloat16)
            total = nt_dot(weights, vt_scr[:, near : near + width])
            extra_ref[step] = total[:, 0:dim] / total[:, dim : dim + 1]
        return carry

    lax.fori_loop(0, extra_ref.shape[0], one_head, 0)


def attend(place, half_window, boundaries, packets, forwarded, share, rows, first, after):
    own, other = packets
    peers, heads = other.shape[:2]
    fwd_heads, pad, dim = forwarded.shape
    scr_rows = 2 * peers * rows + 256
    out_shapes = [(peers, heads, rows, dim), (heads, pad, dim)]
    return in_vmem(
        functools.partial(attend_kernel, peers, rows, share, first, fwd_heads),
        "attend",
        [place, half_window, boundaries],
        [*own, other, forwarded],
        after,
        [jax.ShapeDtypeStruct(shape, jnp.float32) for shape in out_shapes],
        flops=4 * heads * peers * rows * HALF * 2 * dim,
        scratch=[
            pltpu.VMEM((scr_rows, dim), jnp.bfloat16),
            pltpu.VMEM((dim + 16, scr_rows), jnp.bfloat16),
            pltpu.VMEM((peers, rows, dim), jnp.bfloat16),
        ],
    )


def finish_kernel(peers, share, first, unit_epsilon, place_ref, *refs):
    att_ref, base_in_ref, base_out_ref, own_ref, other_ref, patch_ref = refs[:6]
    queries = refs[6 : 6 + peers]
    outs = refs[-2 - peers : -2]
    grad_in_scr, grad_out_scr = refs[-2:]
    chip, core, half = place_ref[0], place_ref[1], place_ref[2]
    rows = att_ref.shape[2]
    hid = base_out_ref.shape[1]
    part = hid // 2

    def one_head(step, carry):
        head = chip * share + first + step
        for summed, lane in ((own_ref, core), (other_ref, 1 - core)):
            at = pl.multiple_of(lane * part, part)
            grad_in_scr[pl.ds(at, part), :] = summed[step, 0:part, :].astype(jnp.float32)
            grad_in_scr[pl.ds(hid + at, part), :] = summed[step, part : 2 * part, :].astype(jnp.float32)
            grad_out_scr[pl.ds(at, part), :] = summed[step, 2 * part :, :].astype(jnp.float32)

        def renewed(base, grad):
            base = base.astype(jnp.float32)
            updated = base - grad
            norm = jnp.sqrt(jnp.sum(base * base, axis=0, keepdims=True))
            squares = jnp.sum(updated * updated, axis=0, keepdims=True)
            return (updated * (norm / jnp.sqrt(squares + epsilon))).astype(jnp.bfloat16)

        new_in = renewed(base_in_ref[head], jnp.transpose(grad_in_scr[...]))
        new_out = renewed(base_out_ref[head], grad_out_scr[...])
        patch = patch_ref[step, 0:8, :][0:1]
        row = lax.broadcasted_iota(jnp.int32, (rows, 1), 0)
        for p in range(peers):
            q = queries[p][step, 0:rows, :].astype(jnp.float32)
            unit = (q * lax.rsqrt(jnp.sum(q * q, axis=1, keepdims=True) + unit_epsilon)).astype(
                jnp.bfloat16
            )
            pre = nn_dot(unit, new_in)
            gate = pre[:, :hid]
            hidden = (gate * jax.nn.sigmoid(gate) * pre[:, hid:]).astype(jnp.bfloat16)
            patched = (half == 1) & (core == 0) & (chip == p)
            attended = jnp.where(patched & (row == 0), patch, att_ref[chip ^ p, step])
            outs[p][step] = (attended + nn_dot(hidden, new_out)).astype(jnp.bfloat16)
        return carry

    lax.fori_loop(0, att_ref.shape[1], one_head, 0)


def finish(place, attended, fast_in, fast_out, sums, patch, own, share, first, unit_epsilon, after):
    peers, heads, rows, dim = attended.shape
    hid = fast_out.shape[1]
    return in_vmem(
        functools.partial(finish_kernel, peers, share, first, unit_epsilon),
        "finish",
        [place],
        [attended, fast_in, fast_out, *sums, patch, *own],
        after,
        [jax.ShapeDtypeStruct((heads, rows, dim), jnp.bfloat16)] * peers,
        flops=12 * heads * peers * rows * hid * dim,
        scratch=[pltpu.VMEM((2 * hid, dim), jnp.float32), pltpu.VMEM((hid, dim), jnp.float32)],
    )


def place_kernel(peers, chunks, share, place_ref, *refs):
    pieces, out_ref, sems = refs[:-2], refs[-2], refs[-1]
    copies = []
    for first, heads in chunks:
        for p in range(peers):
            at = (place_ref[0] ^ p) * share + first
            i = len(copies)
            copies.append(
                pltpu.make_async_copy(pieces[i], out_ref.at[pl.ds(at, heads)], sems.at[i])
            )
    for copy in copies:
        copy.start()
    for copy in copies:
        copy.wait()


def put_in_place(place, pieces, peers, chunks, share):
    _, rows, dim = pieces[0].shape
    return pl.pallas_call(
        functools.partial(place_kernel, peers, chunks, share),
        out_shape=jax.ShapeDtypeStruct((peers * share, rows, dim), jnp.bfloat16),
        in_specs=[pl.BlockSpec(memory_space=pltpu.SMEM)]
        + [pl.BlockSpec(memory_space=pltpu.VMEM)] * len(pieces),
        out_specs=pl.BlockSpec(memory_space=pl.ANY),
        scratch_shapes=[pltpu.SemaphoreType.DMA((len(pieces),))],
        compiler_params=pltpu.CompilerParams(vmem_limit_bytes=VMEM_BYTES),
        name="put_in_place",
    )(place, *pieces)


def regrouping(tok_peers, rows, heads, dim, hid):
    half_peers = tok_peers // 2
    peers = math.gcd(half_peers, heads)
    fits = tok_peers % 2 == 0 and half_peers * rows == 2 * HALF
    fits = fits and half_peers == 2 * peers and peers & (peers - 1) == 0
    fits = fits and rows % 256 == 0 and dim == 128 and hid % 256 == 0
    return peers if fits else 0


def regrouped_body(
    peers,
    query_rows,
    key_rows,
    value_rows,
    query_gain,
    key_gain,
    rate_in,
    rate_out,
    fast_in,
    fast_out,
    half_window,
    boundaries,
):
    rows, heads, dim = query_rows.shape
    share = heads // peers
    tok_peers = lax.axis_size("tok")
    half_peers = tok_peers // 2
    width_all = heads * dim * lax.axis_size("head")
    chunks = [(0, (share + 1) // 2), ((share + 1) // 2, share // 2)]
    aux_rows = 2 * -(-max(4 * (rows // 128), 3 * -(-share // chunks[0][1])) // 16) * 16
    own_index = lax.axis_index("tok")
    half = own_index // half_peers
    chip = own_index % half_peers // 2
    core = own_index % 2
    place = jnp.stack([chip, core, half]).astype(jnp.int32)

    def dealt(sent):
        pairs = [
            [(t, t // half_peers * half_peers + ((t % half_peers) ^ (2 * p))) for t in range(tok_peers)]
            for p in range(peers)
        ]
        return [sent[0]] + [exchanged(sent[p], pairs[p]) for p in range(1, peers)]

    core_pairs = [(t, t ^ 1) for t in range(tok_peers)]
    half_pairs = [(t, (t + half_peers) % tok_peers) for t in range(tok_peers)]
    forward_pairs = [(t + half_peers, t) for t in range(half_peers)]
    back_pairs = [(t, t - 1 + half_peers) for t in range(half_peers) if t % 2 == 1]

    q = jnp.transpose(query_rows, (1, 0, 2))
    k = jnp.transpose(key_rows, (1, 0, 2))
    v = jnp.transpose(value_rows, (1, 0, 2))
    q_float = q.astype(jnp.float32)
    k_float = k.astype(jnp.float32)
    squares = jnp.stack(
        [jnp.sum(q_float * q_float, axis=(0, 2)), jnp.sum(k_float * k_float, axis=(0, 2))]
    )
    if lax.axis_size("head") == 2:
        sums = (squares, lax.ppermute(squares, "head", [(0, 1), (1, 0)]))
    else:
        sums = (lax.psum(squares, "head"), jnp.zeros_like(squares))
    fold = math.log2(math.e) / math.sqrt(dim)
    sent = [
        pack(
            place,
            sums,
            q,
            k,
            v,
            (query_gain, key_gain),
            (rate_in, rate_out),
            peers,
            aux_rows,
            first,
            count,
            width_all,
            fold,
        )
        for first, count in chunks
    ]
    received = []
    for each in sent:
        if received:
            each = [lax.optimization_barrier(pair)[0] for pair in zip(each, received[-1])]
        received.append(dealt(each))
    def finished(ready, after):
        attended, sums, patch, own, first = ready
        return finish(
            place,
            attended,
            fast_in,
            fast_out,
            sums,
            patch,
            own,
            share,
            first,
            epsilon * fold * fold,
            after,
        )

    forwarded = ready = None
    pieces = []
    for (first, count), own in zip(chunks, received):
        if ready:
            *own, _ = lax.optimization_barrier((*own, ready[1][0]))
        else:
            own = lax.optimization_barrier((*own, *sent[-1]))[:peers]
        stack = stacked(own, rows)
        packets = (own, exchanged(stack, core_pairs))
        if forwarded is None:
            forwarded = exchanged(lone_rows(place, stack, packets[1], rows), forward_pairs)
        before = [ready[0]] if ready else []
        grad = gradients(place, fast_in, fast_out, packets, share, rows, first, before)
        from_half = exchanged(grad, half_pairs)
        before = [grad]
        if ready:
            outs = finished(ready, [grad])
            before.append(outs[0])
            pieces = pieces + dealt(outs)
        attended, extra = attend(
            place,
            half_window,
            boundaries,
            packets,
            forwarded,
            share,
            rows,
            first,
            before,
        )
        patch = exchanged(extra, back_pairs)
        from_half, _ = lax.optimization_barrier((from_half, attended))
        own_sum = (grad.astype(jnp.float32) + from_half.astype(jnp.float32)).astype(jnp.bfloat16)
        ready = (attended, (own_sum, exchanged(own_sum, core_pairs)), patch, own, first)
    pieces = pieces + dealt(finished(ready, pieces))
    whole = put_in_place(place, pieces, peers, chunks, share)
    return jnp.transpose(whole, (1, 0, 2))


def body(query_rows, *others):
    rows, heads, dim = query_rows.shape
    hid = others[7].shape[1]
    peers = regrouping(lax.axis_size("tok"), rows, heads, dim, hid)
    if peers:
        return regrouped_body(peers, query_rows, *others)
    return sliding_body(query_rows, *others)


def solution(mesh):
    in_specs = (
        P("tok", "head", None),
        P("tok", "head", None),
        P("tok", "head", None),
        P("head", None),
        P("head", None),
        P("head", "tok"),
        P("head", "tok"),
        P("head", None, None),
        P("head", None, None),
        P("head"),
        P(),
    )
    out_specs = P("tok", "head", None)
    return jax.shard_map(body, mesh=mesh, in_specs=in_specs, out_specs=out_specs, check_vma=False)
```

```python
import functools
import math

import jax
import jax.numpy as jnp
from jax import lax
from jax.experimental import pallas as pl
from jax.experimental.pallas import tpu as pltpu
from jax.sharding import PartitionSpec as P

HALF = 1024


epsilon = 1e-06


def passed_along(x, axis, by):
    peers = lax.axis_size(axis)
    pairs = [(i, i + by) for i in range(peers) if 0 <= i + by < peers]
    return lax.ppermute(x, axis, pairs)


def unit_rows(matrix):
    as_float = matrix.astype(jnp.float32)
    return (
        as_float * lax.rsqrt(jnp.sum(as_float * as_float, axis=-1, keepdims=True) + epsilon)
    ).astype(jnp.bfloat16)


def rescale(updated, base_norm, squares):
    return (updated * (base_norm / jnp.sqrt(squares + epsilon))[:, None, :]).astype(jnp.bfloat16)


def sliding_body(
    query_rows,
    key_rows,
    value_rows,
    query_gain,
    key_gain,
    rate_in,
    rate_out,
    fast_in,
    fast_out,
    half_window,
    boundaries,
):
    tok_rows = query_rows.shape[0]
    local_heads = query_rows.shape[1]
    head_dim = query_rows.shape[2]
    fast_hid = fast_out.shape[1]
    width_all = local_heads * head_dim * lax.axis_size("head")
    tok_count = tok_rows * lax.axis_size("tok")
    own_index = lax.axis_index("tok")
    first_row = own_index * tok_rows
    query_float = query_rows.astype(jnp.float32)
    key_float = key_rows.astype(jnp.float32)
    query_sq, key_sq = lax.psum(
        (
            jnp.sum(query_float * query_float, axis=(1, 2)),
            jnp.sum(key_float * key_float, axis=(1, 2)),
        ),
        "head",
    )
    q_normed = (
        query_float * lax.rsqrt(query_sq / width_all + epsilon)[:, None, None] * query_gain[None]
    ).astype(jnp.bfloat16)
    k_normed = (
        key_float * lax.rsqrt(key_sq / width_all + epsilon)[:, None, None] * key_gain[None]
    ).astype(jnp.bfloat16)

    def clip_of(places):
        return jnp.sum((places[:, None] >= boundaries[None, :]).astype(jnp.int32), axis=1)

    positions = first_row + jnp.arange(tok_rows, dtype=jnp.int32)
    query_clip = clip_of(positions)
    scaling = 1.0 / math.sqrt(head_dim)

    def absorb(state_now, block_keys, block_values, key_first):
        best, denominator, accum = state_now
        key_places = key_first + jnp.arange(tok_rows, dtype=jnp.int32)
        scores = (
            jnp.einsum("qhd,khd->hqk", q_normed, block_keys, preferred_element_type=jnp.float32)
            * scaling
        )
        inside = (key_places >= 0) & (key_places < tok_count)
        pair_ok = (query_clip[:, None] == clip_of(key_places)[None, :]) & inside[None, :]
        distance = jnp.abs(positions[:, None] - key_places[None, :])
        allowed = (distance[None, :, :] <= half_window[:, None, None]) & pair_ok[None, :, :]
        masked = jnp.where(allowed, scores, -jnp.inf)
        new_best = jnp.maximum(best, jnp.max(masked, axis=2))
        weights = jnp.exp(masked - new_best[:, :, None])
        shrink = jnp.exp(best - new_best)
        denominator = denominator * shrink + jnp.sum(weights, axis=2)
        accum = accum * shrink[:, :, None] + jnp.einsum(
            "hqk,khd->hqd",
            weights.astype(jnp.bfloat16),
            block_values,
            preferred_element_type=jnp.float32,
        )
        return (new_best, denominator, accum)

    start_state = (
        jnp.full((local_heads, tok_rows), -jnp.inf, jnp.float32),
        jnp.zeros((local_heads, tok_rows), jnp.float32),
        jnp.zeros((local_heads, tok_rows, head_dim), jnp.float32),
    )
    state_now = absorb(start_state, k_normed, value_rows, first_row)
    reach_blocks = HALF // tok_rows
    for distance_step in range(1, reach_blocks + 1):
        left_keys, left_values = passed_along((k_normed, value_rows), "tok", distance_step)
        state_now = absorb(state_now, left_keys, left_values, first_row - distance_step * tok_rows)
        right_keys, right_values = passed_along((k_normed, value_rows), "tok", -distance_step)
        state_now = absorb(
            state_now, right_keys, right_values, first_row + distance_step * tok_rows
        )
    attended = state_now[2] / state_now[1][:, :, None]
    key_unit = unit_rows(k_normed)
    query_unit = unit_rows(q_normed)
    pre_keys = jnp.einsum("thd,hdf->htf", key_unit, fast_in, preferred_element_type=jnp.float32)
    gate_part = pre_keys[:, :, :fast_hid]
    lin_part = pre_keys[:, :, fast_hid:]
    sigmoid_gate = jax.nn.sigmoid(gate_part)
    swish_gate = gate_part * sigmoid_gate
    hidden = (swish_gate * lin_part).astype(jnp.bfloat16)
    value_float = value_rows.astype(jnp.float32)
    push_out = (-jnp.transpose(rate_out)[:, :, None] * value_float).astype(jnp.bfloat16)
    push_in = (-jnp.transpose(rate_in)[:, :, None] * value_float).astype(jnp.bfloat16)
    grad_out = jnp.einsum("htf,thd->hfd", hidden, push_out, preferred_element_type=jnp.float32)
    hidden_grad = jnp.einsum("thd,hfd->htf", push_in, fast_out, preferred_element_type=jnp.float32)
    d_gate = hidden_grad * lin_part * sigmoid_gate * (1.0 + gate_part * (1.0 - sigmoid_gate))
    d_lin = hidden_grad * swish_gate
    d_pre = jnp.concatenate([d_gate, d_lin], axis=2).astype(jnp.bfloat16)
    grad_in = jnp.einsum("thd,htf->hdf", key_unit, d_pre, preferred_element_type=jnp.float32)
    in_float = fast_in.astype(jnp.float32)
    out_float = fast_out.astype(jnp.float32)
    in_base = jnp.sqrt(jnp.sum(in_float * in_float, axis=1))
    out_base = jnp.sqrt(jnp.sum(out_float * out_float, axis=1))
    summed_in, summed_out = lax.psum((grad_in, grad_out), "tok")
    updated_in = in_float - summed_in
    updated_out = out_float - summed_out
    new_in = rescale(updated_in, in_base, jnp.sum(updated_in * updated_in, axis=1))
    new_out = rescale(updated_out, out_base, jnp.sum(updated_out * updated_out, axis=1))
    pre_query = jnp.einsum("thd,hdf->htf", query_unit, new_in, preferred_element_type=jnp.float32)
    query_gate = pre_query[:, :, :fast_hid]
    query_hidden = (query_gate * jax.nn.sigmoid(query_gate) * pre_query[:, :, fast_hid:]).astype(
        jnp.bfloat16
    )
    fast_result = jnp.einsum(
        "htf,hfd->htd", query_hidden, new_out, preferred_element_type=jnp.float32
    )
    combined = attended + fast_result
    return jnp.transpose(combined, (1, 0, 2)).astype(jnp.bfloat16)


VMEM_BYTES = 16 * 1024 * 1024
HIDDEN_MASK = -1e30
NT = (((1,), (1,)), ((), ()))


def exchanged(x, pairs):
    return lax.ppermute(x, "tok", pairs)


def nt_dot(a, b):
    return lax.dot_general(a, b, NT, preferred_element_type=jnp.float32)


def nn_dot(a, b):
    return jnp.dot(a, b, preferred_element_type=jnp.float32)


def in_vmem(kernel, name, scalars, arrays, after, out_shape, flops=0, scratch=()):
    specs = [pl.BlockSpec(memory_space=pltpu.SMEM)] * len(scalars)
    specs += [pl.BlockSpec(memory_space=pltpu.VMEM)] * len(arrays)
    specs += [pl.BlockSpec(memory_space=pl.ANY)] * len(after)
    return pl.pallas_call(
        kernel,
        out_shape=out_shape,
        in_specs=specs,
        out_specs=jax.tree.map(lambda _: pl.BlockSpec(memory_space=pltpu.VMEM), out_shape),
        scratch_shapes=scratch,
        compiler_params=pltpu.CompilerParams(vmem_limit_bytes=VMEM_BYTES),
        cost_estimate=pl.CostEstimate(flops=16 * flops, bytes_accessed=0, transcendentals=0),
        name=name,
    )(*scalars, *arrays, *after)


def pack_kernel(peers, first, count, width_all, fold, with_lone, place_ref, *refs):
    squares_ref, more_ref, q_gain_ref, k_gain_ref, rate_in_ref, rate_out_ref = refs[:6]
    q_ref, k_ref, v_ref = refs[6:9]
    outs = refs[-3 - peers : -3]
    aux_ref, q_scale_ref, k_scale_ref = refs[-3:]
    rows, dim = q_scale_ref.shape
    share = q_gain_ref.shape[0] // peers
    scales = lax.rsqrt((squares_ref[...] + more_ref[...]) / width_all + epsilon)
    q_scale_ref[...] = jnp.transpose(jnp.broadcast_to(scales[0:1] * fold, (dim, rows)))
    k_scale_ref[...] = jnp.transpose(jnp.broadcast_to(scales[1:2], (dim, rows)))
    aux_ref[...] = jnp.zeros_like(aux_ref)

    def normed(ref, c, scale_ref, gain_ref, head, some):
        gain = gain_ref[pl.ds(c * share + head, 1), :]
        scaled = ref[c, head, 0:some].astype(jnp.float32) * scale_ref[0:some] * gain
        return scaled.astype(jnp.bfloat16)

    def one_head(step, carry):
        for p in range(peers):
            c = place_ref[0] ^ p
            head = first + step
            outs[p][step, 0:rows, :] = normed(q_ref, c, q_scale_ref, q_gain_ref, head, rows)
            outs[p][step, rows : 2 * rows, :] = normed(
                k_ref, c, k_scale_ref, k_gain_ref, head, rows
            )
            for i in range(0, rows, 128):
                outs[p][step, 2 * rows + i : 2 * rows + i + 128, :] = jnp.transpose(
                    v_ref[c, head, i : i + 128, :]
                )
            at = 0
            for rate_ref in (rate_in_ref, rate_out_ref):
                rate = rate_ref[pl.ds(c * share + head, 1), :]
                high = rate.astype(jnp.bfloat16).astype(jnp.float32)
                for part in (high, rate - high):
                    for i in range(0, rows, 128):
                        aux_ref[at : at + 1, :] = part[:, i : i + 128]
                        at += 1
            if with_lone:
                for i in range(-(-share // count)):
                    head = jnp.minimum(step + i * count, share - 1)
                    q0 = normed(q_ref, c, q_scale_ref, q_gain_ref, head, 16)
                    k0 = normed(k_ref, c, k_scale_ref, k_gain_ref, head, 16)
                    for at, array in enumerate((q0, k0, v_ref[c, head, 0:16])):
                        at += aux_ref.shape[0] // 2 + 3 * i
                        aux_ref[at : at + 1, :] = array.astype(jnp.float32)[0:1]
            some = outs[p].shape[1] - 3 * rows
            outs[p][step, 3 * rows :, :] = aux_ref[0:some, :].astype(jnp.bfloat16)
        return carry

    lax.fori_loop(0, count, one_head, 0)


def pack(place, sums, q, k, v, gains, rates, peers, aux_rows, first, count, width_all, fold):
    heads, rows, dim = q.shape
    out_shape = (count, 3 * rows + aux_rows // (2 if first else 1), dim)
    q, k, v = [x.reshape(peers, heads // peers, rows, dim) for x in (q, k, v)]
    return in_vmem(
        functools.partial(pack_kernel, peers, first, count, width_all, fold, not first),
        "pack",
        [place],
        [*sums, *gains, *rates, q, k, v],
        [],
        [jax.ShapeDtypeStruct(out_shape, jnp.bfloat16)] * peers,
        scratch=[
            pltpu.VMEM((aux_rows, dim), jnp.float32),
            pltpu.VMEM((rows, dim), jnp.float32),
            pltpu.VMEM((rows, dim), jnp.float32),
        ],
    )


def stack_kernel(from_row, *refs):
    for p, ref in enumerate(refs[:-1]):
        refs[-1][p] = ref[:, from_row:, :]


def stacked(arrays, from_row):
    heads, rows, dim = arrays[0].shape
    return in_vmem(
        functools.partial(stack_kernel, from_row),
        "stack",
        [],
        arrays,
        [],
        jax.ShapeDtypeStruct((len(arrays), heads, rows - from_row, dim), jnp.bfloat16),
    )


def lone_kernel(place_ref, own_ref, other_ref, out_ref):
    extra = out_ref.shape[1]
    at = own_ref.shape[2] - extra
    mine = jnp.full(out_ref.shape, place_ref[1]) == 0
    own = own_ref[place_ref[0], :, at:, :].astype(jnp.float32)
    other = other_ref[place_ref[0], :, at:, :].astype(jnp.float32)
    out_ref[...] = jnp.where(mine, own, other).astype(jnp.bfloat16)


def lone_rows(place, own, other, rows):
    _, count, all_rows, dim = own.shape
    out_shape = (count, (all_rows - 2 * rows) // 2, dim)
    return in_vmem(
        lone_kernel,
        "lone_rows",
        [place],
        [own, other],
        [],
        jax.ShapeDtypeStruct(out_shape, jnp.bfloat16),
    )


def key_value_blocks(peers, rows, step, refs):
    for p in range(peers):
        yield p, True, refs[p].at[step, rows : 2 * rows], refs[p].at[step, 2 * rows :]
        yield p, False, refs[peers].at[p, step, 0:rows], refs[peers].at[p, step, rows:]


def grads_kernel(peers, rows, rate_rows, share, first, place_ref, in_ref, out_ref, *refs):
    grad_ref = refs[-1]
    hid = out_ref.shape[1]
    part = hid // 2
    own = pl.multiple_of(place_ref[1] * part, part)

    def one_head(step, carry):
        head = place_ref[0] * share + first + step
        in_half = jnp.concatenate(
            [
                jnp.transpose(in_ref[head, :, pl.ds(at, part)].astype(jnp.float32))
                for at in (own, pl.multiple_of(hid + own, part))
            ],
            axis=0,
        ).astype(jnp.bfloat16)
        out_half = out_ref[head, pl.ds(own, part), :]
        sum_in = jnp.zeros((2 * part, in_half.shape[1]), jnp.float32)
        sum_out = jnp.zeros((part, in_half.shape[1]), jnp.float32)
        for _, _, keys, values in key_value_blocks(peers, rows, step, refs):
            k = keys[...].astype(jnp.float32)
            v_t = jnp.concatenate([values[at : at + 128, :] for at in range(0, rows, 128)], axis=1)
            aux = values[rows : rows + 16, :].astype(jnp.float32)

            def rate(at):
                both = aux[at : at + rate_rows] + aux[at + rate_rows : at + 2 * rate_rows]
                return jnp.concatenate([both[i : i + 1] for i in range(rate_rows)], axis=1)

            rate_in, rate_out = rate(0), rate(2 * rate_rows)
            unit = (k * lax.rsqrt(jnp.sum(k * k, axis=1, keepdims=True) + epsilon)).astype(
                jnp.bfloat16
            )
            pre = nt_dot(in_half, unit)
            gate, lin = pre[:part], pre[part:]
            sig = jax.nn.sigmoid(gate)
            swish = gate * sig
            pushed = (swish * lin * -rate_out).astype(jnp.bfloat16)
            hidden_grad = nn_dot(out_half, v_t) * -rate_in
            d_gate = hidden_grad * lin * sig * (1.0 + gate * (1.0 - sig))
            d_lin = hidden_grad * swish
            d_pre = jnp.concatenate([d_gate, d_lin], axis=0).astype(jnp.bfloat16)
            sum_in += nn_dot(d_pre, unit)
            sum_out += nt_dot(pushed, v_t)
        grad_ref[step, 0 : 2 * part, :] = sum_in.astype(jnp.bfloat16)
        grad_ref[step, 2 * part :, :] = sum_out.astype(jnp.bfloat16)
        return carry

    lax.fori_loop(0, grad_ref.shape[0], one_head, 0)


def gradients(place, fast_in, fast_out, packets, share, rows, first, after):
    _, hid, dim = fast_out.shape
    own, other = packets
    peers, heads = other.shape[:2]
    return in_vmem(
        functools.partial(grads_kernel, peers, rows, rows // 128, share, first),
        "gradients",
        [place],
        [fast_in, fast_out, *own, other],
        after,
        jax.ShapeDtypeStruct((heads, 3 * hid // 2, dim), jnp.bfloat16),
    )


def attend_kernel(peers, rows, share, first, fwd_heads, place_ref, window_ref, edge_ref, *refs):
    fwd_ref = refs[peers + 1]
    out_ref, extra_ref, k_scr, vt_scr, q_scr = refs[-5:]
    span = 2 * peers * rows
    dim = k_scr.shape[1]
    pad = fwd_ref.shape[1]
    chip, core, half = place_ref[0], place_ref[1], place_ref[2]
    base = half * span
    limit = span + 1 - half
    k_scr[span:, :] = jnp.zeros((k_scr.shape[0] - span, dim), k_scr.dtype)
    vt_scr[:, span:] = jnp.zeros((vt_scr.shape[0], vt_scr.shape[1] - span), vt_scr.dtype)
    vt_scr[dim:, :] = jnp.ones((vt_scr.shape[0] - dim, vt_scr.shape[1]), vt_scr.dtype)

    def one_head(step, carry):
        window = window_ref[chip * share + first + step]
        for p, own, keys, values in key_value_blocks(peers, rows, step, refs):
            at = pl.multiple_of(((chip ^ p) * 2 + (core if own else 1 - core)) * rows, rows)
            k_scr[pl.ds(at, rows), :] = keys[...]
            for i in range(0, rows, 128):
                vt_scr[0:dim, pl.ds(pl.multiple_of(at + i, 128), 128)] = values[i : i + 128, :]
        for p in range(peers):
            q_scr[chip ^ p] = refs[p][step, 0:rows, :]
        fwd = fwd_ref[lax.rem(first + step, fwd_heads)].astype(jnp.float32)
        turn = (first + step) // fwd_heads
        q_lone, k_lone, v_lone = (
            sum(
                jnp.where(turn == t, fwd[3 * t + i : 3 * t + i + 1], 0.0)
                for t in range(-(-share // fwd_heads))
            )
            for i in range(3)
        )
        k_scr[span : span + pad, :] = jnp.broadcast_to(k_lone, (pad, dim)).astype(jnp.bfloat16)
        vt_scr[0:dim, span : span + 128] = jnp.transpose(
            jnp.broadcast_to(v_lone, (128, dim))
        ).astype(jnp.bfloat16)

        def clip_start(place):
            start = jnp.zeros_like(place)
            for i in range(edge_ref.shape[0]):
                start = jnp.maximum(start, jnp.where(edge_ref[i] <= place, edge_ref[i], 0))
            return start

        def clip_stop(place):
            stop = jnp.full_like(place, base + limit)
            for i in range(edge_ref.shape[0]):
                stop = jnp.minimum(stop, jnp.where(edge_ref[i] > place, edge_ref[i], base + limit))
            return stop

        def lowest(place):
            return jnp.maximum(jnp.maximum(place - window, clip_start(place)), base) - base

        def highest(place):
            return jnp.minimum(place + window, clip_stop(place) - 1) - base

        def one_pair(i, carry):
            pair = []
            for c in (i, peers - 1 - i):
                start = (c * 2 + core) * rows
                place = base + start + lax.broadcasted_iota(jnp.int32, (1, rows), 1)
                from_key = lowest(base + start) // 128 * 128
                count = (highest(base + start + rows - 1) - from_key) // 256 + 1
                pair.append((c, lowest(place), highest(place), from_key, count))
            count = jnp.maximum(pair[0][4], pair[1][4])
            clear = True
            for c, _, _, from_key, _ in pair:
                at = jnp.minimum(from_key, k_scr.shape[0] - count * 256)
                place = base + (c * 2 + core) * rows
                clear &= lowest(place + rows - 1) <= at + 2 * 256
                clear &= highest(place) >= at + (count - 2) * 256 - 1

            def variant(chunks, unseen_only_outside):
                froms = [
                    pl.multiple_of(jnp.minimum(each[3], k_scr.shape[0] - chunks * 256), 128)
                    for each in pair
                ]
                key = lax.broadcasted_iota(jnp.int32, (256, rows), 0)
                scores = [[], []]
                tops = [None, None]
                for i in range(chunks):
                    for n, (each, at) in enumerate(zip(pair, froms)):
                        from_key = pl.multiple_of(at + i * 256, 128)
                        piece = nt_dot(k_scr[pl.ds(from_key, 256), :], q_scr[each[0]])
                        if not (unseen_only_outside and 2 <= i < chunks - 2):
                            seen = (key >= each[1] - from_key) & (key <= each[2] - from_key)
                            piece = jnp.where(seen, piece, HIDDEN_MASK)
                        top = jnp.max(piece.reshape(32, 8, rows), axis=0)
                        tops[n] = top if i == 0 else jnp.maximum(tops[n], top)
                        scores[n].append(piece)
                tops = [jnp.max(top, axis=0, keepdims=True) for top in tops]
                totals = [0.0, 0.0]
                for i in range(chunks):
                    for n, at in enumerate(froms):
                        weights = jnp.exp2((scores[n][i] - tops[n]).astype(jnp.bfloat16))
                        from_key = pl.multiple_of(at + i * 256, 128)
                        totals[n] += nn_dot(vt_scr[:, pl.ds(from_key, 256)], weights)
                for each, total in zip(pair, totals):
                    attended = total[0:dim] * (1.0 / total[dim : dim + 1])
                    out_ref[each[0], step] = jnp.transpose(attended)

            for chunks in range(1, span // 256 + 2):
                for inner in (False, True) if chunks > 4 else (None,):
                    wanted = count == chunks
                    if inner is not None:
                        wanted &= clear == inner

                    @pl.when(wanted)
                    def _(chunks=chunks, inner=inner):
                        variant(chunks, bool(inner))

            return carry

        lax.fori_loop(0, peers // 2, one_pair, 0)
        extra_ref[step] = jnp.zeros(extra_ref.shape[1:], jnp.float32)

        @pl.when((half == 0) & (core == 1))
        def _():
            near = span - HALF
            width = HALF + 128
            q = jnp.broadcast_to(q_lone, (pad, dim)).astype(jnp.bfloat16)
            scores = nt_dot(q, k_scr[near : near + width, :])
            key = near + lax.broadcasted_iota(jnp.int32, (1, width), 1)
            scores = jnp.where((key >= span - window) & (key <= span), scores, HIDDEN_MASK)
            top = jnp.max(scores, axis=1, keepdims=True)
            weights = jnp.exp2(scores - top).astype(jnp.bfloat16)
            total = nt_dot(weights, vt_scr[:, near : near + width])
            extra_ref[step] = total[:, 0:dim] / total[:, dim : dim + 1]
        return carry

    lax.fori_loop(0, extra_ref.shape[0], one_head, 0)


def attend(place, half_window, boundaries, packets, forwarded, share, rows, first, after):
    own, other = packets
    peers, heads = other.shape[:2]
    fwd_heads, pad, dim = forwarded.shape
    scr_rows = 2 * peers * rows + 256
    out_shapes = [(peers, heads, rows, dim), (heads, pad, dim)]
    return in_vmem(
        functools.partial(attend_kernel, peers, rows, share, first, fwd_heads),
        "attend",
        [place, half_window, boundaries],
        [*own, other, forwarded],
        after,
        [jax.ShapeDtypeStruct(shape, jnp.float32) for shape in out_shapes],
        flops=4 * heads * peers * rows * HALF * 2 * dim,
        scratch=[
            pltpu.VMEM((scr_rows, dim), jnp.bfloat16),
            pltpu.VMEM((dim + 16, scr_rows), jnp.bfloat16),
            pltpu.VMEM((peers, rows, dim), jnp.bfloat16),
        ],
    )


def finish_kernel(peers, share, first, unit_epsilon, place_ref, *refs):
    att_ref, base_in_ref, base_out_ref, own_ref, other_ref, patch_ref = refs[:6]
    queries = refs[6 : 6 + peers]
    outs = refs[-2 - peers : -2]
    grad_in_scr, grad_out_scr = refs[-2:]
    chip, core, half = place_ref[0], place_ref[1], place_ref[2]
    rows = att_ref.shape[2]
    hid = base_out_ref.shape[1]
    part = hid // 2

    def one_head(step, carry):
        head = chip * share + first + step
        for summed, lane in ((own_ref, core), (other_ref, 1 - core)):
            at = pl.multiple_of(lane * part, part)
            grad_in_scr[pl.ds(at, part), :] = summed[step, 0:part, :].astype(jnp.float32)
            grad_in_scr[pl.ds(hid + at, part), :] = summed[step, part : 2 * part, :].astype(jnp.float32)
            grad_out_scr[pl.ds(at, part), :] = summed[step, 2 * part :, :].astype(jnp.float32)

        def renewed(base, grad):
            base = base.astype(jnp.float32)
            updated = base - grad
            norm = jnp.sqrt(jnp.sum(base * base, axis=0, keepdims=True))
            squares = jnp.sum(updated * updated, axis=0, keepdims=True)
            return (updated * (norm / jnp.sqrt(squares + epsilon))).astype(jnp.bfloat16)

        new_in = renewed(base_in_ref[head], jnp.transpose(grad_in_scr[...]))
        new_out = renewed(base_out_ref[head], grad_out_scr[...])
        patch = patch_ref[step, 0:8, :][0:1]
        row = lax.broadcasted_iota(jnp.int32, (rows, 1), 0)
        for p in range(peers):
            q = queries[p][step, 0:rows, :].astype(jnp.float32)
            unit = (q * lax.rsqrt(jnp.sum(q * q, axis=1, keepdims=True) + unit_epsilon)).astype(
                jnp.bfloat16
            )
            pre = nn_dot(unit, new_in)
            gate = pre[:, :hid]
            hidden = (gate * jax.nn.sigmoid(gate) * pre[:, hid:]).astype(jnp.bfloat16)
            patched = (half == 1) & (core == 0) & (chip == p)
            attended = jnp.where(patched & (row == 0), patch, att_ref[chip ^ p, step])
            outs[p][step] = (attended + nn_dot(hidden, new_out)).astype(jnp.bfloat16)
        return carry

    lax.fori_loop(0, att_ref.shape[1], one_head, 0)


def finish(place, attended, fast_in, fast_out, sums, patch, own, share, first, unit_epsilon, after):
    peers, heads, rows, dim = attended.shape
    hid = fast_out.shape[1]
    return in_vmem(
        functools.partial(finish_kernel, peers, share, first, unit_epsilon),
        "finish",
        [place],
        [attended, fast_in, fast_out, *sums, patch, *own],
        after,
        [jax.ShapeDtypeStruct((heads, rows, dim), jnp.bfloat16)] * peers,
        flops=12 * heads * peers * rows * hid * dim,
        scratch=[pltpu.VMEM((2 * hid, dim), jnp.float32), pltpu.VMEM((hid, dim), jnp.float32)],
    )


def place_kernel(peers, chunks, share, place_ref, *refs):
    pieces, out_ref, sems = refs[:-2], refs[-2], refs[-1]
    copies = []
    for first, heads in chunks:
        for p in range(peers):
            at = (place_ref[0] ^ p) * share + first
            i = len(copies)
            copies.append(
                pltpu.make_async_copy(pieces[i], out_ref.at[pl.ds(at, heads)], sems.at[i])
            )
    for copy in copies:
        copy.start()
    for copy in copies:
        copy.wait()


def put_in_place(place, pieces, peers, chunks, share):
    _, rows, dim = pieces[0].shape
    return pl.pallas_call(
        functools.partial(place_kernel, peers, chunks, share),
        out_shape=jax.ShapeDtypeStruct((peers * share, rows, dim), jnp.bfloat16),
        in_specs=[pl.BlockSpec(memory_space=pltpu.SMEM)]
        + [pl.BlockSpec(memory_space=pltpu.VMEM)] * len(pieces),
        out_specs=pl.BlockSpec(memory_space=pl.ANY),
        scratch_shapes=[pltpu.SemaphoreType.DMA((len(pieces),))],
        compiler_params=pltpu.CompilerParams(vmem_limit_bytes=VMEM_BYTES),
        name="put_in_place",
    )(place, *pieces)


def regrouping(tok_peers, rows, heads, dim, hid):
    half_peers = tok_peers // 2
    peers = math.gcd(half_peers, heads)
    fits = tok_peers % 2 == 0 and half_peers * rows == 2 * HALF
    fits = fits and half_peers == 2 * peers and peers & (peers - 1) == 0
    fits = fits and rows % 256 == 0 and dim == 128 and hid % 256 == 0
    return peers if fits else 0


def regrouped_body(
    peers,
    query_rows,
    key_rows,
    value_rows,
    query_gain,
    key_gain,
    rate_in,
    rate_out,
    fast_in,
    fast_out,
    half_window,
    boundaries,
):
    rows, heads, dim = query_rows.shape
    share = heads // peers
    tok_peers = lax.axis_size("tok")
    half_peers = tok_peers // 2
    width_all = heads * dim * lax.axis_size("head")
    chunks = [(0, (share + 1) // 2), ((share + 1) // 2, share // 2)]
    aux_rows = 2 * -(-max(4 * (rows // 128), 3 * -(-share // chunks[0][1])) // 16) * 16
    own_index = lax.axis_index("tok")
    half = own_index // half_peers
    chip = own_index % half_peers // 2
    core = own_index % 2
    place = jnp.stack([chip, core, half]).astype(jnp.int32)

    def dealt(sent):
        pairs = [
            [(t, t // half_peers * half_peers + ((t % half_peers) ^ (2 * p))) for t in range(tok_peers)]
            for p in range(peers)
        ]
        return [sent[0]] + [exchanged(sent[p], pairs[p]) for p in range(1, peers)]

    core_pairs = [(t, t ^ 1) for t in range(tok_peers)]
    half_pairs = [(t, (t + half_peers) % tok_peers) for t in range(tok_peers)]
    forward_pairs = [(t + half_peers, t) for t in range(half_peers)]
    back_pairs = [(t, t - 1 + half_peers) for t in range(half_peers) if t % 2 == 1]

    q = jnp.transpose(query_rows, (1, 0, 2))
    k = jnp.transpose(key_rows, (1, 0, 2))
    v = jnp.transpose(value_rows, (1, 0, 2))
    q_float = q.astype(jnp.float32)
    k_float = k.astype(jnp.float32)
    squares = jnp.stack(
        [jnp.sum(q_float * q_float, axis=(0, 2)), jnp.sum(k_float * k_float, axis=(0, 2))]
    )
    if lax.axis_size("head") == 2:
        sums = (squares, lax.ppermute(squares, "head", [(0, 1), (1, 0)]))
    else:
        sums = (lax.psum(squares, "head"), jnp.zeros_like(squares))
    fold = math.log2(math.e) / math.sqrt(dim)
    sent = [
        pack(
            place,
            sums,
            q,
            k,
            v,
            (query_gain, key_gain),
            (rate_in, rate_out),
            peers,
            aux_rows,
            first,
            count,
            width_all,
            fold,
        )
        for first, count in chunks
    ]
    received = []
    for each in sent:
        if received:
            each = [lax.optimization_barrier(pair)[0] for pair in zip(each, received[-1])]
        received.append(dealt(each))
    def finished(ready, after):
        attended, sums, patch, own, first = ready
        return finish(
            place,
            attended,
            fast_in,
            fast_out,
            sums,
            patch,
            own,
            share,
            first,
            epsilon * fold * fold,
            after,
        )

    forwarded = ready = None
    pieces = []
    for (first, count), own in zip(chunks, received):
        if ready:
            *own, _ = lax.optimization_barrier((*own, ready[1][0]))
        else:
            own = lax.optimization_barrier((*own, *sent[-1]))[:peers]
        stack = stacked(own, rows)
        packets = (own, exchanged(stack, core_pairs))
        if forwarded is None:
            forwarded = exchanged(lone_rows(place, stack, packets[1], rows), forward_pairs)
        before = [ready[0]] if ready else []
        grad = gradients(place, fast_in, fast_out, packets, share, rows, first, before)
        from_half = exchanged(grad, half_pairs)
        before = [grad]
        if ready:
            outs = finished(ready, [grad])
            before.append(outs[0])
            pieces = pieces + dealt(outs)
        attended, extra = attend(
            place,
            half_window,
            boundaries,
            packets,
            forwarded,
            share,
            rows,
            first,
            before,
        )
        patch = exchanged(extra, back_pairs)
        from_half, _ = lax.optimization_barrier((from_half, attended))
        own_sum = (grad.astype(jnp.float32) + from_half.astype(jnp.float32)).astype(jnp.bfloat16)
        ready = (attended, (own_sum, exchanged(own_sum, core_pairs)), patch, own, first)
    pieces = pieces + dealt(finished(ready, pieces))
    whole = put_in_place(place, pieces, peers, chunks, share)
    return jnp.transpose(whole, (1, 0, 2))


def body(query_rows, *others):
    rows, heads, dim = query_rows.shape
    hid = others[7].shape[1]
    peers = regrouping(lax.axis_size("tok"), rows, heads, dim, hid)
    if peers:
        return regrouped_body(peers, query_rows, *others)
    return sliding_body(query_rows, *others)


def solution(mesh):
    in_specs = (
        P("tok", "head", None),
        P("tok", "head", None),
        P("tok", "head", None),
        P("head", None),
        P("head", None),
        P("head", "tok"),
        P("head", "tok"),
        P("head", None, None),
        P("head", None, None),
        P("head"),
        P(),
    )
    out_specs = P("tok", "head", None)
    return jax.shard_map(body, mesh=mesh, in_specs=in_specs, out_specs=out_specs, check_vma=False)
```

```python
import functools
import math

import jax
import jax.numpy as jnp
from jax import lax
from jax.experimental import pallas as pl
from jax.experimental.pallas import tpu as pltpu
from jax.sharding import PartitionSpec as P

HALF = 1024


epsilon = 1e-06


def passed_along(x, axis, by):
    peers = lax.axis_size(axis)
    pairs = [(i, i + by) for i in range(peers) if 0 <= i + by < peers]
    return lax.ppermute(x, axis, pairs)


def unit_rows(matrix):
    as_float = matrix.astype(jnp.float32)
    return (
        as_float * lax.rsqrt(jnp.sum(as_float * as_float, axis=-1, keepdims=True) + epsilon)
    ).astype(jnp.bfloat16)


def rescale(updated, base_norm, squares):
    return (updated * (base_norm / jnp.sqrt(squares + epsilon))[:, None, :]).astype(jnp.bfloat16)


def sliding_body(
    query_rows,
    key_rows,
    value_rows,
    query_gain,
    key_gain,
    rate_in,
    rate_out,
    fast_in,
    fast_out,
    half_window,
    boundaries,
):
    tok_rows = query_rows.shape[0]
    local_heads = query_rows.shape[1]
    head_dim = query_rows.shape[2]
    fast_hid = fast_out.shape[1]
    width_all = local_heads * head_dim * lax.axis_size("head")
    tok_count = tok_rows * lax.axis_size("tok")
    own_index = lax.axis_index("tok")
    first_row = own_index * tok_rows
    query_float = query_rows.astype(jnp.float32)
    key_float = key_rows.astype(jnp.float32)
    query_sq, key_sq = lax.psum(
        (
            jnp.sum(query_float * query_float, axis=(1, 2)),
            jnp.sum(key_float * key_float, axis=(1, 2)),
        ),
        "head",
    )
    q_normed = (
        query_float * lax.rsqrt(query_sq / width_all + epsilon)[:, None, None] * query_gain[None]
    ).astype(jnp.bfloat16)
    k_normed = (
        key_float * lax.rsqrt(key_sq / width_all + epsilon)[:, None, None] * key_gain[None]
    ).astype(jnp.bfloat16)

    def clip_of(places):
        return jnp.sum((places[:, None] >= boundaries[None, :]).astype(jnp.int32), axis=1)

    positions = first_row + jnp.arange(tok_rows, dtype=jnp.int32)
    query_clip = clip_of(positions)
    scaling = 1.0 / math.sqrt(head_dim)

    def absorb(state_now, block_keys, block_values, key_first):
        best, denominator, accum = state_now
        key_places = key_first + jnp.arange(tok_rows, dtype=jnp.int32)
        scores = (
            jnp.einsum("qhd,khd->hqk", q_normed, block_keys, preferred_element_type=jnp.float32)
            * scaling
        )
        inside = (key_places >= 0) & (key_places < tok_count)
        pair_ok = (query_clip[:, None] == clip_of(key_places)[None, :]) & inside[None, :]
        distance = jnp.abs(positions[:, None] - key_places[None, :])
        allowed = (distance[None, :, :] <= half_window[:, None, None]) & pair_ok[None, :, :]
        masked = jnp.where(allowed, scores, -jnp.inf)
        new_best = jnp.maximum(best, jnp.max(masked, axis=2))
        weights = jnp.exp(masked - new_best[:, :, None])
        shrink = jnp.exp(best - new_best)
        denominator = denominator * shrink + jnp.sum(weights, axis=2)
        accum = accum * shrink[:, :, None] + jnp.einsum(
            "hqk,khd->hqd",
            weights.astype(jnp.bfloat16),
            block_values,
            preferred_element_type=jnp.float32,
        )
        return (new_best, denominator, accum)

    start_state = (
        jnp.full((local_heads, tok_rows), -jnp.inf, jnp.float32),
        jnp.zeros((local_heads, tok_rows), jnp.float32),
        jnp.zeros((local_heads, tok_rows, head_dim), jnp.float32),
    )
    state_now = absorb(start_state, k_normed, value_rows, first_row)
    reach_blocks = HALF // tok_rows
    for distance_step in range(1, reach_blocks + 1):
        left_keys, left_values = passed_along((k_normed, value_rows), "tok", distance_step)
        state_now = absorb(state_now, left_keys, left_values, first_row - distance_step * tok_rows)
        right_keys, right_values = passed_along((k_normed, value_rows), "tok", -distance_step)
        state_now = absorb(
            state_now, right_keys, right_values, first_row + distance_step * tok_rows
        )
    attended = state_now[2] / state_now[1][:, :, None]
    key_unit = unit_rows(k_normed)
    query_unit = unit_rows(q_normed)
    pre_keys = jnp.einsum("thd,hdf->htf", key_unit, fast_in, preferred_element_type=jnp.float32)
    gate_part = pre_keys[:, :, :fast_hid]
    lin_part = pre_keys[:, :, fast_hid:]
    sigmoid_gate = jax.nn.sigmoid(gate_part)
    swish_gate = gate_part * sigmoid_gate
    hidden = (swish_gate * lin_part).astype(jnp.bfloat16)
    value_float = value_rows.astype(jnp.float32)
    push_out = (-jnp.transpose(rate_out)[:, :, None] * value_float).astype(jnp.bfloat16)
    push_in = (-jnp.transpose(rate_in)[:, :, None] * value_float).astype(jnp.bfloat16)
    grad_out = jnp.einsum("htf,thd->hfd", hidden, push_out, preferred_element_type=jnp.float32)
    hidden_grad = jnp.einsum("thd,hfd->htf", push_in, fast_out, preferred_element_type=jnp.float32)
    d_gate = hidden_grad * lin_part * sigmoid_gate * (1.0 + gate_part * (1.0 - sigmoid_gate))
    d_lin = hidden_grad * swish_gate
    d_pre = jnp.concatenate([d_gate, d_lin], axis=2).astype(jnp.bfloat16)
    grad_in = jnp.einsum("thd,htf->hdf", key_unit, d_pre, preferred_element_type=jnp.float32)
    in_float = fast_in.astype(jnp.float32)
    out_float = fast_out.astype(jnp.float32)
    in_base = jnp.sqrt(jnp.sum(in_float * in_float, axis=1))
    out_base = jnp.sqrt(jnp.sum(out_float * out_float, axis=1))
    summed_in, summed_out = lax.psum((grad_in, grad_out), "tok")
    updated_in = in_float - summed_in
    updated_out = out_float - summed_out
    new_in = rescale(updated_in, in_base, jnp.sum(updated_in * updated_in, axis=1))
    new_out = rescale(updated_out, out_base, jnp.sum(updated_out * updated_out, axis=1))
    pre_query = jnp.einsum("thd,hdf->htf", query_unit, new_in, preferred_element_type=jnp.float32)
    query_gate = pre_query[:, :, :fast_hid]
    query_hidden = (query_gate * jax.nn.sigmoid(query_gate) * pre_query[:, :, fast_hid:]).astype(
        jnp.bfloat16
    )
    fast_result = jnp.einsum(
        "htf,hfd->htd", query_hidden, new_out, preferred_element_type=jnp.float32
    )
    combined = attended + fast_result
    return jnp.transpose(combined, (1, 0, 2)).astype(jnp.bfloat16)


VMEM_BYTES = 24 * 1024 * 1024
HIDDEN_MASK = -1e30
NT = (((1,), (1,)), ((), ()))


def exchanged(x, pairs):
    return lax.ppermute(x, "tok", pairs)


def nt_dot(a, b):
    return lax.dot_general(a, b, NT, preferred_element_type=jnp.float32)


def nn_dot(a, b):
    return jnp.dot(a, b, preferred_element_type=jnp.float32)


def in_vmem(kernel, name, scalars, arrays, after, out_shape, flops=0, scratch=()):
    specs = [pl.BlockSpec(memory_space=pltpu.SMEM)] * len(scalars)
    specs += [pl.BlockSpec(memory_space=pltpu.VMEM)] * len(arrays)
    specs += [pl.BlockSpec(memory_space=pl.ANY)] * len(after)
    return pl.pallas_call(
        kernel,
        out_shape=out_shape,
        in_specs=specs,
        out_specs=jax.tree.map(lambda _: pl.BlockSpec(memory_space=pltpu.VMEM), out_shape),
        scratch_shapes=scratch,
        compiler_params=pltpu.CompilerParams(vmem_limit_bytes=VMEM_BYTES),
        cost_estimate=pl.CostEstimate(flops=16 * flops, bytes_accessed=0, transcendentals=0),
        name=name,
    )(*scalars, *arrays, *after)


def pack_kernel(peers, first, count, width_all, fold, with_lone, place_ref, *refs):
    squares_ref, more_ref, q_gain_ref, k_gain_ref, rate_in_ref, rate_out_ref = refs[:6]
    q_ref, k_ref, v_ref = refs[6:9]
    outs = refs[-3 - peers : -3]
    aux_ref, q_scale_ref, k_scale_ref = refs[-3:]
    rows, dim = q_scale_ref.shape
    share = q_gain_ref.shape[0] // peers
    scales = lax.rsqrt((squares_ref[...] + more_ref[...]) / width_all + epsilon)
    q_scale_ref[...] = jnp.transpose(jnp.broadcast_to(scales[0:1] * fold, (dim, rows)))
    k_scale_ref[...] = jnp.transpose(jnp.broadcast_to(scales[1:2], (dim, rows)))
    aux_ref[...] = jnp.zeros_like(aux_ref)

    def normed(ref, c, scale_ref, gain_ref, head, some):
        gain = gain_ref[pl.ds(c * share + head, 1), :]
        scaled = ref[c, head, 0:some].astype(jnp.float32) * scale_ref[0:some] * gain
        return scaled.astype(jnp.bfloat16)

    def one_head(step, carry):
        for p in range(peers):
            c = place_ref[0] ^ p
            head = first + step
            outs[p][step, 0:rows, :] = normed(q_ref, c, q_scale_ref, q_gain_ref, head, rows)
            outs[p][step, rows : 2 * rows, :] = normed(
                k_ref, c, k_scale_ref, k_gain_ref, head, rows
            )
            for i in range(0, rows, 128):
                outs[p][step, 2 * rows + i : 2 * rows + i + 128, :] = jnp.transpose(
                    v_ref[c, head, i : i + 128, :]
                )
            at = 0
            for rate_ref in (rate_in_ref, rate_out_ref):
                rate = rate_ref[pl.ds(c * share + head, 1), :]
                high = rate.astype(jnp.bfloat16).astype(jnp.float32)
                for part in (high, rate - high):
                    for i in range(0, rows, 128):
                        aux_ref[at : at + 1, :] = part[:, i : i + 128]
                        at += 1
            if with_lone:
                for i in range(-(-share // count)):
                    head = jnp.minimum(step + i * count, share - 1)
                    q0 = normed(q_ref, c, q_scale_ref, q_gain_ref, head, 16)
                    k0 = normed(k_ref, c, k_scale_ref, k_gain_ref, head, 16)
                    for at, array in enumerate((q0, k0, v_ref[c, head, 0:16])):
                        at += aux_ref.shape[0] // 2 + 3 * i
                        aux_ref[at : at + 1, :] = array.astype(jnp.float32)[0:1]
            some = outs[p].shape[1] - 3 * rows
            outs[p][step, 3 * rows :, :] = aux_ref[0:some, :].astype(jnp.bfloat16)
        return carry

    lax.fori_loop(0, count, one_head, 0)


def pack(place, sums, q, k, v, gains, rates, peers, aux_rows, first, count, width_all, fold):
    heads, rows, dim = q.shape
    out_shape = (count, 3 * rows + aux_rows // (2 if first else 1), dim)
    q, k, v = [x.reshape(peers, heads // peers, rows, dim) for x in (q, k, v)]
    return in_vmem(
        functools.partial(pack_kernel, peers, first, count, width_all, fold, not first),
        "pack",
        [place],
        [*sums, *gains, *rates, q, k, v],
        [],
        [jax.ShapeDtypeStruct(out_shape, jnp.bfloat16)] * peers,
        scratch=[
            pltpu.VMEM((aux_rows, dim), jnp.float32),
            pltpu.VMEM((rows, dim), jnp.float32),
            pltpu.VMEM((rows, dim), jnp.float32),
        ],
    )


def stack_kernel(from_row, *refs):
    for p, ref in enumerate(refs[:-1]):
        refs[-1][p] = ref[:, from_row:, :]


def stacked(arrays, from_row):
    heads, rows, dim = arrays[0].shape
    return in_vmem(
        functools.partial(stack_kernel, from_row),
        "stack",
        [],
        arrays,
        [],
        jax.ShapeDtypeStruct((len(arrays), heads, rows - from_row, dim), jnp.bfloat16),
    )


def lone_kernel(place_ref, own_ref, other_ref, out_ref):
    extra = out_ref.shape[1]
    at = own_ref.shape[2] - extra
    mine = jnp.full(out_ref.shape, place_ref[1]) == 0
    own = own_ref[place_ref[0], :, at:, :].astype(jnp.float32)
    other = other_ref[place_ref[0], :, at:, :].astype(jnp.float32)
    out_ref[...] = jnp.where(mine, own, other).astype(jnp.bfloat16)


def lone_rows(place, own, other, rows):
    _, count, all_rows, dim = own.shape
    out_shape = (count, (all_rows - 2 * rows) // 2, dim)
    return in_vmem(
        lone_kernel,
        "lone_rows",
        [place],
        [own, other],
        [],
        jax.ShapeDtypeStruct(out_shape, jnp.bfloat16),
    )


def key_value_blocks(peers, rows, step, refs):
    for p in range(peers):
        yield p, True, refs[p].at[step, rows : 2 * rows], refs[p].at[step, 2 * rows :]
        yield p, False, refs[peers].at[p, step, 0:rows], refs[peers].at[p, step, rows:]


def grads_kernel(peers, rows, rate_rows, share, first, place_ref, in_ref, out_ref, *refs):
    grad_ref = refs[-1]
    hid = out_ref.shape[1]
    part = hid // 2
    own = pl.multiple_of(place_ref[1] * part, part)

    def one_head(step, carry):
        head = place_ref[0] * share + first + step
        in_half = jnp.concatenate(
            [
                jnp.transpose(in_ref[head, :, pl.ds(at, part)].astype(jnp.float32))
                for at in (own, pl.multiple_of(hid + own, part))
            ],
            axis=0,
        ).astype(jnp.bfloat16)
        out_half = out_ref[head, pl.ds(own, part), :]
        sum_in = jnp.zeros((2 * part, in_half.shape[1]), jnp.float32)
        sum_out = jnp.zeros((part, in_half.shape[1]), jnp.float32)
        for _, _, keys, values in key_value_blocks(peers, rows, step, refs):
            k = keys[...].astype(jnp.float32)
            v_t = jnp.concatenate([values[at : at + 128, :] for at in range(0, rows, 128)], axis=1)
            aux = values[rows : rows + 16, :].astype(jnp.float32)

            def rate(at):
                both = aux[at : at + rate_rows] + aux[at + rate_rows : at + 2 * rate_rows]
                return jnp.concatenate([both[i : i + 1] for i in range(rate_rows)], axis=1)

            rate_in, rate_out = rate(0), rate(2 * rate_rows)
            unit = (k * lax.rsqrt(jnp.sum(k * k, axis=1, keepdims=True) + epsilon)).astype(
                jnp.bfloat16
            )
            pre = nt_dot(in_half, unit)
            gate, lin = pre[:part], pre[part:]
            sig = jax.nn.sigmoid(gate)
            swish = gate * sig
            pushed = (swish * lin * -rate_out).astype(jnp.bfloat16)
            hidden_grad = nn_dot(out_half, v_t) * -rate_in
            d_gate = hidden_grad * lin * sig * (1.0 + gate * (1.0 - sig))
            d_lin = hidden_grad * swish
            d_pre = jnp.concatenate([d_gate, d_lin], axis=0).astype(jnp.bfloat16)
            sum_in += nn_dot(d_pre, unit)
            sum_out += nt_dot(pushed, v_t)
        grad_ref[step, 0 : 2 * part, :] = sum_in.astype(jnp.bfloat16)
        grad_ref[step, 2 * part :, :] = sum_out.astype(jnp.bfloat16)
        return carry

    lax.fori_loop(0, grad_ref.shape[0], one_head, 0)


def gradients(place, fast_in, fast_out, packets, share, rows, first, after):
    _, hid, dim = fast_out.shape
    own, other = packets
    peers, heads = other.shape[:2]
    return in_vmem(
        functools.partial(grads_kernel, peers, rows, rows // 128, share, first),
        "gradients",
        [place],
        [fast_in, fast_out, *own, other],
        after,
        jax.ShapeDtypeStruct((heads, 3 * hid // 2, dim), jnp.bfloat16),
    )


def attend_kernel(peers, rows, share, first, fwd_heads, place_ref, window_ref, edge_ref, *refs):
    fwd_ref = refs[peers + 1]
    out_ref, extra_ref, k_scr, vt_scr, q_scr, s_scr, sum_scr = refs[-7:]
    span = 2 * peers * rows
    dim = k_scr.shape[1]
    pad = fwd_ref.shape[1]
    chip, core, half = place_ref[0], place_ref[1], place_ref[2]
    base = half * span
    limit = span + 1 - half
    k_scr[span:, :] = jnp.zeros((k_scr.shape[0] - span, dim), k_scr.dtype)
    vt_scr[:, span:] = jnp.zeros((vt_scr.shape[0], vt_scr.shape[1] - span), vt_scr.dtype)
    vt_scr[dim:, :] = jnp.ones((vt_scr.shape[0] - dim, vt_scr.shape[1]), vt_scr.dtype)

    def one_head(step, carry):
        window = window_ref[chip * share + first + step]
        for p, own, keys, values in key_value_blocks(peers, rows, step, refs):
            at = pl.multiple_of(((chip ^ p) * 2 + (core if own else 1 - core)) * rows, rows)
            k_scr[pl.ds(at, rows), :] = keys[...]
            for i in range(0, rows, 128):
                vt_scr[0:dim, pl.ds(pl.multiple_of(at + i, 128), 128)] = values[i : i + 128, :]
        for p in range(peers):
            q_scr[chip ^ p] = refs[p][step, 0:rows, :]
        fwd = fwd_ref[lax.rem(first + step, fwd_heads)].astype(jnp.float32)
        turn = (first + step) // fwd_heads
        q_lone, k_lone, v_lone = (
            sum(
                jnp.where(turn == t, fwd[3 * t + i : 3 * t + i + 1], 0.0)
                for t in range(-(-share // fwd_heads))
            )
            for i in range(3)
        )
        k_scr[span : span + pad, :] = jnp.broadcast_to(k_lone, (pad, dim)).astype(jnp.bfloat16)
        vt_scr[0:dim, span : span + 128] = jnp.transpose(
            jnp.broadcast_to(v_lone, (128, dim))
        ).astype(jnp.bfloat16)

        def clip_start(place):
            start = jnp.zeros_like(place)
            for i in range(edge_ref.shape[0]):
                start = jnp.maximum(start, jnp.where(edge_ref[i] <= place, edge_ref[i], 0))
            return start

        def clip_stop(place):
            stop = jnp.full_like(place, base + limit)
            for i in range(edge_ref.shape[0]):
                stop = jnp.minimum(stop, jnp.where(edge_ref[i] > place, edge_ref[i], base + limit))
            return stop

        def lowest(place):
            return jnp.maximum(jnp.maximum(place - window, clip_start(place)), base) - base

        def highest(place):
            return jnp.minimum(place + window, clip_stop(place) - 1) - base

        blocks = []
        count = 1
        for c in range(peers):
            start = (c * 2 + core) * rows
            places = base + start + lax.broadcasted_iota(jnp.int32, (1, rows), 1)
            from_key = lowest(base + start) // 128 * 128
            pieces = (highest(base + start + rows - 1) - from_key) // 256 + 1
            count = jnp.maximum(count, pieces)
            blocks.append((from_key, lowest(places), highest(places)))
        last = k_scr.shape[0] - count * 256
        froms = [jnp.minimum(from_key, last) for from_key, _, _ in blocks]
        key = lax.broadcasted_iota(jnp.int32, (256, rows), 0)

        def piece_at(i, at):
            return pl.ds(pl.multiple_of(at + i * 256, 128), 256)

        def score(i, tops):
            new = []
            for c, (at, (_, low, high)) in enumerate(zip(froms, blocks)):
                piece = nt_dot(k_scr[piece_at(i, at), :], q_scr[c])
                seen = (key >= low - at - i * 256) & (key <= high - at - i * 256)
                piece = jnp.where(seen, piece, HIDDEN_MASK)
                s_scr[c, piece_at(i, 0), :] = piece
                new.append(jnp.maximum(tops[c], jnp.max(piece.reshape(32, 8, rows), axis=0)))
            return tuple(new)

        tops = lax.fori_loop(
            0, count, score, (jnp.full((8, rows), HIDDEN_MASK, jnp.float32),) * peers
        )
        tops = [jnp.max(top, axis=0, keepdims=True) for top in tops]
        sum_scr[...] = jnp.zeros_like(sum_scr)

        def weigh(i, carry):
            for c, at in enumerate(froms):
                below = s_scr[c, piece_at(i, 0), :] - tops[c]
                weights = jnp.exp2(below.astype(jnp.bfloat16))
                sum_scr[c] += nn_dot(vt_scr[:, piece_at(i, at)], weights)
            return carry

        lax.fori_loop(0, count, weigh, 0)
        for c in range(peers):
            attended = sum_scr[c, 0:dim] * (1.0 / sum_scr[c, dim : dim + 1])
            out_ref[c, step] = jnp.transpose(attended)
        extra_ref[step] = jnp.zeros(extra_ref.shape[1:], jnp.float32)

        @pl.when((half == 0) & (core == 1))
        def _():
            near = span - HALF
            width = HALF + 128
            q = jnp.broadcast_to(q_lone, (pad, dim)).astype(jnp.bfloat16)
            scores = nt_dot(q, k_scr[near : near + width, :])
            key = near + lax.broadcasted_iota(jnp.int32, (1, width), 1)
            scores = jnp.where((key >= span - window) & (key <= span), scores, HIDDEN_MASK)
            top = jnp.max(scores, axis=1, keepdims=True)
            weights = jnp.exp2(scores - top).astype(jnp.bfloat16)
            total = nt_dot(weights, vt_scr[:, near : near + width])
            extra_ref[step] = total[:, 0:dim] / total[:, dim : dim + 1]
        return carry

    lax.fori_loop(0, extra_ref.shape[0], one_head, 0)


def attend(place, half_window, boundaries, packets, forwarded, share, rows, first, after):
    own, other = packets
    peers, heads = other.shape[:2]
    fwd_heads, pad, dim = forwarded.shape
    scr_rows = 2 * peers * rows + 256
    out_shapes = [(peers, heads, rows, dim), (heads, pad, dim)]
    return in_vmem(
        functools.partial(attend_kernel, peers, rows, share, first, fwd_heads),
        "attend",
        [place, half_window, boundaries],
        [*own, other, forwarded],
        after,
        [jax.ShapeDtypeStruct(shape, jnp.float32) for shape in out_shapes],
        flops=4 * heads * peers * rows * HALF * 2 * dim,
        scratch=[
            pltpu.VMEM((scr_rows, dim), jnp.bfloat16),
            pltpu.VMEM((dim + 16, scr_rows), jnp.bfloat16),
            pltpu.VMEM((peers, rows, dim), jnp.bfloat16),
            pltpu.VMEM((peers, scr_rows, rows), jnp.float32),
            pltpu.VMEM((peers, dim + 16, rows), jnp.float32),
        ],
    )


def finish_kernel(peers, share, first, unit_epsilon, place_ref, *refs):
    att_ref, base_in_ref, base_out_ref, own_ref, other_ref, patch_ref = refs[:6]
    queries = refs[6 : 6 + peers]
    outs = refs[-2 - peers : -2]
    grad_in_scr, grad_out_scr = refs[-2:]
    chip, core, half = place_ref[0], place_ref[1], place_ref[2]
    rows = att_ref.shape[2]
    hid = base_out_ref.shape[1]
    part = hid // 2

    def one_head(step, carry):
        head = chip * share + first + step
        for summed, lane in ((own_ref, core), (other_ref, 1 - core)):
            at = pl.multiple_of(lane * part, part)
            grad_in_scr[pl.ds(at, part), :] = summed[step, 0:part, :].astype(jnp.float32)
            grad_in_scr[pl.ds(hid + at, part), :] = summed[step, part : 2 * part, :].astype(jnp.float32)
            grad_out_scr[pl.ds(at, part), :] = summed[step, 2 * part :, :].astype(jnp.float32)

        def renewed(base, grad):
            base = base.astype(jnp.float32)
            updated = base - grad
            norm = jnp.sqrt(jnp.sum(base * base, axis=0, keepdims=True))
            squares = jnp.sum(updated * updated, axis=0, keepdims=True)
            return (updated * (norm / jnp.sqrt(squares + epsilon))).astype(jnp.bfloat16)

        new_in = renewed(base_in_ref[head], jnp.transpose(grad_in_scr[...]))
        new_out = renewed(base_out_ref[head], grad_out_scr[...])
        patch = patch_ref[step, 0:8, :][0:1]
        row = lax.broadcasted_iota(jnp.int32, (rows, 1), 0)
        for p in range(peers):
            q = queries[p][step, 0:rows, :].astype(jnp.float32)
            unit = (q * lax.rsqrt(jnp.sum(q * q, axis=1, keepdims=True) + unit_epsilon)).astype(
                jnp.bfloat16
            )
            pre = nn_dot(unit, new_in)
            gate = pre[:, :hid]
            hidden = (gate * jax.nn.sigmoid(gate) * pre[:, hid:]).astype(jnp.bfloat16)
            patched = (half == 1) & (core == 0) & (chip == p)
            attended = jnp.where(patched & (row == 0), patch, att_ref[chip ^ p, step])
            outs[p][step] = (attended + nn_dot(hidden, new_out)).astype(jnp.bfloat16)
        return carry

    lax.fori_loop(0, att_ref.shape[1], one_head, 0)


def finish(place, attended, fast_in, fast_out, sums, patch, own, share, first, unit_epsilon, after):
    peers, heads, rows, dim = attended.shape
    hid = fast_out.shape[1]
    return in_vmem(
        functools.partial(finish_kernel, peers, share, first, unit_epsilon),
        "finish",
        [place],
        [attended, fast_in, fast_out, *sums, patch, *own],
        after,
        [jax.ShapeDtypeStruct((heads, rows, dim), jnp.bfloat16)] * peers,
        flops=12 * heads * peers * rows * hid * dim,
        scratch=[pltpu.VMEM((2 * hid, dim), jnp.float32), pltpu.VMEM((hid, dim), jnp.float32)],
    )


def place_kernel(peers, chunks, share, place_ref, *refs):
    pieces, out_ref, sems = refs[:-2], refs[-2], refs[-1]
    copies = []
    for first, heads in chunks:
        for p in range(peers):
            at = (place_ref[0] ^ p) * share + first
            i = len(copies)
            copies.append(
                pltpu.make_async_copy(pieces[i], out_ref.at[pl.ds(at, heads)], sems.at[i])
            )
    for copy in copies:
        copy.start()
    for copy in copies:
        copy.wait()


def put_in_place(place, pieces, peers, chunks, share):
    _, rows, dim = pieces[0].shape
    return pl.pallas_call(
        functools.partial(place_kernel, peers, chunks, share),
        out_shape=jax.ShapeDtypeStruct((peers * share, rows, dim), jnp.bfloat16),
        in_specs=[pl.BlockSpec(memory_space=pltpu.SMEM)]
        + [pl.BlockSpec(memory_space=pltpu.VMEM)] * len(pieces),
        out_specs=pl.BlockSpec(memory_space=pl.ANY),
        scratch_shapes=[pltpu.SemaphoreType.DMA((len(pieces),))],
        compiler_params=pltpu.CompilerParams(vmem_limit_bytes=VMEM_BYTES),
        name="put_in_place",
    )(place, *pieces)


def regrouping(tok_peers, rows, heads, dim, hid):
    half_peers = tok_peers // 2
    peers = math.gcd(half_peers, heads)
    fits = tok_peers % 2 == 0 and half_peers * rows == 2 * HALF
    fits = fits and half_peers == 2 * peers and peers & (peers - 1) == 0
    fits = fits and rows % 256 == 0 and dim == 128 and hid % 256 == 0
    return peers if fits else 0


def regrouped_body(
    peers,
    query_rows,
    key_rows,
    value_rows,
    query_gain,
    key_gain,
    rate_in,
    rate_out,
    fast_in,
    fast_out,
    half_window,
    boundaries,
):
    rows, heads, dim = query_rows.shape
    share = heads // peers
    tok_peers = lax.axis_size("tok")
    half_peers = tok_peers // 2
    width_all = heads * dim * lax.axis_size("head")
    chunks = [(0, (share + 1) // 2), ((share + 1) // 2, share // 2)]
    aux_rows = 2 * -(-max(4 * (rows // 128), 3 * -(-share // chunks[0][1])) // 16) * 16
    own_index = lax.axis_index("tok")
    half = own_index // half_peers
    chip = own_index % half_peers // 2
    core = own_index % 2
    place = jnp.stack([chip, core, half]).astype(jnp.int32)

    def dealt(sent):
        pairs = [
            [(t, t // half_peers * half_peers + ((t % half_peers) ^ (2 * p))) for t in range(tok_peers)]
            for p in range(peers)
        ]
        return [sent[0]] + [exchanged(sent[p], pairs[p]) for p in range(1, peers)]

    core_pairs = [(t, t ^ 1) for t in range(tok_peers)]
    half_pairs = [(t, (t + half_peers) % tok_peers) for t in range(tok_peers)]
    forward_pairs = [(t + half_peers, t) for t in range(half_peers)]
    back_pairs = [(t, t - 1 + half_peers) for t in range(half_peers) if t % 2 == 1]

    q = jnp.transpose(query_rows, (1, 0, 2))
    k = jnp.transpose(key_rows, (1, 0, 2))
    v = jnp.transpose(value_rows, (1, 0, 2))
    q_float = q.astype(jnp.float32)
    k_float = k.astype(jnp.float32)
    squares = jnp.stack(
        [jnp.sum(q_float * q_float, axis=(0, 2)), jnp.sum(k_float * k_float, axis=(0, 2))]
    )
    if lax.axis_size("head") == 2:
        sums = (squares, lax.ppermute(squares, "head", [(0, 1), (1, 0)]))
    else:
        sums = (lax.psum(squares, "head"), jnp.zeros_like(squares))
    fold = math.log2(math.e) / math.sqrt(dim)
    sent = [
        pack(
            place,
            sums,
            q,
            k,
            v,
            (query_gain, key_gain),
            (rate_in, rate_out),
            peers,
            aux_rows,
            first,
            count,
            width_all,
            fold,
        )
        for first, count in chunks
    ]
    received = []
    for each in sent:
        if received:
            each = [lax.optimization_barrier(pair)[0] for pair in zip(each, received[-1])]
        received.append(dealt(each))
    def finished(ready, after):
        attended, sums, patch, own, first = ready
        return finish(
            place,
            attended,
            fast_in,
            fast_out,
            sums,
            patch,
            own,
            share,
            first,
            epsilon * fold * fold,
            after,
        )

    forwarded = ready = None
    pieces = []
    for (first, count), own in zip(chunks, received):
        if ready:
            *own, _ = lax.optimization_barrier((*own, ready[1][0]))
        else:
            own = lax.optimization_barrier((*own, *sent[-1]))[:peers]
        stack = stacked(own, rows)
        packets = (own, exchanged(stack, core_pairs))
        if forwarded is None:
            forwarded = exchanged(lone_rows(place, stack, packets[1], rows), forward_pairs)
        before = [ready[0]] if ready else []
        grad = gradients(place, fast_in, fast_out, packets, share, rows, first, before)
        from_half = exchanged(grad, half_pairs)
        before = [grad]
        if ready:
            outs = finished(ready, [grad])
            before.append(outs[0])
            pieces = pieces + dealt(outs)
        attended, extra = attend(
            place,
            half_window,
            boundaries,
            packets,
            forwarded,
            share,
            rows,
            first,
            before,
        )
        patch = exchanged(extra, back_pairs)
        from_half, _ = lax.optimization_barrier((from_half, attended))
        own_sum = (grad.astype(jnp.float32) + from_half.astype(jnp.float32)).astype(jnp.bfloat16)
        ready = (attended, (own_sum, exchanged(own_sum, core_pairs)), patch, own, first)
    pieces = pieces + dealt(finished(ready, pieces))
    whole = put_in_place(place, pieces, peers, chunks, share)
    return jnp.transpose(whole, (1, 0, 2))


def body(query_rows, *others):
    rows, heads, dim = query_rows.shape
    hid = others[7].shape[1]
    peers = regrouping(lax.axis_size("tok"), rows, heads, dim, hid)
    if peers:
        return regrouped_body(peers, query_rows, *others)
    return sliding_body(query_rows, *others)


def solution(mesh):
    in_specs = (
        P("tok", "head", None),
        P("tok", "head", None),
        P("tok", "head", None),
        P("head", None),
        P("head", None),
        P("head", "tok"),
        P("head", "tok"),
        P("head", None, None),
        P("head", None, None),
        P("head"),
        P(),
    )
    out_specs = P("tok", "head", None)
    return jax.shard_map(body, mesh=mesh, in_specs=in_specs, out_specs=out_specs, check_vma=False)
```

```python
import functools
import math

import jax
import jax.numpy as jnp
from jax import lax
from jax.experimental import pallas as pl
from jax.experimental.pallas import tpu as pltpu
from jax.sharding import PartitionSpec as P

HALF = 1024


epsilon = 1e-06


def passed_along(x, axis, by):
    peers = lax.axis_size(axis)
    pairs = [(i, i + by) for i in range(peers) if 0 <= i + by < peers]
    return lax.ppermute(x, axis, pairs)


def unit_rows(matrix):
    as_float = matrix.astype(jnp.float32)
    return (
        as_float * lax.rsqrt(jnp.sum(as_float * as_float, axis=-1, keepdims=True) + epsilon)
    ).astype(jnp.bfloat16)


def rescale(updated, base_norm, squares):
    return (updated * (base_norm / jnp.sqrt(squares + epsilon))[:, None, :]).astype(jnp.bfloat16)


def sliding_body(
    query_rows,
    key_rows,
    value_rows,
    query_gain,
    key_gain,
    rate_in,
    rate_out,
    fast_in,
    fast_out,
    half_window,
    boundaries,
):
    tok_rows = query_rows.shape[0]
    local_heads = query_rows.shape[1]
    head_dim = query_rows.shape[2]
    fast_hid = fast_out.shape[1]
    width_all = local_heads * head_dim * lax.axis_size("head")
    tok_count = tok_rows * lax.axis_size("tok")
    own_index = lax.axis_index("tok")
    first_row = own_index * tok_rows
    query_float = query_rows.astype(jnp.float32)
    key_float = key_rows.astype(jnp.float32)
    query_sq, key_sq = lax.psum(
        (
            jnp.sum(query_float * query_float, axis=(1, 2)),
            jnp.sum(key_float * key_float, axis=(1, 2)),
        ),
        "head",
    )
    q_normed = (
        query_float * lax.rsqrt(query_sq / width_all + epsilon)[:, None, None] * query_gain[None]
    ).astype(jnp.bfloat16)
    k_normed = (
        key_float * lax.rsqrt(key_sq / width_all + epsilon)[:, None, None] * key_gain[None]
    ).astype(jnp.bfloat16)

    def clip_of(places):
        return jnp.sum((places[:, None] >= boundaries[None, :]).astype(jnp.int32), axis=1)

    positions = first_row + jnp.arange(tok_rows, dtype=jnp.int32)
    query_clip = clip_of(positions)
    scaling = 1.0 / math.sqrt(head_dim)

    def absorb(state_now, block_keys, block_values, key_first):
        best, denominator, accum = state_now
        key_places = key_first + jnp.arange(tok_rows, dtype=jnp.int32)
        scores = (
            jnp.einsum("qhd,khd->hqk", q_normed, block_keys, preferred_element_type=jnp.float32)
            * scaling
        )
        inside = (key_places >= 0) & (key_places < tok_count)
        pair_ok = (query_clip[:, None] == clip_of(key_places)[None, :]) & inside[None, :]
        distance = jnp.abs(positions[:, None] - key_places[None, :])
        allowed = (distance[None, :, :] <= half_window[:, None, None]) & pair_ok[None, :, :]
        masked = jnp.where(allowed, scores, -jnp.inf)
        new_best = jnp.maximum(best, jnp.max(masked, axis=2))
        weights = jnp.exp(masked - new_best[:, :, None])
        shrink = jnp.exp(best - new_best)
        denominator = denominator * shrink + jnp.sum(weights, axis=2)
        accum = accum * shrink[:, :, None] + jnp.einsum(
            "hqk,khd->hqd",
            weights.astype(jnp.bfloat16),
            block_values,
            preferred_element_type=jnp.float32,
        )
        return (new_best, denominator, accum)

    start_state = (
        jnp.full((local_heads, tok_rows), -jnp.inf, jnp.float32),
        jnp.zeros((local_heads, tok_rows), jnp.float32),
        jnp.zeros((local_heads, tok_rows, head_dim), jnp.float32),
    )
    state_now = absorb(start_state, k_normed, value_rows, first_row)
    reach_blocks = HALF // tok_rows
    for distance_step in range(1, reach_blocks + 1):
        left_keys, left_values = passed_along((k_normed, value_rows), "tok", distance_step)
        state_now = absorb(state_now, left_keys, left_values, first_row - distance_step * tok_rows)
        right_keys, right_values = passed_along((k_normed, value_rows), "tok", -distance_step)
        state_now = absorb(
            state_now, right_keys, right_values, first_row + distance_step * tok_rows
        )
    attended = state_now[2] / state_now[1][:, :, None]
    key_unit = unit_rows(k_normed)
    query_unit = unit_rows(q_normed)
    pre_keys = jnp.einsum("thd,hdf->htf", key_unit, fast_in, preferred_element_type=jnp.float32)
    gate_part = pre_keys[:, :, :fast_hid]
    lin_part = pre_keys[:, :, fast_hid:]
    sigmoid_gate = jax.nn.sigmoid(gate_part)
    swish_gate = gate_part * sigmoid_gate
    hidden = (swish_gate * lin_part).astype(jnp.bfloat16)
    value_float = value_rows.astype(jnp.float32)
    push_out = (-jnp.transpose(rate_out)[:, :, None] * value_float).astype(jnp.bfloat16)
    push_in = (-jnp.transpose(rate_in)[:, :, None] * value_float).astype(jnp.bfloat16)
    grad_out = jnp.einsum("htf,thd->hfd", hidden, push_out, preferred_element_type=jnp.float32)
    hidden_grad = jnp.einsum("thd,hfd->htf", push_in, fast_out, preferred_element_type=jnp.float32)
    d_gate = hidden_grad * lin_part * sigmoid_gate * (1.0 + gate_part * (1.0 - sigmoid_gate))
    d_lin = hidden_grad * swish_gate
    d_pre = jnp.concatenate([d_gate, d_lin], axis=2).astype(jnp.bfloat16)
    grad_in = jnp.einsum("thd,htf->hdf", key_unit, d_pre, preferred_element_type=jnp.float32)
    in_float = fast_in.astype(jnp.float32)
    out_float = fast_out.astype(jnp.float32)
    in_base = jnp.sqrt(jnp.sum(in_float * in_float, axis=1))
    out_base = jnp.sqrt(jnp.sum(out_float * out_float, axis=1))
    summed_in, summed_out = lax.psum((grad_in, grad_out), "tok")
    updated_in = in_float - summed_in
    updated_out = out_float - summed_out
    new_in = rescale(updated_in, in_base, jnp.sum(updated_in * updated_in, axis=1))
    new_out = rescale(updated_out, out_base, jnp.sum(updated_out * updated_out, axis=1))
    pre_query = jnp.einsum("thd,hdf->htf", query_unit, new_in, preferred_element_type=jnp.float32)
    query_gate = pre_query[:, :, :fast_hid]
    query_hidden = (query_gate * jax.nn.sigmoid(query_gate) * pre_query[:, :, fast_hid:]).astype(
        jnp.bfloat16
    )
    fast_result = jnp.einsum(
        "htf,hfd->htd", query_hidden, new_out, preferred_element_type=jnp.float32
    )
    combined = attended + fast_result
    return jnp.transpose(combined, (1, 0, 2)).astype(jnp.bfloat16)


VMEM_BYTES = 16 * 1024 * 1024
HIDDEN_MASK = -1e30
NT = (((1,), (1,)), ((), ()))


def exchanged(x, pairs):
    return lax.ppermute(x, "tok", pairs)


def nt_dot(a, b):
    return lax.dot_general(a, b, NT, preferred_element_type=jnp.float32)


def nn_dot(a, b):
    return jnp.dot(a, b, preferred_element_type=jnp.float32)


def in_vmem(kernel, name, scalars, arrays, after, out_shape, flops=0, scratch=()):
    specs = [pl.BlockSpec(memory_space=pltpu.SMEM)] * len(scalars)
    specs += [pl.BlockSpec(memory_space=pltpu.VMEM)] * len(arrays)
    specs += [pl.BlockSpec(memory_space=pl.ANY)] * len(after)
    return pl.pallas_call(
        kernel,
        out_shape=out_shape,
        in_specs=specs,
        out_specs=jax.tree.map(lambda _: pl.BlockSpec(memory_space=pltpu.VMEM), out_shape),
        scratch_shapes=scratch,
        compiler_params=pltpu.CompilerParams(vmem_limit_bytes=VMEM_BYTES),
        cost_estimate=pl.CostEstimate(flops=16 * flops, bytes_accessed=0, transcendentals=0),
        name=name,
    )(*scalars, *arrays, *after)


def pack_kernel(peers, first, count, width_all, fold, with_lone, place_ref, *refs):
    squares_ref, more_ref, q_gain_ref, k_gain_ref, rate_in_ref, rate_out_ref = refs[:6]
    q_ref, k_ref, v_ref = refs[6:9]
    outs = refs[-3 - peers : -3]
    aux_ref, q_scale_ref, k_scale_ref = refs[-3:]
    rows, dim = q_scale_ref.shape
    share = q_gain_ref.shape[0] // peers
    scales = lax.rsqrt((squares_ref[...] + more_ref[...]) / width_all + epsilon)
    q_scale_ref[...] = jnp.transpose(jnp.broadcast_to(scales[0:1] * fold, (dim, rows)))
    k_scale_ref[...] = jnp.transpose(jnp.broadcast_to(scales[1:2], (dim, rows)))
    aux_ref[...] = jnp.zeros_like(aux_ref)

    def normed(ref, c, scale_ref, gain_ref, head, some):
        gain = gain_ref[pl.ds(c * share + head, 1), :]
        scaled = ref[c, head, 0:some].astype(jnp.float32) * scale_ref[0:some] * gain
        return scaled.astype(jnp.bfloat16)

    def one_head(step, carry):
        for p in range(peers):
            c = place_ref[0] ^ p
            head = first + step
            outs[p][step, 0:rows, :] = normed(q_ref, c, q_scale_ref, q_gain_ref, head, rows)
            outs[p][step, rows : 2 * rows, :] = normed(
                k_ref, c, k_scale_ref, k_gain_ref, head, rows
            )
            for i in range(0, rows, 128):
                outs[p][step, 2 * rows + i : 2 * rows + i + 128, :] = jnp.transpose(
                    v_ref[c, head, i : i + 128, :]
                )
            at = 0
            for rate_ref in (rate_in_ref, rate_out_ref):
                rate = rate_ref[pl.ds(c * share + head, 1), :]
                high = rate.astype(jnp.bfloat16).astype(jnp.float32)
                for part in (high, rate - high):
                    for i in range(0, rows, 128):
                        aux_ref[at : at + 1, :] = part[:, i : i + 128]
                        at += 1
            if with_lone:
                for i in range(-(-share // count)):
                    head = jnp.minimum(step + i * count, share - 1)
                    q0 = normed(q_ref, c, q_scale_ref, q_gain_ref, head, 16)
                    k0 = normed(k_ref, c, k_scale_ref, k_gain_ref, head, 16)
                    for at, array in enumerate((q0, k0, v_ref[c, head, 0:16])):
                        at += aux_ref.shape[0] // 2 + 3 * i
                        aux_ref[at : at + 1, :] = array.astype(jnp.float32)[0:1]
            some = outs[p].shape[1] - 3 * rows
            outs[p][step, 3 * rows :, :] = aux_ref[0:some, :].astype(jnp.bfloat16)
        return carry

    lax.fori_loop(0, count, one_head, 0)


def pack(place, sums, q, k, v, gains, rates, peers, aux_rows, first, count, width_all, fold):
    heads, rows, dim = q.shape
    out_shape = (count, 3 * rows + aux_rows // (2 if first else 1), dim)
    q, k, v = [x.reshape(peers, heads // peers, rows, dim) for x in (q, k, v)]
    return in_vmem(
        functools.partial(pack_kernel, peers, first, count, width_all, fold, not first),
        "pack",
        [place],
        [*sums, *gains, *rates, q, k, v],
        [],
        [jax.ShapeDtypeStruct(out_shape, jnp.bfloat16)] * peers,
        scratch=[
            pltpu.VMEM((aux_rows, dim), jnp.float32),
            pltpu.VMEM((rows, dim), jnp.float32),
            pltpu.VMEM((rows, dim), jnp.float32),
        ],
    )


def stack_kernel(from_row, *refs):
    for p, ref in enumerate(refs[:-1]):
        refs[-1][p] = ref[:, from_row:, :]


def stacked(arrays, from_row):
    heads, rows, dim = arrays[0].shape
    return in_vmem(
        functools.partial(stack_kernel, from_row),
        "stack",
        [],
        arrays,
        [],
        jax.ShapeDtypeStruct((len(arrays), heads, rows - from_row, dim), jnp.bfloat16),
    )


def lone_kernel(peers, place_ref, *refs):
    own, others, out_ref = refs[:peers], refs[peers:-1], refs[-1]
    extra = out_ref.shape[1]
    blocks = [ref.at[i] for ref in others for i in range(ref.shape[0])]
    for p in range(peers):
        for lane, ref in enumerate((own[p], blocks[p])):

            @pl.when((place_ref[0] == p) & (place_ref[1] == lane))
            def _(ref=ref):
                out_ref[...] = ref[:, ref.shape[1] - extra :, :]


def lone_rows(place, packets, extra):
    own, others = packets
    count, _, dim = own[0].shape
    return in_vmem(
        functools.partial(lone_kernel, len(own)),
        "lone_rows",
        [place],
        [*own, *others],
        [],
        jax.ShapeDtypeStruct((count, extra, dim), jnp.bfloat16),
    )


def key_value_blocks(peers, rows, step, refs):
    for p in range(peers):
        yield p, True, refs[p].at[step, rows : 2 * rows], refs[p].at[step, 2 * rows :]
    p = 0
    for ref in refs[peers:]:
        for i in range(ref.shape[0]):
            yield p, False, ref.at[i, step, 0:rows], ref.at[i, step, rows:]
            p += 1


def grads_kernel(peers, held, rows, rate_rows, share, first, place_ref, in_ref, out_ref, *refs):
    grad_ref = refs[-1]
    hid = out_ref.shape[1]
    part = hid // 2
    own = pl.multiple_of(place_ref[1] * part, part)

    def one_head(step, carry):
        head = place_ref[0] * share + first + step
        in_half = jnp.concatenate(
            [
                jnp.transpose(in_ref[head, :, pl.ds(at, part)].astype(jnp.float32))
                for at in (own, pl.multiple_of(hid + own, part))
            ],
            axis=0,
        ).astype(jnp.bfloat16)
        out_half = out_ref[head, pl.ds(own, part), :]
        sum_in = jnp.zeros((2 * part, in_half.shape[1]), jnp.float32)
        sum_out = jnp.zeros((part, in_half.shape[1]), jnp.float32)
        for _, _, keys, values in key_value_blocks(peers, rows, step, refs[:held]):
            k = keys[...].astype(jnp.float32)
            v_t = jnp.concatenate([values[at : at + 128, :] for at in range(0, rows, 128)], axis=1)
            aux = values[rows : rows + 16, :].astype(jnp.float32)

            def rate(at):
                both = aux[at : at + rate_rows] + aux[at + rate_rows : at + 2 * rate_rows]
                return jnp.concatenate([both[i : i + 1] for i in range(rate_rows)], axis=1)

            rate_in, rate_out = rate(0), rate(2 * rate_rows)
            unit = (k * lax.rsqrt(jnp.sum(k * k, axis=1, keepdims=True) + epsilon)).astype(
                jnp.bfloat16
            )
            pre = nt_dot(in_half, unit)
            gate, lin = pre[:part], pre[part:]
            sig = jax.nn.sigmoid(gate)
            swish = gate * sig
            pushed = (swish * lin * -rate_out).astype(jnp.bfloat16)
            hidden_grad = nn_dot(out_half, v_t) * -rate_in
            d_gate = hidden_grad * lin * sig * (1.0 + gate * (1.0 - sig))
            d_lin = hidden_grad * swish
            d_pre = jnp.concatenate([d_gate, d_lin], axis=0).astype(jnp.bfloat16)
            sum_in += nn_dot(d_pre, unit)
            sum_out += nt_dot(pushed, v_t)
        grad_ref[step, 0 : 2 * part, :] = sum_in.astype(jnp.bfloat16)
        grad_ref[step, 2 * part :, :] = sum_out.astype(jnp.bfloat16)
        return carry

    lax.fori_loop(0, grad_ref.shape[0], one_head, 0)


def gradients(place, fast_in, fast_out, packets, share, rows, first, after):
    _, hid, dim = fast_out.shape
    own, others = packets
    heads = others[0].shape[1]
    held = len(own) + len(others)
    return in_vmem(
        functools.partial(grads_kernel, len(own), held, rows, rows // 128, share, first),
        "gradients",
        [place],
        [fast_in, fast_out, *own, *others],
        after,
        jax.ShapeDtypeStruct((heads, 3 * hid // 2, dim), jnp.bfloat16),
    )


def attend_kernel(peers, held, rows, share, first, fwd_heads, place_ref, window_ref, edge_ref, *refs):
    fwd_ref = refs[held]
    out_ref, extra_ref, k_scr, vt_scr, q_scr = refs[-5:]
    span = 2 * peers * rows
    dim = k_scr.shape[1]
    pad = fwd_ref.shape[1]
    chip, core, half = place_ref[0], place_ref[1], place_ref[2]
    base = half * span
    limit = span + 1 - half
    k_scr[span:, :] = jnp.zeros((k_scr.shape[0] - span, dim), k_scr.dtype)
    vt_scr[:, span:] = jnp.zeros((vt_scr.shape[0], vt_scr.shape[1] - span), vt_scr.dtype)
    vt_scr[dim:, :] = jnp.ones((vt_scr.shape[0] - dim, vt_scr.shape[1]), vt_scr.dtype)

    def one_head(step, carry):
        window = window_ref[chip * share + first + step]
        for p, own, keys, values in key_value_blocks(peers, rows, step, refs[:held]):
            at = pl.multiple_of(((chip ^ p) * 2 + (core if own else 1 - core)) * rows, rows)
            k_scr[pl.ds(at, rows), :] = keys[...]
            for i in range(0, rows, 128):
                vt_scr[0:dim, pl.ds(pl.multiple_of(at + i, 128), 128)] = values[i : i + 128, :]
        for p in range(peers):
            q_scr[chip ^ p] = refs[p][step, 0:rows, :]
        fwd = fwd_ref[lax.rem(first + step, fwd_heads)].astype(jnp.float32)
        turn = (first + step) // fwd_heads
        q_lone, k_lone, v_lone = (
            sum(
                jnp.where(turn == t, fwd[3 * t + i : 3 * t + i + 1], 0.0)
                for t in range(-(-share // fwd_heads))
            )
            for i in range(3)
        )
        k_scr[span : span + pad, :] = jnp.broadcast_to(k_lone, (pad, dim)).astype(jnp.bfloat16)
        vt_scr[0:dim, span : span + 128] = jnp.transpose(
            jnp.broadcast_to(v_lone, (128, dim))
        ).astype(jnp.bfloat16)

        def clip_start(place):
            start = jnp.zeros_like(place)
            for i in range(edge_ref.shape[0]):
                start = jnp.maximum(start, jnp.where(edge_ref[i] <= place, edge_ref[i], 0))
            return start

        def clip_stop(place):
            stop = jnp.full_like(place, base + limit)
            for i in range(edge_ref.shape[0]):
                stop = jnp.minimum(stop, jnp.where(edge_ref[i] > place, edge_ref[i], base + limit))
            return stop

        def lowest(place):
            return jnp.maximum(jnp.maximum(place - window, clip_start(place)), base) - base

        def highest(place):
            return jnp.minimum(place + window, clip_stop(place) - 1) - base

        def one_pair(i, carry):
            pair = []
            for c in (i, peers - 1 - i):
                start = (c * 2 + core) * rows
                place = base + start + lax.broadcasted_iota(jnp.int32, (1, rows), 1)
                from_key = lowest(base + start) // 128 * 128
                count = (highest(base + start + rows - 1) - from_key) // 256 + 1
                pair.append((c, lowest(place), highest(place), from_key, count))
            count = jnp.maximum(pair[0][4], pair[1][4])

            def variant(chunks):
                froms = [
                    pl.multiple_of(jnp.minimum(each[3], k_scr.shape[0] - chunks * 256), 128)
                    for each in pair
                ]
                key = lax.broadcasted_iota(jnp.int32, (256, rows), 0)
                scores = [[], []]
                tops = [None, None]
                for i in range(chunks):
                    for n, (each, at) in enumerate(zip(pair, froms)):
                        from_key = pl.multiple_of(at + i * 256, 128)
                        piece = nt_dot(k_scr[pl.ds(from_key, 256), :], q_scr[each[0]])
                        seen = (key >= each[1] - from_key) & (key <= each[2] - from_key)
                        piece = jnp.where(seen, piece, HIDDEN_MASK)
                        top = jnp.max(piece.reshape(32, 8, rows), axis=0)
                        tops[n] = top if i == 0 else jnp.maximum(tops[n], top)
                        scores[n].append(piece)
                tops = [jnp.max(top, axis=0, keepdims=True) for top in tops]
                totals = [0.0, 0.0]
                for i in range(chunks):
                    for n, at in enumerate(froms):
                        weights = jnp.exp2(scores[n][i] - tops[n]).astype(jnp.bfloat16)
                        from_key = pl.multiple_of(at + i * 256, 128)
                        totals[n] += nn_dot(vt_scr[:, pl.ds(from_key, 256)], weights)
                for each, total in zip(pair, totals):
                    attended = total[0:dim] * (1.0 / total[dim : dim + 1])
                    out_ref[each[0], step] = jnp.transpose(attended)

            for chunks in range(1, span // 256 + 2):

                @pl.when(count == chunks)
                def _(chunks=chunks):
                    variant(chunks)

            return carry

        lax.fori_loop(0, peers // 2, one_pair, 0)
        extra_ref[step] = jnp.zeros(extra_ref.shape[1:], jnp.float32)

        @pl.when((half == 0) & (core == 1))
        def _():
            near = span - HALF
            width = HALF + 128
            q = jnp.broadcast_to(q_lone, (pad, dim)).astype(jnp.bfloat16)
            scores = nt_dot(q, k_scr[near : near + width, :])
            key = near + lax.broadcasted_iota(jnp.int32, (1, width), 1)
            scores = jnp.where((key >= span - window) & (key <= span), scores, HIDDEN_MASK)
            top = jnp.max(scores, axis=1, keepdims=True)
            weights = jnp.exp2(scores - top).astype(jnp.bfloat16)
            total = nt_dot(weights, vt_scr[:, near : near + width])
            extra_ref[step] = total[:, 0:dim] / total[:, dim : dim + 1]
        return carry

    lax.fori_loop(0, extra_ref.shape[0], one_head, 0)


def attend(place, half_window, boundaries, packets, forwarded, share, rows, first, after):
    own, others = packets
    peers, heads = len(own), others[0].shape[1]
    held = peers + len(others)
    fwd_heads, pad, dim = forwarded.shape
    scr_rows = 2 * peers * rows + 256
    out_shapes = [(peers, heads, rows, dim), (heads, pad, dim)]
    return in_vmem(
        functools.partial(attend_kernel, peers, held, rows, share, first, fwd_heads),
        "attend",
        [place, half_window, boundaries],
        [*own, *others, forwarded],
        after,
        [jax.ShapeDtypeStruct(shape, jnp.float32) for shape in out_shapes],
        flops=4 * heads * peers * rows * HALF * 2 * dim,
        scratch=[
            pltpu.VMEM((scr_rows, dim), jnp.bfloat16),
            pltpu.VMEM((dim + 16, scr_rows), jnp.bfloat16),
            pltpu.VMEM((peers, rows, dim), jnp.bfloat16),
        ],
    )


def finish_kernel(peers, share, first, unit_epsilon, place_ref, *refs):
    att_ref, base_in_ref, base_out_ref, own_ref, other_ref, patch_ref = refs[:6]
    queries = refs[6 : 6 + peers]
    outs = refs[-2 - peers : -2]
    grad_in_scr, grad_out_scr = refs[-2:]
    chip, core, half = place_ref[0], place_ref[1], place_ref[2]
    rows = att_ref.shape[2]
    hid = base_out_ref.shape[1]
    part = hid // 2

    def one_head(step, carry):
        head = chip * share + first + step
        for summed, lane in ((own_ref, core), (other_ref, 1 - core)):
            at = pl.multiple_of(lane * part, part)
            grad_in_scr[pl.ds(at, part), :] = summed[step, 0:part, :].astype(jnp.float32)
            grad_in_scr[pl.ds(hid + at, part), :] = summed[step, part : 2 * part, :].astype(jnp.float32)
            grad_out_scr[pl.ds(at, part), :] = summed[step, 2 * part :, :].astype(jnp.float32)

        def renewed(base, grad):
            base = base.astype(jnp.float32)
            updated = base - grad
            norm = jnp.sqrt(jnp.sum(base * base, axis=0, keepdims=True))
            squares = jnp.sum(updated * updated, axis=0, keepdims=True)
            return (updated * (norm / jnp.sqrt(squares + epsilon))).astype(jnp.bfloat16)

        new_in = renewed(base_in_ref[head], jnp.transpose(grad_in_scr[...]))
        new_out = renewed(base_out_ref[head], grad_out_scr[...])
        patch = patch_ref[step, 0:8, :][0:1]
        row = lax.broadcasted_iota(jnp.int32, (rows, 1), 0)
        for p in range(peers):
            q = queries[p][step, 0:rows, :].astype(jnp.float32)
            unit = (q * lax.rsqrt(jnp.sum(q * q, axis=1, keepdims=True) + unit_epsilon)).astype(
                jnp.bfloat16
            )
            pre = nn_dot(unit, new_in)
            gate = pre[:, :hid]
            hidden = (gate * jax.nn.sigmoid(gate) * pre[:, hid:]).astype(jnp.bfloat16)
            patched = (half == 1) & (core == 0) & (chip == p)
            attended = jnp.where(patched & (row == 0), patch, att_ref[chip ^ p, step])
            outs[p][step] = (attended + nn_dot(hidden, new_out)).astype(jnp.bfloat16)
        return carry

    lax.fori_loop(0, att_ref.shape[1], one_head, 0)


def finish(place, attended, fast_in, fast_out, sums, patch, own, share, first, unit_epsilon, after):
    peers, heads, rows, dim = attended.shape
    hid = fast_out.shape[1]
    return in_vmem(
        functools.partial(finish_kernel, peers, share, first, unit_epsilon),
        "finish",
        [place],
        [attended, fast_in, fast_out, *sums, patch, *own],
        after,
        [jax.ShapeDtypeStruct((heads, rows, dim), jnp.bfloat16)] * peers,
        flops=12 * heads * peers * rows * hid * dim,
        scratch=[pltpu.VMEM((2 * hid, dim), jnp.float32), pltpu.VMEM((hid, dim), jnp.float32)],
    )


def place_kernel(peers, share, first, place_ref, *refs):
    pieces, out_ref, sems = refs[:peers], refs[-2], refs[-1]
    heads = pieces[0].shape[0]
    copies = [
        pltpu.make_async_copy(
            pieces[p],
            out_ref.at[pl.ds((place_ref[0] ^ p) * share + first, heads)],
            sems.at[p],
        )
        for p in range(peers)
    ]
    for copy in copies:
        copy.start()
    for copy in copies:
        copy.wait()


def put_in_place(place, pieces, whole, share, first):
    peers = len(pieces)
    _, rows, dim = pieces[0].shape
    anywhere = pl.BlockSpec(memory_space=pl.ANY)
    return pl.pallas_call(
        functools.partial(place_kernel, peers, share, first),
        out_shape=jax.ShapeDtypeStruct((peers * share, rows, dim), jnp.bfloat16),
        in_specs=[pl.BlockSpec(memory_space=pltpu.SMEM)]
        + [pl.BlockSpec(memory_space=pltpu.VMEM)] * peers
        + [anywhere] * len(whole),
        out_specs=anywhere,
        input_output_aliases={1 + peers: 0} if whole else {},
        scratch_shapes=[pltpu.SemaphoreType.DMA((peers,))],
        compiler_params=pltpu.CompilerParams(vmem_limit_bytes=VMEM_BYTES),
        name="put_in_place",
    )(place, *pieces, *whole)


def regrouping(tok_peers, rows, heads, dim, hid):
    half_peers = tok_peers // 2
    peers = math.gcd(half_peers, heads)
    fits = tok_peers % 2 == 0 and half_peers * rows == 2 * HALF
    fits = fits and half_peers == 2 * peers and peers & (peers - 1) == 0
    fits = fits and rows % 256 == 0 and dim == 128 and hid % 256 == 0
    return peers if fits else 0


def regrouped_body(
    peers,
    query_rows,
    key_rows,
    value_rows,
    query_gain,
    key_gain,
    rate_in,
    rate_out,
    fast_in,
    fast_out,
    half_window,
    boundaries,
):
    rows, heads, dim = query_rows.shape
    share = heads // peers
    tok_peers = lax.axis_size("tok")
    half_peers = tok_peers // 2
    width_all = heads * dim * lax.axis_size("head")
    chunks = [(0, (share + 1) // 2), ((share + 1) // 2, share // 2)]
    aux_rows = 2 * -(-max(4 * (rows // 128), 3 * -(-share // chunks[0][1])) // 16) * 16
    own_index = lax.axis_index("tok")
    half = own_index // half_peers
    chip = own_index % half_peers // 2
    core = own_index % 2
    place = jnp.stack([chip, core, half]).astype(jnp.int32)

    def dealt(sent):
        pairs = [
            [(t, t // half_peers * half_peers + ((t % half_peers) ^ (2 * p))) for t in range(tok_peers)]
            for p in range(peers)
        ]
        return [sent[0]] + [exchanged(sent[p], pairs[p]) for p in range(1, peers)]

    core_pairs = [(t, t ^ 1) for t in range(tok_peers)]
    half_pairs = [(t, (t + half_peers) % tok_peers) for t in range(tok_peers)]
    forward_pairs = [(t + half_peers, t) for t in range(half_peers)]
    back_pairs = [(t, t - 1 + half_peers) for t in range(half_peers) if t % 2 == 1]

    q = jnp.transpose(query_rows, (1, 0, 2))
    k = jnp.transpose(key_rows, (1, 0, 2))
    v = jnp.transpose(value_rows, (1, 0, 2))
    q_float = q.astype(jnp.float32)
    k_float = k.astype(jnp.float32)
    squares = jnp.stack(
        [jnp.sum(q_float * q_float, axis=(0, 2)), jnp.sum(k_float * k_float, axis=(0, 2))]
    )
    if lax.axis_size("head") == 2:
        sums = (squares, lax.ppermute(squares, "head", [(0, 1), (1, 0)]))
    else:
        sums = (lax.psum(squares, "head"), jnp.zeros_like(squares))
    fold = math.log2(math.e) / math.sqrt(dim)
    sent = [
        pack(
            place,
            sums,
            q,
            k,
            v,
            (query_gain, key_gain),
            (rate_in, rate_out),
            peers,
            aux_rows,
            first,
            count,
            width_all,
            fold,
        )
        for first, count in chunks
    ]
    received = []
    for each in sent:
        if received:
            each = [lax.optimization_barrier(pair)[0] for pair in zip(each, received[-1])]
        received.append(dealt(each))
    def finished(ready, after):
        attended, sums, patch, own, first = ready
        return finish(
            place,
            attended,
            fast_in,
            fast_out,
            sums,
            patch,
            own,
            share,
            first,
            epsilon * fold * fold,
            after,
        )

    forwarded = ready = None
    pieces = []
    for (first, count), own in zip(chunks, received):
        if ready:
            *own, _ = lax.optimization_barrier((*own, ready[1][0]))
        else:
            own = lax.optimization_barrier((*own, *sent[-1]))[:peers]
        if forwarded is None:
            others = [exchanged(stacked(own[:-1], rows), core_pairs)]
            farthest, _ = lax.optimization_barrier((own[-1], others[0]))
            own = [*own[:-1], farthest]
            others.append(exchanged(stacked([farthest], rows), core_pairs))
            packets = (own, others)
            forwarded = exchanged(lone_rows(place, packets, aux_rows // 2), forward_pairs)
        else:
            packets = (own, [exchanged(stacked(own, rows), core_pairs)])
        before = [ready[0]] if ready else []
        grad = gradients(place, fast_in, fast_out, packets, share, rows, first, before)
        from_half = exchanged(grad, half_pairs)
        before = [grad]
        if not ready and len(received) > 1:
            before += received[1][1:-1]
        if ready:
            outs = finished(ready, [grad])
            before.append(outs[0])
            pieces.append(dealt(outs))
        attended, extra = attend(
            place,
            half_window,
            boundaries,
            packets,
            forwarded,
            share,
            rows,
            first,
            before,
        )
        patch = exchanged(extra, back_pairs)
        from_half, _ = lax.optimization_barrier((from_half, attended))
        own_sum = (grad.astype(jnp.float32) + from_half.astype(jnp.float32)).astype(jnp.bfloat16)
        ready = (attended, (own_sum, exchanged(own_sum, core_pairs)), patch, own, first)
    pieces.append(dealt(finished(ready, sum(pieces, []))))
    whole = []
    for (first, _), chunk_pieces in zip(chunks, pieces):
        whole = [put_in_place(place, chunk_pieces, whole, share, first)]
    return jnp.transpose(whole[0], (1, 0, 2))


def body(query_rows, *others):
    rows, heads, dim = query_rows.shape
    hid = others[7].shape[1]
    peers = regrouping(lax.axis_size("tok"), rows, heads, dim, hid)
    if peers:
        return regrouped_body(peers, query_rows, *others)
    return sliding_body(query_rows, *others)


def solution(mesh):
    in_specs = (
        P("tok", "head", None),
        P("tok", "head", None),
        P("tok", "head", None),
        P("head", None),
        P("head", None),
        P("head", "tok"),
        P("head", "tok"),
        P("head", None, None),
        P("head", None, None),
        P("head"),
        P(),
    )
    out_specs = P("tok", "head", None)
    return jax.shard_map(body, mesh=mesh, in_specs=in_specs, out_specs=out_specs, check_vma=False)
```

```python
import functools
import math

import jax
import jax.numpy as jnp
from jax import lax
from jax.experimental import pallas as pl
from jax.experimental.pallas import tpu as pltpu
from jax.sharding import PartitionSpec as P

HALF = 1024


epsilon = 1e-06


def passed_along(x, axis, by):
    peers = lax.axis_size(axis)
    pairs = [(i, i + by) for i in range(peers) if 0 <= i + by < peers]
    return lax.ppermute(x, axis, pairs)


def unit_rows(matrix):
    as_float = matrix.astype(jnp.float32)
    return (
        as_float * lax.rsqrt(jnp.sum(as_float * as_float, axis=-1, keepdims=True) + epsilon)
    ).astype(jnp.bfloat16)


def rescale(updated, base_norm, squares):
    return (updated * (base_norm / jnp.sqrt(squares + epsilon))[:, None, :]).astype(jnp.bfloat16)


def sliding_body(
    query_rows,
    key_rows,
    value_rows,
    query_gain,
    key_gain,
    rate_in,
    rate_out,
    fast_in,
    fast_out,
    half_window,
    boundaries,
):
    tok_rows = query_rows.shape[0]
    local_heads = query_rows.shape[1]
    head_dim = query_rows.shape[2]
    fast_hid = fast_out.shape[1]
    width_all = local_heads * head_dim * lax.axis_size("head")
    tok_count = tok_rows * lax.axis_size("tok")
    own_index = lax.axis_index("tok")
    first_row = own_index * tok_rows
    query_float = query_rows.astype(jnp.float32)
    key_float = key_rows.astype(jnp.float32)
    query_sq, key_sq = lax.psum(
        (
            jnp.sum(query_float * query_float, axis=(1, 2)),
            jnp.sum(key_float * key_float, axis=(1, 2)),
        ),
        "head",
    )
    q_normed = (
        query_float * lax.rsqrt(query_sq / width_all + epsilon)[:, None, None] * query_gain[None]
    ).astype(jnp.bfloat16)
    k_normed = (
        key_float * lax.rsqrt(key_sq / width_all + epsilon)[:, None, None] * key_gain[None]
    ).astype(jnp.bfloat16)

    def clip_of(places):
        return jnp.sum((places[:, None] >= boundaries[None, :]).astype(jnp.int32), axis=1)

    positions = first_row + jnp.arange(tok_rows, dtype=jnp.int32)
    query_clip = clip_of(positions)
    scaling = 1.0 / math.sqrt(head_dim)

    def absorb(state_now, block_keys, block_values, key_first):
        best, denominator, accum = state_now
        key_places = key_first + jnp.arange(tok_rows, dtype=jnp.int32)
        scores = (
            jnp.einsum("qhd,khd->hqk", q_normed, block_keys, preferred_element_type=jnp.float32)
            * scaling
        )
        inside = (key_places >= 0) & (key_places < tok_count)
        pair_ok = (query_clip[:, None] == clip_of(key_places)[None, :]) & inside[None, :]
        distance = jnp.abs(positions[:, None] - key_places[None, :])
        allowed = (distance[None, :, :] <= half_window[:, None, None]) & pair_ok[None, :, :]
        masked = jnp.where(allowed, scores, -jnp.inf)
        new_best = jnp.maximum(best, jnp.max(masked, axis=2))
        weights = jnp.exp(masked - new_best[:, :, None])
        shrink = jnp.exp(best - new_best)
        denominator = denominator * shrink + jnp.sum(weights, axis=2)
        accum = accum * shrink[:, :, None] + jnp.einsum(
            "hqk,khd->hqd",
            weights.astype(jnp.bfloat16),
            block_values,
            preferred_element_type=jnp.float32,
        )
        return (new_best, denominator, accum)

    start_state = (
        jnp.full((local_heads, tok_rows), -jnp.inf, jnp.float32),
        jnp.zeros((local_heads, tok_rows), jnp.float32),
        jnp.zeros((local_heads, tok_rows, head_dim), jnp.float32),
    )
    state_now = absorb(start_state, k_normed, value_rows, first_row)
    reach_blocks = HALF // tok_rows
    for distance_step in range(1, reach_blocks + 1):
        left_keys, left_values = passed_along((k_normed, value_rows), "tok", distance_step)
        state_now = absorb(state_now, left_keys, left_values, first_row - distance_step * tok_rows)
        right_keys, right_values = passed_along((k_normed, value_rows), "tok", -distance_step)
        state_now = absorb(
            state_now, right_keys, right_values, first_row + distance_step * tok_rows
        )
    attended = state_now[2] / state_now[1][:, :, None]
    key_unit = unit_rows(k_normed)
    query_unit = unit_rows(q_normed)
    pre_keys = jnp.einsum("thd,hdf->htf", key_unit, fast_in, preferred_element_type=jnp.float32)
    gate_part = pre_keys[:, :, :fast_hid]
    lin_part = pre_keys[:, :, fast_hid:]
    sigmoid_gate = jax.nn.sigmoid(gate_part)
    swish_gate = gate_part * sigmoid_gate
    hidden = (swish_gate * lin_part).astype(jnp.bfloat16)
    value_float = value_rows.astype(jnp.float32)
    push_out = (-jnp.transpose(rate_out)[:, :, None] * value_float).astype(jnp.bfloat16)
    push_in = (-jnp.transpose(rate_in)[:, :, None] * value_float).astype(jnp.bfloat16)
    grad_out = jnp.einsum("htf,thd->hfd", hidden, push_out, preferred_element_type=jnp.float32)
    hidden_grad = jnp.einsum("thd,hfd->htf", push_in, fast_out, preferred_element_type=jnp.float32)
    d_gate = hidden_grad * lin_part * sigmoid_gate * (1.0 + gate_part * (1.0 - sigmoid_gate))
    d_lin = hidden_grad * swish_gate
    d_pre = jnp.concatenate([d_gate, d_lin], axis=2).astype(jnp.bfloat16)
    grad_in = jnp.einsum("thd,htf->hdf", key_unit, d_pre, preferred_element_type=jnp.float32)
    in_float = fast_in.astype(jnp.float32)
    out_float = fast_out.astype(jnp.float32)
    in_base = jnp.sqrt(jnp.sum(in_float * in_float, axis=1))
    out_base = jnp.sqrt(jnp.sum(out_float * out_float, axis=1))
    summed_in, summed_out = lax.psum((grad_in, grad_out), "tok")
    updated_in = in_float - summed_in
    updated_out = out_float - summed_out
    new_in = rescale(updated_in, in_base, jnp.sum(updated_in * updated_in, axis=1))
    new_out = rescale(updated_out, out_base, jnp.sum(updated_out * updated_out, axis=1))
    pre_query = jnp.einsum("thd,hdf->htf", query_unit, new_in, preferred_element_type=jnp.float32)
    query_gate = pre_query[:, :, :fast_hid]
    query_hidden = (query_gate * jax.nn.sigmoid(query_gate) * pre_query[:, :, fast_hid:]).astype(
        jnp.bfloat16
    )
    fast_result = jnp.einsum(
        "htf,hfd->htd", query_hidden, new_out, preferred_element_type=jnp.float32
    )
    combined = attended + fast_result
    return jnp.transpose(combined, (1, 0, 2)).astype(jnp.bfloat16)


VMEM_BYTES = 16 * 1024 * 1024
HIDDEN_MASK = -1e30
NT = (((1,), (1,)), ((), ()))


def exchanged(x, pairs):
    return lax.ppermute(x, "tok", pairs)


def nt_dot(a, b):
    return lax.dot_general(a, b, NT, preferred_element_type=jnp.float32)


def nn_dot(a, b):
    return jnp.dot(a, b, preferred_element_type=jnp.float32)


def in_vmem(kernel, name, scalars, arrays, after, out_shape, flops=0, scratch=()):
    specs = [pl.BlockSpec(memory_space=pltpu.SMEM)] * len(scalars)
    specs += [pl.BlockSpec(memory_space=pltpu.VMEM)] * len(arrays)
    specs += [pl.BlockSpec(memory_space=pl.ANY)] * len(after)
    return pl.pallas_call(
        kernel,
        out_shape=out_shape,
        in_specs=specs,
        out_specs=jax.tree.map(lambda _: pl.BlockSpec(memory_space=pltpu.VMEM), out_shape),
        scratch_shapes=scratch,
        compiler_params=pltpu.CompilerParams(vmem_limit_bytes=VMEM_BYTES),
        cost_estimate=pl.CostEstimate(flops=16 * flops, bytes_accessed=0, transcendentals=0),
        name=name,
    )(*scalars, *arrays, *after)


def head_at(place_ref, share, chip, i):
    return place_ref[3 + chip * share + i]


def pack_kernel(peers, first, count, width_all, fold, with_lone, place_ref, *refs):
    squares_ref, more_ref, q_gain_ref, k_gain_ref, rate_in_ref, rate_out_ref = refs[:6]
    q_ref, k_ref, v_ref = refs[6:9]
    outs = refs[-3 - peers : -3]
    aux_ref, q_scale_ref, k_scale_ref = refs[-3:]
    rows, dim = q_scale_ref.shape
    share = q_gain_ref.shape[0] // peers
    scales = lax.rsqrt((squares_ref[...] + more_ref[...]) / width_all + epsilon)
    q_scale_ref[...] = jnp.transpose(jnp.broadcast_to(scales[0:1] * fold, (dim, rows)))
    k_scale_ref[...] = jnp.transpose(jnp.broadcast_to(scales[1:2], (dim, rows)))
    aux_ref[...] = jnp.zeros_like(aux_ref)

    def normed(ref, scale_ref, gain_ref, head, some):
        gain = gain_ref[pl.ds(head, 1), :]
        scaled = ref[head, 0:some].astype(jnp.float32) * scale_ref[0:some] * gain
        return scaled.astype(jnp.bfloat16)

    def one_head(step, carry):
        for p in range(peers):
            c = place_ref[0] ^ p
            head = head_at(place_ref, share, c, first + step)
            outs[p][step, 0:rows, :] = normed(q_ref, q_scale_ref, q_gain_ref, head, rows)
            outs[p][step, rows : 2 * rows, :] = normed(
                k_ref, k_scale_ref, k_gain_ref, head, rows
            )
            for i in range(0, rows, 128):
                outs[p][step, 2 * rows + i : 2 * rows + i + 128, :] = jnp.transpose(
                    v_ref[head, i : i + 128, :]
                )
            at = 0
            for rate_ref in (rate_in_ref, rate_out_ref):
                rate = rate_ref[pl.ds(head, 1), :]
                high = rate.astype(jnp.bfloat16).astype(jnp.float32)
                for part in (high, rate - high):
                    for i in range(0, rows, 128):
                        aux_ref[at : at + 1, :] = part[:, i : i + 128]
                        at += 1
            if with_lone:
                for i in range(-(-share // count)):
                    head = head_at(place_ref, share, c, jnp.minimum(step + i * count, share - 1))
                    q0 = normed(q_ref, q_scale_ref, q_gain_ref, head, 16)
                    k0 = normed(k_ref, k_scale_ref, k_gain_ref, head, 16)
                    for at, array in enumerate((q0, k0, v_ref[head, 0:16])):
                        at += aux_ref.shape[0] // 2 + 3 * i
                        aux_ref[at : at + 1, :] = array.astype(jnp.float32)[0:1]
            some = outs[p].shape[1] - 3 * rows
            outs[p][step, 3 * rows :, :] = aux_ref[0:some, :].astype(jnp.bfloat16)
        return carry

    lax.fori_loop(0, count, one_head, 0)


def pack(place, sums, q, k, v, gains, rates, peers, aux_rows, first, count, width_all, fold):
    heads, rows, dim = q.shape
    out_shape = (count, 3 * rows + aux_rows // (2 if first else 1), dim)
    return in_vmem(
        functools.partial(pack_kernel, peers, first, count, width_all, fold, not first),
        "pack",
        [place],
        [*sums, *gains, *rates, q, k, v],
        [],
        [jax.ShapeDtypeStruct(out_shape, jnp.bfloat16)] * peers,
        scratch=[
            pltpu.VMEM((aux_rows, dim), jnp.float32),
            pltpu.VMEM((rows, dim), jnp.float32),
            pltpu.VMEM((rows, dim), jnp.float32),
        ],
    )


def stack_kernel(from_row, *refs):
    for p, ref in enumerate(refs[:-1]):
        refs[-1][p] = ref[:, from_row:, :]


def stacked(arrays, from_row):
    heads, rows, dim = arrays[0].shape
    return in_vmem(
        functools.partial(stack_kernel, from_row),
        "stack",
        [],
        arrays,
        [],
        jax.ShapeDtypeStruct((len(arrays), heads, rows - from_row, dim), jnp.bfloat16),
    )


def lone_kernel(place_ref, own_ref, other_ref, out_ref):
    extra = out_ref.shape[1]
    at = own_ref.shape[2] - extra
    mine = jnp.full(out_ref.shape, place_ref[1]) == 0
    own = own_ref[place_ref[0], :, at:, :].astype(jnp.float32)
    other = other_ref[place_ref[0], :, at:, :].astype(jnp.float32)
    out_ref[...] = jnp.where(mine, own, other).astype(jnp.bfloat16)


def lone_rows(place, own, other, rows):
    _, count, all_rows, dim = own.shape
    out_shape = (count, (all_rows - 2 * rows) // 2, dim)
    return in_vmem(
        lone_kernel,
        "lone_rows",
        [place],
        [own, other],
        [],
        jax.ShapeDtypeStruct(out_shape, jnp.bfloat16),
    )


def key_value_blocks(peers, rows, step, refs):
    for p in range(peers):
        yield p, True, refs[p].at[step, rows : 2 * rows], refs[p].at[step, 2 * rows :]
        yield p, False, refs[peers].at[p, step, 0:rows], refs[peers].at[p, step, rows:]


def grads_kernel(peers, rows, rate_rows, share, first, place_ref, in_ref, out_ref, *refs):
    grad_ref = refs[-1]
    hid = out_ref.shape[1]
    part = hid // 2
    own = pl.multiple_of(place_ref[1] * part, part)

    def one_head(step, carry):
        head = head_at(place_ref, share, place_ref[0], first + step)
        in_half = jnp.concatenate(
            [
                jnp.transpose(in_ref[head, :, pl.ds(at, part)].astype(jnp.float32))
                for at in (own, pl.multiple_of(hid + own, part))
            ],
            axis=0,
        ).astype(jnp.bfloat16)
        out_half = out_ref[head, pl.ds(own, part), :]
        sum_in = jnp.zeros((2 * part, in_half.shape[1]), jnp.float32)
        sum_out = jnp.zeros((part, in_half.shape[1]), jnp.float32)
        for _, _, keys, values in key_value_blocks(peers, rows, step, refs):
            k = keys[...].astype(jnp.float32)
            v_t = jnp.concatenate([values[at : at + 128, :] for at in range(0, rows, 128)], axis=1)
            aux = values[rows : rows + 16, :].astype(jnp.float32)

            def rate(at):
                both = aux[at : at + rate_rows] + aux[at + rate_rows : at + 2 * rate_rows]
                return jnp.concatenate([both[i : i + 1] for i in range(rate_rows)], axis=1)

            rate_in, rate_out = rate(0), rate(2 * rate_rows)
            unit = (k * lax.rsqrt(jnp.sum(k * k, axis=1, keepdims=True) + epsilon)).astype(
                jnp.bfloat16
            )
            pre = nt_dot(in_half, unit)
            gate, lin = pre[:part], pre[part:]
            sig = jax.nn.sigmoid(gate)
            swish = gate * sig
            pushed = (swish * lin * -rate_out).astype(jnp.bfloat16)
            hidden_grad = nn_dot(out_half, v_t) * -rate_in
            d_gate = hidden_grad * lin * sig * (1.0 + gate * (1.0 - sig))
            d_lin = hidden_grad * swish
            d_pre = jnp.concatenate([d_gate, d_lin], axis=0).astype(jnp.bfloat16)
            sum_in += nn_dot(d_pre, unit)
            sum_out += nt_dot(pushed, v_t)
        grad_ref[step, 0 : 2 * part, :] = sum_in.astype(jnp.bfloat16)
        grad_ref[step, 2 * part :, :] = sum_out.astype(jnp.bfloat16)
        return carry

    lax.fori_loop(0, grad_ref.shape[0], one_head, 0)


def gradients(place, fast_in, fast_out, packets, share, rows, first, after):
    _, hid, dim = fast_out.shape
    own, other = packets
    peers, heads = other.shape[:2]
    return in_vmem(
        functools.partial(grads_kernel, peers, rows, rows // 128, share, first),
        "gradients",
        [place],
        [fast_in, fast_out, *own, other],
        after,
        jax.ShapeDtypeStruct((heads, 3 * hid // 2, dim), jnp.bfloat16),
    )


def attend_kernel(peers, rows, share, first, fwd_heads, place_ref, window_ref, edge_ref, *refs):
    fwd_ref = refs[peers + 1]
    out_ref, extra_ref, k_scr, vt_scr, q_scr = refs[-5:]
    span = 2 * peers * rows
    dim = k_scr.shape[1]
    pad = fwd_ref.shape[1]
    chip, core, half = place_ref[0], place_ref[1], place_ref[2]
    base = half * span
    limit = span + 1 - half
    k_scr[span:, :] = jnp.zeros((k_scr.shape[0] - span, dim), k_scr.dtype)
    vt_scr[:, span:] = jnp.zeros((vt_scr.shape[0], vt_scr.shape[1] - span), vt_scr.dtype)
    vt_scr[dim:, :] = jnp.ones((vt_scr.shape[0] - dim, vt_scr.shape[1]), vt_scr.dtype)

    def one_head(step, carry):
        window = window_ref[head_at(place_ref, share, chip, first + step)]
        for p, own, keys, values in key_value_blocks(peers, rows, step, refs):
            at = pl.multiple_of(((chip ^ p) * 2 + (core if own else 1 - core)) * rows, rows)
            k_scr[pl.ds(at, rows), :] = keys[...]
            for i in range(0, rows, 128):
                vt_scr[0:dim, pl.ds(pl.multiple_of(at + i, 128), 128)] = values[i : i + 128, :]
        for p in range(peers):
            q_scr[chip ^ p] = refs[p][step, 0:rows, :]
        fwd = fwd_ref[lax.rem(first + step, fwd_heads)].astype(jnp.float32)
        turn = (first + step) // fwd_heads
        q_lone, k_lone, v_lone = (
            sum(
                jnp.where(turn == t, fwd[3 * t + i : 3 * t + i + 1], 0.0)
                for t in range(-(-share // fwd_heads))
            )
            for i in range(3)
        )
        k_scr[span : span + pad, :] = jnp.broadcast_to(k_lone, (pad, dim)).astype(jnp.bfloat16)
        vt_scr[0:dim, span : span + 128] = jnp.transpose(
            jnp.broadcast_to(v_lone, (128, dim))
        ).astype(jnp.bfloat16)

        def clip_start(place):
            start = jnp.zeros_like(place)
            for i in range(edge_ref.shape[0]):
                start = jnp.maximum(start, jnp.where(edge_ref[i] <= place, edge_ref[i], 0))
            return start

        def clip_stop(place):
            stop = jnp.full_like(place, base + limit)
            for i in range(edge_ref.shape[0]):
                stop = jnp.minimum(stop, jnp.where(edge_ref[i] > place, edge_ref[i], base + limit))
            return stop

        def lowest(place):
            return jnp.maximum(jnp.maximum(place - window, clip_start(place)), base) - base

        def highest(place):
            return jnp.minimum(place + window, clip_stop(place) - 1) - base

        def one_pair(i, carry):
            pair = []
            for c in (i, peers - 1 - i):
                start = (c * 2 + core) * rows
                place = base + start + lax.broadcasted_iota(jnp.int32, (1, rows), 1)
                from_key = lowest(base + start) // 128 * 128
                count = (highest(base + start + rows - 1) - from_key) // 256 + 1
                pair.append((c, lowest(place), highest(place), from_key, count))
            count = jnp.maximum(pair[0][4], pair[1][4])

            def variant(chunks):
                froms = [
                    pl.multiple_of(jnp.minimum(each[3], k_scr.shape[0] - chunks * 256), 128)
                    for each in pair
                ]
                key = lax.broadcasted_iota(jnp.int32, (256, rows), 0)
                scores = [[], []]
                tops = [None, None]
                for i in range(chunks):
                    for n, (each, at) in enumerate(zip(pair, froms)):
                        from_key = pl.multiple_of(at + i * 256, 128)
                        piece = nt_dot(k_scr[pl.ds(from_key, 256), :], q_scr[each[0]])
                        seen = (key >= each[1] - from_key) & (key <= each[2] - from_key)
                        piece = jnp.where(seen, piece, HIDDEN_MASK)
                        top = jnp.max(piece.reshape(32, 8, rows), axis=0)
                        tops[n] = top if i == 0 else jnp.maximum(tops[n], top)
                        scores[n].append(piece)
                tops = [jnp.max(top, axis=0, keepdims=True) for top in tops]
                totals = [0.0, 0.0]
                for i in range(chunks):
                    for n, at in enumerate(froms):
                        weights = jnp.exp2(scores[n][i] - tops[n]).astype(jnp.bfloat16)
                        from_key = pl.multiple_of(at + i * 256, 128)
                        totals[n] += nn_dot(vt_scr[:, pl.ds(from_key, 256)], weights)
                for each, total in zip(pair, totals):
                    attended = total[0:dim] * (1.0 / total[dim : dim + 1])
                    out_ref[each[0], step] = jnp.transpose(attended)

            for chunks in range(1, span // 256 + 2):

                @pl.when(count == chunks)
                def _(chunks=chunks):
                    variant(chunks)

            return carry

        lax.fori_loop(0, peers // 2, one_pair, 0)
        extra_ref[step] = jnp.zeros(extra_ref.shape[1:], jnp.float32)

        @pl.when((half == 0) & (core == 1))
        def _():
            near = span - HALF
            width = HALF + 128
            q = jnp.broadcast_to(q_lone, (pad, dim)).astype(jnp.bfloat16)
            scores = nt_dot(q, k_scr[near : near + width, :])
            key = near + lax.broadcasted_iota(jnp.int32, (1, width), 1)
            scores = jnp.where((key >= span - window) & (key <= span), scores, HIDDEN_MASK)
            top = jnp.max(scores, axis=1, keepdims=True)
            weights = jnp.exp2(scores - top).astype(jnp.bfloat16)
            total = nt_dot(weights, vt_scr[:, near : near + width])
            extra_ref[step] = total[:, 0:dim] / total[:, dim : dim + 1]
        return carry

    lax.fori_loop(0, extra_ref.shape[0], one_head, 0)


def attend(place, half_window, boundaries, packets, forwarded, share, rows, first, after):
    own, other = packets
    peers, heads = other.shape[:2]
    fwd_heads, pad, dim = forwarded.shape
    scr_rows = 2 * peers * rows + 256
    out_shapes = [(peers, heads, rows, dim), (heads, pad, dim)]
    return in_vmem(
        functools.partial(attend_kernel, peers, rows, share, first, fwd_heads),
        "attend",
        [place, half_window, boundaries],
        [*own, other, forwarded],
        after,
        [jax.ShapeDtypeStruct(shape, jnp.float32) for shape in out_shapes],
        flops=4 * heads * peers * rows * HALF * 2 * dim,
        scratch=[
            pltpu.VMEM((scr_rows, dim), jnp.bfloat16),
            pltpu.VMEM((dim + 16, scr_rows), jnp.bfloat16),
            pltpu.VMEM((peers, rows, dim), jnp.bfloat16),
        ],
    )


def finish_kernel(peers, share, first, unit_epsilon, place_ref, *refs):
    att_ref, base_in_ref, base_out_ref, own_ref, other_ref, patch_ref = refs[:6]
    queries = refs[6 : 6 + peers]
    outs = refs[-2 - peers : -2]
    grad_in_scr, grad_out_scr = refs[-2:]
    chip, core, half = place_ref[0], place_ref[1], place_ref[2]
    rows = att_ref.shape[2]
    hid = base_out_ref.shape[1]
    part = hid // 2

    def one_head(step, carry):
        head = head_at(place_ref, share, chip, first + step)
        for summed, lane in ((own_ref, core), (other_ref, 1 - core)):
            at = pl.multiple_of(lane * part, part)
            grad_in_scr[pl.ds(at, part), :] = summed[step, 0:part, :].astype(jnp.float32)
            grad_in_scr[pl.ds(hid + at, part), :] = summed[step, part : 2 * part, :].astype(jnp.float32)
            grad_out_scr[pl.ds(at, part), :] = summed[step, 2 * part :, :].astype(jnp.float32)

        def renewed(base, grad):
            base = base.astype(jnp.float32)
            updated = base - grad
            norm = jnp.sqrt(jnp.sum(base * base, axis=0, keepdims=True))
            squares = jnp.sum(updated * updated, axis=0, keepdims=True)
            return (updated * (norm / jnp.sqrt(squares + epsilon))).astype(jnp.bfloat16)

        new_in = renewed(base_in_ref[head], jnp.transpose(grad_in_scr[...]))
        new_out = renewed(base_out_ref[head], grad_out_scr[...])
        patch = patch_ref[step, 0:8, :][0:1]
        row = lax.broadcasted_iota(jnp.int32, (rows, 1), 0)
        for p in range(peers):
            q = queries[p][step, 0:rows, :].astype(jnp.float32)
            unit = (q * lax.rsqrt(jnp.sum(q * q, axis=1, keepdims=True) + unit_epsilon)).astype(
                jnp.bfloat16
            )
            pre = nn_dot(unit, new_in)
            gate = pre[:, :hid]
            hidden = (gate * jax.nn.sigmoid(gate) * pre[:, hid:]).astype(jnp.bfloat16)
            patched = (half == 1) & (core == 0) & (chip == p)
            attended = jnp.where(patched & (row == 0), patch, att_ref[chip ^ p, step])
            outs[p][step] = (attended + nn_dot(hidden, new_out)).astype(jnp.bfloat16)
        return carry

    lax.fori_loop(0, att_ref.shape[1], one_head, 0)


def finish(place, attended, fast_in, fast_out, sums, patch, own, share, first, unit_epsilon, after):
    peers, heads, rows, dim = attended.shape
    hid = fast_out.shape[1]
    return in_vmem(
        functools.partial(finish_kernel, peers, share, first, unit_epsilon),
        "finish",
        [place],
        [attended, fast_in, fast_out, *sums, patch, *own],
        after,
        [jax.ShapeDtypeStruct((heads, rows, dim), jnp.bfloat16)] * peers,
        flops=12 * heads * peers * rows * hid * dim,
        scratch=[pltpu.VMEM((2 * hid, dim), jnp.float32), pltpu.VMEM((hid, dim), jnp.float32)],
    )


def place_kernel(peers, chunks, share, place_ref, *refs):
    pieces, out_ref, sems = refs[:-2], refs[-2], refs[-1]
    copies = []
    for n, (first, heads) in enumerate(chunks):
        for p in range(peers):
            for i in range(heads):
                head = head_at(place_ref, share, place_ref[0] ^ p, first + i)
                copies.append(
                    pltpu.make_async_copy(
                        pieces[n * peers + p].at[i], out_ref.at[head], sems.at[len(copies)]
                    )
                )
    for copy in copies:
        copy.start()
    for copy in copies:
        copy.wait()


def put_in_place(place, pieces, peers, chunks, share):
    _, rows, dim = pieces[0].shape
    return pl.pallas_call(
        functools.partial(place_kernel, peers, chunks, share),
        out_shape=jax.ShapeDtypeStruct((peers * share, rows, dim), jnp.bfloat16),
        in_specs=[pl.BlockSpec(memory_space=pltpu.SMEM)]
        + [pl.BlockSpec(memory_space=pltpu.VMEM)] * len(pieces),
        out_specs=pl.BlockSpec(memory_space=pl.ANY),
        scratch_shapes=[pltpu.SemaphoreType.DMA((peers * share,))],
        compiler_params=pltpu.CompilerParams(vmem_limit_bytes=VMEM_BYTES),
        name="put_in_place",
    )(place, *pieces)


def regrouping(tok_peers, rows, heads, dim, hid):
    half_peers = tok_peers // 2
    peers = math.gcd(half_peers, heads)
    fits = tok_peers % 2 == 0 and half_peers * rows == 2 * HALF
    fits = fits and half_peers == 2 * peers and peers & (peers - 1) == 0
    fits = fits and rows % 256 == 0 and dim == 128 and hid % 256 == 0
    return peers if fits else 0


def regrouped_body(
    peers,
    query_rows,
    key_rows,
    value_rows,
    query_gain,
    key_gain,
    rate_in,
    rate_out,
    fast_in,
    fast_out,
    half_window,
    boundaries,
):
    rows, heads, dim = query_rows.shape
    share = heads // peers
    tok_peers = lax.axis_size("tok")
    half_peers = tok_peers // 2
    width_all = heads * dim * lax.axis_size("head")
    chunks = [(0, (share + 1) // 2), ((share + 1) // 2, share // 2)]
    aux_rows = 2 * -(-max(4 * (rows // 128), 3 * -(-share // chunks[0][1])) // 16) * 16
    own_index = lax.axis_index("tok")
    half = own_index // half_peers
    chip = own_index % half_peers // 2
    core = own_index % 2
    number = jnp.arange(heads, dtype=jnp.int32)
    order = half_window * heads + number
    rank = jnp.sum((order[None, :] > order[:, None]).astype(jnp.int32), axis=1)
    turn, seat = rank // peers, rank % peers
    taker = jnp.where(turn % 2 == 0, seat, peers - 1 - seat)
    slot = taker * share + jnp.where(turn % 2 == 0, 0, chunks[0][1]) + turn // 2
    table = jnp.sum(jnp.where(slot[:, None] == number[None, :], number[:, None], 0), axis=0)
    place = jnp.concatenate([jnp.stack([chip, core, half]).astype(jnp.int32), table])

    def dealt(sent):
        pairs = [
            [(t, t // half_peers * half_peers + ((t % half_peers) ^ (2 * p))) for t in range(tok_peers)]
            for p in range(peers)
        ]
        return [sent[0]] + [exchanged(sent[p], pairs[p]) for p in range(1, peers)]

    core_pairs = [(t, t ^ 1) for t in range(tok_peers)]
    half_pairs = [(t, (t + half_peers) % tok_peers) for t in range(tok_peers)]
    forward_pairs = [(t + half_peers, t) for t in range(half_peers)]
    back_pairs = [(t, t - 1 + half_peers) for t in range(half_peers) if t % 2 == 1]

    q = jnp.transpose(query_rows, (1, 0, 2))
    k = jnp.transpose(key_rows, (1, 0, 2))
    v = jnp.transpose(value_rows, (1, 0, 2))
    q_float = q.astype(jnp.float32)
    k_float = k.astype(jnp.float32)
    squares = jnp.stack(
        [jnp.sum(q_float * q_float, axis=(0, 2)), jnp.sum(k_float * k_float, axis=(0, 2))]
    )
    if lax.axis_size("head") == 2:
        sums = (squares, lax.ppermute(squares, "head", [(0, 1), (1, 0)]))
    else:
        sums = (lax.psum(squares, "head"), jnp.zeros_like(squares))
    fold = math.log2(math.e) / math.sqrt(dim)
    sent = [
        pack(
            place,
            sums,
            q,
            k,
            v,
            (query_gain, key_gain),
            (rate_in, rate_out),
            peers,
            aux_rows,
            first,
            count,
            width_all,
            fold,
        )
        for first, count in chunks
    ]
    received = []
    for each in sent:
        if received:
            each = [lax.optimization_barrier(pair)[0] for pair in zip(each, received[-1])]
        received.append(dealt(each))
    def finished(ready, after):
        attended, sums, patch, own, first = ready
        return finish(
            place,
            attended,
            fast_in,
            fast_out,
            sums,
            patch,
            own,
            share,
            first,
            epsilon * fold * fold,
            after,
        )

    forwarded = ready = None
    pieces = []
    for (first, count), own in zip(chunks, received):
        if ready:
            *own, _ = lax.optimization_barrier((*own, ready[1][0]))
        else:
            own = lax.optimization_barrier((*own, *sent[-1]))[:peers]
        stack = stacked(own, rows)
        packets = (own, exchanged(stack, core_pairs))
        if forwarded is None:
            forwarded = exchanged(lone_rows(place, stack, packets[1], rows), forward_pairs)
        before = [ready[0]] if ready else []
        grad = gradients(place, fast_in, fast_out, packets, share, rows, first, before)
        from_half = exchanged(grad, half_pairs)
        before = [grad]
        if ready:
            outs = finished(ready, [grad])
            before.append(outs[0])
            pieces = pieces + dealt(outs)
        attended, extra = attend(
            place,
            half_window,
            boundaries,
            packets,
            forwarded,
            share,
            rows,
            first,
            before,
        )
        patch = exchanged(extra, back_pairs)
        from_half, _ = lax.optimization_barrier((from_half, attended))
        own_sum = (grad.astype(jnp.float32) + from_half.astype(jnp.float32)).astype(jnp.bfloat16)
        ready = (attended, (own_sum, exchanged(own_sum, core_pairs)), patch, own, first)
    pieces = pieces + dealt(finished(ready, pieces))
    whole = put_in_place(place, pieces, peers, chunks, share)
    return jnp.transpose(whole, (1, 0, 2))


def body(query_rows, *others):
    rows, heads, dim = query_rows.shape
    hid = others[7].shape[1]
    peers = regrouping(lax.axis_size("tok"), rows, heads, dim, hid)
    if peers:
        return regrouped_body(peers, query_rows, *others)
    return sliding_body(query_rows, *others)


def solution(mesh):
    in_specs = (
        P("tok", "head", None),
        P("tok", "head", None),
        P("tok", "head", None),
        P("head", None),
        P("head", None),
        P("head", "tok"),
        P("head", "tok"),
        P("head", None, None),
        P("head", None, None),
        P("head"),
        P(),
    )
    out_specs = P("tok", "head", None)
    return jax.shard_map(body, mesh=mesh, in_specs=in_specs, out_specs=out_specs, check_vma=False)
```

```python
import functools
import math

import jax
import jax.numpy as jnp
from jax import lax
from jax.experimental import pallas as pl
from jax.experimental.pallas import tpu as pltpu
from jax.sharding import PartitionSpec as P

HALF = 1024


epsilon = 1e-06


def passed_along(x, axis, by):
    peers = lax.axis_size(axis)
    pairs = [(i, i + by) for i in range(peers) if 0 <= i + by < peers]
    return lax.ppermute(x, axis, pairs)


def unit_rows(matrix):
    as_float = matrix.astype(jnp.float32)
    return (
        as_float * lax.rsqrt(jnp.sum(as_float * as_float, axis=-1, keepdims=True) + epsilon)
    ).astype(jnp.bfloat16)


def rescale(updated, base_norm, squares):
    return (updated * (base_norm / jnp.sqrt(squares + epsilon))[:, None, :]).astype(jnp.bfloat16)


def sliding_body(
    query_rows,
    key_rows,
    value_rows,
    query_gain,
    key_gain,
    rate_in,
    rate_out,
    fast_in,
    fast_out,
    half_window,
    boundaries,
):
    tok_rows = query_rows.shape[0]
    local_heads = query_rows.shape[1]
    head_dim = query_rows.shape[2]
    fast_hid = fast_out.shape[1]
    width_all = local_heads * head_dim * lax.axis_size("head")
    tok_count = tok_rows * lax.axis_size("tok")
    own_index = lax.axis_index("tok")
    first_row = own_index * tok_rows
    query_float = query_rows.astype(jnp.float32)
    key_float = key_rows.astype(jnp.float32)
    query_sq, key_sq = lax.psum(
        (
            jnp.sum(query_float * query_float, axis=(1, 2)),
            jnp.sum(key_float * key_float, axis=(1, 2)),
        ),
        "head",
    )
    q_normed = (
        query_float * lax.rsqrt(query_sq / width_all + epsilon)[:, None, None] * query_gain[None]
    ).astype(jnp.bfloat16)
    k_normed = (
        key_float * lax.rsqrt(key_sq / width_all + epsilon)[:, None, None] * key_gain[None]
    ).astype(jnp.bfloat16)

    def clip_of(places):
        return jnp.sum((places[:, None] >= boundaries[None, :]).astype(jnp.int32), axis=1)

    positions = first_row + jnp.arange(tok_rows, dtype=jnp.int32)
    query_clip = clip_of(positions)
    scaling = 1.0 / math.sqrt(head_dim)

    def absorb(state_now, block_keys, block_values, key_first):
        best, denominator, accum = state_now
        key_places = key_first + jnp.arange(tok_rows, dtype=jnp.int32)
        scores = (
            jnp.einsum("qhd,khd->hqk", q_normed, block_keys, preferred_element_type=jnp.float32)
            * scaling
        )
        inside = (key_places >= 0) & (key_places < tok_count)
        pair_ok = (query_clip[:, None] == clip_of(key_places)[None, :]) & inside[None, :]
        distance = jnp.abs(positions[:, None] - key_places[None, :])
        allowed = (distance[None, :, :] <= half_window[:, None, None]) & pair_ok[None, :, :]
        masked = jnp.where(allowed, scores, -jnp.inf)
        new_best = jnp.maximum(best, jnp.max(masked, axis=2))
        weights = jnp.exp(masked - new_best[:, :, None])
        shrink = jnp.exp(best - new_best)
        denominator = denominator * shrink + jnp.sum(weights, axis=2)
        accum = accum * shrink[:, :, None] + jnp.einsum(
            "hqk,khd->hqd",
            weights.astype(jnp.bfloat16),
            block_values,
            preferred_element_type=jnp.float32,
        )
        return (new_best, denominator, accum)

    start_state = (
        jnp.full((local_heads, tok_rows), -jnp.inf, jnp.float32),
        jnp.zeros((local_heads, tok_rows), jnp.float32),
        jnp.zeros((local_heads, tok_rows, head_dim), jnp.float32),
    )
    state_now = absorb(start_state, k_normed, value_rows, first_row)
    reach_blocks = HALF // tok_rows
    for distance_step in range(1, reach_blocks + 1):
        left_keys, left_values = passed_along((k_normed, value_rows), "tok", distance_step)
        state_now = absorb(state_now, left_keys, left_values, first_row - distance_step * tok_rows)
        right_keys, right_values = passed_along((k_normed, value_rows), "tok", -distance_step)
        state_now = absorb(
            state_now, right_keys, right_values, first_row + distance_step * tok_rows
        )
    attended = state_now[2] / state_now[1][:, :, None]
    key_unit = unit_rows(k_normed)
    query_unit = unit_rows(q_normed)
    pre_keys = jnp.einsum("thd,hdf->htf", key_unit, fast_in, preferred_element_type=jnp.float32)
    gate_part = pre_keys[:, :, :fast_hid]
    lin_part = pre_keys[:, :, fast_hid:]
    sigmoid_gate = jax.nn.sigmoid(gate_part)
    swish_gate = gate_part * sigmoid_gate
    hidden = (swish_gate * lin_part).astype(jnp.bfloat16)
    value_float = value_rows.astype(jnp.float32)
    push_out = (-jnp.transpose(rate_out)[:, :, None] * value_float).astype(jnp.bfloat16)
    push_in = (-jnp.transpose(rate_in)[:, :, None] * value_float).astype(jnp.bfloat16)
    grad_out = jnp.einsum("htf,thd->hfd", hidden, push_out, preferred_element_type=jnp.float32)
    hidden_grad = jnp.einsum("thd,hfd->htf", push_in, fast_out, preferred_element_type=jnp.float32)
    d_gate = hidden_grad * lin_part * sigmoid_gate * (1.0 + gate_part * (1.0 - sigmoid_gate))
    d_lin = hidden_grad * swish_gate
    d_pre = jnp.concatenate([d_gate, d_lin], axis=2).astype(jnp.bfloat16)
    grad_in = jnp.einsum("thd,htf->hdf", key_unit, d_pre, preferred_element_type=jnp.float32)
    in_float = fast_in.astype(jnp.float32)
    out_float = fast_out.astype(jnp.float32)
    in_base = jnp.sqrt(jnp.sum(in_float * in_float, axis=1))
    out_base = jnp.sqrt(jnp.sum(out_float * out_float, axis=1))
    summed_in, summed_out = lax.psum((grad_in, grad_out), "tok")
    updated_in = in_float - summed_in
    updated_out = out_float - summed_out
    new_in = rescale(updated_in, in_base, jnp.sum(updated_in * updated_in, axis=1))
    new_out = rescale(updated_out, out_base, jnp.sum(updated_out * updated_out, axis=1))
    pre_query = jnp.einsum("thd,hdf->htf", query_unit, new_in, preferred_element_type=jnp.float32)
    query_gate = pre_query[:, :, :fast_hid]
    query_hidden = (query_gate * jax.nn.sigmoid(query_gate) * pre_query[:, :, fast_hid:]).astype(
        jnp.bfloat16
    )
    fast_result = jnp.einsum(
        "htf,hfd->htd", query_hidden, new_out, preferred_element_type=jnp.float32
    )
    combined = attended + fast_result
    return jnp.transpose(combined, (1, 0, 2)).astype(jnp.bfloat16)


VMEM_BYTES = 16 * 1024 * 1024
HIDDEN_MASK = -1e30
NT = (((1,), (1,)), ((), ()))


def exchanged(x, pairs):
    return lax.ppermute(x, "tok", pairs)


def nt_dot(a, b):
    return lax.dot_general(a, b, NT, preferred_element_type=jnp.float32)


def nn_dot(a, b):
    return jnp.dot(a, b, preferred_element_type=jnp.float32)


def in_vmem(kernel, name, scalars, arrays, after, out_shape, flops=0, scratch=()):
    specs = [pl.BlockSpec(memory_space=pltpu.SMEM)] * len(scalars)
    specs += [pl.BlockSpec(memory_space=pltpu.VMEM)] * len(arrays)
    specs += [pl.BlockSpec(memory_space=pl.ANY)] * len(after)
    return pl.pallas_call(
        kernel,
        out_shape=out_shape,
        in_specs=specs,
        out_specs=jax.tree.map(lambda _: pl.BlockSpec(memory_space=pltpu.VMEM), out_shape),
        scratch_shapes=scratch,
        compiler_params=pltpu.CompilerParams(vmem_limit_bytes=VMEM_BYTES),
        cost_estimate=pl.CostEstimate(flops=16 * flops, bytes_accessed=0, transcendentals=0),
        name=name,
    )(*scalars, *arrays, *after)


def head_at(place_ref, share, chip, i):
    return place_ref[3 + chip * share + i]


def pack_kernel(peers, first, count, width_all, fold, with_lone, place_ref, *refs):
    squares_ref, more_ref, q_gain_ref, k_gain_ref, rate_in_ref, rate_out_ref = refs[:6]
    q_ref, k_ref, v_ref = refs[6:9]
    outs = refs[-3 - peers : -3]
    aux_ref, q_scale_ref, k_scale_ref = refs[-3:]
    rows, dim = q_scale_ref.shape
    share = q_gain_ref.shape[0] // peers
    scales = lax.rsqrt((squares_ref[...] + more_ref[...]) / width_all + epsilon)
    q_scale_ref[...] = jnp.transpose(jnp.broadcast_to(scales[0:1] * fold, (dim, rows)))
    k_scale_ref[...] = jnp.transpose(jnp.broadcast_to(scales[1:2], (dim, rows)))
    aux_ref[...] = jnp.zeros_like(aux_ref)

    def normed(ref, scale_ref, gain_ref, head, some):
        gain = gain_ref[pl.ds(head, 1), :]
        scaled = ref[head, 0:some].astype(jnp.float32) * scale_ref[0:some] * gain
        return scaled.astype(jnp.bfloat16)

    def one_head(step, carry):
        for p in range(peers):
            c = place_ref[0] ^ p
            head = head_at(place_ref, share, c, first + step)
            outs[p][step, 0:rows, :] = normed(q_ref, q_scale_ref, q_gain_ref, head, rows)
            outs[p][step, rows : 2 * rows, :] = normed(
                k_ref, k_scale_ref, k_gain_ref, head, rows
            )
            for i in range(0, rows, 128):
                outs[p][step, 2 * rows + i : 2 * rows + i + 128, :] = jnp.transpose(
                    v_ref[head, i : i + 128, :]
                )
            at = 0
            for rate_ref in (rate_in_ref, rate_out_ref):
                rate = rate_ref[pl.ds(head, 1), :]
                high = rate.astype(jnp.bfloat16).astype(jnp.float32)
                for part in (high, rate - high):
                    for i in range(0, rows, 128):
                        aux_ref[at : at + 1, :] = part[:, i : i + 128]
                        at += 1
            if with_lone:
                for i in range(-(-share // count)):
                    head = head_at(place_ref, share, c, jnp.minimum(step + i * count, share - 1))
                    q0 = normed(q_ref, q_scale_ref, q_gain_ref, head, 16)
                    k0 = normed(k_ref, k_scale_ref, k_gain_ref, head, 16)
                    for at, array in enumerate((q0, k0, v_ref[head, 0:16])):
                        at += aux_ref.shape[0] // 2 + 3 * i
                        aux_ref[at : at + 1, :] = array.astype(jnp.float32)[0:1]
            some = outs[p].shape[1] - 3 * rows
            outs[p][step, 3 * rows :, :] = aux_ref[0:some, :].astype(jnp.bfloat16)
        return carry

    lax.fori_loop(0, count, one_head, 0)


def pack(place, sums, q, k, v, gains, rates, peers, aux_rows, first, count, width_all, fold):
    heads, rows, dim = q.shape
    out_shape = (count, 3 * rows + aux_rows // (2 if first else 1), dim)
    return in_vmem(
        functools.partial(pack_kernel, peers, first, count, width_all, fold, not first),
        "pack",
        [place],
        [*sums, *gains, *rates, q, k, v],
        [],
        [jax.ShapeDtypeStruct(out_shape, jnp.bfloat16)] * peers,
        scratch=[
            pltpu.VMEM((aux_rows, dim), jnp.float32),
            pltpu.VMEM((rows, dim), jnp.float32),
            pltpu.VMEM((rows, dim), jnp.float32),
        ],
    )


def stack_kernel(from_row, *refs):
    for p, ref in enumerate(refs[:-1]):
        refs[-1][p] = ref[:, from_row:, :]


def stacked(arrays, from_row):
    heads, rows, dim = arrays[0].shape
    return in_vmem(
        functools.partial(stack_kernel, from_row),
        "stack",
        [],
        arrays,
        [],
        jax.ShapeDtypeStruct((len(arrays), heads, rows - from_row, dim), jnp.bfloat16),
    )


def lone_kernel(place_ref, own_ref, other_ref, out_ref):
    extra = out_ref.shape[1]
    at = own_ref.shape[2] - extra
    mine = jnp.full(out_ref.shape, place_ref[1]) == 0
    own = own_ref[place_ref[0], :, at:, :].astype(jnp.float32)
    other = other_ref[place_ref[0], :, at:, :].astype(jnp.float32)
    out_ref[...] = jnp.where(mine, own, other).astype(jnp.bfloat16)


def lone_rows(place, own, other, rows):
    _, count, all_rows, dim = own.shape
    out_shape = (count, (all_rows - 2 * rows) // 2, dim)
    return in_vmem(
        lone_kernel,
        "lone_rows",
        [place],
        [own, other],
        [],
        jax.ShapeDtypeStruct(out_shape, jnp.bfloat16),
    )


def key_value_blocks(peers, rows, step, refs):
    for p in range(peers):
        yield p, True, refs[p].at[step, rows : 2 * rows], refs[p].at[step, 2 * rows :]
        yield p, False, refs[peers].at[p, step, 0:rows], refs[peers].at[p, step, rows:]


def grads_kernel(peers, rows, rate_rows, share, first, place_ref, in_ref, out_ref, *refs):
    grad_ref = refs[-1]
    hid = out_ref.shape[1]
    part = hid // 2
    own = pl.multiple_of(place_ref[1] * part, part)

    def one_head(step, carry):
        head = head_at(place_ref, share, place_ref[0], first + step)
        in_half = jnp.concatenate(
            [
                jnp.transpose(in_ref[head, :, pl.ds(at, part)].astype(jnp.float32))
                for at in (own, pl.multiple_of(hid + own, part))
            ],
            axis=0,
        ).astype(jnp.bfloat16)
        out_half = out_ref[head, pl.ds(own, part), :]
        sum_in = jnp.zeros((2 * part, in_half.shape[1]), jnp.float32)
        sum_out = jnp.zeros((part, in_half.shape[1]), jnp.float32)
        for _, _, keys, values in key_value_blocks(peers, rows, step, refs):
            k = keys[...].astype(jnp.float32)
            v_t = jnp.concatenate([values[at : at + 128, :] for at in range(0, rows, 128)], axis=1)
            aux = values[rows : rows + 16, :].astype(jnp.float32)

            def rate(at):
                both = aux[at : at + rate_rows] + aux[at + rate_rows : at + 2 * rate_rows]
                return jnp.concatenate([both[i : i + 1] for i in range(rate_rows)], axis=1)

            rate_in, rate_out = rate(0), rate(2 * rate_rows)
            unit = (k * lax.rsqrt(jnp.sum(k * k, axis=1, keepdims=True) + epsilon)).astype(
                jnp.bfloat16
            )
            pre = nt_dot(in_half, unit)
            gate, lin = pre[:part], pre[part:]
            sig = jax.nn.sigmoid(gate)
            swish = gate * sig
            pushed = (swish * lin * -rate_out).astype(jnp.bfloat16)
            hidden_grad = nn_dot(out_half, v_t) * -rate_in
            d_gate = hidden_grad * lin * sig * (1.0 + gate * (1.0 - sig))
            d_lin = hidden_grad * swish
            d_pre = jnp.concatenate([d_gate, d_lin], axis=0).astype(jnp.bfloat16)
            sum_in += nn_dot(d_pre, unit)
            sum_out += nt_dot(pushed, v_t)
        grad_ref[step, 0 : 2 * part, :] = sum_in.astype(jnp.bfloat16)
        grad_ref[step, 2 * part :, :] = sum_out.astype(jnp.bfloat16)
        return carry

    lax.fori_loop(0, grad_ref.shape[0], one_head, 0)


def gradients(place, fast_in, fast_out, packets, share, rows, first, after):
    _, hid, dim = fast_out.shape
    own, other = packets
    peers, heads = other.shape[:2]
    return in_vmem(
        functools.partial(grads_kernel, peers, rows, rows // 128, share, first),
        "gradients",
        [place],
        [fast_in, fast_out, *own, other],
        after,
        jax.ShapeDtypeStruct((heads, 3 * hid // 2, dim), jnp.bfloat16),
    )


def attend_kernel(peers, rows, share, first, fwd_heads, place_ref, window_ref, edge_ref, *refs):
    fwd_ref = refs[peers + 1]
    out_ref, extra_ref, k_scr, vt_scr, q_scr = refs[-5:]
    span = 2 * peers * rows
    dim = k_scr.shape[1]
    pad = fwd_ref.shape[1]
    chip, core, half = place_ref[0], place_ref[1], place_ref[2]
    base = half * span
    limit = span + 1 - half
    k_scr[span:, :] = jnp.zeros((k_scr.shape[0] - span, dim), k_scr.dtype)
    vt_scr[:, span:] = jnp.zeros((vt_scr.shape[0], vt_scr.shape[1] - span), vt_scr.dtype)
    vt_scr[dim:, :] = jnp.ones((vt_scr.shape[0] - dim, vt_scr.shape[1]), vt_scr.dtype)

    def one_head(step, carry):
        window = window_ref[head_at(place_ref, share, chip, first + step)]
        for p, own, keys, values in key_value_blocks(peers, rows, step, refs):
            at = pl.multiple_of(((chip ^ p) * 2 + (core if own else 1 - core)) * rows, rows)
            k_scr[pl.ds(at, rows), :] = keys[...]
            for i in range(0, rows, 128):
                vt_scr[0:dim, pl.ds(pl.multiple_of(at + i, 128), 128)] = values[i : i + 128, :]
        for p in range(peers):
            q_scr[chip ^ p] = refs[p][step, 0:rows, :]
        fwd = fwd_ref[lax.rem(first + step, fwd_heads)].astype(jnp.float32)
        turn = (first + step) // fwd_heads
        q_lone, k_lone, v_lone = (
            sum(
                jnp.where(turn == t, fwd[3 * t + i : 3 * t + i + 1], 0.0)
                for t in range(-(-share // fwd_heads))
            )
            for i in range(3)
        )
        k_scr[span : span + pad, :] = jnp.broadcast_to(k_lone, (pad, dim)).astype(jnp.bfloat16)
        vt_scr[0:dim, span : span + 128] = jnp.transpose(
            jnp.broadcast_to(v_lone, (128, dim))
        ).astype(jnp.bfloat16)

        def clip_start(place):
            start = jnp.zeros_like(place)
            for i in range(edge_ref.shape[0]):
                start = jnp.maximum(start, jnp.where(edge_ref[i] <= place, edge_ref[i], 0))
            return start

        def clip_stop(place):
            stop = jnp.full_like(place, base + limit)
            for i in range(edge_ref.shape[0]):
                stop = jnp.minimum(stop, jnp.where(edge_ref[i] > place, edge_ref[i], base + limit))
            return stop

        def lowest(place):
            return jnp.maximum(jnp.maximum(place - window, clip_start(place)), base) - base

        def highest(place):
            return jnp.minimum(place + window, clip_stop(place) - 1) - base

        def one_pair(i, carry):
            pair = []
            for c in (i, peers - 1 - i):
                start = (c * 2 + core) * rows
                place = base + start + lax.broadcasted_iota(jnp.int32, (1, rows), 1)
                from_key = lowest(base + start) // 128 * 128
                count = (highest(base + start + rows - 1) - from_key) // 256 + 1
                pair.append((c, lowest(place), highest(place), from_key, count))
            count = jnp.maximum(pair[0][4], pair[1][4])

            def variant(chunks):
                froms = [
                    pl.multiple_of(jnp.minimum(each[3], k_scr.shape[0] - chunks * 256), 128)
                    for each in pair
                ]
                key = lax.broadcasted_iota(jnp.int32, (256, rows), 0)
                scores = [[], []]
                tops = [None, None]
                for i in range(chunks):
                    for n, (each, at) in enumerate(zip(pair, froms)):
                        from_key = pl.multiple_of(at + i * 256, 128)
                        piece = nt_dot(k_scr[pl.ds(from_key, 256), :], q_scr[each[0]])
                        seen = (key >= each[1] - from_key) & (key <= each[2] - from_key)
                        piece = jnp.where(seen, piece, HIDDEN_MASK)
                        top = jnp.max(piece.reshape(32, 8, rows), axis=0)
                        tops[n] = top if i == 0 else jnp.maximum(tops[n], top)
                        scores[n].append(piece)
                tops = [jnp.max(top, axis=0, keepdims=True) for top in tops]
                totals = [0.0, 0.0]
                for i in range(chunks):
                    for n, at in enumerate(froms):
                        weights = jnp.exp2(scores[n][i] - tops[n]).astype(jnp.bfloat16)
                        from_key = pl.multiple_of(at + i * 256, 128)
                        totals[n] += nn_dot(vt_scr[:, pl.ds(from_key, 256)], weights)
                for each, total in zip(pair, totals):
                    attended = total[0:dim] * (1.0 / total[dim : dim + 1])
                    out_ref[each[0], step] = jnp.transpose(attended)

            for chunks in range(1, span // 256 + 2):

                @pl.when(count == chunks)
                def _(chunks=chunks):
                    variant(chunks)

            return carry

        lax.fori_loop(0, peers // 2, one_pair, 0)
        extra_ref[step] = jnp.zeros(extra_ref.shape[1:], jnp.float32)

        @pl.when((half == 0) & (core == 1))
        def _():
            near = span - HALF
            width = HALF + 128
            q = jnp.broadcast_to(q_lone, (pad, dim)).astype(jnp.bfloat16)
            scores = nt_dot(q, k_scr[near : near + width, :])
            key = near + lax.broadcasted_iota(jnp.int32, (1, width), 1)
            scores = jnp.where((key >= span - window) & (key <= span), scores, HIDDEN_MASK)
            top = jnp.max(scores, axis=1, keepdims=True)
            weights = jnp.exp2(scores - top).astype(jnp.bfloat16)
            total = nt_dot(weights, vt_scr[:, near : near + width])
            extra_ref[step] = total[:, 0:dim] / total[:, dim : dim + 1]
        return carry

    lax.fori_loop(0, extra_ref.shape[0], one_head, 0)


def attend(place, half_window, boundaries, packets, forwarded, share, rows, first, after):
    own, other = packets
    peers, heads = other.shape[:2]
    fwd_heads, pad, dim = forwarded.shape
    scr_rows = 2 * peers * rows + 256
    out_shapes = [(peers, heads, rows, dim), (heads, pad, dim)]
    return in_vmem(
        functools.partial(attend_kernel, peers, rows, share, first, fwd_heads),
        "attend",
        [place, half_window, boundaries],
        [*own, other, forwarded],
        after,
        [jax.ShapeDtypeStruct(shape, jnp.float32) for shape in out_shapes],
        flops=4 * heads * peers * rows * HALF * 2 * dim,
        scratch=[
            pltpu.VMEM((scr_rows, dim), jnp.bfloat16),
            pltpu.VMEM((dim + 16, scr_rows), jnp.bfloat16),
            pltpu.VMEM((peers, rows, dim), jnp.bfloat16),
        ],
    )


def finish_kernel(peers, share, first, unit_epsilon, place_ref, *refs):
    att_ref, base_in_ref, base_out_ref, own_ref, other_ref, patch_ref = refs[:6]
    queries = refs[6 : 6 + peers]
    outs = refs[-2 - peers : -2]
    grad_in_scr, grad_out_scr = refs[-2:]
    chip, core, half = place_ref[0], place_ref[1], place_ref[2]
    rows = att_ref.shape[2]
    hid = base_out_ref.shape[1]
    part = hid // 2

    def one_head(step, carry):
        head = head_at(place_ref, share, chip, first + step)
        for summed, lane in ((own_ref, core), (other_ref, 1 - core)):
            at = pl.multiple_of(lane * part, part)
            grad_in_scr[pl.ds(at, part), :] = summed[step, 0:part, :].astype(jnp.float32)
            grad_in_scr[pl.ds(hid + at, part), :] = summed[step, part : 2 * part, :].astype(jnp.float32)
            grad_out_scr[pl.ds(at, part), :] = summed[step, 2 * part :, :].astype(jnp.float32)

        def renewed(base, grad):
            base = base.astype(jnp.float32)
            updated = base - grad
            norm = jnp.sqrt(jnp.sum(base * base, axis=0, keepdims=True))
            squares = jnp.sum(updated * updated, axis=0, keepdims=True)
            return (updated * (norm / jnp.sqrt(squares + epsilon))).astype(jnp.bfloat16)

        new_in = renewed(base_in_ref[head], jnp.transpose(grad_in_scr[...]))
        new_out = renewed(base_out_ref[head], grad_out_scr[...])
        patch = patch_ref[step, 0:8, :][0:1]
        row = lax.broadcasted_iota(jnp.int32, (rows, 1), 0)
        for p in range(peers):
            q = queries[p][step, 0:rows, :].astype(jnp.float32)
            unit = (q * lax.rsqrt(jnp.sum(q * q, axis=1, keepdims=True) + unit_epsilon)).astype(
                jnp.bfloat16
            )
            pre = nn_dot(unit, new_in)
            gate = pre[:, :hid]
            hidden = (gate * jax.nn.sigmoid(gate) * pre[:, hid:]).astype(jnp.bfloat16)
            patched = (half == 1) & (core == 0) & (chip == p)
            attended = jnp.where(patched & (row == 0), patch, att_ref[chip ^ p, step])
            outs[p][step] = (attended + nn_dot(hidden, new_out)).astype(jnp.bfloat16)
        return carry

    lax.fori_loop(0, att_ref.shape[1], one_head, 0)


def finish(place, attended, fast_in, fast_out, sums, patch, own, share, first, unit_epsilon, after):
    peers, heads, rows, dim = attended.shape
    hid = fast_out.shape[1]
    return in_vmem(
        functools.partial(finish_kernel, peers, share, first, unit_epsilon),
        "finish",
        [place],
        [attended, fast_in, fast_out, *sums, patch, *own],
        after,
        [jax.ShapeDtypeStruct((heads, rows, dim), jnp.bfloat16)] * peers,
        flops=12 * heads * peers * rows * hid * dim,
        scratch=[pltpu.VMEM((2 * hid, dim), jnp.float32), pltpu.VMEM((hid, dim), jnp.float32)],
    )


def place_kernel(peers, chunks, share, place_ref, *refs):
    pieces, out_ref, sems = refs[:-2], refs[-2], refs[-1]
    copies = []
    for n, (first, heads) in enumerate(chunks):
        for p in range(peers):
            for i in range(heads):
                head = head_at(place_ref, share, place_ref[0] ^ p, first + i)
                copies.append(
                    pltpu.make_async_copy(
                        pieces[n * peers + p].at[i], out_ref.at[head], sems.at[len(copies)]
                    )
                )
    for copy in copies:
        copy.start()
    for copy in copies:
        copy.wait()


def put_in_place(place, pieces, peers, chunks, share):
    _, rows, dim = pieces[0].shape
    return pl.pallas_call(
        functools.partial(place_kernel, peers, chunks, share),
        out_shape=jax.ShapeDtypeStruct((peers * share, rows, dim), jnp.bfloat16),
        in_specs=[pl.BlockSpec(memory_space=pltpu.SMEM)]
        + [pl.BlockSpec(memory_space=pltpu.VMEM)] * len(pieces),
        out_specs=pl.BlockSpec(memory_space=pl.ANY),
        scratch_shapes=[pltpu.SemaphoreType.DMA((peers * share,))],
        compiler_params=pltpu.CompilerParams(vmem_limit_bytes=VMEM_BYTES),
        name="put_in_place",
    )(place, *pieces)


def regrouping(tok_peers, rows, heads, dim, hid):
    half_peers = tok_peers // 2
    peers = math.gcd(half_peers, heads)
    fits = tok_peers % 2 == 0 and half_peers * rows == 2 * HALF
    fits = fits and half_peers == 2 * peers and peers & (peers - 1) == 0
    fits = fits and rows % 256 == 0 and dim == 128 and hid % 256 == 0
    return peers if fits else 0


def regrouped_body(
    peers,
    query_rows,
    key_rows,
    value_rows,
    query_gain,
    key_gain,
    rate_in,
    rate_out,
    fast_in,
    fast_out,
    half_window,
    boundaries,
):
    rows, heads, dim = query_rows.shape
    share = heads // peers
    tok_peers = lax.axis_size("tok")
    half_peers = tok_peers // 2
    width_all = heads * dim * lax.axis_size("head")
    chunks = [(0, (share + 1) // 2), ((share + 1) // 2, share // 2)]
    aux_rows = 2 * -(-max(4 * (rows // 128), 3 * -(-share // chunks[0][1])) // 16) * 16
    own_index = lax.axis_index("tok")
    half = own_index // half_peers
    chip = own_index % half_peers // 2
    core = own_index % 2
    number = jnp.arange(heads, dtype=jnp.int32)
    order = half_window * heads + number
    rank = jnp.sum((order[None, :] > order[:, None]).astype(jnp.int32), axis=1)
    turn, seat = rank // peers, rank % peers
    taker = jnp.where(turn % 2 == 0, seat, peers - 1 - seat)
    slot = taker * share + jnp.where(turn % 2 == 0, 0, chunks[0][1]) + turn // 2
    table = jnp.sum(jnp.where(slot[:, None] == number[None, :], number[:, None], 0), axis=0)
    place = jnp.concatenate([jnp.stack([chip, core, half]).astype(jnp.int32), table])

    def dealt(sent):
        pairs = [
            [(t, t // half_peers * half_peers + ((t % half_peers) ^ (2 * p))) for t in range(tok_peers)]
            for p in range(peers)
        ]
        return [sent[0]] + [exchanged(sent[p], pairs[p]) for p in range(1, peers)]

    core_pairs = [(t, t ^ 1) for t in range(tok_peers)]
    half_pairs = [(t, (t + half_peers) % tok_peers) for t in range(tok_peers)]
    forward_pairs = [(t + half_peers, t) for t in range(half_peers)]
    back_pairs = [(t, t - 1 + half_peers) for t in range(half_peers) if t % 2 == 1]

    q = jnp.transpose(query_rows, (1, 0, 2))
    k = jnp.transpose(key_rows, (1, 0, 2))
    v = jnp.transpose(value_rows, (1, 0, 2))
    q_float = q.astype(jnp.float32)
    k_float = k.astype(jnp.float32)
    squares = jnp.stack(
        [jnp.sum(q_float * q_float, axis=(0, 2)), jnp.sum(k_float * k_float, axis=(0, 2))]
    )
    if lax.axis_size("head") == 2:
        sums = (squares, lax.ppermute(squares, "head", [(0, 1), (1, 0)]))
    else:
        sums = (lax.psum(squares, "head"), jnp.zeros_like(squares))
    fold = math.log2(math.e) / math.sqrt(dim)
    sent = [
        pack(
            place,
            sums,
            q,
            k,
            v,
            (query_gain, key_gain),
            (rate_in, rate_out),
            peers,
            aux_rows,
            first,
            count,
            width_all,
            fold,
        )
        for first, count in chunks
    ]
    received = []
    for each in sent:
        if received:
            each = [lax.optimization_barrier(pair)[0] for pair in zip(each, received[-1])]
        received.append(dealt(each))
    def finished(ready, after):
        attended, sums, patch, own, first = ready
        return finish(
            place,
            attended,
            fast_in,
            fast_out,
            sums,
            patch,
            own,
            share,
            first,
            epsilon * fold * fold,
            after,
        )

    forwarded = ready = None
    pieces = []
    for (first, count), own in zip(chunks, received):
        if ready:
            *own, _ = lax.optimization_barrier((*own, ready[1][0]))
        else:
            own = lax.optimization_barrier((*own, *sent[-1]))[:peers]
        stack = stacked(own, rows)
        packets = (own, exchanged(stack, core_pairs))
        if forwarded is None:
            forwarded = exchanged(lone_rows(place, stack, packets[1], rows), forward_pairs)
        before = [ready[0]] if ready else []
        grad = gradients(place, fast_in, fast_out, packets, share, rows, first, before)
        from_half = exchanged(grad, half_pairs)
        before = [grad]
        if not ready and len(received) > 1:
            before += received[1][1:2]
        if ready:
            outs = finished(ready, [grad])
            before.append(outs[0])
            pieces = pieces + dealt(outs)
        attended, extra = attend(
            place,
            half_window,
            boundaries,
            packets,
            forwarded,
            share,
            rows,
            first,
            before,
        )
        patch = exchanged(extra, back_pairs)
        from_half, _ = lax.optimization_barrier((from_half, attended))
        own_sum = (grad.astype(jnp.float32) + from_half.astype(jnp.float32)).astype(jnp.bfloat16)
        ready = (attended, (own_sum, exchanged(own_sum, core_pairs)), patch, own, first)
    pieces = pieces + dealt(finished(ready, pieces))
    whole = put_in_place(place, pieces, peers, chunks, share)
    return jnp.transpose(whole, (1, 0, 2))


def body(query_rows, *others):
    rows, heads, dim = query_rows.shape
    hid = others[7].shape[1]
    peers = regrouping(lax.axis_size("tok"), rows, heads, dim, hid)
    if peers:
        return regrouped_body(peers, query_rows, *others)
    return sliding_body(query_rows, *others)


def solution(mesh):
    in_specs = (
        P("tok", "head", None),
        P("tok", "head", None),
        P("tok", "head", None),
        P("head", None),
        P("head", None),
        P("head", "tok"),
        P("head", "tok"),
        P("head", None, None),
        P("head", None, None),
        P("head"),
        P(),
    )
    out_specs = P("tok", "head", None)
    return jax.shard_map(body, mesh=mesh, in_specs=in_specs, out_specs=out_specs, check_vma=False)
```

```python
import functools
import math

import jax
import jax.numpy as jnp
from jax import lax
from jax.experimental import pallas as pl
from jax.experimental.pallas import tpu as pltpu
from jax.sharding import PartitionSpec as P

HALF = 1024


epsilon = 1e-06


def passed_along(x, axis, by):
    peers = lax.axis_size(axis)
    pairs = [(i, i + by) for i in range(peers) if 0 <= i + by < peers]
    return lax.ppermute(x, axis, pairs)


def unit_rows(matrix):
    as_float = matrix.astype(jnp.float32)
    return (
        as_float * lax.rsqrt(jnp.sum(as_float * as_float, axis=-1, keepdims=True) + epsilon)
    ).astype(jnp.bfloat16)


def rescale(updated, base_norm, squares):
    return (updated * (base_norm / jnp.sqrt(squares + epsilon))[:, None, :]).astype(jnp.bfloat16)


def sliding_body(
    query_rows,
    key_rows,
    value_rows,
    query_gain,
    key_gain,
    rate_in,
    rate_out,
    fast_in,
    fast_out,
    half_window,
    boundaries,
):
    tok_rows = query_rows.shape[0]
    local_heads = query_rows.shape[1]
    head_dim = query_rows.shape[2]
    fast_hid = fast_out.shape[1]
    width_all = local_heads * head_dim * lax.axis_size("head")
    tok_count = tok_rows * lax.axis_size("tok")
    own_index = lax.axis_index("tok")
    first_row = own_index * tok_rows
    query_float = query_rows.astype(jnp.float32)
    key_float = key_rows.astype(jnp.float32)
    query_sq, key_sq = lax.psum(
        (
            jnp.sum(query_float * query_float, axis=(1, 2)),
            jnp.sum(key_float * key_float, axis=(1, 2)),
        ),
        "head",
    )
    q_normed = (
        query_float * lax.rsqrt(query_sq / width_all + epsilon)[:, None, None] * query_gain[None]
    ).astype(jnp.bfloat16)
    k_normed = (
        key_float * lax.rsqrt(key_sq / width_all + epsilon)[:, None, None] * key_gain[None]
    ).astype(jnp.bfloat16)

    def clip_of(places):
        return jnp.sum((places[:, None] >= boundaries[None, :]).astype(jnp.int32), axis=1)

    positions = first_row + jnp.arange(tok_rows, dtype=jnp.int32)
    query_clip = clip_of(positions)
    scaling = 1.0 / math.sqrt(head_dim)

    def absorb(state_now, block_keys, block_values, key_first):
        best, denominator, accum = state_now
        key_places = key_first + jnp.arange(tok_rows, dtype=jnp.int32)
        scores = (
            jnp.einsum("qhd,khd->hqk", q_normed, block_keys, preferred_element_type=jnp.float32)
            * scaling
        )
        inside = (key_places >= 0) & (key_places < tok_count)
        pair_ok = (query_clip[:, None] == clip_of(key_places)[None, :]) & inside[None, :]
        distance = jnp.abs(positions[:, None] - key_places[None, :])
        allowed = (distance[None, :, :] <= half_window[:, None, None]) & pair_ok[None, :, :]
        masked = jnp.where(allowed, scores, -jnp.inf)
        new_best = jnp.maximum(best, jnp.max(masked, axis=2))
        weights = jnp.exp(masked - new_best[:, :, None])
        shrink = jnp.exp(best - new_best)
        denominator = denominator * shrink + jnp.sum(weights, axis=2)
        accum = accum * shrink[:, :, None] + jnp.einsum(
            "hqk,khd->hqd",
            weights.astype(jnp.bfloat16),
            block_values,
            preferred_element_type=jnp.float32,
        )
        return (new_best, denominator, accum)

    start_state = (
        jnp.full((local_heads, tok_rows), -jnp.inf, jnp.float32),
        jnp.zeros((local_heads, tok_rows), jnp.float32),
        jnp.zeros((local_heads, tok_rows, head_dim), jnp.float32),
    )
    state_now = absorb(start_state, k_normed, value_rows, first_row)
    reach_blocks = HALF // tok_rows
    for distance_step in range(1, reach_blocks + 1):
        left_keys, left_values = passed_along((k_normed, value_rows), "tok", distance_step)
        state_now = absorb(state_now, left_keys, left_values, first_row - distance_step * tok_rows)
        right_keys, right_values = passed_along((k_normed, value_rows), "tok", -distance_step)
        state_now = absorb(
            state_now, right_keys, right_values, first_row + distance_step * tok_rows
        )
    attended = state_now[2] / state_now[1][:, :, None]
    key_unit = unit_rows(k_normed)
    query_unit = unit_rows(q_normed)
    pre_keys = jnp.einsum("thd,hdf->htf", key_unit, fast_in, preferred_element_type=jnp.float32)
    gate_part = pre_keys[:, :, :fast_hid]
    lin_part = pre_keys[:, :, fast_hid:]
    sigmoid_gate = jax.nn.sigmoid(gate_part)
    swish_gate = gate_part * sigmoid_gate
    hidden = (swish_gate * lin_part).astype(jnp.bfloat16)
    value_float = value_rows.astype(jnp.float32)
    push_out = (-jnp.transpose(rate_out)[:, :, None] * value_float).astype(jnp.bfloat16)
    push_in = (-jnp.transpose(rate_in)[:, :, None] * value_float).astype(jnp.bfloat16)
    grad_out = jnp.einsum("htf,thd->hfd", hidden, push_out, preferred_element_type=jnp.float32)
    hidden_grad = jnp.einsum("thd,hfd->htf", push_in, fast_out, preferred_element_type=jnp.float32)
    d_gate = hidden_grad * lin_part * sigmoid_gate * (1.0 + gate_part * (1.0 - sigmoid_gate))
    d_lin = hidden_grad * swish_gate
    d_pre = jnp.concatenate([d_gate, d_lin], axis=2).astype(jnp.bfloat16)
    grad_in = jnp.einsum("thd,htf->hdf", key_unit, d_pre, preferred_element_type=jnp.float32)
    in_float = fast_in.astype(jnp.float32)
    out_float = fast_out.astype(jnp.float32)
    in_base = jnp.sqrt(jnp.sum(in_float * in_float, axis=1))
    out_base = jnp.sqrt(jnp.sum(out_float * out_float, axis=1))
    summed_in, summed_out = lax.psum((grad_in, grad_out), "tok")
    updated_in = in_float - summed_in
    updated_out = out_float - summed_out
    new_in = rescale(updated_in, in_base, jnp.sum(updated_in * updated_in, axis=1))
    new_out = rescale(updated_out, out_base, jnp.sum(updated_out * updated_out, axis=1))
    pre_query = jnp.einsum("thd,hdf->htf", query_unit, new_in, preferred_element_type=jnp.float32)
    query_gate = pre_query[:, :, :fast_hid]
    query_hidden = (query_gate * jax.nn.sigmoid(query_gate) * pre_query[:, :, fast_hid:]).astype(
        jnp.bfloat16
    )
    fast_result = jnp.einsum(
        "htf,hfd->htd", query_hidden, new_out, preferred_element_type=jnp.float32
    )
    combined = attended + fast_result
    return jnp.transpose(combined, (1, 0, 2)).astype(jnp.bfloat16)


VMEM_BYTES = 16 * 1024 * 1024
HIDDEN_MASK = -1e30
NT = (((1,), (1,)), ((), ()))


def exchanged(x, pairs):
    return lax.ppermute(x, "tok", pairs)


def nt_dot(a, b):
    return lax.dot_general(a, b, NT, preferred_element_type=jnp.float32)


def nn_dot(a, b):
    return jnp.dot(a, b, preferred_element_type=jnp.float32)


def in_vmem(kernel, name, scalars, arrays, after, out_shape, flops=0, scratch=()):
    specs = [pl.BlockSpec(memory_space=pltpu.SMEM)] * len(scalars)
    specs += [pl.BlockSpec(memory_space=pltpu.VMEM)] * len(arrays)
    specs += [pl.BlockSpec(memory_space=pl.ANY)] * len(after)
    return pl.pallas_call(
        kernel,
        out_shape=out_shape,
        in_specs=specs,
        out_specs=jax.tree.map(lambda _: pl.BlockSpec(memory_space=pltpu.VMEM), out_shape),
        scratch_shapes=scratch,
        compiler_params=pltpu.CompilerParams(vmem_limit_bytes=VMEM_BYTES),
        cost_estimate=pl.CostEstimate(flops=16 * flops, bytes_accessed=0, transcendentals=0),
        name=name,
    )(*scalars, *arrays, *after)


def head_at(place_ref, share, chip, i):
    return place_ref[3 + chip * share + i]


def pack_kernel(peers, first, count, width_all, fold, with_lone, place_ref, *refs):
    squares_ref, more_ref, q_gain_ref, k_gain_ref, rate_in_ref, rate_out_ref = refs[:6]
    q_ref, k_ref, v_ref = refs[6:9]
    outs = refs[-3 - peers : -3]
    aux_ref, q_scale_ref, k_scale_ref = refs[-3:]
    rows, dim = q_scale_ref.shape
    share = q_gain_ref.shape[0] // peers
    scales = lax.rsqrt((squares_ref[...] + more_ref[...]) / width_all + epsilon)
    q_scale_ref[...] = jnp.transpose(jnp.broadcast_to(scales[0:1] * fold, (dim, rows)))
    k_scale_ref[...] = jnp.transpose(jnp.broadcast_to(scales[1:2], (dim, rows)))
    aux_ref[...] = jnp.zeros_like(aux_ref)

    def normed(ref, scale_ref, gain_ref, head, some):
        gain = gain_ref[pl.ds(head, 1), :]
        scaled = ref[head, 0:some].astype(jnp.float32) * scale_ref[0:some] * gain
        return scaled.astype(jnp.bfloat16)

    def one_head(step, carry):
        for p in range(peers):
            c = place_ref[0] ^ p
            head = head_at(place_ref, share, c, first + step)
            outs[p][step, 0:rows, :] = normed(q_ref, q_scale_ref, q_gain_ref, head, rows)
            outs[p][step, rows : 2 * rows, :] = normed(
                k_ref, k_scale_ref, k_gain_ref, head, rows
            )
            for i in range(0, rows, 128):
                outs[p][step, 2 * rows + i : 2 * rows + i + 128, :] = jnp.transpose(
                    v_ref[head, i : i + 128, :]
                )
            at = 0
            for rate_ref in (rate_in_ref, rate_out_ref):
                rate = rate_ref[pl.ds(head, 1), :]
                high = rate.astype(jnp.bfloat16).astype(jnp.float32)
                for part in (high, rate - high):
                    for i in range(0, rows, 128):
                        aux_ref[at : at + 1, :] = part[:, i : i + 128]
                        at += 1
            if with_lone:
                for i in range(-(-share // count)):
                    head = head_at(place_ref, share, c, jnp.minimum(step + i * count, share - 1))
                    q0 = normed(q_ref, q_scale_ref, q_gain_ref, head, 16)
                    k0 = normed(k_ref, k_scale_ref, k_gain_ref, head, 16)
                    for at, array in enumerate((q0, k0, v_ref[head, 0:16])):
                        at += aux_ref.shape[0] // 2 + 3 * i
                        aux_ref[at : at + 1, :] = array.astype(jnp.float32)[0:1]
            some = outs[p].shape[1] - 3 * rows
            outs[p][step, 3 * rows :, :] = aux_ref[0:some, :].astype(jnp.bfloat16)
        return carry

    lax.fori_loop(0, count, one_head, 0)


def pack(place, sums, q, k, v, gains, rates, peers, aux_rows, first, count, width_all, fold):
    heads, rows, dim = q.shape
    out_shape = (count, 3 * rows + aux_rows // (2 if first else 1), dim)
    return in_vmem(
        functools.partial(pack_kernel, peers, first, count, width_all, fold, not first),
        "pack",
        [place],
        [*sums, *gains, *rates, q, k, v],
        [],
        [jax.ShapeDtypeStruct(out_shape, jnp.bfloat16)] * peers,
        scratch=[
            pltpu.VMEM((aux_rows, dim), jnp.float32),
            pltpu.VMEM((rows, dim), jnp.float32),
            pltpu.VMEM((rows, dim), jnp.float32),
        ],
    )


def stack_kernel(from_row, *refs):
    for p, ref in enumerate(refs[:-1]):
        refs[-1][p] = ref[:, from_row:, :]


def stacked(arrays, from_row):
    heads, rows, dim = arrays[0].shape
    return in_vmem(
        functools.partial(stack_kernel, from_row),
        "stack",
        [],
        arrays,
        [],
        jax.ShapeDtypeStruct((len(arrays), heads, rows - from_row, dim), jnp.bfloat16),
    )


def lone_kernel(place_ref, own_ref, other_ref, out_ref):
    extra = out_ref.shape[1]
    at = own_ref.shape[2] - extra
    mine = jnp.full(out_ref.shape, place_ref[1]) == 0
    own = own_ref[place_ref[0], :, at:, :].astype(jnp.float32)
    other = other_ref[place_ref[0], :, at:, :].astype(jnp.float32)
    out_ref[...] = jnp.where(mine, own, other).astype(jnp.bfloat16)


def lone_rows(place, own, other, rows):
    _, count, all_rows, dim = own.shape
    out_shape = (count, (all_rows - 2 * rows) // 2, dim)
    return in_vmem(
        lone_kernel,
        "lone_rows",
        [place],
        [own, other],
        [],
        jax.ShapeDtypeStruct(out_shape, jnp.bfloat16),
    )


def key_value_blocks(peers, rows, step, refs):
    for p in range(peers):
        yield p, True, refs[p].at[step, rows : 2 * rows], refs[p].at[step, 2 * rows :]
        yield p, False, refs[peers].at[p, step, 0:rows], refs[peers].at[p, step, rows:]


def grads_kernel(peers, rows, rate_rows, share, first, place_ref, in_ref, out_ref, *refs):
    grad_ref = refs[-1]
    hid = out_ref.shape[1]
    part = hid // 2
    own = pl.multiple_of(place_ref[1] * part, part)

    def one_head(step, carry):
        head = head_at(place_ref, share, place_ref[0], first + step)
        in_half = jnp.concatenate(
            [
                jnp.transpose(in_ref[head, :, pl.ds(at, part)].astype(jnp.float32))
                for at in (own, pl.multiple_of(hid + own, part))
            ],
            axis=0,
        ).astype(jnp.bfloat16)
        out_half = out_ref[head, pl.ds(own, part), :]
        sum_in = jnp.zeros((2 * part, in_half.shape[1]), jnp.float32)
        sum_out = jnp.zeros((part, in_half.shape[1]), jnp.float32)
        for _, _, keys, values in key_value_blocks(peers, rows, step, refs):
            k = keys[...].astype(jnp.float32)
            v_t = jnp.concatenate([values[at : at + 128, :] for at in range(0, rows, 128)], axis=1)
            aux = values[rows : rows + 16, :].astype(jnp.float32)

            def rate(at):
                both = aux[at : at + rate_rows] + aux[at + rate_rows : at + 2 * rate_rows]
                return jnp.concatenate([both[i : i + 1] for i in range(rate_rows)], axis=1)

            rate_in, rate_out = rate(0), rate(2 * rate_rows)
            unit = (k * lax.rsqrt(jnp.sum(k * k, axis=1, keepdims=True) + epsilon)).astype(
                jnp.bfloat16
            )
            pre = nt_dot(in_half, unit)
            gate, lin = pre[:part], pre[part:]
            sig = jax.nn.sigmoid(gate)
            swish = gate * sig
            pushed = (swish * lin * -rate_out).astype(jnp.bfloat16)
            hidden_grad = nn_dot(out_half, v_t) * -rate_in
            d_gate = hidden_grad * lin * sig * (1.0 + gate * (1.0 - sig))
            d_lin = hidden_grad * swish
            d_pre = jnp.concatenate([d_gate, d_lin], axis=0).astype(jnp.bfloat16)
            sum_in += nn_dot(d_pre, unit)
            sum_out += nt_dot(pushed, v_t)
        grad_ref[step, 0 : 2 * part, :] = sum_in.astype(jnp.bfloat16)
        grad_ref[step, 2 * part :, :] = sum_out.astype(jnp.bfloat16)
        return carry

    lax.fori_loop(0, grad_ref.shape[0], one_head, 0)


def gradients(place, fast_in, fast_out, packets, share, rows, first, after):
    _, hid, dim = fast_out.shape
    own, other = packets
    peers, heads = other.shape[:2]
    return in_vmem(
        functools.partial(grads_kernel, peers, rows, rows // 128, share, first),
        "gradients",
        [place],
        [fast_in, fast_out, *own, other],
        after,
        jax.ShapeDtypeStruct((heads, 3 * hid // 2, dim), jnp.bfloat16),
    )


def attend_kernel(peers, rows, share, first, fwd_heads, place_ref, window_ref, edge_ref, *refs):
    fwd_ref = refs[peers + 1]
    out_ref, extra_ref, k_scr, vt_scr, q_scr = refs[-5:]
    span = 2 * peers * rows
    dim = k_scr.shape[1]
    pad = fwd_ref.shape[1]
    chip, core, half = place_ref[0], place_ref[1], place_ref[2]
    base = half * span
    limit = span + 1 - half
    k_scr[span:, :] = jnp.zeros((k_scr.shape[0] - span, dim), k_scr.dtype)
    vt_scr[:, span:] = jnp.zeros((vt_scr.shape[0], vt_scr.shape[1] - span), vt_scr.dtype)
    vt_scr[dim:, :] = jnp.ones((vt_scr.shape[0] - dim, vt_scr.shape[1]), vt_scr.dtype)

    def one_head(step, carry):
        window = window_ref[head_at(place_ref, share, chip, first + step)]
        for p, own, keys, values in key_value_blocks(peers, rows, step, refs):
            at = pl.multiple_of(((chip ^ p) * 2 + (core if own else 1 - core)) * rows, rows)
            k_scr[pl.ds(at, rows), :] = keys[...]
            for i in range(0, rows, 128):
                vt_scr[0:dim, pl.ds(pl.multiple_of(at + i, 128), 128)] = values[i : i + 128, :]
        for p in range(peers):
            q_scr[chip ^ p] = refs[p][step, 0:rows, :]
        fwd = fwd_ref[lax.rem(first + step, fwd_heads)].astype(jnp.float32)
        turn = (first + step) // fwd_heads
        q_lone, k_lone, v_lone = (
            sum(
                jnp.where(turn == t, fwd[3 * t + i : 3 * t + i + 1], 0.0)
                for t in range(-(-share // fwd_heads))
            )
            for i in range(3)
        )
        k_scr[span : span + pad, :] = jnp.broadcast_to(k_lone, (pad, dim)).astype(jnp.bfloat16)
        vt_scr[0:dim, span : span + 128] = jnp.transpose(
            jnp.broadcast_to(v_lone, (128, dim))
        ).astype(jnp.bfloat16)

        def clip_start(place):
            start = jnp.zeros_like(place)
            for i in range(edge_ref.shape[0]):
                start = jnp.maximum(start, jnp.where(edge_ref[i] <= place, edge_ref[i], 0))
            return start

        def clip_stop(place):
            stop = jnp.full_like(place, base + limit)
            for i in range(edge_ref.shape[0]):
                stop = jnp.minimum(stop, jnp.where(edge_ref[i] > place, edge_ref[i], base + limit))
            return stop

        def lowest(place):
            return jnp.maximum(jnp.maximum(place - window, clip_start(place)), base) - base

        def highest(place):
            return jnp.minimum(place + window, clip_stop(place) - 1) - base

        def one_pair(i, carry):
            pair = []
            for c in (i, peers - 1 - i):
                start = (c * 2 + core) * rows
                place = base + start + lax.broadcasted_iota(jnp.int32, (1, rows), 1)
                from_key = lowest(base + start) // 128 * 128
                count = (highest(base + start + rows - 1) - from_key) // 256 + 1
                pair.append((c, lowest(place), highest(place), from_key, count))
            count = jnp.maximum(pair[0][4], pair[1][4])

            def variant(chunks):
                froms = [
                    pl.multiple_of(jnp.minimum(each[3], k_scr.shape[0] - chunks * 256), 128)
                    for each in pair
                ]
                key = lax.broadcasted_iota(jnp.int32, (256, rows), 0)
                scores = [[], []]
                tops = [None, None]
                for i in range(chunks):
                    for n, (each, at) in enumerate(zip(pair, froms)):
                        from_key = pl.multiple_of(at + i * 256, 128)
                        piece = nt_dot(k_scr[pl.ds(from_key, 256), :], q_scr[each[0]])
                        seen = (key >= each[1] - from_key) & (key <= each[2] - from_key)
                        piece = jnp.where(seen, piece, HIDDEN_MASK)
                        top = jnp.max(piece.reshape(32, 8, rows), axis=0)
                        tops[n] = top if i == 0 else jnp.maximum(tops[n], top)
                        scores[n].append(piece)
                tops = [jnp.max(top, axis=0, keepdims=True) for top in tops]
                totals = [0.0, 0.0]
                for i in range(chunks):
                    for n, at in enumerate(froms):
                        weights = jnp.exp2(scores[n][i] - tops[n]).astype(jnp.bfloat16)
                        from_key = pl.multiple_of(at + i * 256, 128)
                        totals[n] += nn_dot(vt_scr[:, pl.ds(from_key, 256)], weights)
                for each, total in zip(pair, totals):
                    attended = total[0:dim] * (1.0 / total[dim : dim + 1])
                    out_ref[each[0], step] = jnp.transpose(attended)

            for chunks in range(1, span // 256 + 2):

                @pl.when(count == chunks)
                def _(chunks=chunks):
                    variant(chunks)

            return carry

        lax.fori_loop(0, peers // 2, one_pair, 0)
        extra_ref[step] = jnp.zeros(extra_ref.shape[1:], jnp.float32)

        @pl.when((half == 0) & (core == 1))
        def _():
            near = span - HALF
            width = HALF + 128
            q = jnp.broadcast_to(q_lone, (pad, dim)).astype(jnp.bfloat16)
            scores = nt_dot(q, k_scr[near : near + width, :])
            key = near + lax.broadcasted_iota(jnp.int32, (1, width), 1)
            scores = jnp.where((key >= span - window) & (key <= span), scores, HIDDEN_MASK)
            top = jnp.max(scores, axis=1, keepdims=True)
            weights = jnp.exp2(scores - top).astype(jnp.bfloat16)
            total = nt_dot(weights, vt_scr[:, near : near + width])
            extra_ref[step] = total[:, 0:dim] / total[:, dim : dim + 1]
        return carry

    lax.fori_loop(0, extra_ref.shape[0], one_head, 0)


def attend(place, half_window, boundaries, packets, forwarded, share, rows, first, after):
    own, other = packets
    peers, heads = other.shape[:2]
    fwd_heads, pad, dim = forwarded.shape
    scr_rows = 2 * peers * rows + 256
    out_shapes = [(peers, heads, rows, dim), (heads, pad, dim)]
    return in_vmem(
        functools.partial(attend_kernel, peers, rows, share, first, fwd_heads),
        "attend",
        [place, half_window, boundaries],
        [*own, other, forwarded],
        after,
        [jax.ShapeDtypeStruct(shape, jnp.float32) for shape in out_shapes],
        flops=4 * heads * peers * rows * HALF * 2 * dim,
        scratch=[
            pltpu.VMEM((scr_rows, dim), jnp.bfloat16),
            pltpu.VMEM((dim + 16, scr_rows), jnp.bfloat16),
            pltpu.VMEM((peers, rows, dim), jnp.bfloat16),
        ],
    )


def finish_kernel(peers, share, first, unit_epsilon, place_ref, *refs):
    att_ref, base_in_ref, base_out_ref, own_ref, other_ref, patch_ref = refs[:6]
    queries = refs[6 : 6 + peers]
    outs = refs[-2 - peers : -2]
    grad_in_scr, grad_out_scr = refs[-2:]
    chip, core, half = place_ref[0], place_ref[1], place_ref[2]
    rows = att_ref.shape[2]
    hid = base_out_ref.shape[1]
    part = hid // 2

    def one_head(step, carry):
        head = head_at(place_ref, share, chip, first + step)
        for summed, lane in ((own_ref, core), (other_ref, 1 - core)):
            at = pl.multiple_of(lane * part, part)
            grad_in_scr[pl.ds(at, part), :] = summed[step, 0:part, :].astype(jnp.float32)
            grad_in_scr[pl.ds(hid + at, part), :] = summed[step, part : 2 * part, :].astype(jnp.float32)
            grad_out_scr[pl.ds(at, part), :] = summed[step, 2 * part :, :].astype(jnp.float32)

        def renewed(base, grad):
            base = base.astype(jnp.float32)
            updated = base - grad
            norm = jnp.sqrt(jnp.sum(base * base, axis=0, keepdims=True))
            squares = jnp.sum(updated * updated, axis=0, keepdims=True)
            return (updated * (norm / jnp.sqrt(squares + epsilon))).astype(jnp.bfloat16)

        new_in = renewed(base_in_ref[head], jnp.transpose(grad_in_scr[...]))
        new_out = renewed(base_out_ref[head], grad_out_scr[...])
        patch = patch_ref[step, 0:8, :][0:1]
        row = lax.broadcasted_iota(jnp.int32, (rows, 1), 0)
        for p in range(peers):
            q = queries[p][step, 0:rows, :].astype(jnp.float32)
            unit = (q * lax.rsqrt(jnp.sum(q * q, axis=1, keepdims=True) + unit_epsilon)).astype(
                jnp.bfloat16
            )
            pre = nn_dot(unit, new_in)
            gate = pre[:, :hid]
            hidden = (gate * jax.nn.sigmoid(gate) * pre[:, hid:]).astype(jnp.bfloat16)
            patched = (half == 1) & (core == 0) & (chip == p)
            attended = jnp.where(patched & (row == 0), patch, att_ref[chip ^ p, step])
            outs[p][step] = (attended + nn_dot(hidden, new_out)).astype(jnp.bfloat16)
        return carry

    lax.fori_loop(0, att_ref.shape[1], one_head, 0)


def finish(place, attended, fast_in, fast_out, sums, patch, own, share, first, unit_epsilon, after):
    peers, heads, rows, dim = attended.shape
    hid = fast_out.shape[1]
    return in_vmem(
        functools.partial(finish_kernel, peers, share, first, unit_epsilon),
        "finish",
        [place],
        [attended, fast_in, fast_out, *sums, patch, *own],
        after,
        [jax.ShapeDtypeStruct((heads, rows, dim), jnp.bfloat16)] * peers,
        flops=12 * heads * peers * rows * hid * dim,
        scratch=[pltpu.VMEM((2 * hid, dim), jnp.float32), pltpu.VMEM((hid, dim), jnp.float32)],
    )


def place_kernel(peers, chunks, share, place_ref, *refs):
    pieces, out_ref, sems = refs[:-2], refs[-2], refs[-1]
    copies = []
    for n, (first, heads) in enumerate(chunks):
        for p in range(peers):
            for i in range(heads):
                head = head_at(place_ref, share, place_ref[0] ^ p, first + i)
                copies.append(
                    pltpu.make_async_copy(
                        pieces[n * peers + p].at[i], out_ref.at[head], sems.at[len(copies)]
                    )
                )
    for copy in copies:
        copy.start()
    for copy in copies:
        copy.wait()


def put_in_place(place, pieces, peers, chunks, share):
    _, rows, dim = pieces[0].shape
    return pl.pallas_call(
        functools.partial(place_kernel, peers, chunks, share),
        out_shape=jax.ShapeDtypeStruct((peers * share, rows, dim), jnp.bfloat16),
        in_specs=[pl.BlockSpec(memory_space=pltpu.SMEM)]
        + [pl.BlockSpec(memory_space=pltpu.VMEM)] * len(pieces),
        out_specs=pl.BlockSpec(memory_space=pl.ANY),
        scratch_shapes=[pltpu.SemaphoreType.DMA((peers * share,))],
        compiler_params=pltpu.CompilerParams(vmem_limit_bytes=VMEM_BYTES),
        name="put_in_place",
    )(place, *pieces)


def regrouping(tok_peers, rows, heads, dim, hid):
    half_peers = tok_peers // 2
    peers = math.gcd(half_peers, heads)
    fits = tok_peers % 2 == 0 and half_peers * rows == 2 * HALF
    fits = fits and half_peers == 2 * peers and peers & (peers - 1) == 0
    fits = fits and rows % 256 == 0 and dim == 128 and hid % 256 == 0
    return peers if fits else 0


def regrouped_body(
    peers,
    query_rows,
    key_rows,
    value_rows,
    query_gain,
    key_gain,
    rate_in,
    rate_out,
    fast_in,
    fast_out,
    half_window,
    boundaries,
):
    rows, heads, dim = query_rows.shape
    share = heads // peers
    tok_peers = lax.axis_size("tok")
    half_peers = tok_peers // 2
    width_all = heads * dim * lax.axis_size("head")
    chunks = [(0, (share + 1) // 2), ((share + 1) // 2, share // 2)]
    aux_rows = 2 * -(-max(4 * (rows // 128), 3 * -(-share // chunks[0][1])) // 16) * 16
    own_index = lax.axis_index("tok")
    half = own_index // half_peers
    chip = own_index % half_peers // 2
    core = own_index % 2
    number = jnp.arange(heads, dtype=jnp.int32)
    order = half_window * heads + number
    rank = jnp.sum((order[None, :] > order[:, None]).astype(jnp.int32), axis=1)
    turn, seat = rank // peers, rank % peers
    taker = jnp.where(turn % 2 == 0, seat, peers - 1 - seat)
    slot = taker * share + turn
    table = jnp.sum(jnp.where(slot[:, None] == number[None, :], number[:, None], 0), axis=0)
    place = jnp.concatenate([jnp.stack([chip, core, half]).astype(jnp.int32), table])

    def dealt(sent):
        pairs = [
            [(t, t // half_peers * half_peers + ((t % half_peers) ^ (2 * p))) for t in range(tok_peers)]
            for p in range(peers)
        ]
        return [sent[0]] + [exchanged(sent[p], pairs[p]) for p in range(1, peers)]

    core_pairs = [(t, t ^ 1) for t in range(tok_peers)]
    half_pairs = [(t, (t + half_peers) % tok_peers) for t in range(tok_peers)]
    forward_pairs = [(t + half_peers, t) for t in range(half_peers)]
    back_pairs = [(t, t - 1 + half_peers) for t in range(half_peers) if t % 2 == 1]

    q = jnp.transpose(query_rows, (1, 0, 2))
    k = jnp.transpose(key_rows, (1, 0, 2))
    v = jnp.transpose(value_rows, (1, 0, 2))
    q_float = q.astype(jnp.float32)
    k_float = k.astype(jnp.float32)
    squares = jnp.stack(
        [jnp.sum(q_float * q_float, axis=(0, 2)), jnp.sum(k_float * k_float, axis=(0, 2))]
    )
    if lax.axis_size("head") == 2:
        sums = (squares, lax.ppermute(squares, "head", [(0, 1), (1, 0)]))
    else:
        sums = (lax.psum(squares, "head"), jnp.zeros_like(squares))
    fold = math.log2(math.e) / math.sqrt(dim)
    sent = [
        pack(
            place,
            sums,
            q,
            k,
            v,
            (query_gain, key_gain),
            (rate_in, rate_out),
            peers,
            aux_rows,
            first,
            count,
            width_all,
            fold,
        )
        for first, count in chunks
    ]
    received = []
    for each in sent:
        if received:
            each = [lax.optimization_barrier(pair)[0] for pair in zip(each, received[-1])]
        received.append(dealt(each))
    def finished(ready, after):
        attended, sums, patch, own, first = ready
        return finish(
            place,
            attended,
            fast_in,
            fast_out,
            sums,
            patch,
            own,
            share,
            first,
            epsilon * fold * fold,
            after,
        )

    forwarded = ready = None
    pieces = []
    for (first, count), own in zip(chunks, received):
        if ready:
            *own, _ = lax.optimization_barrier((*own, ready[1][0]))
        else:
            own = lax.optimization_barrier((*own, *sent[-1]))[:peers]
        stack = stacked(own, rows)
        packets = (own, exchanged(stack, core_pairs))
        if forwarded is None:
            forwarded = exchanged(lone_rows(place, stack, packets[1], rows), forward_pairs)
        before = [ready[0]] if ready else []
        grad = gradients(place, fast_in, fast_out, packets, share, rows, first, before)
        from_half = exchanged(grad, half_pairs)
        before = [grad]
        if not ready and len(received) > 1:
            before += received[1][1:2]
        if ready:
            outs = finished(ready, [grad])
            before.append(outs[0])
            pieces = pieces + dealt(outs)
        attended, extra = attend(
            place,
            half_window,
            boundaries,
            packets,
            forwarded,
            share,
            rows,
            first,
            before,
        )
        patch = exchanged(extra, back_pairs)
        from_half, _ = lax.optimization_barrier((from_half, attended))
        own_sum = (grad.astype(jnp.float32) + from_half.astype(jnp.float32)).astype(jnp.bfloat16)
        ready = (attended, (own_sum, exchanged(own_sum, core_pairs)), patch, own, first)
    pieces = pieces + dealt(finished(ready, pieces))
    whole = put_in_place(place, pieces, peers, chunks, share)
    return jnp.transpose(whole, (1, 0, 2))


def body(query_rows, *others):
    rows, heads, dim = query_rows.shape
    hid = others[7].shape[1]
    peers = regrouping(lax.axis_size("tok"), rows, heads, dim, hid)
    if peers:
        return regrouped_body(peers, query_rows, *others)
    return sliding_body(query_rows, *others)


def solution(mesh):
    in_specs = (
        P("tok", "head", None),
        P("tok", "head", None),
        P("tok", "head", None),
        P("head", None),
        P("head", None),
        P("head", "tok"),
        P("head", "tok"),
        P("head", None, None),
        P("head", None, None),
        P("head"),
        P(),
    )
    out_specs = P("tok", "head", None)
    return jax.shard_map(body, mesh=mesh, in_specs=in_specs, out_specs=out_specs, check_vma=False)
```

```python
import functools
import math

import jax
import jax.numpy as jnp
from jax import lax
from jax.experimental import pallas as pl
from jax.experimental.pallas import tpu as pltpu
from jax.sharding import PartitionSpec as P

HALF = 1024


epsilon = 1e-06


def passed_along(x, axis, by):
    peers = lax.axis_size(axis)
    pairs = [(i, i + by) for i in range(peers) if 0 <= i + by < peers]
    return lax.ppermute(x, axis, pairs)


def unit_rows(matrix):
    as_float = matrix.astype(jnp.float32)
    return (
        as_float * lax.rsqrt(jnp.sum(as_float * as_float, axis=-1, keepdims=True) + epsilon)
    ).astype(jnp.bfloat16)


def rescale(updated, base_norm, squares):
    return (updated * (base_norm / jnp.sqrt(squares + epsilon))[:, None, :]).astype(jnp.bfloat16)


def sliding_body(
    query_rows,
    key_rows,
    value_rows,
    query_gain,
    key_gain,
    rate_in,
    rate_out,
    fast_in,
    fast_out,
    half_window,
    boundaries,
):
    tok_rows = query_rows.shape[0]
    local_heads = query_rows.shape[1]
    head_dim = query_rows.shape[2]
    fast_hid = fast_out.shape[1]
    width_all = local_heads * head_dim * lax.axis_size("head")
    tok_count = tok_rows * lax.axis_size("tok")
    own_index = lax.axis_index("tok")
    first_row = own_index * tok_rows
    query_float = query_rows.astype(jnp.float32)
    key_float = key_rows.astype(jnp.float32)
    query_sq, key_sq = lax.psum(
        (
            jnp.sum(query_float * query_float, axis=(1, 2)),
            jnp.sum(key_float * key_float, axis=(1, 2)),
        ),
        "head",
    )
    q_normed = (
        query_float * lax.rsqrt(query_sq / width_all + epsilon)[:, None, None] * query_gain[None]
    ).astype(jnp.bfloat16)
    k_normed = (
        key_float * lax.rsqrt(key_sq / width_all + epsilon)[:, None, None] * key_gain[None]
    ).astype(jnp.bfloat16)

    def clip_of(places):
        return jnp.sum((places[:, None] >= boundaries[None, :]).astype(jnp.int32), axis=1)

    positions = first_row + jnp.arange(tok_rows, dtype=jnp.int32)
    query_clip = clip_of(positions)
    scaling = 1.0 / math.sqrt(head_dim)

    def absorb(state_now, block_keys, block_values, key_first):
        best, denominator, accum = state_now
        key_places = key_first + jnp.arange(tok_rows, dtype=jnp.int32)
        scores = (
            jnp.einsum("qhd,khd->hqk", q_normed, block_keys, preferred_element_type=jnp.float32)
            * scaling
        )
        inside = (key_places >= 0) & (key_places < tok_count)
        pair_ok = (query_clip[:, None] == clip_of(key_places)[None, :]) & inside[None, :]
        distance = jnp.abs(positions[:, None] - key_places[None, :])
        allowed = (distance[None, :, :] <= half_window[:, None, None]) & pair_ok[None, :, :]
        masked = jnp.where(allowed, scores, -jnp.inf)
        new_best = jnp.maximum(best, jnp.max(masked, axis=2))
        weights = jnp.exp(masked - new_best[:, :, None])
        shrink = jnp.exp(best - new_best)
        denominator = denominator * shrink + jnp.sum(weights, axis=2)
        accum = accum * shrink[:, :, None] + jnp.einsum(
            "hqk,khd->hqd",
            weights.astype(jnp.bfloat16),
            block_values,
            preferred_element_type=jnp.float32,
        )
        return (new_best, denominator, accum)

    start_state = (
        jnp.full((local_heads, tok_rows), -jnp.inf, jnp.float32),
        jnp.zeros((local_heads, tok_rows), jnp.float32),
        jnp.zeros((local_heads, tok_rows, head_dim), jnp.float32),
    )
    state_now = absorb(start_state, k_normed, value_rows, first_row)
    reach_blocks = HALF // tok_rows
    for distance_step in range(1, reach_blocks + 1):
        left_keys, left_values = passed_along((k_normed, value_rows), "tok", distance_step)
        state_now = absorb(state_now, left_keys, left_values, first_row - distance_step * tok_rows)
        right_keys, right_values = passed_along((k_normed, value_rows), "tok", -distance_step)
        state_now = absorb(
            state_now, right_keys, right_values, first_row + distance_step * tok_rows
        )
    attended = state_now[2] / state_now[1][:, :, None]
    key_unit = unit_rows(k_normed)
    query_unit = unit_rows(q_normed)
    pre_keys = jnp.einsum("thd,hdf->htf", key_unit, fast_in, preferred_element_type=jnp.float32)
    gate_part = pre_keys[:, :, :fast_hid]
    lin_part = pre_keys[:, :, fast_hid:]
    sigmoid_gate = jax.nn.sigmoid(gate_part)
    swish_gate = gate_part * sigmoid_gate
    hidden = (swish_gate * lin_part).astype(jnp.bfloat16)
    value_float = value_rows.astype(jnp.float32)
    push_out = (-jnp.transpose(rate_out)[:, :, None] * value_float).astype(jnp.bfloat16)
    push_in = (-jnp.transpose(rate_in)[:, :, None] * value_float).astype(jnp.bfloat16)
    grad_out = jnp.einsum("htf,thd->hfd", hidden, push_out, preferred_element_type=jnp.float32)
    hidden_grad = jnp.einsum("thd,hfd->htf", push_in, fast_out, preferred_element_type=jnp.float32)
    d_gate = hidden_grad * lin_part * sigmoid_gate * (1.0 + gate_part * (1.0 - sigmoid_gate))
    d_lin = hidden_grad * swish_gate
    d_pre = jnp.concatenate([d_gate, d_lin], axis=2).astype(jnp.bfloat16)
    grad_in = jnp.einsum("thd,htf->hdf", key_unit, d_pre, preferred_element_type=jnp.float32)
    in_float = fast_in.astype(jnp.float32)
    out_float = fast_out.astype(jnp.float32)
    in_base = jnp.sqrt(jnp.sum(in_float * in_float, axis=1))
    out_base = jnp.sqrt(jnp.sum(out_float * out_float, axis=1))
    summed_in, summed_out = lax.psum((grad_in, grad_out), "tok")
    updated_in = in_float - summed_in
    updated_out = out_float - summed_out
    new_in = rescale(updated_in, in_base, jnp.sum(updated_in * updated_in, axis=1))
    new_out = rescale(updated_out, out_base, jnp.sum(updated_out * updated_out, axis=1))
    pre_query = jnp.einsum("thd,hdf->htf", query_unit, new_in, preferred_element_type=jnp.float32)
    query_gate = pre_query[:, :, :fast_hid]
    query_hidden = (query_gate * jax.nn.sigmoid(query_gate) * pre_query[:, :, fast_hid:]).astype(
        jnp.bfloat16
    )
    fast_result = jnp.einsum(
        "htf,hfd->htd", query_hidden, new_out, preferred_element_type=jnp.float32
    )
    combined = attended + fast_result
    return jnp.transpose(combined, (1, 0, 2)).astype(jnp.bfloat16)


VMEM_BYTES = 16 * 1024 * 1024
HIDDEN_MASK = -1e30
NT = (((1,), (1,)), ((), ()))


def exchanged(x, pairs):
    return lax.ppermute(x, "tok", pairs)


def nt_dot(a, b):
    return lax.dot_general(a, b, NT, preferred_element_type=jnp.float32)


def nn_dot(a, b):
    return jnp.dot(a, b, preferred_element_type=jnp.float32)


def in_vmem(kernel, name, scalars, arrays, after, out_shape, flops=0, scratch=()):
    specs = [pl.BlockSpec(memory_space=pltpu.SMEM)] * len(scalars)
    specs += [pl.BlockSpec(memory_space=pltpu.VMEM)] * len(arrays)
    specs += [pl.BlockSpec(memory_space=pl.ANY)] * len(after)
    return pl.pallas_call(
        kernel,
        out_shape=out_shape,
        in_specs=specs,
        out_specs=jax.tree.map(lambda _: pl.BlockSpec(memory_space=pltpu.VMEM), out_shape),
        scratch_shapes=scratch,
        compiler_params=pltpu.CompilerParams(vmem_limit_bytes=VMEM_BYTES),
        cost_estimate=pl.CostEstimate(flops=16 * flops, bytes_accessed=0, transcendentals=0),
        name=name,
    )(*scalars, *arrays, *after)


def head_at(place_ref, share, chip, i):
    return place_ref[3 + chip * share + i]


def pack_kernel(peers, first, count, width_all, fold, with_lone, place_ref, *refs):
    squares_ref, more_ref, q_gain_ref, k_gain_ref, rate_in_ref, rate_out_ref = refs[:6]
    q_ref, k_ref, v_ref = refs[6:9]
    outs = refs[-3 - peers : -3]
    aux_ref, q_scale_ref, k_scale_ref = refs[-3:]
    rows, dim = q_scale_ref.shape
    share = q_gain_ref.shape[0] // peers
    scales = lax.rsqrt((squares_ref[...] + more_ref[...]) / width_all + epsilon)
    q_scale_ref[...] = jnp.transpose(jnp.broadcast_to(scales[0:1] * fold, (dim, rows)))
    k_scale_ref[...] = jnp.transpose(jnp.broadcast_to(scales[1:2], (dim, rows)))
    aux_ref[...] = jnp.zeros_like(aux_ref)

    def normed(ref, scale_ref, gain_ref, head, some):
        gain = gain_ref[pl.ds(head, 1), :]
        scaled = ref[head, 0:some].astype(jnp.float32) * scale_ref[0:some] * gain
        return scaled.astype(jnp.bfloat16)

    def one_head(step, carry):
        for p in range(peers):
            c = place_ref[0] ^ p
            head = head_at(place_ref, share, c, first + step)
            outs[p][step, 0:rows, :] = normed(q_ref, q_scale_ref, q_gain_ref, head, rows)
            outs[p][step, rows : 2 * rows, :] = normed(
                k_ref, k_scale_ref, k_gain_ref, head, rows
            )
            for i in range(0, rows, 128):
                outs[p][step, 2 * rows + i : 2 * rows + i + 128, :] = jnp.transpose(
                    v_ref[head, i : i + 128, :]
                )
            at = 0
            for rate_ref in (rate_in_ref, rate_out_ref):
                rate = rate_ref[pl.ds(head, 1), :]
                high = rate.astype(jnp.bfloat16).astype(jnp.float32)
                for part in (high, rate - high):
                    for i in range(0, rows, 128):
                        aux_ref[at : at + 1, :] = part[:, i : i + 128]
                        at += 1
            if with_lone:
                for i in range(-(-share // count)):
                    head = head_at(place_ref, share, c, jnp.minimum(step + i * count, share - 1))
                    q0 = normed(q_ref, q_scale_ref, q_gain_ref, head, 16)
                    k0 = normed(k_ref, k_scale_ref, k_gain_ref, head, 16)
                    for at, array in enumerate((q0, k0, v_ref[head, 0:16])):
                        at += aux_ref.shape[0] // 2 + 3 * i
                        aux_ref[at : at + 1, :] = array.astype(jnp.float32)[0:1]
            some = outs[p].shape[1] - 3 * rows
            outs[p][step, 3 * rows :, :] = aux_ref[0:some, :].astype(jnp.bfloat16)
        return carry

    lax.fori_loop(0, count, one_head, 0)


def pack(place, sums, q, k, v, gains, rates, peers, aux_rows, first, count, width_all, fold):
    heads, rows, dim = q.shape
    out_shape = (count, 3 * rows + aux_rows // (2 if first else 1), dim)
    return in_vmem(
        functools.partial(pack_kernel, peers, first, count, width_all, fold, not first),
        "pack",
        [place],
        [*sums, *gains, *rates, q, k, v],
        [],
        [jax.ShapeDtypeStruct(out_shape, jnp.bfloat16)] * peers,
        scratch=[
            pltpu.VMEM((aux_rows, dim), jnp.float32),
            pltpu.VMEM((rows, dim), jnp.float32),
            pltpu.VMEM((rows, dim), jnp.float32),
        ],
    )


def stack_kernel(from_row, *refs):
    for p, ref in enumerate(refs[:-1]):
        refs[-1][p] = ref[:, from_row:, :]


def stacked(arrays, from_row):
    heads, rows, dim = arrays[0].shape
    return in_vmem(
        functools.partial(stack_kernel, from_row),
        "stack",
        [],
        arrays,
        [],
        jax.ShapeDtypeStruct((len(arrays), heads, rows - from_row, dim), jnp.bfloat16),
    )


def lone_kernel(place_ref, own_ref, other_ref, out_ref):
    extra = out_ref.shape[1]
    at = own_ref.shape[2] - extra
    mine = jnp.full(out_ref.shape, place_ref[1]) == 0
    own = own_ref[place_ref[0], :, at:, :].astype(jnp.float32)
    other = other_ref[place_ref[0], :, at:, :].astype(jnp.float32)
    out_ref[...] = jnp.where(mine, own, other).astype(jnp.bfloat16)


def lone_rows(place, own, other, rows):
    _, count, all_rows, dim = own.shape
    out_shape = (count, (all_rows - 2 * rows) // 2, dim)
    return in_vmem(
        lone_kernel,
        "lone_rows",
        [place],
        [own, other],
        [],
        jax.ShapeDtypeStruct(out_shape, jnp.bfloat16),
    )


def key_value_blocks(peers, rows, step, refs):
    for p in range(peers):
        yield p, True, refs[p].at[step, rows : 2 * rows], refs[p].at[step, 2 * rows :]
        yield p, False, refs[peers].at[p, step, 0:rows], refs[peers].at[p, step, rows:]


def grads_kernel(peers, rows, rate_rows, share, first, place_ref, in_ref, out_ref, *refs):
    grad_ref = refs[-1]
    hid = out_ref.shape[1]
    part = hid // 2
    own = pl.multiple_of(place_ref[1] * part, part)

    def one_head(step, carry):
        head = head_at(place_ref, share, place_ref[0], first + step)
        in_half = jnp.concatenate(
            [
                jnp.transpose(in_ref[head, :, pl.ds(at, part)].astype(jnp.float32))
                for at in (own, pl.multiple_of(hid + own, part))
            ],
            axis=0,
        ).astype(jnp.bfloat16)
        out_half = out_ref[head, pl.ds(own, part), :]
        sum_in = jnp.zeros((2 * part, in_half.shape[1]), jnp.float32)
        sum_out = jnp.zeros((part, in_half.shape[1]), jnp.float32)
        for _, _, keys, values in key_value_blocks(peers, rows, step, refs):
            k = keys[...].astype(jnp.float32)
            v_t = jnp.concatenate([values[at : at + 128, :] for at in range(0, rows, 128)], axis=1)
            aux = values[rows : rows + 16, :].astype(jnp.float32)

            def rate(at):
                both = aux[at : at + rate_rows] + aux[at + rate_rows : at + 2 * rate_rows]
                return jnp.concatenate([both[i : i + 1] for i in range(rate_rows)], axis=1)

            rate_in, rate_out = rate(0), rate(2 * rate_rows)
            unit = (k * lax.rsqrt(jnp.sum(k * k, axis=1, keepdims=True) + epsilon)).astype(
                jnp.bfloat16
            )
            pre = nt_dot(in_half, unit)
            gate, lin = pre[:part], pre[part:]
            sig = jax.nn.sigmoid(gate)
            swish = gate * sig
            pushed = (swish * lin * -rate_out).astype(jnp.bfloat16)
            hidden_grad = nn_dot(out_half, v_t) * -rate_in
            d_gate = hidden_grad * lin * sig * (1.0 + gate * (1.0 - sig))
            d_lin = hidden_grad * swish
            d_pre = jnp.concatenate([d_gate, d_lin], axis=0).astype(jnp.bfloat16)
            sum_in += nn_dot(d_pre, unit)
            sum_out += nt_dot(pushed, v_t)
        grad_ref[step, 0 : 2 * part, :] = sum_in.astype(jnp.bfloat16)
        grad_ref[step, 2 * part :, :] = sum_out.astype(jnp.bfloat16)
        return carry

    lax.fori_loop(0, grad_ref.shape[0], one_head, 0)


def gradients(place, fast_in, fast_out, packets, share, rows, first, after):
    _, hid, dim = fast_out.shape
    own, other = packets
    peers, heads = other.shape[:2]
    return in_vmem(
        functools.partial(grads_kernel, peers, rows, rows // 128, share, first),
        "gradients",
        [place],
        [fast_in, fast_out, *own, other],
        after,
        jax.ShapeDtypeStruct((heads, 3 * hid // 2, dim), jnp.bfloat16),
    )


def attend_kernel(peers, rows, share, first, fwd_heads, place_ref, window_ref, edge_ref, *refs):
    fwd_ref = refs[peers + 1]
    out_ref, extra_ref, k_scr, vt_scr, q_scr = refs[-5:]
    span = 2 * peers * rows
    dim = k_scr.shape[1]
    pad = fwd_ref.shape[1]
    chip, core, half = place_ref[0], place_ref[1], place_ref[2]
    base = half * span
    limit = span + 1 - half
    k_scr[span:, :] = jnp.zeros((k_scr.shape[0] - span, dim), k_scr.dtype)
    vt_scr[:, span:] = jnp.zeros((vt_scr.shape[0], vt_scr.shape[1] - span), vt_scr.dtype)
    vt_scr[dim:, :] = jnp.ones((vt_scr.shape[0] - dim, vt_scr.shape[1]), vt_scr.dtype)

    def one_head(step, carry):
        window = window_ref[head_at(place_ref, share, chip, first + step)]
        for p, own, keys, values in key_value_blocks(peers, rows, step, refs):
            at = pl.multiple_of(((chip ^ p) * 2 + (core if own else 1 - core)) * rows, rows)
            k_scr[pl.ds(at, rows), :] = keys[...]
            for i in range(0, rows, 128):
                vt_scr[0:dim, pl.ds(pl.multiple_of(at + i, 128), 128)] = values[i : i + 128, :]
        for p in range(peers):
            q_scr[chip ^ p] = refs[p][step, 0:rows, :]
        fwd = fwd_ref[lax.rem(first + step, fwd_heads)].astype(jnp.float32)
        turn = (first + step) // fwd_heads
        q_lone, k_lone, v_lone = (
            sum(
                jnp.where(turn == t, fwd[3 * t + i : 3 * t + i + 1], 0.0)
                for t in range(-(-share // fwd_heads))
            )
            for i in range(3)
        )
        k_scr[span : span + pad, :] = jnp.broadcast_to(k_lone, (pad, dim)).astype(jnp.bfloat16)
        vt_scr[0:dim, span : span + 128] = jnp.transpose(
            jnp.broadcast_to(v_lone, (128, dim))
        ).astype(jnp.bfloat16)

        def clip_start(place):
            start = jnp.zeros_like(place)
            for i in range(edge_ref.shape[0]):
                start = jnp.maximum(start, jnp.where(edge_ref[i] <= place, edge_ref[i], 0))
            return start

        def clip_stop(place):
            stop = jnp.full_like(place, base + limit)
            for i in range(edge_ref.shape[0]):
                stop = jnp.minimum(stop, jnp.where(edge_ref[i] > place, edge_ref[i], base + limit))
            return stop

        def lowest(place):
            return jnp.maximum(jnp.maximum(place - window, clip_start(place)), base) - base

        def highest(place):
            return jnp.minimum(place + window, clip_stop(place) - 1) - base

        def one_pair(i, carry):
            pair = []
            for c in (i, peers - 1 - i):
                start = (c * 2 + core) * rows
                place = base + start + lax.broadcasted_iota(jnp.int32, (1, rows), 1)
                from_key = lowest(base + start) // 128 * 128
                count = (highest(base + start + rows - 1) - from_key) // 256 + 1
                pair.append((c, lowest(place), highest(place), from_key, count))
            count = jnp.maximum(pair[0][4], pair[1][4])

            def variant(chunks):
                froms = [
                    pl.multiple_of(jnp.minimum(each[3], k_scr.shape[0] - chunks * 256), 128)
                    for each in pair
                ]
                key = lax.broadcasted_iota(jnp.int32, (256, rows), 0)
                scores = [[], []]
                tops = [None, None]
                for i in range(chunks):
                    for n, (each, at) in enumerate(zip(pair, froms)):
                        from_key = pl.multiple_of(at + i * 256, 128)
                        piece = nt_dot(k_scr[pl.ds(from_key, 256), :], q_scr[each[0]])
                        seen = (key >= each[1] - from_key) & (key <= each[2] - from_key)
                        piece = jnp.where(seen, piece, HIDDEN_MASK)
                        top = jnp.max(piece.reshape(32, 8, rows), axis=0)
                        tops[n] = top if i == 0 else jnp.maximum(tops[n], top)
                        scores[n].append(piece)
                tops = [jnp.max(top, axis=0, keepdims=True) for top in tops]
                totals = [0.0, 0.0]
                for i in range(chunks):
                    for n, at in enumerate(froms):
                        weights = jnp.exp2(scores[n][i] - tops[n]).astype(jnp.bfloat16)
                        from_key = pl.multiple_of(at + i * 256, 128)
                        totals[n] += nn_dot(vt_scr[:, pl.ds(from_key, 256)], weights)
                for each, total in zip(pair, totals):
                    attended = total[0:dim] * (1.0 / total[dim : dim + 1])
                    out_ref[each[0], step] = jnp.transpose(attended)

            for chunks in range(1, span // 256 + 2):

                @pl.when(count == chunks)
                def _(chunks=chunks):
                    variant(chunks)

            return carry

        lax.fori_loop(0, peers // 2, one_pair, 0)
        extra_ref[step] = jnp.zeros(extra_ref.shape[1:], jnp.float32)

        @pl.when((half == 0) & (core == 1))
        def _():
            near = span - HALF
            width = HALF + 128
            q = jnp.broadcast_to(q_lone, (pad, dim)).astype(jnp.bfloat16)
            scores = nt_dot(q, k_scr[near : near + width, :])
            key = near + lax.broadcasted_iota(jnp.int32, (1, width), 1)
            scores = jnp.where((key >= span - window) & (key <= span), scores, HIDDEN_MASK)
            top = jnp.max(scores, axis=1, keepdims=True)
            weights = jnp.exp2(scores - top).astype(jnp.bfloat16)
            total = nt_dot(weights, vt_scr[:, near : near + width])
            extra_ref[step] = total[:, 0:dim] / total[:, dim : dim + 1]
        return carry

    lax.fori_loop(0, extra_ref.shape[0], one_head, 0)


def attend(place, half_window, boundaries, packets, forwarded, share, rows, first, after):
    own, other = packets
    peers, heads = other.shape[:2]
    fwd_heads, pad, dim = forwarded.shape
    scr_rows = 2 * peers * rows + 256
    out_shapes = [(peers, heads, rows, dim), (heads, pad, dim)]
    return in_vmem(
        functools.partial(attend_kernel, peers, rows, share, first, fwd_heads),
        "attend",
        [place, half_window, boundaries],
        [*own, other, forwarded],
        after,
        [jax.ShapeDtypeStruct(shape, jnp.float32) for shape in out_shapes],
        flops=4 * heads * peers * rows * HALF * 2 * dim,
        scratch=[
            pltpu.VMEM((scr_rows, dim), jnp.bfloat16),
            pltpu.VMEM((dim + 16, scr_rows), jnp.bfloat16),
            pltpu.VMEM((peers, rows, dim), jnp.bfloat16),
        ],
    )


def finish_kernel(peers, share, first, unit_epsilon, place_ref, *refs):
    att_ref, base_in_ref, base_out_ref, own_ref, other_ref, patch_ref = refs[:6]
    queries = refs[6 : 6 + peers]
    outs = refs[-2 - peers : -2]
    grad_in_scr, grad_out_scr = refs[-2:]
    chip, core, half = place_ref[0], place_ref[1], place_ref[2]
    rows = att_ref.shape[2]
    hid = base_out_ref.shape[1]
    part = hid // 2

    def one_head(step, carry):
        head = head_at(place_ref, share, chip, first + step)
        for summed, lane in ((own_ref, core), (other_ref, 1 - core)):
            at = pl.multiple_of(lane * part, part)
            grad_in_scr[pl.ds(at, part), :] = summed[step, 0:part, :].astype(jnp.float32)
            grad_in_scr[pl.ds(hid + at, part), :] = summed[step, part : 2 * part, :].astype(jnp.float32)
            grad_out_scr[pl.ds(at, part), :] = summed[step, 2 * part :, :].astype(jnp.float32)

        def renewed(base, grad):
            base = base.astype(jnp.float32)
            updated = base - grad
            norm = jnp.sqrt(jnp.sum(base * base, axis=0, keepdims=True))
            squares = jnp.sum(updated * updated, axis=0, keepdims=True)
            return (updated * (norm / jnp.sqrt(squares + epsilon))).astype(jnp.bfloat16)

        new_in = renewed(base_in_ref[head], jnp.transpose(grad_in_scr[...]))
        new_out = renewed(base_out_ref[head], grad_out_scr[...])
        patch = patch_ref[step, 0:8, :][0:1]
        row = lax.broadcasted_iota(jnp.int32, (rows, 1), 0)
        for p in range(peers):
            q = queries[p][step, 0:rows, :].astype(jnp.float32)
            unit = (q * lax.rsqrt(jnp.sum(q * q, axis=1, keepdims=True) + unit_epsilon)).astype(
                jnp.bfloat16
            )
            pre = nn_dot(unit, new_in)
            gate = pre[:, :hid]
            hidden = (gate * jax.nn.sigmoid(gate) * pre[:, hid:]).astype(jnp.bfloat16)
            patched = (half == 1) & (core == 0) & (chip == p)
            attended = jnp.where(patched & (row == 0), patch, att_ref[chip ^ p, step])
            outs[p][step] = (attended + nn_dot(hidden, new_out)).astype(jnp.bfloat16)
        return carry

    lax.fori_loop(0, att_ref.shape[1], one_head, 0)


def finish(place, attended, fast_in, fast_out, sums, patch, own, share, first, unit_epsilon, after):
    peers, heads, rows, dim = attended.shape
    hid = fast_out.shape[1]
    return in_vmem(
        functools.partial(finish_kernel, peers, share, first, unit_epsilon),
        "finish",
        [place],
        [attended, fast_in, fast_out, *sums, patch, *own],
        after,
        [jax.ShapeDtypeStruct((heads, rows, dim), jnp.bfloat16)] * peers,
        flops=12 * heads * peers * rows * hid * dim,
        scratch=[pltpu.VMEM((2 * hid, dim), jnp.float32), pltpu.VMEM((hid, dim), jnp.float32)],
    )


def place_kernel(peers, chunks, share, place_ref, *refs):
    pieces, out_ref, sems = refs[:-2], refs[-2], refs[-1]
    copies = []
    for n, (first, heads) in enumerate(chunks):
        for p in range(peers):
            for i in range(heads):
                head = head_at(place_ref, share, place_ref[0] ^ p, first + i)
                copies.append(
                    pltpu.make_async_copy(
                        pieces[n * peers + p].at[i], out_ref.at[head], sems.at[len(copies)]
                    )
                )
    for copy in copies:
        copy.start()
    for copy in copies:
        copy.wait()


def put_in_place(place, pieces, peers, chunks, share):
    _, rows, dim = pieces[0].shape
    return pl.pallas_call(
        functools.partial(place_kernel, peers, chunks, share),
        out_shape=jax.ShapeDtypeStruct((peers * share, rows, dim), jnp.bfloat16),
        in_specs=[pl.BlockSpec(memory_space=pltpu.SMEM)]
        + [pl.BlockSpec(memory_space=pltpu.VMEM)] * len(pieces),
        out_specs=pl.BlockSpec(memory_space=pl.ANY),
        scratch_shapes=[pltpu.SemaphoreType.DMA((peers * share,))],
        compiler_params=pltpu.CompilerParams(vmem_limit_bytes=VMEM_BYTES),
        name="put_in_place",
    )(place, *pieces)


def regrouping(tok_peers, rows, heads, dim, hid):
    half_peers = tok_peers // 2
    peers = math.gcd(half_peers, heads)
    fits = tok_peers % 2 == 0 and half_peers * rows == 2 * HALF
    fits = fits and half_peers == 2 * peers and peers & (peers - 1) == 0
    fits = fits and rows % 256 == 0 and dim == 128 and hid % 256 == 0
    return peers if fits else 0


def regrouped_body(
    peers,
    query_rows,
    key_rows,
    value_rows,
    query_gain,
    key_gain,
    rate_in,
    rate_out,
    fast_in,
    fast_out,
    half_window,
    boundaries,
):
    rows, heads, dim = query_rows.shape
    share = heads // peers
    tok_peers = lax.axis_size("tok")
    half_peers = tok_peers // 2
    width_all = heads * dim * lax.axis_size("head")
    chunks = [(0, (share + 1) // 2), ((share + 1) // 2, share // 2)]
    aux_rows = 2 * -(-max(4 * (rows // 128), 3 * -(-share // chunks[0][1])) // 16) * 16
    own_index = lax.axis_index("tok")
    half = own_index // half_peers
    chip = own_index % half_peers // 2
    core = own_index % 2
    number = jnp.arange(heads, dtype=jnp.int32)
    order = half_window * heads + number
    rank = jnp.sum((order[None, :] > order[:, None]).astype(jnp.int32), axis=1)
    turn, seat = rank // peers, rank % peers
    taker = jnp.where(turn % 2 == 0, seat, peers - 1 - seat)
    slot = taker * share + turn
    table = jnp.sum(jnp.where(slot[:, None] == number[None, :], number[:, None], 0), axis=0)
    place = jnp.concatenate([jnp.stack([chip, core, half]).astype(jnp.int32), table])

    def dealt(sent):
        pairs = [
            [(t, t // half_peers * half_peers + ((t % half_peers) ^ (2 * p))) for t in range(tok_peers)]
            for p in range(peers)
        ]
        return [sent[0]] + [exchanged(sent[p], pairs[p]) for p in range(1, peers)]

    core_pairs = [(t, t ^ 1) for t in range(tok_peers)]
    half_pairs = [(t, (t + half_peers) % tok_peers) for t in range(tok_peers)]
    forward_pairs = [(t + half_peers, t) for t in range(half_peers)]
    back_pairs = [(t, t - 1 + half_peers) for t in range(half_peers) if t % 2 == 1]

    q = jnp.transpose(query_rows, (1, 0, 2))
    k = jnp.transpose(key_rows, (1, 0, 2))
    v = jnp.transpose(value_rows, (1, 0, 2))
    q_float = q.astype(jnp.float32)
    k_float = k.astype(jnp.float32)
    squares = jnp.stack(
        [jnp.sum(q_float * q_float, axis=(0, 2)), jnp.sum(k_float * k_float, axis=(0, 2))]
    )
    if lax.axis_size("head") == 2:
        sums = (squares, lax.ppermute(squares, "head", [(0, 1), (1, 0)]))
    else:
        sums = (lax.psum(squares, "head"), jnp.zeros_like(squares))
    fold = math.log2(math.e) / math.sqrt(dim)
    sent = [
        pack(
            place,
            sums,
            q,
            k,
            v,
            (query_gain, key_gain),
            (rate_in, rate_out),
            peers,
            aux_rows,
            first,
            count,
            width_all,
            fold,
        )
        for first, count in chunks
    ]
    received = []
    for each in sent:
        if received:
            each = [lax.optimization_barrier(pair)[0] for pair in zip(each, received[-1])]
        received.append(dealt(each))
    def finished(ready, after):
        attended, sums, patch, own, first = ready
        return finish(
            place,
            attended,
            fast_in,
            fast_out,
            sums,
            patch,
            own,
            share,
            first,
            epsilon * fold * fold,
            after,
        )

    forwarded = ready = None
    pieces = []
    for (first, count), own in zip(chunks, received):
        if ready:
            *own, _ = lax.optimization_barrier((*own, ready[1][0]))
        else:
            own = lax.optimization_barrier((*own, *sent[-1]))[:peers]
        stack = stacked(own, rows)
        packets = (own, exchanged(stack, core_pairs))
        if forwarded is None:
            forwarded = exchanged(lone_rows(place, stack, packets[1], rows), forward_pairs)
        before = [ready[0]] if ready else []
        grad = gradients(place, fast_in, fast_out, packets, share, rows, first, before)
        from_half = exchanged(grad, half_pairs)
        before = [grad]
        if not ready and len(received) > 1:
            before += received[1][1:2]
        if ready:
            outs = finished(ready, [grad])
            before.append(outs[0])
            pieces = pieces + dealt(outs)
        attended, extra = attend(
            place,
            half_window,
            boundaries,
            packets,
            forwarded,
            share,
            rows,
            first,
            before,
        )
        patch = exchanged(extra, back_pairs)
        from_half, _ = lax.optimization_barrier((from_half, attended))
        own_sum = (grad.astype(jnp.float32) + from_half.astype(jnp.float32)).astype(jnp.bfloat16)
        ready = (attended, (own_sum, exchanged(own_sum, core_pairs)), patch, own, first)
    pieces = pieces + dealt(finished(ready, pieces[:-1]))
    whole = put_in_place(place, pieces, peers, chunks, share)
    return jnp.transpose(whole, (1, 0, 2))


def body(query_rows, *others):
    rows, heads, dim = query_rows.shape
    hid = others[7].shape[1]
    peers = regrouping(lax.axis_size("tok"), rows, heads, dim, hid)
    if peers:
        return regrouped_body(peers, query_rows, *others)
    return sliding_body(query_rows, *others)


def solution(mesh):
    in_specs = (
        P("tok", "head", None),
        P("tok", "head", None),
        P("tok", "head", None),
        P("head", None),
        P("head", None),
        P("head", "tok"),
        P("head", "tok"),
        P("head", None, None),
        P("head", None, None),
        P("head"),
        P(),
    )
    out_specs = P("tok", "head", None)
    return jax.shard_map(body, mesh=mesh, in_specs=in_specs, out_specs=out_specs, check_vma=False)
```
